32 devices in a mesh: bead: 4 (over y, x), space: 8 (over z, core).
Axes of the slice: x: 2, y: 2, z: 4, core: 2. Of those that a mesh axis runs over, the one named last changes fastest.
Arguments:
- positions: float32 [32, 3, 128, 128], P('bead', None, 'space'), may hold values from -0.1 to 1.1
- momenta: float32 [32, 3, 128, 128], P('bead', None, 'space'), may hold values from -6 to 6
- molecules: int32 [128, 42, 3], P('space'), may hold values from 0 to 128, as said below
Outputs:
- final_positions: float32 [32, 3, 128, 128], P('bead', None, 'space')
- final_momenta: float32 [32, 3, 128, 128], P('bead', None, 'space')
The draws below stay inside these ranges and needn't reach their ends.
Inputs may be any that keep to these rules, and one draw needn't show every extreme that they name: In each cell, the slots of all listed atoms differ; used molecules come first and unused ones carry 128 in all three places; each cell has 21 to 42 used molecules.
All inputs are finite; a program needn't handle non-finite values.
Results may differ from the reference program's by a relative error of at most 0.0003.
Values sent between devices are 32-bit elements; how exact they have to be, the bound alone decides.
No kernel may reach another device: no remote copies, remote signals or barrier semaphores. Data moves between devices by JAX's collectives and lax.ppermute only.
A program may use at most 64 MiB of HBM per device.

```python
import jax
import jax.numpy as jnp
from jax import lax

BEADS = 32
SLOTS = 128
MOLS = 42
REACH = 1
NEIGH = 3
CELLS = 128


def molecule_table(key):
    base_key = jax.random.fold_in(key, 17)
    count_key, full_key, order_key = jax.random.split(base_key, 3)
    counts = jax.random.randint(count_key, (CELLS,), MOLS // 2, MOLS + 1)
    full_cell = jax.random.randint(full_key, (), 0, CELLS)
    counts = jnp.where(jnp.arange(CELLS) == full_cell, MOLS, counts)
    slot_rows = jnp.broadcast_to(jnp.arange(SLOTS, dtype=jnp.int32), (CELLS, SLOTS))
    shuffled = jax.random.permutation(order_key, slot_rows, axis=1, independent=True)
    chosen = shuffled[:, :3 * MOLS].reshape(CELLS, MOLS, 3)
    used = jnp.arange(MOLS)[None, :, None] < counts[:, None, None]
    return jnp.where(used, chosen, SLOTS).astype(jnp.int32)


def draw_molecules(key, part):
    return molecule_table(key)


def draw_momenta(key, part):
    moment_key = jax.random.fold_in(key, 73)
    sign_key, size_key = jax.random.split(moment_key, 2)
    shape = (BEADS, 3, CELLS, SLOTS)
    flips = jax.random.bernoulli(sign_key, 0.5, shape)
    signs = jnp.where(flips, 1.0, -1.0).astype(jnp.float32)
    magnitude = jax.random.uniform(size_key, shape, jnp.float32, 4.5, 6.0)
    values = signs * magnitude
    return values.astype(jnp.float32)


def draw_positions(key, part):
    table = molecule_table(key)
    place_key = jax.random.fold_in(key, 41)
    centre_key, first_key, second_key, noise_key = jax.random.split(place_key, 4)
    centres = jax.random.uniform(centre_key, (CELLS, SLOTS, 3), jnp.float32, 0.05, 0.95)
    cell_rows = jnp.broadcast_to(jnp.arange(CELLS)[:, None], (CELLS, MOLS))
    oxygen_slots = jnp.minimum(table[:, :, 0], SLOTS - 1)
    oxygen_sites = centres[cell_rows, oxygen_slots]
    first_dir = jax.random.normal(first_key, (CELLS, MOLS, 3), jnp.float32)
    first_dir = first_dir / (jnp.sqrt(jnp.sum(first_dir * first_dir, axis=2, keepdims=True)) + 1e-06)
    other_dir = jax.random.normal(second_key, (CELLS, MOLS, 3), jnp.float32)
    other_dir = other_dir - jnp.sum(other_dir * first_dir, axis=2, keepdims=True) * first_dir
    other_dir = other_dir / (jnp.sqrt(jnp.sum(other_dir * other_dir, axis=2, keepdims=True)) + 1e-06)
    second_dir = jnp.cos(1.8239) * first_dir + jnp.sin(1.8239) * other_dir
    first_site = oxygen_sites + 0.09 * first_dir
    second_site = oxygen_sites + 0.09 * second_dir
    centres = centres.at[cell_rows, table[:, :, 1]].set(first_site, mode='drop')
    centres = centres.at[cell_rows, table[:, :, 2]].set(second_site, mode='drop')
    spread = 0.015 * jnp.clip(jax.random.normal(noise_key, (BEADS, CELLS, SLOTS, 3), jnp.float32), -4.0, 4.0)
    sites = jnp.clip(centres[None] + spread, -0.1, 1.1)
    return jnp.transpose(sites, (0, 3, 1, 2)).astype(jnp.float32)


def setup_inputs(seed: int = 0) -> dict:
    arg_keys = jax.random.split(jax.random.key(seed), 4)
    positions = draw_positions(jax.random.fold_in(arg_keys[3], 71), 0)
    momenta = draw_momenta(jax.random.fold_in(arg_keys[3], 71), 0)
    molecules = draw_molecules(jax.random.fold_in(arg_keys[3], 71), 0)
    return {"positions": positions, "momenta": momenta, "molecules": molecules}


charge_oxygen = -0.8476
charge_hydrogen = 0.4238
coulomb_scale = 24.0
coulomb_soft = 0.004
well_depth = 0.02
sigma_square = 0.0841
lennard_soft = 0.04
bond_stiffness = 20000.0
bond_square = 0.0081
angle_stiffness = 5000.0
angle_square = 0.0204
cycle_frequency = 60.0
outer_step = 0.02
inner_step = 0.01

def entry_shifts(reach):
    return [0] + list(range(-reach, 0)) + list(range(1, reach + 1))

def cell_tables(molecules, slot_count):
    slot_ids = jnp.arange(slot_count, dtype=jnp.int32)
    one_hot = (jnp.transpose(molecules, (0, 2, 1))[..., None] == slot_ids).astype(jnp.float32)
    members = lax.optimization_barrier(jnp.sum(one_hot, axis=1))
    oxygen = lax.optimization_barrier(jnp.sum(one_hot[:, 0], axis=1))
    hydrogen = lax.optimization_barrier(jnp.sum(one_hot[:, 1] + one_hot[:, 2], axis=1))
    charges = charge_oxygen * oxygen + charge_hydrogen * hydrogen
    masses = 1.0 + 15.0 * oxygen
    same_molecule = jnp.einsum('cmi,cmj->cij', members, members, precision=lax.Precision.HIGHEST)
    return (one_hot, oxygen, charges, masses, 1.0 - same_molecule)

def mode_tables(beads):
    bead_ids = jnp.arange(beads, dtype=jnp.int32)
    products = bead_ids[:, None] * bead_ids[None, :] % beads
    angles = 2.0 * jnp.pi / beads * products.astype(jnp.float32)
    columns = bead_ids[None, :]
    half_beads = beads // 2
    transform = jnp.where(columns == 0, jnp.sqrt(1.0 / beads), jnp.where(columns < half_beads, jnp.sqrt(2.0 / beads) * jnp.cos(angles), jnp.where(columns == half_beads, jnp.sqrt(1.0 / beads) * jnp.cos(angles), jnp.sqrt(2.0 / beads) * jnp.sin(angles))))
    transform = transform.astype(jnp.float32)
    frequencies = 2.0 * cycle_frequency * jnp.sin(jnp.pi * bead_ids.astype(jnp.float32) / beads)
    cosines = jnp.cos(frequencies * inner_step)
    spring_factor = frequencies * jnp.sin(frequencies * inner_step)
    safe_freq = jnp.where(bead_ids == 0, 1.0, frequencies)
    drift_factor = jnp.where(bead_ids == 0, inner_step, jnp.sin(frequencies * inner_step) / safe_freq)
    return (transform, cosines, spring_factor, drift_factor)

def pair_force(own_atoms, peer_atoms, own_charge, peer_charge, own_oxygen, peer_oxygen, exclusion):
    gap_x = own_atoms[0][:, :, None] - peer_atoms[0][:, None, :]
    gap_y = own_atoms[1][:, :, None] - peer_atoms[1][:, None, :]
    gap_z = own_atoms[2][:, :, None] - peer_atoms[2][:, None, :]
    squares = gap_x * gap_x + gap_y * gap_y + gap_z * gap_z
    charge_pair = own_charge[:, :, None] * peer_charge[:, None, :]
    oxygen_pair = own_oxygen[:, :, None] * peer_oxygen[:, None, :]
    inverse_coulomb = 1.0 / (squares + coulomb_soft)
    coulomb = coulomb_scale * charge_pair * inverse_coulomb * jnp.sqrt(inverse_coulomb)
    inverse_lennard = 1.0 / (squares + lennard_soft)
    sigma_ratio = sigma_square * inverse_lennard
    ratio_cubed = sigma_ratio * sigma_ratio * sigma_ratio
    lennard = 24.0 * well_depth * oxygen_pair * (2.0 * ratio_cubed * ratio_cubed - ratio_cubed) * inverse_lennard
    strength = coulomb + lennard
    if exclusion is not None:
        strength = strength * exclusion
    totals = lax.optimization_barrier(jnp.sum(strength, axis=2))
    weighted = jnp.einsum('nij,knj->kni', strength, peer_atoms, precision=lax.Precision.HIGHEST)
    return own_atoms * totals[None] - weighted

def bond_forces(coords, one_hot):
    parts = jnp.einsum('ctms,bkcs->tbkcm', one_hot, coords, precision=lax.Precision.HIGHEST)
    first_bond = parts[0] - parts[1]
    second_bond = parts[0] - parts[2]
    third_bond = parts[1] - parts[2]
    first_pull = bond_stiffness * (lax.optimization_barrier(jnp.sum(first_bond * first_bond, axis=1, keepdims=True)) - bond_square)
    second_pull = bond_stiffness * (lax.optimization_barrier(jnp.sum(second_bond * second_bond, axis=1, keepdims=True)) - bond_square)
    third_pull = angle_stiffness * (lax.optimization_barrier(jnp.sum(third_bond * third_bond, axis=1, keepdims=True)) - angle_square)
    on_parts = jnp.stack([-first_pull * first_bond - second_pull * second_bond, first_pull * first_bond - third_pull * third_bond, second_pull * second_bond + third_pull * third_bond])
    return jnp.einsum('ctms,tbkcm->bkcs', one_hot, on_parts, precision=lax.Precision.HIGHEST)

def free_polymer(coords, moments, masses, transform, cosines, spring_factor, drift_factor):
    shape = coords.shape
    coord_modes = jnp.dot(transform.T, coords.reshape(shape[0], -1), precision=lax.Precision.HIGHEST).reshape(shape)
    moment_modes = jnp.dot(transform.T, moments.reshape(shape[0], -1), precision=lax.Precision.HIGHEST).reshape(shape)
    weight = masses[None, None]
    cos_col = cosines[:, None, None, None]
    spring_col = spring_factor[:, None, None, None]
    drift_col = drift_factor[:, None, None, None]
    new_moments = cos_col * moment_modes - spring_col * weight * coord_modes
    new_coords = drift_col * moment_modes / weight + cos_col * coord_modes
    coords_out = jnp.dot(transform, new_coords.reshape(shape[0], -1), precision=lax.Precision.HIGHEST).reshape(shape)
    moments_out = jnp.dot(transform, new_moments.reshape(shape[0], -1), precision=lax.Precision.HIGHEST).reshape(shape)
    return (coords_out, moments_out)

def inter_forces(coords, charges, oxygen, exclusion):
    unit_x = jnp.array([1.0, 0.0, 0.0], dtype=jnp.float32)[:, None, None]
    shifts = entry_shifts(REACH)

    def per_cell(cell_index):
        own_atoms = jnp.swapaxes(lax.dynamic_index_in_dim(coords, cell_index, 2, keepdims=False), 0, 1)
        total_force = jnp.zeros_like(own_atoms)
        for entry_index in range(NEIGH):
            shift_cells = shifts[entry_index]
            peer_cell = ((cell_index + shift_cells) % CELLS).astype(jnp.int32)
            peer_atoms = jnp.swapaxes(lax.dynamic_index_in_dim(coords, peer_cell, 2, keepdims=False), 0, 1)
            peer_atoms = peer_atoms + float(shift_cells) * unit_x
            excluded = exclusion[cell_index][None] if entry_index == 0 else None
            total_force = total_force + pair_force(own_atoms, peer_atoms, charges[cell_index][None], charges[peer_cell][None], oxygen[cell_index][None], oxygen[peer_cell][None], excluded)
        return jnp.swapaxes(total_force, 0, 1)
    forces = lax.map(per_cell, jnp.arange(CELLS, dtype=jnp.int32))
    return jnp.transpose(forces, (1, 2, 0, 3))

def reference(positions, momenta, molecules):
    one_hot, oxygen, charges, masses, exclusion = cell_tables(molecules, SLOTS)
    transform, cosines, spring_factor, drift_factor = mode_tables(BEADS)
    coords = positions
    moments = momenta
    outer_force = inter_forces(coords, charges, oxygen, exclusion)
    inner_force = bond_forces(coords, one_hot)
    for outer_index in range(1):
        moments = moments + 0.5 * outer_step * outer_force
        for inner_index in range(2):
            moments = moments + 0.5 * inner_step * inner_force
            coords, moments = free_polymer(coords, moments, masses, transform, cosines, spring_factor, drift_factor)
            inner_force = bond_forces(coords, one_hot)
            moments = moments + 0.5 * inner_step * inner_force
        outer_force = inter_forces(coords, charges, oxygen, exclusion)
        moments = moments + 0.5 * outer_step * outer_force
    return (coords, moments)
```

```python
import functools

import jax
import jax.numpy as jnp
import ml_dtypes
import numpy as np
from jax import lax
from jax.experimental import pallas as pl
from jax.experimental.pallas import tpu as pltpu
from jax.sharding import PartitionSpec as P

charge_oxygen = -0.8476
charge_hydrogen = 0.4238
coulomb_scale = 24.0
coulomb_soft = 0.004
well_depth = 0.02
sigma_square = 0.0841
lennard_soft = 0.04
bond_stiffness = 20000.0
bond_square = 0.0081
angle_stiffness = 5000.0
angle_square = 0.0204
cycle_frequency = 60.0
outer_step = 0.02
inner_step = 0.01
oxygen_mass = 16.0

REACH = 1
X_HALO = 2 * REACH
P_HALO = REACH

F32 = jnp.float32
BF16 = jnp.bfloat16


def rounded(a):
    return a.astype(BF16).astype(F32)


def split3(a):
    high = rounded(a)
    rest = a - high
    mid = rounded(rest)
    return high, mid, rest - mid


def two_part(a):
    high = rounded(a)
    return high + rounded(a - high)


def dot_nn(a, b):
    return lax.dot_general(a, b, (((1,), (0,)), ((), ())), preferred_element_type=F32)


def dot_nt(a, b):
    return lax.dot_general(a, b, (((1,), (1,)), ((), ())), preferred_element_type=F32)


def propagator(beads, beads_dev):
    j = np.arange(beads)
    angles = 2.0 * np.pi * ((j[:, None] * j[None, :]) % beads) / beads
    half = beads // 2
    col = j[None, :]
    u = np.where(
        col == 0,
        np.sqrt(1.0 / beads),
        np.where(
            col < half,
            np.sqrt(2.0 / beads) * np.cos(angles),
            np.where(
                col == half,
                np.sqrt(1.0 / beads) * np.cos(angles),
                np.sqrt(2.0 / beads) * np.sin(angles),
            ),
        ),
    )
    w = 2.0 * cycle_frequency * np.sin(np.pi * j / beads)
    cosines = np.cos(w * inner_step)
    spring = w * np.sin(w * inner_step)
    drift = np.where(j == 0, inner_step, np.sin(w * inner_step) / np.where(j == 0, 1.0, w))
    k = j // beads_dev
    i = j % beads_dev
    index = (beads_dev * (k[None, :] - k[:, None]) + i[:, None] - i[None, :]) % beads

    def circulant(values):
        return ((u * values) @ u.T)[:, 0][index]

    a = circulant(cosines)
    whole = np.block([[a, circulant(drift)], [-circulant(spring), a]])
    high = whole.astype(ml_dtypes.bfloat16)
    rest = whole - high.astype(np.float64)
    mid = rest.astype(ml_dtypes.bfloat16)
    low = (rest - mid.astype(np.float64)).astype(ml_dtypes.bfloat16)
    return np.concatenate([high, high, mid, mid, high, low], axis=1)


def pack_kernel(nb, group, lb, cells, b_ref, x_ref, p_ref, *outs):
    b = b_ref[0]
    xs, ps, es = outs[:nb], outs[nb : 2 * nb], outs[2 * nb :]

    def take(ref, comp, cell):
        return ref[pl.ds(comp * cells + cell, lb, stride=3 * cells), :]

    for k in range(nb):
        target = lax.rem(b + k, nb)
        for ref, dst, halo in ((x_ref, xs[k], X_HALO), (p_ref, ps[k], P_HALO)):
            for w in range(group + 2 * halo):
                cell = jnp.clip(target * group - halo + w, 0, cells - 1)
                for comp in range(3):
                    dst[pl.ds((w * 3 + comp) * lb, lb), :] = take(ref, comp, cell)
    for j in range(nb):
        target = lax.rem(b - j + nb, nb)
        left = target * group < X_HALO
        base = jnp.where(left, cells - X_HALO, 0)
        for w in range(X_HALO):
            for comp in range(3):
                es[j][pl.ds((w * 3 + comp) * lb, lb), :] = take(x_ref, comp, base + w)
        cell = jnp.where(left, cells - P_HALO, 0)
        for comp in range(3):
            es[j][pl.ds((X_HALO * 3 + comp) * lb, lb), :] = take(p_ref, comp, cell)


def table_kernel(window, slots, mols, lane_ref, perm_ref, charge_ref):
    row = lax.broadcasted_iota(jnp.int32, (slots, slots), 0).astype(F32)
    col = lax.broadcasted_iota(jnp.int32, (slots, slots), 1).astype(F32)
    before = (col < row).astype(BF16)
    upper = (row < col).astype(BF16)
    ones = jnp.ones((slots, slots), BF16)
    lanes = lane_ref[...].astype(F32)
    lane = lax.broadcasted_iota(jnp.int32, lanes.shape, 1)
    unit = jnp.where(lane < mols, charge_oxygen / charge_hydrogen, 1.0)
    charge_ref[...] = jnp.where(lanes < slots, unit, 0.0)
    far = 4.0 * slots
    for w in range(window):
        key = jnp.broadcast_to(lanes[w : w + 1], (8, slots))
        free = key >= slots
        rank = dot_nn(free.astype(F32).astype(BF16), upper)
        key = jnp.where(free, far + rank, key)[0:1]
        held = (row == key).astype(F32).astype(BF16)
        used = dot_nn(held, ones)
        count = dot_nn(before, used.astype(BF16))
        slot_key = jnp.where(used > 0.5, row, far + row - count)
        perm_ref[w] = (slot_key == key).astype(F32).astype(BF16)


def put_tiles(scratch, slot, beads, rows):
    for index, value in rows:
        scratch[pl.ds(slot * beads * 8 + index, beads, stride=8), :] = value


def build_tiles(tl, ts, tn, slot, beads, x, y, z):
    ya = two_part(y - 0.5)
    za = two_part(z - 0.5)
    xa = two_part(x - 1.0)
    xb = two_part(x)
    side = ya * ya + za * za
    na = side + xa * xa
    nb = side + xb * xb

    def parts(n):
        high = two_part(n)
        return high, n - high

    la, lb = parts(na + coulomb_soft)
    put_tiles(
        tl, slot, beads, ((0, -2.0 * xa), (1, -2.0 * ya), (2, -2.0 * za), (3, la), (4, lb))
    )
    sa, sb = parts(na)
    put_tiles(ts, slot, beads, ((0, xa), (1, ya), (2, za), (5, sa), (6, sb)))
    ba, bb = parts(nb)
    put_tiles(tn, slot, beads, ((0, xb), (1, ya), (2, za), (5, ba), (6, bb)))


def pair_forces(tl, ts, tn, out, keep, q_ref, q_first, count, mols, beads, slots):
    orows = -(-mols // 8) * 8
    pair_scale = coulomb_scale * charge_hydrogen * charge_hydrogen
    k3 = sigma_square**3
    lj_a = 24.0 * well_depth * 2.0 * k3 * k3
    lj_b = 24.0 * well_depth * k3
    row8 = lax.broadcasted_iota(jnp.int32, (8, slots), 0)
    lane8 = lax.broadcasted_iota(jnp.int32, (8, slots), 1)
    left_rows = row8 < 5
    left_fill = jnp.where((row8 == 5) | (row8 == 6), 1.0, 0.0)
    right_rows = (row8 < 3) | (row8 == 5) | (row8 == 6)
    right_fill = jnp.where((row8 == 3) | (row8 == 4), 1.0, 0.0)
    own_lanes = lane8 < mols
    lj_row = lax.broadcasted_iota(jnp.int32, (orows, slots), 0)
    lj_lane = lax.broadcasted_iota(jnp.int32, (orows, slots), 1)
    lj_keep = (lj_row != lj_lane).astype(F32)
    lj_pad = jnp.zeros((slots - orows, slots), BF16)

    def halves(tile):
        high = rounded(tile)
        return high, tile - high

    def stack(*tiles):
        return jnp.concatenate(tiles, axis=0).astype(BF16)

    def assemble(sums, tile, scale):
        total = sums[0:8] + sums[8:16]
        return (tile * total[3:4] - total) * scale

    def bead_step(r, carry):
        def load(ref, w):
            return ref[pl.ds(pl.multiple_of((w * beads + r) * 8, 8), 8), :]

        acc = None
        for c in range(count - 1):
            inner = c >= 1
            back = c + 1 <= count - 2
            qc = q_ref[q_first + c : q_first + c + 1, :]
            qn = q_ref[q_first + c + 1 : q_first + c + 2, :]
            oc = (qc < -1.5).astype(F32)
            on = (qn < -1.5).astype(F32)
            tile_l = jnp.where(left_rows, load(tl, c), left_fill)
            lh, lm = halves(tile_l)
            left = stack(lh, lh, lm, lm).T
            tile_s = jnp.where(right_rows, load(ts, c), right_fill)
            sh, sm = halves(tile_s)
            tile_n = jnp.where(right_rows, load(tn, c + 1), right_fill)
            nh, nm = halves(tile_n)
            right_n = stack(nh, nm, nh, nm)
            if inner:
                right = jnp.concatenate([stack(sh, sm, sh, sm), right_n], axis=1)
            else:
                right = right_n
            squares = dot_nn(left, right)
            root = lax.rsqrt(squares)
            strength = root * root * root
            if inner:
                strength = jnp.concatenate(
                    [strength[:, :slots] * keep[...], strength[:, slots:]], axis=1
                )
            g_high = strength.astype(BF16)
            g_low = (strength - g_high.astype(F32)).astype(BF16)
            rc = stack(sh * qc, sm * qc)
            tile_o = jnp.where(own_lanes, tile_s, pltpu.roll(tile_n, mols, 1))
            oh, om = halves(tile_o)
            o_pack = jnp.where(
                own_lanes, oc, jnp.where(lane8 < 2 * mols, pltpu.roll(
                    jnp.broadcast_to(on, (8, slots)), mols, 1), 0.0)
            )
            lj_squares = dot_nn(left[:orows], stack(oh, om, oh, om))
            lj_root = lax.rsqrt(lj_squares + (lennard_soft - coulomb_soft))
            inv = lj_root * lj_root
            cube = inv * inv * inv
            lj = (cube * lj_a - lj_b) * (cube * inv) * lj_keep
            lj_high = lj.astype(BF16)
            lj_low = (lj - lj_high.astype(F32)).astype(BF16)
            lj_high = jnp.concatenate([lj_high, lj_pad], axis=0)
            lj_low = jnp.concatenate([lj_low, lj_pad], axis=0)
            if inner:
                rn = stack(nh * qn, nm * qn)
                both = jnp.concatenate([rc, rn], axis=1)
                sums = dot_nt(both, g_high) + dot_nt(both, g_low)
                force = assemble(sums, tile_s, pair_scale * qc)
                ro = stack(oh * o_pack, om * o_pack)
                lj_sums = dot_nt(ro, lj_high) + dot_nt(ro, lj_low)
                force = force + assemble(lj_sums, tile_s, oc)
                if acc is not None:
                    force = force + acc
                out[pl.ds(pl.multiple_of(((c - 1) * beads + r) * 8, 8), 8), :] = force
            if back:
                gh = g_high[:, slots:] if inner else g_high
                gl = g_low[:, slots:] if inner else g_low
                sums = dot_nn(rc, gh) + dot_nn(rc, gl)
                acc = assemble(sums, tile_n, pair_scale * qn)
                so = stack(sh * oc, sm * oc)
                lj_sums = dot_nn(so, lj_high) + dot_nn(so, lj_low)
                lj_sums = pltpu.roll(lj_sums, slots - mols, 1)
                acc = acc + assemble(lj_sums, tile_n, on)
        return carry

    lax.fori_loop(0, beads, bead_step, 0)


def fill_keep(keep, mols, slots):
    i = lax.broadcasted_iota(jnp.int32, (slots, slots), 0)
    j = lax.broadcasted_iota(jnp.int32, (slots, slots), 1)
    i = jnp.where(i >= 2 * mols, i - 2 * mols, jnp.where(i >= mols, i - mols, i))
    j = jnp.where(j >= 2 * mols, j - 2 * mols, jnp.where(j >= mols, j - mols, j))
    keep[...] = (i != j).astype(F32)


def permuted(rows, perm):
    n = rows.shape[0]
    stacked = jnp.concatenate(split3(rows), axis=0).astype(BF16)
    moved = dot_nn(stacked, perm)
    return moved[:n] + moved[n : 2 * n] + moved[2 * n :]


def unpermuted(rows, perm):
    n = rows.shape[0]
    stacked = jnp.concatenate(split3(rows), axis=0).astype(BF16)
    moved = dot_nt(stacked, perm)
    return moved[:n] + moved[n : 2 * n] + moved[2 * n :]


def outer_kernel(nb, group, lb, cells, mols, slots, b_ref, *refs):
    xs, es = refs[:nb], refs[nb : 2 * nb]
    perm_ref, q_ref, x_out, f_out, tl, ts, tn, ft, keep = refs[2 * nb :]
    beads = nb * lb
    window = group + 2 * X_HALO
    b = b_ref[0]
    fill_keep(keep, mols, slots)
    for w in range(window):
        local = b * group - X_HALO + w
        blocks = []
        for comp in range(3):
            for k in range(nb):
                value = xs[k][pl.ds((w * 3 + comp) * lb, lb), :]
                edge = es[(nb - k) % nb]
                if w < X_HALO:
                    e = w if group >= X_HALO else jnp.clip(local + X_HALO, 0, X_HALO - 1)
                    side = edge[pl.ds((e * 3 + comp) * lb, lb), :]
                    value = jnp.where(local < 0, side, value)
                elif w >= group + X_HALO:
                    e = (
                        w - group - X_HALO
                        if group >= X_HALO
                        else jnp.clip(local - cells, 0, X_HALO - 1)
                    )
                    side = edge[pl.ds((e * 3 + comp) * lb, lb), :]
                    value = jnp.where(local >= cells, side, value)
                blocks.append(value)
        rows = permuted(jnp.concatenate(blocks, axis=0), perm_ref[w])
        if 1 <= w <= window - 2:
            x_out[w - 1] = rows
        build_tiles(
            tl, ts, tn, w, beads, rows[:beads], rows[beads : 2 * beads], rows[2 * beads :]
        )
    pair_forces(tl, ts, tn, ft, keep, q_ref, 0, window, mols, beads, slots)
    for w in range(window - 2):
        for comp in range(3):
            f_out[w, pl.ds(comp * beads, beads), :] = ft[
                pl.ds(w * beads * 8 + comp, beads, stride=8), :
            ]


def bond_forces(x, y, z, used, mols, slots):
    def partner(a, t):
        return pltpu.roll(a, slots - t * mols, 1)

    first = [a - partner(a, 1) for a in (x, y, z)]
    second = [a - partner(a, 2) for a in (x, y, z)]
    third = [s - f for f, s in zip(first, second)]

    def pull(bond, stiffness, square):
        length = bond[0] * bond[0] + bond[1] * bond[1] + bond[2] * bond[2]
        return (stiffness * used) * (length - square)

    c1 = pull(first, bond_stiffness, bond_square)
    c2 = pull(second, bond_stiffness, bond_square)
    c3 = pull(third, angle_stiffness, angle_square)
    out = []
    for f, s, t in zip(first, second, third):
        on_first = c1 * f - c3 * t
        on_second = c2 * s + c3 * t
        on_oxygen = -(c1 * f + c2 * s)
        out.append(
            on_oxygen + pltpu.roll(on_first, mols, 1) + pltpu.roll(on_second, 2 * mols, 1)
        )
    return out


def inner_kernel(nb, group, lb, cells, mols, slots, b_ref, *refs):
    ps, es = refs[:nb], refs[nb : 2 * nb]
    step_ref, perm_ref, q_ref, x_ref, f_ref = refs[2 * nb : 2 * nb + 5]
    ys = refs[2 * nb + 5 : 3 * nb + 5]
    xv, tl, ts, tn, ft, keep = refs[3 * nb + 5 :]
    beads = nb * lb
    window = group + 2 * P_HALO
    b = b_ref[0]
    fill_keep(keep, mols, slots)
    step = step_ref[...]

    def advance(pos, vel):
        out_x, out_v = [], []
        for x, v in zip(pos, vel):
            high, mid, low = split3(jnp.concatenate([x, v], axis=0))
            stacked = jnp.concatenate([high, mid, high, mid, low, high], axis=0).astype(BF16)
            new = dot_nn(step, stacked)
            out_x.append(new[:beads])
            out_v.append(new[beads:])
        return out_x, out_v

    for w in range(window):
        local = b * group - P_HALO + w
        blocks = []
        for comp in range(3):
            for k in range(nb):
                value = ps[k][pl.ds((w * 3 + comp) * lb, lb), :]
                edge = es[(nb - k) % nb]
                side = edge[pl.ds((X_HALO * 3 + comp) * lb, lb), :]
                if w < P_HALO:
                    value = jnp.where(local < 0, side, value)
                elif w >= group + P_HALO:
                    value = jnp.where(local >= cells, side, value)
                blocks.append(value)
        moments = permuted(jnp.concatenate(blocks, axis=0), perm_ref[w + 1])
        q = q_ref[w + 1 : w + 2, :]
        oxygen = (q < -1.5).astype(F32)
        inverse = jnp.where(q < -1.5, 1.0 / oxygen_mass, 1.0)
        moments = (moments + (0.5 * outer_step) * f_ref[w]) * inverse
        pos = [x_ref[w, pl.ds(c * beads, beads), :] for c in range(3)]
        vel = [moments[c * beads : (c + 1) * beads] for c in range(3)]
        half = (0.5 * inner_step) * inverse
        full = inner_step * inverse
        force = bond_forces(*pos, oxygen, mols, slots)
        vel = [v + half * f for v, f in zip(vel, force)]
        pos, vel = advance(pos, vel)
        force = bond_forces(*pos, oxygen, mols, slots)
        vel = [v + full * f for v, f in zip(vel, force)]
        pos, vel = advance(pos, vel)
        if 1 <= w <= window - 2:
            force = bond_forces(*pos, oxygen, mols, slots)
            vel = [v + half * f for v, f in zip(vel, force)]
            mass = jnp.where(q < -1.5, oxygen_mass, 1.0)
            for c in range(3):
                xv[w - 1, pl.ds(c * beads, beads), :] = pos[c]
                xv[w - 1, pl.ds((3 + c) * beads, beads), :] = vel[c] * mass
        build_tiles(tl, ts, tn, w, beads, *pos)
    pair_forces(tl, ts, tn, ft, keep, q_ref, 1, window, mols, beads, slots)
    for w in range(group):
        force = jnp.concatenate(
            [ft[pl.ds(w * beads * 8 + c, beads, stride=8), :] for c in range(3)], axis=0
        )
        old = xv[w]
        n = 3 * beads
        state = jnp.concatenate([old[:n], old[n:] + (0.5 * outer_step) * force], axis=0)
        state = unpermuted(state, perm_ref[w + 2])
        for a in range(2):
            for c in range(3):
                for k in range(nb):
                    row = (a * 3 + c) * beads + k * lb
                    ys[k][pl.ds(((a * group + w) * 3 + c) * lb, lb), :] = state[row : row + lb]


def unpack_kernel(nb, group, lb, cells, b_ref, *refs):
    ys = refs[:nb]
    outs = refs[nb:]
    b = b_ref[0]
    for k in range(nb):
        source = lax.rem(b + k, nb)
        for a in range(2):
            for w in range(group):
                for c in range(3):
                    outs[a][pl.ds(c * cells + source * group + w, lb, stride=3 * cells), :] = ys[
                        k
                    ][pl.ds(((a * group + w) * 3 + c) * lb, lb), :]


def call(kernel, outs, scratch, scalar, *operands):
    vmem = pl.BlockSpec(memory_space=pltpu.VMEM)
    smem = pl.BlockSpec(memory_space=pltpu.SMEM)
    return pl.pallas_call(
        kernel,
        out_shape=outs,
        in_specs=([] if scalar is None else [smem]) + [vmem] * len(operands),
        out_specs=[vmem] * len(outs),
        scratch_shapes=scratch,
        compiler_params=pltpu.CompilerParams(vmem_limit_bytes=48 * 1024 * 1024),
    )(*(() if scalar is None else (scalar,)), *operands)


def local(nb, ns, positions, momenta, molecules):
    lb, _, cells, slots = positions.shape
    mols = molecules.shape[1]
    group = cells // nb
    beads = lb * nb
    b = lax.axis_index("bead").astype(jnp.int32).reshape(1)

    def shape(*dims):
        return jax.ShapeDtypeStruct(dims, F32)

    x_cells = group + 2 * X_HALO
    p_cells = group + 2 * P_HALO
    packed = call(
        functools.partial(pack_kernel, nb, group, lb, cells),
        [shape(x_cells * 3 * lb, slots)] * nb
        + [shape(p_cells * 3 * lb, slots)] * nb
        + [shape((X_HALO + P_HALO) * 3 * lb, slots)] * nb,
        [],
        b,
        positions.reshape(lb * 3 * cells, slots),
        momenta.reshape(lb * 3 * cells, slots),
    )
    packed, molecules = lax.optimization_barrier((packed, molecules))
    xs, ps, es = packed[:nb], packed[nb : 2 * nb], packed[2 * nb :]
    mol_left = lax.ppermute(
        molecules[cells - X_HALO :], "space", [(s, (s + 1) % ns) for s in range(ns)]
    )
    mol_right = lax.ppermute(
        molecules[:X_HALO], "space", [(s, (s - 1) % ns) for s in range(ns)]
    )
    xs = [xs[0]] + [
        lax.ppermute(xs[k], "bead", [(i, (i + k) % nb) for i in range(nb)]) for k in range(1, nb)
    ]
    edges = []
    for j in range(nb):
        pairs = []
        for source in range(nb):
            target = (source - j) % nb
            for s in range(ns):
                if target * group < X_HALO:
                    pairs.append((source * ns + s, target * ns + (s + 1) % ns))
                elif (target + 1) * group + X_HALO > cells:
                    pairs.append((source * ns + s, target * ns + (s - 1) % ns))
        edges.append(lax.ppermute(es[j], ("bead", "space"), pairs))
    ps = [ps[0]] + [
        lax.ppermute(ps[k], "bead", [(i, (i + k) % nb) for i in range(nb)]) for k in range(1, nb)
    ]

    wide = jnp.concatenate([mol_left, molecules, mol_right], axis=0)
    near = lax.dynamic_slice_in_dim(wide, b[0] * group, x_cells, 0)
    lanes = jnp.transpose(near, (0, 2, 1)).reshape(x_cells, 3 * mols)
    rows = -(-x_cells // 8) * 8
    lanes = jnp.pad(
        lanes, ((0, rows - x_cells), (0, slots - 3 * mols)), constant_values=slots
    )
    perm, charges = call(
        functools.partial(table_kernel, x_cells, slots, mols),
        [jax.ShapeDtypeStruct((x_cells, slots, slots), BF16), shape(rows, slots)],
        [],
        None,
        lanes,
    )

    def tiles(count):
        return pltpu.VMEM((count * beads * 8, slots), F32)

    keep = pltpu.VMEM((slots, slots), F32)
    x_near, force = call(
        functools.partial(outer_kernel, nb, group, lb, cells, mols, slots),
        [shape(p_cells, 3 * beads, slots)] * 2,
        [tiles(x_cells)] * 3 + [tiles(p_cells), keep],
        b,
        *xs,
        *edges,
        perm,
        charges,
    )
    step = jnp.asarray(propagator(beads, lb))
    ys = call(
        functools.partial(inner_kernel, nb, group, lb, cells, mols, slots),
        [shape(2 * group * 3 * lb, slots)] * nb,
        [pltpu.VMEM((group, 6 * beads, slots), F32)]
        + [tiles(p_cells)] * 3
        + [tiles(group), keep],
        b,
        *ps,
        *edges,
        step,
        perm,
        charges,
        x_near,
        force,
    )
    ys = [ys[0]] + [
        lax.ppermute(ys[k], "bead", [(i, (i - k) % nb) for i in range(nb)]) for k in range(1, nb)
    ]
    new_x, new_p = call(
        functools.partial(unpack_kernel, nb, group, lb, cells),
        [shape(lb * 3 * cells, slots)] * 2,
        [],
        b,
        *ys,
    )
    return new_x.reshape(positions.shape), new_p.reshape(positions.shape)


def solution(mesh):
    spec = P("bead", None, "space", None)
    return jax.shard_map(
        functools.partial(local, mesh.shape["bead"], mesh.shape["space"]),
        mesh=mesh,
        in_specs=(spec, spec, P("space", None, None)),
        out_specs=(spec, spec),
        check_vma=False,
    )
```

```python
import functools

import jax
import jax.numpy as jnp
import ml_dtypes
import numpy as np
from jax import lax
from jax.experimental import pallas as pl
from jax.experimental.pallas import tpu as pltpu
from jax.sharding import PartitionSpec as P

charge_oxygen = -0.8476
charge_hydrogen = 0.4238
coulomb_scale = 24.0
coulomb_soft = 0.004
well_depth = 0.02
sigma_square = 0.0841
lennard_soft = 0.04
bond_stiffness = 20000.0
bond_square = 0.0081
angle_stiffness = 5000.0
angle_square = 0.0204
cycle_frequency = 60.0
outer_step = 0.02
inner_step = 0.01
oxygen_mass = 16.0

REACH = 1
X_HALO = 2 * REACH
P_HALO = REACH

F32 = jnp.float32
BF16 = jnp.bfloat16


def rounded(a):
    return a.astype(BF16).astype(F32)


def split3(a):
    high = rounded(a)
    rest = a - high
    mid = rounded(rest)
    return high, mid, rest - mid


def two_part(a):
    high = rounded(a)
    return high + rounded(a - high)


def dot_nn(a, b):
    return lax.dot_general(a, b, (((1,), (0,)), ((), ())), preferred_element_type=F32)


def dot_nt(a, b):
    return lax.dot_general(a, b, (((1,), (1,)), ((), ())), preferred_element_type=F32)


def propagator(beads, beads_dev):
    j = np.arange(beads)
    angles = 2.0 * np.pi * ((j[:, None] * j[None, :]) % beads) / beads
    half = beads // 2
    col = j[None, :]
    u = np.where(
        col == 0,
        np.sqrt(1.0 / beads),
        np.where(
            col < half,
            np.sqrt(2.0 / beads) * np.cos(angles),
            np.where(
                col == half,
                np.sqrt(1.0 / beads) * np.cos(angles),
                np.sqrt(2.0 / beads) * np.sin(angles),
            ),
        ),
    )
    w = 2.0 * cycle_frequency * np.sin(np.pi * j / beads)
    cosines = np.cos(w * inner_step)
    spring = w * np.sin(w * inner_step)
    drift = np.where(j == 0, inner_step, np.sin(w * inner_step) / np.where(j == 0, 1.0, w))
    k = j // beads_dev
    i = j % beads_dev
    index = (beads_dev * (k[None, :] - k[:, None]) + i[:, None] - i[None, :]) % beads

    def circulant(values):
        return ((u * values) @ u.T)[:, 0][index]

    a = circulant(cosines)
    whole = np.block([[a, circulant(drift)], [-circulant(spring), a]])
    high = whole.astype(ml_dtypes.bfloat16)
    rest = whole - high.astype(np.float64)
    mid = rest.astype(ml_dtypes.bfloat16)
    low = (rest - mid.astype(np.float64)).astype(ml_dtypes.bfloat16)
    return np.concatenate([high, high, mid, mid, high, low], axis=1)


def lane_tables(lanes, mols, slots):
    lane = lax.broadcasted_iota(jnp.int32, lanes.shape, 1)
    unit = jnp.where(lane < mols, charge_oxygen / charge_hydrogen, 1.0)
    return jnp.where(lanes < slots, unit, 0.0)


def lane_matrix(lanes, slots, row, before, upper, ones):
    far = 4.0 * slots
    key = jnp.broadcast_to(lanes.astype(F32), (8, slots))
    free = key >= slots
    rank = dot_nn(free.astype(F32).astype(BF16), upper)
    key = jnp.where(free, far + rank, key)[0:1]
    held = (row == key).astype(F32).astype(BF16)
    used = dot_nn(held, ones)
    count = dot_nn(before, used.astype(BF16))
    slot_key = jnp.where(used > 0.5, row, far + row - count)
    return (slot_key == key).astype(F32).astype(BF16)


def permuted(rows, perm):
    n = rows.shape[0]
    stacked = jnp.concatenate(split3(rows), axis=0).astype(BF16)
    moved = dot_nn(stacked, perm)
    return moved[:n] + moved[n : 2 * n] + moved[2 * n :]


def unpermuted(rows, perm):
    n = rows.shape[0]
    stacked = jnp.concatenate(split3(rows), axis=0).astype(BF16)
    moved = dot_nt(stacked, perm)
    return moved[:n] + moved[n : 2 * n] + moved[2 * n :]


def order_kernel(lb, cells, mols, slots, lane_ref, x_ref, p_ref, *outs):
    xo, po, perm_ref, q_ref, to_right, to_left = outs
    row = lax.broadcasted_iota(jnp.int32, (slots, slots), 0).astype(F32)
    col = lax.broadcasted_iota(jnp.int32, (slots, slots), 1).astype(F32)
    before = (col < row).astype(BF16)
    upper = (row < col).astype(BF16)
    ones = jnp.ones((slots, slots), BF16)
    charges = lane_tables(lane_ref[...], mols, slots)
    q_ref[...] = charges
    n = 3 * lb
    for cell in range(cells):
        perm = lane_matrix(lane_ref[cell : cell + 1, :], slots, row, before, upper, ones)
        perm_ref[cell] = perm
        rows = [
            ref[pl.ds(comp * cells + cell, lb, stride=3 * cells), :]
            for ref in (x_ref, p_ref)
            for comp in range(3)
        ]
        moved = permuted(jnp.concatenate(rows, axis=0), perm)
        xo[cell] = moved[:n]
        po[cell] = moved[n:]
    for out, xs, ps in (
        (to_right, (cells - 2, cells - 1), cells - 1),
        (to_left, (0, 1), 0),
    ):
        out[9 * lb :, :] = jnp.zeros((8, slots), F32)
        for e, cell in enumerate(xs):
            out[pl.ds(e * n, n), :] = xo[cell]
            out[pl.ds(9 * lb + e, 1), :] = charges[cell : cell + 1]
        out[pl.ds(2 * n, n), :] = po[ps]


def selectors(slots):
    out = np.zeros((32, 3 * slots), np.float32)
    for comp in range(3):
        for part in (0, 16):
            out[part + comp, comp * slots : (comp + 1) * slots] = -0.5
    return out.astype(ml_dtypes.bfloat16)


def put_tiles(scratch, first, count, rows):
    for index, value in rows:
        scratch[pl.ds(first * 8 + index, count, stride=8), :] = value


def build_tiles(tiles, first, count, x, y, z):
    left, rights = tiles[0], tiles[1:]
    xa = two_part(x - 0.5)
    ya = two_part(y - 0.5)
    za = two_part(z - 0.5)
    side = ya * ya + za * za

    def parts(n):
        high = two_part(n)
        return high, n - high

    n_high, n_low = parts(side + xa * xa + coulomb_soft)
    put_tiles(
        left,
        first,
        count,
        ((0, -2.0 * xa), (1, -2.0 * ya), (2, -2.0 * za), (3, n_high), (4, n_low)),
    )
    for ref, offset in zip(rights, OFFSETS):
        xo = two_part(xa - offset) if offset else xa
        n_high, n_low = parts(side + xo * xo)
        put_tiles(ref, first, count, ((0, xo), (1, ya), (2, za), (5, n_high), (6, n_low)))


OFFSETS = (0.0, 1.0, -1.0)


def pair_scratch(count, beads, slots):
    n = count * beads
    return (
        [pltpu.VMEM((n * 8, slots), F32)] * 4
        + [pltpu.VMEM((n, slots, 32), BF16)]
        + [pltpu.VMEM((n, 32, slots), BF16)] * 6
        + [pltpu.VMEM((count, slots, slots), F32)]
        + [pltpu.VMEM((n * 32, slots), F32)]
        + [pltpu.VMEM((slots, slots), F32)]
    )


def pair_forces(scratch, sel_ref, charges, put, count, mols, beads, slots):
    tiles, lt, rs, packs = scratch[:4], scratch[4], scratch[5:8], scratch[8:11]
    qb, sums, keep = scratch[11:]
    orows = -(-mols // 8) * 8
    pair_scale = coulomb_scale * charge_hydrogen * charge_hydrogen
    k3 = sigma_square**3
    ratio = (charge_hydrogen / charge_oxygen) ** 2 / pair_scale
    lj_a = 24.0 * well_depth * 2.0 * k3 * k3 * ratio
    lj_b = 24.0 * well_depth * k3 * ratio
    row8 = lax.broadcasted_iota(jnp.int32, (8, slots), 0)
    lane8 = lax.broadcasted_iota(jnp.int32, (8, slots), 1)
    left_rows = row8 < 5
    left_fill = jnp.where((row8 == 5) | (row8 == 6), 1.0, 0.0)
    right_rows = (row8 < 3) | (row8 == 5) | (row8 == 6)
    right_fill = jnp.where((row8 == 3) | (row8 == 4), 1.0, 0.0)
    lj_row = lax.broadcasted_iota(jnp.int32, (orows, slots), 0)
    lj_lane = lax.broadcasted_iota(jnp.int32, (orows, slots), 1)
    corner = (lj_row < mols) & (lj_lane < mols)

    i = lax.broadcasted_iota(jnp.int32, (slots, slots), 0)
    j = lax.broadcasted_iota(jnp.int32, (slots, slots), 1)
    i = jnp.where(i >= 2 * mols, i - 2 * mols, jnp.where(i >= mols, i - mols, i))
    j = jnp.where(j >= 2 * mols, j - 2 * mols, jnp.where(j >= mols, j - mols, j))
    keep[...] = (i != j).astype(F32)
    for w in range(count):
        qb[w] = jnp.broadcast_to(charges[w], (slots, slots)).T

    unroll = min(beads, 4)

    def tile(ref, n):
        return ref[pl.ds(pl.multiple_of(n * 8, 8), 8), :]

    def parts(a):
        high = rounded(a)
        mid = a - high
        return high, mid

    def prepare(step, carry):
        for u in range(unroll):
            n = step * unroll + u
            high, mid = parts(jnp.where(left_rows, tile(tiles[0], n), left_fill))
            lt[n] = jnp.concatenate([high, high, mid, mid], axis=0).astype(BF16).T
            for o in range(3):
                value = jnp.where(right_rows, tile(tiles[1 + o], n), right_fill)
                high, mid = parts(value)
                rs[o][n] = jnp.concatenate([high, mid, high, mid], axis=0).astype(BF16)
                value = jnp.where(lane8 < mols, value, 0.0)
                if o:
                    value = pltpu.roll(value, o * mols, 1)
                high, mid = parts(value)
                packs[o][n] = jnp.concatenate([high, mid, high, mid], axis=0).astype(BF16)
        return carry

    lax.fori_loop(0, count * beads // unroll, prepare, 0)

    def down(a):
        return jnp.sum(a.reshape(slots // 8, 8, slots), axis=0)

    def peer(n, w, r, offsets):
        targets = [n - int(OFFSETS[o]) * beads for o in offsets]
        right = jnp.concatenate(
            [rs[o][t] for o, t in zip(offsets, targets)] + [sel_ref[...]], axis=1
        )
        left = lt[n]
        product = dot_nn(left, right)
        width = len(offsets) * slots
        coords = [product[:, width + a * slots : width + (a + 1) * slots] for a in range(3)]
        pack = packs[offsets[0]][targets[0]]
        for o, t in zip(offsets[1:], targets[1:]):
            pack = pack + packs[o][t]
        lj_root = lax.rsqrt(dot_nn(left[:orows], pack) + (lennard_soft - coulomb_soft))
        inverse = lj_root * lj_root
        cube = inverse * inverse * inverse
        lj = (cube * lj_a - lj_b) * (cube * inverse)
        charge = qb[w]
        for k, (o, t) in enumerate(zip(offsets, targets)):
            root = lax.rsqrt(product[:, k * slots : (k + 1) * slots])
            strength = root * root * root
            own = pltpu.roll(lj, slots - o * mols, 1) if o else lj
            strength = jnp.concatenate(
                [strength[:orows] + jnp.where(corner, own, 0.0), strength[orows:]], axis=0
            )
            strength = strength * charge
            if o == 0:
                strength = strength * keep[...]
            total = down(strength)
            parts = [down(strength * c) for c in coords]
            if o:
                parts[0] = parts[0] + OFFSETS[o] * total
            parts.append(total)
            base = pl.multiple_of(t * 32, 32)
            if o != 2:
                parts = [
                    a + sums[pl.ds(base + 8 * i, 8), :] for i, a in enumerate(parts)
                ]
            if o != 1:
                for i, a in enumerate(parts):
                    sums[pl.ds(base + 8 * i, 8), :] = a
            else:
                parts = [jnp.sum(a, axis=0, keepdims=True) for a in parts]
                own = tile(tiles[1], t)
                scale = charges[w - 1] * pair_scale
                for a in range(3):
                    put(w - 1, r, a, (own[a : a + 1] * parts[3] - parts[a]) * scale)

    kinds = []
    for w in range(count):
        offsets = tuple(o for o in (2, 0, 1) if 1 <= w - int(OFFSETS[o]) <= count - 2)
        if kinds and kinds[-1][0] == offsets:
            kinds[-1][2] = w + 1
        else:
            kinds.append([offsets, w, w + 1])
    per_cell = beads // unroll
    for offsets, first, last in kinds:

        def step(index, carry, offsets=offsets):
            w = lax.div(index, per_cell)
            r = lax.rem(index, per_cell) * unroll
            for u in range(unroll):
                peer(w * beads + r + u, w, r + u, offsets)
            return carry

        lax.fori_loop(first * per_cell, last * per_cell, step, 0)


def outer_kernel(nb, group, lb, cells, mols, slots, b_ref, *refs):
    x_ref, p_ref, q_ref, left, right, sel_ref = refs[:6]
    outs, q_out = refs[6 : 6 + nb], refs[6 + nb]
    kicked, scratch = refs[7 + nb], refs[8 + nb :]
    n = 3 * lb
    count = cells + 2 * X_HALO
    b = b_ref[0]

    def cell_rows(w):
        if w < X_HALO:
            return left[pl.ds(w * n, n), :]
        if w >= cells + X_HALO:
            return right[pl.ds((w - cells - X_HALO) * n, n), :]
        return x_ref[w - X_HALO]

    charge_rows = [left[pl.ds(9 * lb + e, 1), :] for e in range(2)]
    charge_rows += [q_ref[c : c + 1, :] for c in range(cells)]
    charge_rows += [right[pl.ds(9 * lb + e, 1), :] for e in range(2)]
    q_out[...] = jnp.zeros(q_out.shape, F32)
    for w in range(count):
        q_out[w : w + 1, :] = charge_rows[w]
    for w in range(count):
        rows = cell_rows(w)
        build_tiles(scratch[:4], w * lb, lb, rows[:lb], rows[lb : 2 * lb], rows[2 * lb :])

    def put(w, r, comp, value):
        kicked[w - 1, pl.ds(comp * lb + r, 1), :] = value

    pair_forces(scratch, sel_ref, Rows(q_out, 0), put, count, mols, lb, slots)
    half = 0.5 * outer_step
    for w in range(1, count - 1):
        if w < X_HALO:
            old = left[pl.ds(2 * n, n), :]
        elif w >= cells + X_HALO:
            old = right[pl.ds(2 * n, n), :]
        else:
            old = p_ref[w - X_HALO]
        kicked[w - 1] = old + half * kicked[w - 1]
    width = group + 2 * P_HALO
    for k in range(nb):
        first = lax.rem(b + k, nb) * group
        for w in range(width):
            outs[k][pl.ds((width + w) * n, n), :] = kicked[first + w]
            source = first + w - P_HALO
            inside = x_ref[jnp.clip(source, 0, cells - 1)]
            if w < P_HALO:
                inside = jnp.where(source < 0, left[pl.ds(n, n), :], inside)
            elif w >= group + P_HALO:
                inside = jnp.where(source >= cells, right[pl.ds(0, n), :], inside)
            outs[k][pl.ds(w * n, n), :] = inside


class Rows:
    def __init__(self, ref, first):
        self.ref, self.first = ref, first

    def __getitem__(self, index):
        return self.ref[pl.ds(self.first + index, 1), :]


def bond_forces(x, y, z, used, mols, slots):
    def partner(a, t):
        return pltpu.roll(a, slots - t * mols, 1)

    first = [a - partner(a, 1) for a in (x, y, z)]
    second = [a - partner(a, 2) for a in (x, y, z)]
    third = [s - f for f, s in zip(first, second)]

    def pull(bond, stiffness, square):
        length = bond[0] * bond[0] + bond[1] * bond[1] + bond[2] * bond[2]
        return (stiffness * used) * (length - square)

    c1 = pull(first, bond_stiffness, bond_square)
    c2 = pull(second, bond_stiffness, bond_square)
    c3 = pull(third, angle_stiffness, angle_square)
    out = []
    for f, s, t in zip(first, second, third):
        on_first = c1 * f - c3 * t
        on_second = c2 * s + c3 * t
        on_oxygen = -(c1 * f + c2 * s)
        out.append(
            on_oxygen + pltpu.roll(on_first, mols, 1) + pltpu.roll(on_second, 2 * mols, 1)
        )
    return out


def inner_kernel(nb, group, lb, cells, mols, slots, b_ref, *refs):
    blocks = refs[:nb]
    step_ref, perm_ref, q_ref, sel_ref = refs[nb : nb + 4]
    ys = refs[nb + 4 : 2 * nb + 4]
    xv, ft, scratch = refs[2 * nb + 4], refs[2 * nb + 5], refs[2 * nb + 6 :]
    beads = nb * lb
    width = group + 2 * P_HALO
    n = 3 * lb
    b = b_ref[0]
    step = step_ref[...]
    charges = Rows(q_ref, b * group + P_HALO)

    def advance(pos, vel):
        out_x, out_v = [], []
        for x, v in zip(pos, vel):
            high, mid, low = split3(jnp.concatenate([x, v], axis=0))
            stacked = jnp.concatenate([high, mid, high, mid, low, high], axis=0).astype(BF16)
            new = dot_nn(step, stacked)
            out_x.append(new[:beads])
            out_v.append(new[beads:])
        return out_x, out_v

    for w in range(width):
        def gather(a, comp):
            return jnp.concatenate(
                [block[pl.ds((a * width + w) * n + comp * lb, lb), :] for block in blocks], axis=0
            )

        q = charges[w]
        oxygen = (q < -1.5).astype(F32)
        inverse = jnp.where(q < -1.5, 1.0 / oxygen_mass, 1.0)
        pos = [gather(0, c) for c in range(3)]
        vel = [gather(1, c) * inverse for c in range(3)]
        half = (0.5 * inner_step) * inverse
        full = inner_step * inverse
        force = bond_forces(*pos, oxygen, mols, slots)
        vel = [v + half * f for v, f in zip(vel, force)]
        pos, vel = advance(pos, vel)
        force = bond_forces(*pos, oxygen, mols, slots)
        vel = [v + full * f for v, f in zip(vel, force)]
        pos, vel = advance(pos, vel)
        if 1 <= w <= width - 2:
            force = bond_forces(*pos, oxygen, mols, slots)
            vel = [v + half * f for v, f in zip(vel, force)]
            mass = jnp.where(q < -1.5, oxygen_mass, 1.0)
            for c in range(3):
                xv[w - 1, pl.ds(c * beads, beads), :] = pos[c]
                xv[w - 1, pl.ds((3 + c) * beads, beads), :] = vel[c] * mass
        build_tiles(scratch[:4], w * beads, beads, *pos)

    def put(w, r, comp, value):
        ft[w - 1, pl.ds(comp * beads + r, 1), :] = value

    pair_forces(scratch, sel_ref, charges, put, width, mols, beads, slots)
    for w in range(group):
        old = xv[w]
        m = 3 * beads
        state = jnp.concatenate([old[:m], old[m:] + (0.5 * outer_step) * ft[w]], axis=0)
        state = unpermuted(state, perm_ref[b * group + w])
        for a in range(2):
            for c in range(3):
                for k in range(nb):
                    row = (a * 3 + c) * beads + k * lb
                    ys[k][pl.ds(((a * group + w) * 3 + c) * lb, lb), :] = state[row : row + lb]


def unpack_kernel(nb, group, lb, cells, b_ref, *refs):
    ys = refs[:nb]
    outs = refs[nb:]
    b = b_ref[0]
    for k in range(nb):
        source = lax.rem(b + k, nb)
        for a in range(2):
            for w in range(group):
                for c in range(3):
                    outs[a][pl.ds(c * cells + source * group + w, lb, stride=3 * cells), :] = ys[
                        k
                    ][pl.ds(((a * group + w) * 3 + c) * lb, lb), :]


def call(kernel, outs, scratch, scalar, *operands):
    vmem = pl.BlockSpec(memory_space=pltpu.VMEM)
    smem = pl.BlockSpec(memory_space=pltpu.SMEM)
    return pl.pallas_call(
        kernel,
        out_shape=outs,
        in_specs=([] if scalar is None else [smem]) + [vmem] * len(operands),
        out_specs=[vmem] * len(outs),
        scratch_shapes=scratch,
        compiler_params=pltpu.CompilerParams(vmem_limit_bytes=48 * 1024 * 1024),
    )(*(() if scalar is None else (scalar,)), *operands)


def local(nb, ns, positions, momenta, molecules):
    lb, _, cells, slots = positions.shape
    mols = molecules.shape[1]
    group = cells // nb
    beads = lb * nb
    width = group + 2 * P_HALO
    b = lax.axis_index("bead").astype(jnp.int32).reshape(1)

    def shape(*dims):
        return jax.ShapeDtypeStruct(dims, F32)

    lanes = jnp.transpose(molecules, (0, 2, 1)).reshape(cells, 3 * mols)
    lanes = jnp.pad(lanes, ((0, 0), (0, slots - 3 * mols)), constant_values=slots)
    edge = shape(9 * lb + 8, slots)
    xs, ps, perm, charges, to_right, to_left = call(
        functools.partial(order_kernel, lb, cells, mols, slots),
        [shape(cells, 3 * lb, slots)] * 2
        + [jax.ShapeDtypeStruct((cells, slots, slots), BF16), shape(cells, slots), edge, edge],
        [],
        None,
        lanes,
        positions.reshape(lb * 3 * cells, slots),
        momenta.reshape(lb * 3 * cells, slots),
    )
    left = lax.ppermute(to_right, "space", [(s, (s + 1) % ns) for s in range(ns)])
    right = lax.ppermute(to_left, "space", [(s, (s - 1) % ns) for s in range(ns)])
    sel = jnp.asarray(selectors(slots))
    q_rows = -(-(cells + 2 * X_HALO) // 8) * 8
    *blocks, q_wide = call(
        functools.partial(outer_kernel, nb, group, lb, cells, mols, slots),
        [shape(2 * width * 3 * lb, slots)] * nb + [shape(q_rows, slots)],
        [pltpu.VMEM((cells + 2 * P_HALO, 3 * lb, slots), F32)]
        + pair_scratch(cells + 2 * X_HALO, lb, slots),
        b,
        xs,
        ps,
        charges,
        left,
        right,
        sel,
    )
    blocks = [blocks[0]] + [
        lax.ppermute(blocks[k], "bead", [(i, (i + k) % nb) for i in range(nb)])
        for k in range(1, nb)
    ]
    step = jnp.asarray(propagator(beads, lb))
    ys = call(
        functools.partial(inner_kernel, nb, group, lb, cells, mols, slots),
        [shape(2 * group * 3 * lb, slots)] * nb,
        [
            pltpu.VMEM((group, 6 * beads, slots), F32),
            pltpu.VMEM((group, 3 * beads, slots), F32),
        ]
        + pair_scratch(width, beads, slots),
        b,
        *blocks,
        step,
        perm,
        q_wide,
        sel,
    )
    ys = [ys[0]] + [
        lax.ppermute(ys[k], "bead", [(i, (i - k) % nb) for i in range(nb)]) for k in range(1, nb)
    ]
    new_x, new_p = call(
        functools.partial(unpack_kernel, nb, group, lb, cells),
        [shape(lb * 3 * cells, slots)] * 2,
        [],
        b,
        *ys,
    )
    return new_x.reshape(positions.shape), new_p.reshape(positions.shape)


def solution(mesh):
    spec = P("bead", None, "space", None)
    return jax.shard_map(
        functools.partial(local, mesh.shape["bead"], mesh.shape["space"]),
        mesh=mesh,
        in_specs=(spec, spec, P("space", None, None)),
        out_specs=(spec, spec),
        check_vma=False,
    )
```

```python
import functools

import jax
import jax.numpy as jnp
import ml_dtypes
import numpy as np
from jax import lax
from jax.experimental import pallas as pl
from jax.experimental.pallas import tpu as pltpu
from jax.sharding import PartitionSpec as P

charge_oxygen = -0.8476
charge_hydrogen = 0.4238
coulomb_scale = 24.0
coulomb_soft = 0.004
well_depth = 0.02
sigma_square = 0.0841
lennard_soft = 0.04
bond_stiffness = 20000.0
bond_square = 0.0081
angle_stiffness = 5000.0
angle_square = 0.0204
cycle_frequency = 60.0
outer_step = 0.02
inner_step = 0.01
oxygen_mass = 16.0

REACH = 1
X_HALO = 2 * REACH
P_HALO = REACH

F32 = jnp.float32
BF16 = jnp.bfloat16


def rounded(a):
    return a.astype(BF16).astype(F32)


def split3(a):
    high = rounded(a)
    rest = a - high
    mid = rounded(rest)
    return high, mid, rest - mid


def two_part(a):
    high = rounded(a)
    return high + rounded(a - high)


def dot_nn(a, b):
    return lax.dot_general(a, b, (((1,), (0,)), ((), ())), preferred_element_type=F32)


def dot_nt(a, b):
    return lax.dot_general(a, b, (((1,), (1,)), ((), ())), preferred_element_type=F32)


def propagator(beads, beads_dev):
    j = np.arange(beads)
    angles = 2.0 * np.pi * ((j[:, None] * j[None, :]) % beads) / beads
    half = beads // 2
    col = j[None, :]
    u = np.where(
        col == 0,
        np.sqrt(1.0 / beads),
        np.where(
            col < half,
            np.sqrt(2.0 / beads) * np.cos(angles),
            np.where(
                col == half,
                np.sqrt(1.0 / beads) * np.cos(angles),
                np.sqrt(2.0 / beads) * np.sin(angles),
            ),
        ),
    )
    w = 2.0 * cycle_frequency * np.sin(np.pi * j / beads)
    cosines = np.cos(w * inner_step)
    spring = w * np.sin(w * inner_step)
    drift = np.where(j == 0, inner_step, np.sin(w * inner_step) / np.where(j == 0, 1.0, w))
    k = j // beads_dev
    i = j % beads_dev
    index = (beads_dev * (k[None, :] - k[:, None]) + i[:, None] - i[None, :]) % beads

    def circulant(values):
        return ((u * values) @ u.T)[:, 0][index]

    a = circulant(cosines)
    whole = np.block([[a, circulant(drift)], [-circulant(spring), a]])
    high = whole.astype(ml_dtypes.bfloat16)
    rest = whole - high.astype(np.float64)
    mid = rest.astype(ml_dtypes.bfloat16)
    low = (rest - mid.astype(np.float64)).astype(ml_dtypes.bfloat16)
    return np.concatenate([high, high, mid, mid, high, low], axis=1)


def lane_tables(lanes, mols, slots):
    lane = lax.broadcasted_iota(jnp.int32, lanes.shape, 1)
    unit = jnp.where(lane < mols, charge_oxygen / charge_hydrogen, 1.0)
    return jnp.where(lanes < slots, unit, 0.0)


def lane_matrix(lanes, slots, row, before, upper, ones):
    far = 4.0 * slots
    key = jnp.broadcast_to(lanes.astype(F32), (8, slots))
    free = key >= slots
    rank = dot_nn(free.astype(F32).astype(BF16), upper)
    key = jnp.where(free, far + rank, key)[0:1]
    held = (row == key).astype(F32).astype(BF16)
    used = dot_nn(held, ones)
    count = dot_nn(before, used.astype(BF16))
    slot_key = jnp.where(used > 0.5, row, far + row - count)
    return (slot_key == key).astype(F32).astype(BF16)


def permuted(rows, perm):
    n = rows.shape[0]
    stacked = jnp.concatenate(split3(rows), axis=0).astype(BF16)
    moved = dot_nn(stacked, perm)
    return moved[:n] + moved[n : 2 * n] + moved[2 * n :]


def unpermuted(rows, perm):
    n = rows.shape[0]
    stacked = jnp.concatenate(split3(rows), axis=0).astype(BF16)
    moved = dot_nt(stacked, perm)
    return moved[:n] + moved[n : 2 * n] + moved[2 * n :]


def order_kernel(lb, cells, mols, slots, lane_ref, x_ref, p_ref, *outs):
    xo, po, perm_ref, q_ref, to_right, to_left = outs
    row = lax.broadcasted_iota(jnp.int32, (slots, slots), 0).astype(F32)
    col = lax.broadcasted_iota(jnp.int32, (slots, slots), 1).astype(F32)
    before = (col < row).astype(BF16)
    upper = (row < col).astype(BF16)
    ones = jnp.ones((slots, slots), BF16)
    charges = lane_tables(lane_ref[...], mols, slots)
    q_ref[...] = charges
    n = 3 * lb
    for cell in range(cells):
        perm = lane_matrix(lane_ref[cell : cell + 1, :], slots, row, before, upper, ones)
        perm_ref[cell] = perm
        rows = [
            ref[pl.ds(comp * cells + cell, lb, stride=3 * cells), :]
            for ref in (x_ref, p_ref)
            for comp in range(3)
        ]
        moved = permuted(jnp.concatenate(rows, axis=0), perm)
        xo[cell] = moved[:n]
        po[cell] = moved[n:]
    for out, xs, ps in (
        (to_right, (cells - 2, cells - 1), cells - 1),
        (to_left, (0, 1), 0),
    ):
        out[9 * lb :, :] = jnp.zeros((8, slots), F32)
        for e, cell in enumerate(xs):
            out[pl.ds(e * n, n), :] = xo[cell]
            out[pl.ds(9 * lb + e, 1), :] = charges[cell : cell + 1]
        out[pl.ds(2 * n, n), :] = po[ps]


def selectors(slots):
    out = np.zeros((32, 3 * slots), np.float32)
    for comp in range(3):
        for part in (0, 16):
            out[part + comp, comp * slots : (comp + 1) * slots] = -0.5
    return out.astype(ml_dtypes.bfloat16)


def put_tiles(scratch, first, count, rows):
    for index, value in rows:
        scratch[pl.ds(first * 8 + index, count, stride=8), :] = value


def build_tiles(tiles, first, count, x, y, z):
    left, rights = tiles[0], tiles[1:]
    xa = two_part(x - 0.5)
    ya = two_part(y - 0.5)
    za = two_part(z - 0.5)
    side = ya * ya + za * za

    def parts(n):
        high = two_part(n)
        return high, n - high

    n_high, n_low = parts(side + xa * xa + coulomb_soft)
    put_tiles(
        left,
        first,
        count,
        ((0, -2.0 * xa), (1, -2.0 * ya), (2, -2.0 * za), (3, n_high), (4, n_low)),
    )
    for ref, offset in zip(rights, OFFSETS):
        xo = two_part(xa - offset) if offset else xa
        n_high, n_low = parts(side + xo * xo)
        put_tiles(ref, first, count, ((0, xo), (1, ya), (2, za), (5, n_high), (6, n_low)))


OFFSETS = (0.0, 1.0, -1.0)


def pair_scratch(count, beads, slots):
    n = count * beads
    return (
        [pltpu.VMEM((n * 8, slots), F32)] * 4
        + [pltpu.VMEM((n, slots, 32), BF16)]
        + [pltpu.VMEM((n, 32, slots), BF16)] * 6
        + [pltpu.VMEM((count, slots, slots), F32)]
        + [pltpu.VMEM((n * 32, slots), F32)]
        + [pltpu.VMEM((slots, slots), F32)]
        + [pltpu.VMEM((slots, 6 * slots), F32)] * 2
        + [pltpu.VMEM((slots, slots), F32)] * 2
    )


def pair_forces(scratch, sel_ref, charges, put, count, mols, beads, slots):
    tiles, lt, rs, packs = scratch[:4], scratch[4], scratch[5:8], scratch[8:11]
    qb, sums, keep = scratch[11:14]
    product, near = scratch[14:16], scratch[16:18]
    orows = -(-mols // 8) * 8
    pair_scale = coulomb_scale * charge_hydrogen * charge_hydrogen
    k3 = sigma_square**3
    ratio = (charge_hydrogen / charge_oxygen) ** 2 / pair_scale
    lj_a = 24.0 * well_depth * 2.0 * k3 * k3 * ratio
    lj_b = 24.0 * well_depth * k3 * ratio
    row8 = lax.broadcasted_iota(jnp.int32, (8, slots), 0)
    lane8 = lax.broadcasted_iota(jnp.int32, (8, slots), 1)
    left_rows = row8 < 5
    left_fill = jnp.where((row8 == 5) | (row8 == 6), 1.0, 0.0)
    right_rows = (row8 < 3) | (row8 == 5) | (row8 == 6)
    right_fill = jnp.where((row8 == 3) | (row8 == 4), 1.0, 0.0)

    i = lax.broadcasted_iota(jnp.int32, (slots, slots), 0)
    j = lax.broadcasted_iota(jnp.int32, (slots, slots), 1)
    i = jnp.where(i >= 2 * mols, i - 2 * mols, jnp.where(i >= mols, i - mols, i))
    j = jnp.where(j >= 2 * mols, j - 2 * mols, jnp.where(j >= mols, j - mols, j))
    keep[...] = (i != j).astype(F32)
    for w in range(count):
        qb[w] = jnp.broadcast_to(charges[w], (slots, slots)).T

    unroll = min(beads, 4)

    def tile(ref, n):
        return ref[pl.ds(pl.multiple_of(n * 8, 8), 8), :]

    def parts(a):
        high = rounded(a)
        mid = a - high
        return high, mid

    def prepare(step, carry):
        for u in range(unroll):
            n = step * unroll + u
            high, mid = parts(jnp.where(left_rows, tile(tiles[0], n), left_fill))
            lt[n] = jnp.concatenate([high, high, mid, mid], axis=0).astype(BF16).T
            for o in range(3):
                value = jnp.where(right_rows, tile(tiles[1 + o], n), right_fill)
                high, mid = parts(value)
                rs[o][n] = jnp.concatenate([high, mid, high, mid], axis=0).astype(BF16)
                value = jnp.where(lane8 < mols, value, 0.0)
                if o:
                    value = pltpu.roll(value, o * mols, 1)
                high, mid = parts(value)
                packs[o][n] = jnp.concatenate([high, mid, high, mid], axis=0).astype(BF16)
        return carry

    lax.fori_loop(0, count * beads // unroll, prepare, 0)

    lanes = slots
    corner = lax.broadcasted_iota(jnp.int32, (8, slots), 1) < mols
    last_rows = (orows - 8) + row8 < mols
    groups = slots // 8

    def rotated(t, o):
        return t - int(OFFSETS[o]) * beads

    def multiply(n, offsets, product, near):
        targets = [rotated(n, o) for o in offsets]
        right = jnp.concatenate(
            [rs[o][t] for o, t in zip(offsets, targets)] + [sel_ref[...]], axis=1
        )
        left = lt[n]
        width = right.shape[1]
        product[:, :width] = dot_nn(left, right)
        pack = packs[offsets[0]][targets[0]]
        for o, t in zip(offsets[1:], targets[1:]):
            pack = pack + packs[o][t]
        near[:orows, :] = dot_nn(left[:orows], pack)

    def gather(n, w, r, offsets, product, near):
        count_targets = len(offsets)
        acc = [[None] * 4 for _ in offsets]

        def add(k, i, value):
            acc[k][i] = value if acc[k][i] is None else acc[k][i] + value

        for g in range(groups):
            rows = slice(8 * g, 8 * g + 8)
            coords = [
                product[rows, (count_targets + a) * lanes : (count_targets + a + 1) * lanes]
                for a in range(3)
            ]
            charge = qb[w, rows, :]
            if 8 * g < orows:
                root = lax.rsqrt(near[rows, :] + (lennard_soft - coulomb_soft))
                inverse = root * root
                cube = inverse * inverse * inverse
                lj = (cube * lj_a - lj_b) * (cube * inverse)
                allowed = corner & last_rows if 8 * g + 8 > mols else corner
            for k, o in enumerate(offsets):
                root = lax.rsqrt(product[rows, k * lanes : (k + 1) * lanes])
                strength = root * root * root
                if 8 * g < orows:
                    own = pltpu.roll(lj, slots - o * mols, 1) if o else lj
                    strength = strength + jnp.where(allowed, own, 0.0)
                strength = strength * charge
                if o == 0:
                    strength = strength * keep[rows, :]
                add(k, 3, strength)
                for a in range(3):
                    add(k, a, strength * coords[a])
        for k, o in enumerate(offsets):
            t = rotated(n, o)
            parts = acc[k]
            if o:
                parts[0] = parts[0] + OFFSETS[o] * parts[3]
            base = pl.multiple_of(t * 32, 32)
            if o != 2:
                parts = [a + sums[pl.ds(base + 8 * i, 8), :] for i, a in enumerate(parts)]
            if o != 1:
                for i, a in enumerate(parts):
                    sums[pl.ds(base + 8 * i, 8), :] = a
            else:
                parts = [jnp.sum(a, axis=0, keepdims=True) for a in parts]
                own = tile(tiles[1], t)
                scale = charges[w - 1] * pair_scale
                for a in range(3):
                    put(w - 1, r, a, (own[a : a + 1] * parts[3] - parts[a]) * scale)

    kinds = []
    for w in range(count):
        offsets = tuple(o for o in (2, 0, 1) if 1 <= w - int(OFFSETS[o]) <= count - 2)
        if kinds and kinds[-1][0] == offsets:
            kinds[-1][2] = w + 1
        else:
            kinds.append([offsets, w, w + 1])
    for offsets, first, last in kinds:
        end = last * beads
        multiply(first * beads, offsets, product[0], near[0])

        def step(index, carry, offsets=offsets, end=end):
            n = index * 2
            w = lax.div(n, beads)
            r = lax.rem(n, beads)
            multiply(n + 1, offsets, product[1], near[1])
            gather(n, w, r, offsets, product[0], near[0])
            multiply(jnp.minimum(n + 2, end - 1), offsets, product[0], near[0])
            gather(n + 1, w, r + 1, offsets, product[1], near[1])
            return carry

        lax.fori_loop(first * beads // 2, end // 2, step, 0)


def outer_kernel(nb, group, lb, cells, mols, slots, b_ref, *refs):
    x_ref, p_ref, q_ref, left, right, sel_ref = refs[:6]
    outs, q_out = refs[6 : 6 + nb], refs[6 + nb]
    kicked, scratch = refs[7 + nb], refs[8 + nb :]
    n = 3 * lb
    count = cells + 2 * X_HALO
    b = b_ref[0]

    def cell_rows(w):
        if w < X_HALO:
            return left[pl.ds(w * n, n), :]
        if w >= cells + X_HALO:
            return right[pl.ds((w - cells - X_HALO) * n, n), :]
        return x_ref[w - X_HALO]

    charge_rows = [left[pl.ds(9 * lb + e, 1), :] for e in range(2)]
    charge_rows += [q_ref[c : c + 1, :] for c in range(cells)]
    charge_rows += [right[pl.ds(9 * lb + e, 1), :] for e in range(2)]
    q_out[...] = jnp.zeros(q_out.shape, F32)
    for w in range(count):
        q_out[w : w + 1, :] = charge_rows[w]
    for w in range(count):
        rows = cell_rows(w)
        build_tiles(scratch[:4], w * lb, lb, rows[:lb], rows[lb : 2 * lb], rows[2 * lb :])

    def put(w, r, comp, value):
        kicked[w - 1, pl.ds(comp * lb + r, 1), :] = value

    pair_forces(scratch, sel_ref, Rows(q_out, 0), put, count, mols, lb, slots)
    half = 0.5 * outer_step
    for w in range(1, count - 1):
        if w < X_HALO:
            old = left[pl.ds(2 * n, n), :]
        elif w >= cells + X_HALO:
            old = right[pl.ds(2 * n, n), :]
        else:
            old = p_ref[w - X_HALO]
        kicked[w - 1] = old + half * kicked[w - 1]
    width = group + 2 * P_HALO
    for k in range(nb):
        first = lax.rem(b + k, nb) * group
        for w in range(width):
            outs[k][pl.ds((width + w) * n, n), :] = kicked[first + w]
            source = first + w - P_HALO
            inside = x_ref[jnp.clip(source, 0, cells - 1)]
            if w < P_HALO:
                inside = jnp.where(source < 0, left[pl.ds(n, n), :], inside)
            elif w >= group + P_HALO:
                inside = jnp.where(source >= cells, right[pl.ds(0, n), :], inside)
            outs[k][pl.ds(w * n, n), :] = inside


class Rows:
    def __init__(self, ref, first):
        self.ref, self.first = ref, first

    def __getitem__(self, index):
        return self.ref[pl.ds(self.first + index, 1), :]


def bond_forces(x, y, z, used, mols, slots):
    def partner(a, t):
        return pltpu.roll(a, slots - t * mols, 1)

    first = [a - partner(a, 1) for a in (x, y, z)]
    second = [a - partner(a, 2) for a in (x, y, z)]
    third = [s - f for f, s in zip(first, second)]

    def pull(bond, stiffness, square):
        length = bond[0] * bond[0] + bond[1] * bond[1] + bond[2] * bond[2]
        return (stiffness * used) * (length - square)

    c1 = pull(first, bond_stiffness, bond_square)
    c2 = pull(second, bond_stiffness, bond_square)
    c3 = pull(third, angle_stiffness, angle_square)
    out = []
    for f, s, t in zip(first, second, third):
        on_first = c1 * f - c3 * t
        on_second = c2 * s + c3 * t
        on_oxygen = -(c1 * f + c2 * s)
        out.append(
            on_oxygen + pltpu.roll(on_first, mols, 1) + pltpu.roll(on_second, 2 * mols, 1)
        )
    return out


def inner_kernel(nb, group, lb, cells, mols, slots, b_ref, *refs):
    blocks = refs[:nb]
    step_ref, perm_ref, q_ref, sel_ref = refs[nb : nb + 4]
    ys = refs[nb + 4 : 2 * nb + 4]
    xv, ft, scratch = refs[2 * nb + 4], refs[2 * nb + 5], refs[2 * nb + 6 :]
    beads = nb * lb
    width = group + 2 * P_HALO
    n = 3 * lb
    b = b_ref[0]
    step = step_ref[...]
    charges = Rows(q_ref, b * group + P_HALO)

    def advance(pos, vel):
        out_x, out_v = [], []
        for x, v in zip(pos, vel):
            high, mid, low = split3(jnp.concatenate([x, v], axis=0))
            stacked = jnp.concatenate([high, mid, high, mid, low, high], axis=0).astype(BF16)
            new = dot_nn(step, stacked)
            out_x.append(new[:beads])
            out_v.append(new[beads:])
        return out_x, out_v

    for w in range(width):
        def gather(a, comp):
            return jnp.concatenate(
                [block[pl.ds((a * width + w) * n + comp * lb, lb), :] for block in blocks], axis=0
            )

        q = charges[w]
        oxygen = (q < -1.5).astype(F32)
        inverse = jnp.where(q < -1.5, 1.0 / oxygen_mass, 1.0)
        pos = [gather(0, c) for c in range(3)]
        vel = [gather(1, c) * inverse for c in range(3)]
        half = (0.5 * inner_step) * inverse
        full = inner_step * inverse
        force = bond_forces(*pos, oxygen, mols, slots)
        vel = [v + half * f for v, f in zip(vel, force)]
        pos, vel = advance(pos, vel)
        force = bond_forces(*pos, oxygen, mols, slots)
        vel = [v + full * f for v, f in zip(vel, force)]
        pos, vel = advance(pos, vel)
        if 1 <= w <= width - 2:
            force = bond_forces(*pos, oxygen, mols, slots)
            vel = [v + half * f for v, f in zip(vel, force)]
            mass = jnp.where(q < -1.5, oxygen_mass, 1.0)
            for c in range(3):
                xv[w - 1, pl.ds(c * beads, beads), :] = pos[c]
                xv[w - 1, pl.ds((3 + c) * beads, beads), :] = vel[c] * mass
        build_tiles(scratch[:4], w * beads, beads, *pos)

    def put(w, r, comp, value):
        ft[w - 1, pl.ds(comp * beads + r, 1), :] = value

    pair_forces(scratch, sel_ref, charges, put, width, mols, beads, slots)
    for w in range(group):
        old = xv[w]
        m = 3 * beads
        state = jnp.concatenate([old[:m], old[m:] + (0.5 * outer_step) * ft[w]], axis=0)
        state = unpermuted(state, perm_ref[b * group + w])
        for a in range(2):
            for c in range(3):
                for k in range(nb):
                    row = (a * 3 + c) * beads + k * lb
                    ys[k][pl.ds(((a * group + w) * 3 + c) * lb, lb), :] = state[row : row + lb]


def unpack_kernel(nb, group, lb, cells, b_ref, *refs):
    ys = refs[:nb]
    outs = refs[nb:]
    b = b_ref[0]
    for k in range(nb):
        source = lax.rem(b + k, nb)
        for a in range(2):
            for w in range(group):
                for c in range(3):
                    outs[a][pl.ds(c * cells + source * group + w, lb, stride=3 * cells), :] = ys[
                        k
                    ][pl.ds(((a * group + w) * 3 + c) * lb, lb), :]


def call(kernel, outs, scratch, scalar, *operands):
    vmem = pl.BlockSpec(memory_space=pltpu.VMEM)
    smem = pl.BlockSpec(memory_space=pltpu.SMEM)
    return pl.pallas_call(
        kernel,
        out_shape=outs,
        in_specs=([] if scalar is None else [smem]) + [vmem] * len(operands),
        out_specs=[vmem] * len(outs),
        scratch_shapes=scratch,
        compiler_params=pltpu.CompilerParams(vmem_limit_bytes=48 * 1024 * 1024),
    )(*(() if scalar is None else (scalar,)), *operands)


def local(nb, ns, positions, momenta, molecules):
    lb, _, cells, slots = positions.shape
    mols = molecules.shape[1]
    group = cells // nb
    beads = lb * nb
    width = group + 2 * P_HALO
    b = lax.axis_index("bead").astype(jnp.int32).reshape(1)

    def shape(*dims):
        return jax.ShapeDtypeStruct(dims, F32)

    lanes = jnp.transpose(molecules, (0, 2, 1)).reshape(cells, 3 * mols)
    lanes = jnp.pad(lanes, ((0, 0), (0, slots - 3 * mols)), constant_values=slots)
    edge = shape(9 * lb + 8, slots)
    xs, ps, perm, charges, to_right, to_left = call(
        functools.partial(order_kernel, lb, cells, mols, slots),
        [shape(cells, 3 * lb, slots)] * 2
        + [jax.ShapeDtypeStruct((cells, slots, slots), BF16), shape(cells, slots), edge, edge],
        [],
        None,
        lanes,
        positions.reshape(lb * 3 * cells, slots),
        momenta.reshape(lb * 3 * cells, slots),
    )
    left = lax.ppermute(to_right, "space", [(s, (s + 1) % ns) for s in range(ns)])
    right = lax.ppermute(to_left, "space", [(s, (s - 1) % ns) for s in range(ns)])
    sel = jnp.asarray(selectors(slots))
    q_rows = -(-(cells + 2 * X_HALO) // 8) * 8
    *blocks, q_wide = call(
        functools.partial(outer_kernel, nb, group, lb, cells, mols, slots),
        [shape(2 * width * 3 * lb, slots)] * nb + [shape(q_rows, slots)],
        [pltpu.VMEM((cells + 2 * P_HALO, 3 * lb, slots), F32)]
        + pair_scratch(cells + 2 * X_HALO, lb, slots),
        b,
        xs,
        ps,
        charges,
        left,
        right,
        sel,
    )
    blocks = [blocks[0]] + [
        lax.ppermute(blocks[k], "bead", [(i, (i + k) % nb) for i in range(nb)])
        for k in range(1, nb)
    ]
    step = jnp.asarray(propagator(beads, lb))
    ys = call(
        functools.partial(inner_kernel, nb, group, lb, cells, mols, slots),
        [shape(2 * group * 3 * lb, slots)] * nb,
        [
            pltpu.VMEM((group, 6 * beads, slots), F32),
            pltpu.VMEM((group, 3 * beads, slots), F32),
        ]
        + pair_scratch(width, beads, slots),
        b,
        *blocks,
        step,
        perm,
        q_wide,
        sel,
    )
    ys = [ys[0]] + [
        lax.ppermute(ys[k], "bead", [(i, (i - k) % nb) for i in range(nb)]) for k in range(1, nb)
    ]
    new_x, new_p = call(
        functools.partial(unpack_kernel, nb, group, lb, cells),
        [shape(lb * 3 * cells, slots)] * 2,
        [],
        b,
        *ys,
    )
    return new_x.reshape(positions.shape), new_p.reshape(positions.shape)


def solution(mesh):
    spec = P("bead", None, "space", None)
    return jax.shard_map(
        functools.partial(local, mesh.shape["bead"], mesh.shape["space"]),
        mesh=mesh,
        in_specs=(spec, spec, P("space", None, None)),
        out_specs=(spec, spec),
        check_vma=False,
    )
```

```python
import functools

import jax
import jax.numpy as jnp
import ml_dtypes
import numpy as np
from jax import lax
from jax.experimental import pallas as pl
from jax.experimental.pallas import tpu as pltpu
from jax.sharding import PartitionSpec as P

charge_oxygen = -0.8476
charge_hydrogen = 0.4238
coulomb_scale = 24.0
coulomb_soft = 0.004
well_depth = 0.02
sigma_square = 0.0841
lennard_soft = 0.04
bond_stiffness = 20000.0
bond_square = 0.0081
angle_stiffness = 5000.0
angle_square = 0.0204
cycle_frequency = 60.0
outer_step = 0.02
inner_step = 0.01
oxygen_mass = 16.0

REACH = 1
X_HALO = 2 * REACH
P_HALO = REACH

F32 = jnp.float32
BF16 = jnp.bfloat16


def rounded(a):
    return a.astype(BF16).astype(F32)


def split3(a):
    high = rounded(a)
    rest = a - high
    mid = rounded(rest)
    return high, mid, rest - mid


def two_part(a):
    high = rounded(a)
    return high + rounded(a - high)


def dot_nn(a, b):
    return lax.dot_general(a, b, (((1,), (0,)), ((), ())), preferred_element_type=F32)


def dot_nt(a, b):
    return lax.dot_general(a, b, (((1,), (1,)), ((), ())), preferred_element_type=F32)


def propagator(beads, beads_dev):
    j = np.arange(beads)
    angles = 2.0 * np.pi * ((j[:, None] * j[None, :]) % beads) / beads
    half = beads // 2
    col = j[None, :]
    u = np.where(
        col == 0,
        np.sqrt(1.0 / beads),
        np.where(
            col < half,
            np.sqrt(2.0 / beads) * np.cos(angles),
            np.where(
                col == half,
                np.sqrt(1.0 / beads) * np.cos(angles),
                np.sqrt(2.0 / beads) * np.sin(angles),
            ),
        ),
    )
    w = 2.0 * cycle_frequency * np.sin(np.pi * j / beads)
    cosines = np.cos(w * inner_step)
    spring = w * np.sin(w * inner_step)
    drift = np.where(j == 0, inner_step, np.sin(w * inner_step) / np.where(j == 0, 1.0, w))
    k = j // beads_dev
    i = j % beads_dev
    index = (beads_dev * (k[None, :] - k[:, None]) + i[:, None] - i[None, :]) % beads

    def circulant(values):
        return ((u * values) @ u.T)[:, 0][index]

    a = circulant(cosines)
    whole = np.block([[a, circulant(drift)], [-circulant(spring), a]])
    high = whole.astype(ml_dtypes.bfloat16)
    rest = whole - high.astype(np.float64)
    mid = rest.astype(ml_dtypes.bfloat16)
    low = (rest - mid.astype(np.float64)).astype(ml_dtypes.bfloat16)
    return np.concatenate([high, high, mid, mid, high, low], axis=1)


def lane_tables(lanes, mols, slots):
    lane = lax.broadcasted_iota(jnp.int32, lanes.shape, 1)
    unit = jnp.where(lane < mols, charge_oxygen / charge_hydrogen, 1.0)
    return jnp.where(lanes < slots, unit, 0.0)


def lane_matrix(lanes, slots, row, before, upper, ones):
    far = 4.0 * slots
    key = jnp.broadcast_to(lanes.astype(F32), (8, slots))
    free = key >= slots
    rank = dot_nn(free.astype(F32).astype(BF16), upper)
    key = jnp.where(free, far + rank, key)[0:1]
    held = (row == key).astype(F32).astype(BF16)
    used = dot_nn(held, ones)
    count = dot_nn(before, used.astype(BF16))
    slot_key = jnp.where(used > 0.5, row, far + row - count)
    return (slot_key == key).astype(F32).astype(BF16)


def permuted(rows, perm):
    n = rows.shape[0]
    stacked = jnp.concatenate(split3(rows), axis=0).astype(BF16)
    moved = dot_nn(stacked, perm)
    return moved[:n] + moved[n : 2 * n] + moved[2 * n :]


def unpermuted(rows, perm):
    n = rows.shape[0]
    stacked = jnp.concatenate(split3(rows), axis=0).astype(BF16)
    moved = dot_nt(stacked, perm)
    return moved[:n] + moved[n : 2 * n] + moved[2 * n :]


def order_kernel(lb, cells, mols, slots, lane_ref, x_ref, p_ref, *outs):
    xo, po, perm_ref, q_ref, to_right, to_left = outs
    row = lax.broadcasted_iota(jnp.int32, (slots, slots), 0).astype(F32)
    col = lax.broadcasted_iota(jnp.int32, (slots, slots), 1).astype(F32)
    before = (col < row).astype(BF16)
    upper = (row < col).astype(BF16)
    ones = jnp.ones((slots, slots), BF16)
    charges = lane_tables(lane_ref[...], mols, slots)
    q_ref[...] = charges
    n = 3 * lb
    for cell in range(cells):
        perm = lane_matrix(lane_ref[cell : cell + 1, :], slots, row, before, upper, ones)
        perm_ref[cell] = perm
        rows = [
            ref[pl.ds(comp * cells + cell, lb, stride=3 * cells), :]
            for ref in (x_ref, p_ref)
            for comp in range(3)
        ]
        moved = permuted(jnp.concatenate(rows, axis=0), perm)
        xo[cell] = moved[:n]
        po[cell] = moved[n:]
    for out, xs, ps in (
        (to_right, (cells - 2, cells - 1), cells - 1),
        (to_left, (0, 1), 0),
    ):
        out[9 * lb :, :] = jnp.zeros((8, slots), F32)
        for e, cell in enumerate(xs):
            out[pl.ds(e * n, n), :] = xo[cell]
            out[pl.ds(9 * lb + e, 1), :] = charges[cell : cell + 1]
        out[pl.ds(2 * n, n), :] = po[ps]


def put_tiles(scratch, first, count, rows):
    for index, value in rows:
        scratch[pl.ds(first * 8 + index, count, stride=8), :] = value


def build_tiles(tiles, first, count, x, y, z):
    left, rights = tiles[0], tiles[1:]
    xa = two_part(x - 0.5)
    ya = two_part(y - 0.5)
    za = two_part(z - 0.5)
    side = ya * ya + za * za

    def parts(n):
        high = two_part(n)
        return high, n - high

    n_high, n_low = parts(side + xa * xa + coulomb_soft)
    put_tiles(
        left,
        first,
        count,
        ((0, -2.0 * xa), (1, -2.0 * ya), (2, -2.0 * za), (3, n_high), (4, n_low)),
    )
    for ref, offset in zip(rights, OFFSETS):
        xo = two_part(xa - offset) if offset else xa
        n_high, n_low = parts(side + xo * xo)
        put_tiles(ref, first, count, ((0, xo), (1, ya), (2, za), (5, n_high), (6, n_low)))


OFFSETS = (0.0, 1.0, -1.0)


def pair_scratch(count, beads, slots):
    n = count * beads
    return (
        [pltpu.VMEM((n * 8, slots), F32)] * 4
        + [pltpu.VMEM((n, slots, 32), BF16)]
        + [pltpu.VMEM((n, 32, slots), BF16)] * 6
        + [pltpu.VMEM((count, slots, slots), F32)]
        + [pltpu.VMEM((n * 32, slots), F32)]
        + [pltpu.VMEM((slots, slots), F32)]
        + [pltpu.VMEM((n, slots, 8), F32)]
    )


def pair_forces(scratch, charges, put, count, mols, beads, slots):
    tiles, lt, rs, packs = scratch[:4], scratch[4], scratch[5:8], scratch[8:11]
    qb, sums, keep, xt = scratch[11:]
    orows = -(-mols // 8) * 8
    pair_scale = coulomb_scale * charge_hydrogen * charge_hydrogen
    k3 = sigma_square**3
    ratio = (charge_hydrogen / charge_oxygen) ** 2 / pair_scale
    lj_a = 24.0 * well_depth * 2.0 * k3 * k3 * ratio
    lj_b = 24.0 * well_depth * k3 * ratio
    row8 = lax.broadcasted_iota(jnp.int32, (8, slots), 0)
    lane8 = lax.broadcasted_iota(jnp.int32, (8, slots), 1)
    left_rows = row8 < 5
    left_fill = jnp.where((row8 == 5) | (row8 == 6), 1.0, 0.0)
    right_rows = (row8 < 3) | (row8 == 5) | (row8 == 6)
    right_fill = jnp.where((row8 == 3) | (row8 == 4), 1.0, 0.0)
    lj_row = lax.broadcasted_iota(jnp.int32, (orows, slots), 0)
    lj_lane = lax.broadcasted_iota(jnp.int32, (orows, slots), 1)
    corner = (lj_row < mols) & (lj_lane < mols)

    i = lax.broadcasted_iota(jnp.int32, (slots, slots), 0)
    j = lax.broadcasted_iota(jnp.int32, (slots, slots), 1)
    i = jnp.where(i >= 2 * mols, i - 2 * mols, jnp.where(i >= mols, i - mols, i))
    j = jnp.where(j >= 2 * mols, j - 2 * mols, jnp.where(j >= mols, j - mols, j))
    keep[...] = (i != j).astype(F32)
    for w in range(count):
        qb[w] = jnp.broadcast_to(charges[w], (slots, slots)).T

    unroll = min(beads, 4)

    def tile(ref, n):
        return ref[pl.ds(pl.multiple_of(n * 8, 8), 8), :]

    def parts(a):
        high = rounded(a)
        mid = a - high
        return high, mid

    def prepare(step, carry):
        for u in range(unroll):
            n = step * unroll + u
            high, mid = parts(jnp.where(left_rows, tile(tiles[0], n), left_fill))
            lt[n] = jnp.concatenate([high, high, mid, mid], axis=0).astype(BF16).T
            xt[n] = jnp.where(row8 < 3, tile(tiles[1], n), 0.0).T
            for o in range(3):
                value = jnp.where(right_rows, tile(tiles[1 + o], n), right_fill)
                high, mid = parts(value)
                rs[o][n] = jnp.concatenate([high, mid, high, mid], axis=0).astype(BF16)
                value = jnp.where(lane8 < mols, value, 0.0)
                if o:
                    value = pltpu.roll(value, o * mols, 1)
                high, mid = parts(value)
                packs[o][n] = jnp.concatenate([high, mid, high, mid], axis=0).astype(BF16)
        return carry

    lax.fori_loop(0, count * beads // unroll, prepare, 0)

    def down(a):
        return jnp.sum(a.reshape(slots // 8, 8, slots), axis=0)

    def peer(n, w, r, offsets):
        targets = [n - int(OFFSETS[o]) * beads for o in offsets]
        right = jnp.concatenate([rs[o][t] for o, t in zip(offsets, targets)], axis=1)
        left = lt[n]
        product = dot_nn(left, right)
        columns = xt[n]
        coords = [jnp.broadcast_to(columns[:, a : a + 1], (slots, slots)) for a in range(3)]
        pack = packs[offsets[0]][targets[0]]
        for o, t in zip(offsets[1:], targets[1:]):
            pack = pack + packs[o][t]
        lj_root = lax.rsqrt(dot_nn(left[:orows], pack) + (lennard_soft - coulomb_soft))
        inverse = lj_root * lj_root
        cube = inverse * inverse * inverse
        lj = (cube * lj_a - lj_b) * (cube * inverse)
        charge = qb[w]
        for k, (o, t) in enumerate(zip(offsets, targets)):
            root = lax.rsqrt(product[:, k * slots : (k + 1) * slots])
            strength = root * root * root
            own = pltpu.roll(lj, slots - o * mols, 1) if o else lj
            strength = jnp.concatenate(
                [strength[:orows] + jnp.where(corner, own, 0.0), strength[orows:]], axis=0
            )
            strength = strength * charge
            if o == 0:
                strength = strength * keep[...]
            total = down(strength)
            parts = [down(strength * c) for c in coords]
            if o:
                parts[0] = parts[0] + OFFSETS[o] * total
            parts.append(total)
            base = pl.multiple_of(t * 32, 32)
            if o != 2:
                parts = [
                    a + sums[pl.ds(base + 8 * i, 8), :] for i, a in enumerate(parts)
                ]
            if o != 1:
                for i, a in enumerate(parts):
                    sums[pl.ds(base + 8 * i, 8), :] = a
            else:
                parts = [jnp.sum(a, axis=0, keepdims=True) for a in parts]
                own = tile(tiles[1], t)
                scale = charges[w - 1] * pair_scale
                for a in range(3):
                    put(w - 1, r, a, (own[a : a + 1] * parts[3] - parts[a]) * scale)

    kinds = []
    for w in range(count):
        offsets = tuple(o for o in (2, 0, 1) if 1 <= w - int(OFFSETS[o]) <= count - 2)
        if kinds and kinds[-1][0] == offsets:
            kinds[-1][2] = w + 1
        else:
            kinds.append([offsets, w, w + 1])
    per_cell = beads // unroll
    for offsets, first, last in kinds:

        def step(index, carry, offsets=offsets):
            w = lax.div(index, per_cell)
            r = lax.rem(index, per_cell) * unroll
            for u in range(unroll):
                peer(w * beads + r + u, w, r + u, offsets)
            return carry

        lax.fori_loop(first * per_cell, last * per_cell, step, 0)


def outer_kernel(nb, group, lb, cells, mols, slots, b_ref, *refs):
    x_ref, p_ref, q_ref, left, right = refs[:5]
    outs, q_out = refs[5 : 5 + nb], refs[5 + nb]
    kicked, scratch = refs[6 + nb], refs[7 + nb :]
    n = 3 * lb
    count = cells + 2 * X_HALO
    b = b_ref[0]

    def cell_rows(w):
        if w < X_HALO:
            return left[pl.ds(w * n, n), :]
        if w >= cells + X_HALO:
            return right[pl.ds((w - cells - X_HALO) * n, n), :]
        return x_ref[w - X_HALO]

    charge_rows = [left[pl.ds(9 * lb + e, 1), :] for e in range(2)]
    charge_rows += [q_ref[c : c + 1, :] for c in range(cells)]
    charge_rows += [right[pl.ds(9 * lb + e, 1), :] for e in range(2)]
    q_out[...] = jnp.zeros(q_out.shape, F32)
    for w in range(count):
        q_out[w : w + 1, :] = charge_rows[w]
    for w in range(count):
        rows = cell_rows(w)
        build_tiles(scratch[:4], w * lb, lb, rows[:lb], rows[lb : 2 * lb], rows[2 * lb :])

    def put(w, r, comp, value):
        kicked[w - 1, pl.ds(comp * lb + r, 1), :] = value

    pair_forces(scratch, Rows(q_out, 0), put, count, mols, lb, slots)
    half = 0.5 * outer_step
    for w in range(1, count - 1):
        if w < X_HALO:
            old = left[pl.ds(2 * n, n), :]
        elif w >= cells + X_HALO:
            old = right[pl.ds(2 * n, n), :]
        else:
            old = p_ref[w - X_HALO]
        kicked[w - 1] = old + half * kicked[w - 1]
    width = group + 2 * P_HALO
    for k in range(nb):
        first = lax.rem(b + k, nb) * group
        for w in range(width):
            outs[k][pl.ds((width + w) * n, n), :] = kicked[first + w]
            source = first + w - P_HALO
            inside = x_ref[jnp.clip(source, 0, cells - 1)]
            if w < P_HALO:
                inside = jnp.where(source < 0, left[pl.ds(n, n), :], inside)
            elif w >= group + P_HALO:
                inside = jnp.where(source >= cells, right[pl.ds(0, n), :], inside)
            outs[k][pl.ds(w * n, n), :] = inside


class Rows:
    def __init__(self, ref, first):
        self.ref, self.first = ref, first

    def __getitem__(self, index):
        return self.ref[pl.ds(self.first + index, 1), :]


def bond_forces(x, y, z, used, mols, slots):
    def partner(a, t):
        return pltpu.roll(a, slots - t * mols, 1)

    first = [a - partner(a, 1) for a in (x, y, z)]
    second = [a - partner(a, 2) for a in (x, y, z)]
    third = [s - f for f, s in zip(first, second)]

    def pull(bond, stiffness, square):
        length = bond[0] * bond[0] + bond[1] * bond[1] + bond[2] * bond[2]
        return (stiffness * used) * (length - square)

    c1 = pull(first, bond_stiffness, bond_square)
    c2 = pull(second, bond_stiffness, bond_square)
    c3 = pull(third, angle_stiffness, angle_square)
    out = []
    for f, s, t in zip(first, second, third):
        on_first = c1 * f - c3 * t
        on_second = c2 * s + c3 * t
        on_oxygen = -(c1 * f + c2 * s)
        out.append(
            on_oxygen + pltpu.roll(on_first, mols, 1) + pltpu.roll(on_second, 2 * mols, 1)
        )
    return out


def inner_kernel(nb, group, lb, cells, mols, slots, b_ref, *refs):
    blocks = refs[:nb]
    step_ref, perm_ref, q_ref = refs[nb : nb + 3]
    ys = refs[nb + 3 : 2 * nb + 3]
    xv, ft, scratch = refs[2 * nb + 3], refs[2 * nb + 4], refs[2 * nb + 5 :]
    beads = nb * lb
    width = group + 2 * P_HALO
    n = 3 * lb
    b = b_ref[0]
    step = step_ref[...]
    charges = Rows(q_ref, b * group + P_HALO)

    def advance(pos, vel):
        out_x, out_v = [], []
        for x, v in zip(pos, vel):
            high, mid, low = split3(jnp.concatenate([x, v], axis=0))
            stacked = jnp.concatenate([high, mid, high, mid, low, high], axis=0).astype(BF16)
            new = dot_nn(step, stacked)
            out_x.append(new[:beads])
            out_v.append(new[beads:])
        return out_x, out_v

    for w in range(width):
        def gather(a, comp):
            return jnp.concatenate(
                [block[pl.ds((a * width + w) * n + comp * lb, lb), :] for block in blocks], axis=0
            )

        q = charges[w]
        oxygen = (q < -1.5).astype(F32)
        inverse = jnp.where(q < -1.5, 1.0 / oxygen_mass, 1.0)
        pos = [gather(0, c) for c in range(3)]
        vel = [gather(1, c) * inverse for c in range(3)]
        half = (0.5 * inner_step) * inverse
        full = inner_step * inverse
        force = bond_forces(*pos, oxygen, mols, slots)
        vel = [v + half * f for v, f in zip(vel, force)]
        pos, vel = advance(pos, vel)
        force = bond_forces(*pos, oxygen, mols, slots)
        vel = [v + full * f for v, f in zip(vel, force)]
        pos, vel = advance(pos, vel)
        if 1 <= w <= width - 2:
            force = bond_forces(*pos, oxygen, mols, slots)
            vel = [v + half * f for v, f in zip(vel, force)]
            mass = jnp.where(q < -1.5, oxygen_mass, 1.0)
            for c in range(3):
                xv[w - 1, pl.ds(c * beads, beads), :] = pos[c]
                xv[w - 1, pl.ds((3 + c) * beads, beads), :] = vel[c] * mass
        build_tiles(scratch[:4], w * beads, beads, *pos)

    def put(w, r, comp, value):
        ft[w - 1, pl.ds(comp * beads + r, 1), :] = value

    pair_forces(scratch, charges, put, width, mols, beads, slots)
    for w in range(group):
        old = xv[w]
        m = 3 * beads
        state = jnp.concatenate([old[:m], old[m:] + (0.5 * outer_step) * ft[w]], axis=0)
        state = unpermuted(state, perm_ref[b * group + w])
        for a in range(2):
            for c in range(3):
                for k in range(nb):
                    row = (a * 3 + c) * beads + k * lb
                    ys[k][pl.ds(((a * group + w) * 3 + c) * lb, lb), :] = state[row : row + lb]


def unpack_kernel(nb, group, lb, cells, b_ref, *refs):
    ys = refs[:nb]
    outs = refs[nb:]
    b = b_ref[0]
    for k in range(nb):
        source = lax.rem(b + k, nb)
        for a in range(2):
            for w in range(group):
                for c in range(3):
                    outs[a][pl.ds(c * cells + source * group + w, lb, stride=3 * cells), :] = ys[
                        k
                    ][pl.ds(((a * group + w) * 3 + c) * lb, lb), :]


def call(kernel, outs, scratch, scalar, *operands):
    vmem = pl.BlockSpec(memory_space=pltpu.VMEM)
    smem = pl.BlockSpec(memory_space=pltpu.SMEM)
    return pl.pallas_call(
        kernel,
        out_shape=outs,
        in_specs=([] if scalar is None else [smem]) + [vmem] * len(operands),
        out_specs=[vmem] * len(outs),
        scratch_shapes=scratch,
        compiler_params=pltpu.CompilerParams(vmem_limit_bytes=48 * 1024 * 1024),
    )(*(() if scalar is None else (scalar,)), *operands)


def local(nb, ns, positions, momenta, molecules):
    lb, _, cells, slots = positions.shape
    mols = molecules.shape[1]
    group = cells // nb
    beads = lb * nb
    width = group + 2 * P_HALO
    b = lax.axis_index("bead").astype(jnp.int32).reshape(1)

    def shape(*dims):
        return jax.ShapeDtypeStruct(dims, F32)

    lanes = jnp.transpose(molecules, (0, 2, 1)).reshape(cells, 3 * mols)
    lanes = jnp.pad(lanes, ((0, 0), (0, slots - 3 * mols)), constant_values=slots)
    edge = shape(9 * lb + 8, slots)
    xs, ps, perm, charges, to_right, to_left = call(
        functools.partial(order_kernel, lb, cells, mols, slots),
        [shape(cells, 3 * lb, slots)] * 2
        + [jax.ShapeDtypeStruct((cells, slots, slots), BF16), shape(cells, slots), edge, edge],
        [],
        None,
        lanes,
        positions.reshape(lb * 3 * cells, slots),
        momenta.reshape(lb * 3 * cells, slots),
    )
    left = lax.ppermute(to_right, "space", [(s, (s + 1) % ns) for s in range(ns)])
    right = lax.ppermute(to_left, "space", [(s, (s - 1) % ns) for s in range(ns)])
    q_rows = -(-(cells + 2 * X_HALO) // 8) * 8
    *blocks, q_wide = call(
        functools.partial(outer_kernel, nb, group, lb, cells, mols, slots),
        [shape(2 * width * 3 * lb, slots)] * nb + [shape(q_rows, slots)],
        [pltpu.VMEM((cells + 2 * P_HALO, 3 * lb, slots), F32)]
        + pair_scratch(cells + 2 * X_HALO, lb, slots),
        b,
        xs,
        ps,
        charges,
        left,
        right,
    )
    blocks = [blocks[0]] + [
        lax.ppermute(blocks[k], "bead", [(i, (i + k) % nb) for i in range(nb)])
        for k in range(1, nb)
    ]
    step = jnp.asarray(propagator(beads, lb))
    ys = call(
        functools.partial(inner_kernel, nb, group, lb, cells, mols, slots),
        [shape(2 * group * 3 * lb, slots)] * nb,
        [
            pltpu.VMEM((group, 6 * beads, slots), F32),
            pltpu.VMEM((group, 3 * beads, slots), F32),
        ]
        + pair_scratch(width, beads, slots),
        b,
        *blocks,
        step,
        perm,
        q_wide,
    )
    ys = [ys[0]] + [
        lax.ppermute(ys[k], "bead", [(i, (i - k) % nb) for i in range(nb)]) for k in range(1, nb)
    ]
    new_x, new_p = call(
        functools.partial(unpack_kernel, nb, group, lb, cells),
        [shape(lb * 3 * cells, slots)] * 2,
        [],
        b,
        *ys,
    )
    return new_x.reshape(positions.shape), new_p.reshape(positions.shape)


def solution(mesh):
    spec = P("bead", None, "space", None)
    return jax.shard_map(
        functools.partial(local, mesh.shape["bead"], mesh.shape["space"]),
        mesh=mesh,
        in_specs=(spec, spec, P("space", None, None)),
        out_specs=(spec, spec),
        check_vma=False,
    )
```

```python
import functools

import jax
import jax.numpy as jnp
import ml_dtypes
import numpy as np
from jax import lax
from jax.experimental import pallas as pl
from jax.experimental.pallas import tpu as pltpu
from jax.sharding import PartitionSpec as P

charge_oxygen = -0.8476
charge_hydrogen = 0.4238
coulomb_scale = 24.0
coulomb_soft = 0.004
well_depth = 0.02
sigma_square = 0.0841
lennard_soft = 0.04
bond_stiffness = 20000.0
bond_square = 0.0081
angle_stiffness = 5000.0
angle_square = 0.0204
cycle_frequency = 60.0
outer_step = 0.02
inner_step = 0.01
oxygen_mass = 16.0

REACH = 1
X_HALO = 2 * REACH
P_HALO = REACH

F32 = jnp.float32
BF16 = jnp.bfloat16


def rounded(a):
    return a.astype(BF16).astype(F32)


def split3(a):
    high = rounded(a)
    rest = a - high
    mid = rounded(rest)
    return high, mid, rest - mid


def two_part(a):
    high = rounded(a)
    return high + rounded(a - high)


def dot_nn(a, b):
    return lax.dot_general(a, b, (((1,), (0,)), ((), ())), preferred_element_type=F32)


def dot_nt(a, b):
    return lax.dot_general(a, b, (((1,), (1,)), ((), ())), preferred_element_type=F32)


def propagator(beads, beads_dev):
    j = np.arange(beads)
    angles = 2.0 * np.pi * ((j[:, None] * j[None, :]) % beads) / beads
    half = beads // 2
    col = j[None, :]
    u = np.where(
        col == 0,
        np.sqrt(1.0 / beads),
        np.where(
            col < half,
            np.sqrt(2.0 / beads) * np.cos(angles),
            np.where(
                col == half,
                np.sqrt(1.0 / beads) * np.cos(angles),
                np.sqrt(2.0 / beads) * np.sin(angles),
            ),
        ),
    )
    w = 2.0 * cycle_frequency * np.sin(np.pi * j / beads)
    cosines = np.cos(w * inner_step)
    spring = w * np.sin(w * inner_step)
    drift = np.where(j == 0, inner_step, np.sin(w * inner_step) / np.where(j == 0, 1.0, w))
    k = j // beads_dev
    i = j % beads_dev
    index = (beads_dev * (k[None, :] - k[:, None]) + i[:, None] - i[None, :]) % beads

    def circulant(values):
        return ((u * values) @ u.T)[:, 0][index]

    a = circulant(cosines)
    whole = np.block([[a, circulant(drift)], [-circulant(spring), a]])
    high = whole.astype(ml_dtypes.bfloat16)
    rest = whole - high.astype(np.float64)
    mid = rest.astype(ml_dtypes.bfloat16)
    low = (rest - mid.astype(np.float64)).astype(ml_dtypes.bfloat16)
    return np.concatenate([high, high, mid, mid, high, low], axis=1)


def lane_tables(lanes, mols, slots):
    lane = lax.broadcasted_iota(jnp.int32, lanes.shape, 1)
    unit = jnp.where(lane < mols, charge_oxygen / charge_hydrogen, 1.0)
    return jnp.where(lanes < slots, unit, 0.0)


def lane_matrix(lanes, slots, row, before, upper, ones):
    far = 4.0 * slots
    key = jnp.broadcast_to(lanes.astype(F32), (8, slots))
    free = key >= slots
    rank = dot_nn(free.astype(F32).astype(BF16), upper)
    key = jnp.where(free, far + rank, key)[0:1]
    held = (row == key).astype(F32).astype(BF16)
    used = dot_nn(held, ones)
    count = dot_nn(before, used.astype(BF16))
    slot_key = jnp.where(used > 0.5, row, far + row - count)
    return (slot_key == key).astype(F32).astype(BF16)


def permuted(rows, perm):
    n = rows.shape[0]
    stacked = jnp.concatenate(split3(rows), axis=0).astype(BF16)
    moved = dot_nn(stacked, perm)
    return moved[:n] + moved[n : 2 * n] + moved[2 * n :]


def unpermuted(rows, perm):
    n = rows.shape[0]
    stacked = jnp.concatenate(split3(rows), axis=0).astype(BF16)
    moved = dot_nt(stacked, perm)
    return moved[:n] + moved[n : 2 * n] + moved[2 * n :]


def order_kernel(lb, cells, mols, slots, lane_ref, x_ref, p_ref, *outs):
    xo, po, perm_ref, q_ref, to_right, to_left = outs
    row = lax.broadcasted_iota(jnp.int32, (slots, slots), 0).astype(F32)
    col = lax.broadcasted_iota(jnp.int32, (slots, slots), 1).astype(F32)
    before = (col < row).astype(BF16)
    upper = (row < col).astype(BF16)
    ones = jnp.ones((slots, slots), BF16)
    charges = lane_tables(lane_ref[...], mols, slots)
    q_ref[...] = charges
    n = 3 * lb
    for cell in range(cells):
        perm = lane_matrix(lane_ref[cell : cell + 1, :], slots, row, before, upper, ones)
        perm_ref[cell] = perm
        rows = [
            ref[pl.ds(comp * cells + cell, lb, stride=3 * cells), :]
            for ref in (x_ref, p_ref)
            for comp in range(3)
        ]
        moved = permuted(jnp.concatenate(rows, axis=0), perm)
        xo[cell] = moved[:n]
        po[cell] = moved[n:]
    for out, xs, ps in (
        (to_right, (cells - 2, cells - 1), cells - 1),
        (to_left, (0, 1), 0),
    ):
        out[9 * lb :, :] = jnp.zeros((8, slots), F32)
        for e, cell in enumerate(xs):
            out[pl.ds(e * n, n), :] = xo[cell]
            out[pl.ds(9 * lb + e, 1), :] = charges[cell : cell + 1]
        out[pl.ds(2 * n, n), :] = po[ps]


def put_tiles(scratch, first, count, rows):
    for index, value in rows:
        scratch[pl.ds(first * 8 + index, count, stride=8), :] = value


OFFSETS = (-1.0, 0.0, 1.0)


def build_tiles(tiles, first, count, x, y, z):
    xa = x - 0.5
    ya = two_part(y - 0.5)
    za = two_part(z - 0.5)
    side = ya * ya + za * za

    def parts(n):
        high = two_part(n)
        return high, n - high

    for ref, offset in zip(tiles, OFFSETS):
        xo = two_part(xa + offset if offset else xa)
        high, low = parts(side + xo * xo + coulomb_soft)
        put_tiles(
            ref, first, count, ((0, -2.0 * xo), (1, -2.0 * ya), (2, -2.0 * za), (3, high), (4, low))
        )
    xa = two_part(xa)
    high, low = parts(side + xa * xa)
    put_tiles(tiles[3], first, count, ((0, xa), (1, ya), (2, za), (5, high), (6, low)))


def pair_scratch(count, beads, slots):
    n = count * beads
    return (
        [pltpu.VMEM((n * 8, slots), F32)] * 5
        + [pltpu.VMEM((n // 2, slots, 64), BF16)] * 3
        + [pltpu.VMEM((n // 2, 32, slots), BF16)] * 3
        + [pltpu.VMEM((n, 32, slots), BF16)]
        + [pltpu.VMEM((slots, slots), F32)]
    )


def pair_forces(scratch, charges, count, mols, beads, slots):
    tiles, forces, lt, rr, rt = scratch[:4], scratch[4], scratch[5:8], scratch[8:11], scratch[11]
    keep = scratch[12]
    orows = -(-mols // 8) * 8
    pair_scale = coulomb_scale * charge_hydrogen * charge_hydrogen
    k3 = sigma_square**3
    ratio = (charge_hydrogen / charge_oxygen) ** 2 / pair_scale
    lj_a = 24.0 * well_depth * 2.0 * k3 * k3 * ratio
    lj_b = 24.0 * well_depth * k3 * ratio
    row8 = lax.broadcasted_iota(jnp.int32, (8, slots), 0)
    peer_rows = row8 < 5
    peer_fill = jnp.where((row8 == 5) | (row8 == 6), 1.0, 0.0)
    target_rows = (row8 < 3) | (row8 == 5) | (row8 == 6)
    target_fill = jnp.where((row8 == 3) | (row8 == 4), 1.0, 0.0)
    lj_row = lax.broadcasted_iota(jnp.int32, (orows, slots), 0)
    lj_lane = lax.broadcasted_iota(jnp.int32, (orows, slots), 1)
    first_lanes, second_lanes = lj_lane < mols, lj_lane < 2 * mols
    corner = (lj_row < mols) & first_lanes

    i = lax.broadcasted_iota(jnp.int32, (slots, slots), 0)
    j = lax.broadcasted_iota(jnp.int32, (slots, slots), 1)
    i = jnp.where(i >= 2 * mols, i - 2 * mols, jnp.where(i >= mols, i - mols, i))
    j = jnp.where(j >= 2 * mols, j - 2 * mols, jnp.where(j >= mols, j - mols, j))
    keep[...] = (i != j).astype(F32)

    pairs = beads // 2
    unroll = min(pairs, 4)
    per_cell = pairs // unroll

    def tile(ref, n):
        return ref[pl.ds(pl.multiple_of(n * 8, 8), 8), :]

    def parts(a):
        high = rounded(a)
        return high, a - high

    def stack(values):
        return jnp.concatenate(values, axis=0).astype(BF16)

    def prepare(step, carry):
        charge = charges[lax.div(step, per_cell)]
        weight = jnp.where(row8 < 3, -0.5 * charge, 0.0)
        unit = jnp.where(row8 == 3, charge, 0.0)
        for u in range(unroll):
            m = step * unroll + u
            for o in range(3):
                left, right = [], []
                for h in range(2):
                    high, mid = parts(jnp.where(peer_rows, tile(tiles[o], 2 * m + h), peer_fill))
                    left += [high, high, mid, mid]
                    right += [high * weight + unit, mid * weight]
                lt[o][m] = stack(left).T
                rr[o][m] = stack(right)
            for h in range(2):
                high, mid = parts(jnp.where(target_rows, tile(tiles[3], 2 * m + h), target_fill))
                rt[2 * m + h] = stack([high, mid, high, mid])
        return carry

    lax.fori_loop(0, count * per_cell, prepare, 0)
    zero = jnp.zeros((32, slots), BF16)

    def target(m, w):
        peers = [m - pairs, m, m + pairs]
        left = jnp.concatenate([lt[o][peers[o]] for o in range(3)], axis=0)
        right = jnp.concatenate(
            [
                jnp.concatenate([rt[2 * m], zero], axis=1),
                jnp.concatenate([zero, rt[2 * m + 1]], axis=1),
            ],
            axis=0,
        )
        squares = dot_nn(left, right)
        blocks = [[], [], []]
        for h in range(2):
            lanes = slice(h * slots, (h + 1) * slots)
            near = [squares[o * slots : o * slots + orows, lanes] for o in range(3)]
            packed = jnp.where(
                first_lanes,
                near[0],
                jnp.where(
                    second_lanes, pltpu.roll(near[1], mols, 1), pltpu.roll(near[2], 2 * mols, 1)
                ),
            )
            root = lax.rsqrt(packed + (lennard_soft - coulomb_soft))
            inverse = root * root
            cube = inverse * inverse * inverse
            lj = (cube * lj_a - lj_b) * (cube * inverse)
            for o in range(3):
                root = lax.rsqrt(squares[o * slots : (o + 1) * slots, lanes])
                strength = root * root * root
                own = pltpu.roll(lj, slots - o * mols, 1) if o else lj
                strength = jnp.concatenate(
                    [strength[:orows] + jnp.where(corner, own, 0.0), strength[orows:]], axis=0
                )
                if o == 1:
                    strength = strength * keep[...]
                high = strength.astype(BF16)
                low = (strength - high.astype(F32)).astype(BF16)
                blocks[o].append(jnp.concatenate([high, low], axis=0))
        sums = None
        for o in range(3):
            weights = rr[o][peers[o]]
            value = dot_nn(
                jnp.concatenate([weights, weights], axis=1), jnp.concatenate(blocks[o], axis=1)
            )
            sums = value if sums is None else sums + value
        scale = charges[w] * pair_scale
        for h in range(2):
            part = sums[16 * h : 16 * h + 16, h * slots : (h + 1) * slots]
            total = part[0:8] + part[8:16]
            n = 2 * m + h
            forces[pl.ds(pl.multiple_of(n * 8, 8), 8), :] = (
                tile(tiles[3], n) * total[3:4] - total
            ) * scale

    def step(index, carry):
        for u in range(unroll):
            target(index * unroll + u, lax.div(index, per_cell))
        return carry

    lax.fori_loop(per_cell, (count - 1) * per_cell, step, 0)

    def read(w, comp):
        return forces[pl.ds(w * beads * 8 + comp, beads, stride=8), :]

    return read


def outer_kernel(nb, group, lb, cells, mols, slots, b_ref, *refs):
    x_ref, p_ref, q_ref, left, right = refs[:5]
    outs, q_out = refs[5 : 5 + nb], refs[5 + nb]
    kicked, scratch = refs[6 + nb], refs[7 + nb :]
    n = 3 * lb
    count = cells + 2 * X_HALO
    b = b_ref[0]

    def cell_rows(w):
        if w < X_HALO:
            return left[pl.ds(w * n, n), :]
        if w >= cells + X_HALO:
            return right[pl.ds((w - cells - X_HALO) * n, n), :]
        return x_ref[w - X_HALO]

    charge_rows = [left[pl.ds(9 * lb + e, 1), :] for e in range(2)]
    charge_rows += [q_ref[c : c + 1, :] for c in range(cells)]
    charge_rows += [right[pl.ds(9 * lb + e, 1), :] for e in range(2)]
    q_out[...] = jnp.zeros(q_out.shape, F32)
    for w in range(count):
        q_out[w : w + 1, :] = charge_rows[w]
    for w in range(count):
        rows = cell_rows(w)
        build_tiles(scratch[:4], w * lb, lb, rows[:lb], rows[lb : 2 * lb], rows[2 * lb :])

    read = pair_forces(scratch, Rows(q_out, 0), count, mols, lb, slots)
    half = 0.5 * outer_step
    for w in range(1, count - 1):
        if w < X_HALO:
            old = left[pl.ds(2 * n, n), :]
        elif w >= cells + X_HALO:
            old = right[pl.ds(2 * n, n), :]
        else:
            old = p_ref[w - X_HALO]
        force = jnp.concatenate([read(w, c) for c in range(3)], axis=0)
        kicked[w - 1] = old + half * force
    width = group + 2 * P_HALO
    for k in range(nb):
        first = lax.rem(b + k, nb) * group
        for w in range(width):
            outs[k][pl.ds((width + w) * n, n), :] = kicked[first + w]
            source = first + w - P_HALO
            inside = x_ref[jnp.clip(source, 0, cells - 1)]
            if w < P_HALO:
                inside = jnp.where(source < 0, left[pl.ds(n, n), :], inside)
            elif w >= group + P_HALO:
                inside = jnp.where(source >= cells, right[pl.ds(0, n), :], inside)
            outs[k][pl.ds(w * n, n), :] = inside


class Rows:
    def __init__(self, ref, first):
        self.ref, self.first = ref, first

    def __getitem__(self, index):
        return self.ref[pl.ds(self.first + index, 1), :]


def bond_forces(x, y, z, used, mols, slots):
    def partner(a, t):
        return pltpu.roll(a, slots - t * mols, 1)

    first = [a - partner(a, 1) for a in (x, y, z)]
    second = [a - partner(a, 2) for a in (x, y, z)]
    third = [s - f for f, s in zip(first, second)]

    def pull(bond, stiffness, square):
        length = bond[0] * bond[0] + bond[1] * bond[1] + bond[2] * bond[2]
        return (stiffness * used) * (length - square)

    c1 = pull(first, bond_stiffness, bond_square)
    c2 = pull(second, bond_stiffness, bond_square)
    c3 = pull(third, angle_stiffness, angle_square)
    out = []
    for f, s, t in zip(first, second, third):
        on_first = c1 * f - c3 * t
        on_second = c2 * s + c3 * t
        on_oxygen = -(c1 * f + c2 * s)
        out.append(
            on_oxygen + pltpu.roll(on_first, mols, 1) + pltpu.roll(on_second, 2 * mols, 1)
        )
    return out


def inner_kernel(nb, group, lb, cells, mols, slots, b_ref, *refs):
    blocks = refs[:nb]
    step_ref, perm_ref, q_ref = refs[nb : nb + 3]
    ys = refs[nb + 3 : 2 * nb + 3]
    xv, scratch = refs[2 * nb + 3], refs[2 * nb + 4 :]
    beads = nb * lb
    width = group + 2 * P_HALO
    n = 3 * lb
    b = b_ref[0]
    step = step_ref[...]
    charges = Rows(q_ref, b * group + P_HALO)

    def advance(pos, vel):
        out_x, out_v = [], []
        for x, v in zip(pos, vel):
            high, mid, low = split3(jnp.concatenate([x, v], axis=0))
            stacked = jnp.concatenate([high, mid, high, mid, low, high], axis=0).astype(BF16)
            new = dot_nn(step, stacked)
            out_x.append(new[:beads])
            out_v.append(new[beads:])
        return out_x, out_v

    for w in range(width):
        def gather(a, comp):
            return jnp.concatenate(
                [block[pl.ds((a * width + w) * n + comp * lb, lb), :] for block in blocks], axis=0
            )

        q = charges[w]
        oxygen = (q < -1.5).astype(F32)
        inverse = jnp.where(q < -1.5, 1.0 / oxygen_mass, 1.0)
        pos = [gather(0, c) for c in range(3)]
        vel = [gather(1, c) * inverse for c in range(3)]
        half = (0.5 * inner_step) * inverse
        full = inner_step * inverse
        force = bond_forces(*pos, oxygen, mols, slots)
        vel = [v + half * f for v, f in zip(vel, force)]
        pos, vel = advance(pos, vel)
        force = bond_forces(*pos, oxygen, mols, slots)
        vel = [v + full * f for v, f in zip(vel, force)]
        pos, vel = advance(pos, vel)
        if 1 <= w <= width - 2:
            force = bond_forces(*pos, oxygen, mols, slots)
            vel = [v + half * f for v, f in zip(vel, force)]
            mass = jnp.where(q < -1.5, oxygen_mass, 1.0)
            for c in range(3):
                xv[w - 1, pl.ds(c * beads, beads), :] = pos[c]
                xv[w - 1, pl.ds((3 + c) * beads, beads), :] = vel[c] * mass
        build_tiles(scratch[:4], w * beads, beads, *pos)

    read = pair_forces(scratch, charges, width, mols, beads, slots)
    for w in range(group):
        old = xv[w]
        m = 3 * beads
        force = jnp.concatenate([read(w + 1, c) for c in range(3)], axis=0)
        state = jnp.concatenate([old[:m], old[m:] + (0.5 * outer_step) * force], axis=0)
        state = unpermuted(state, perm_ref[b * group + w])
        for a in range(2):
            for c in range(3):
                for k in range(nb):
                    row = (a * 3 + c) * beads + k * lb
                    ys[k][pl.ds(((a * group + w) * 3 + c) * lb, lb), :] = state[row : row + lb]


def unpack_kernel(nb, group, lb, cells, b_ref, *refs):
    ys = refs[:nb]
    outs = refs[nb:]
    b = b_ref[0]
    for k in range(nb):
        source = lax.rem(b + k, nb)
        for a in range(2):
            for w in range(group):
                for c in range(3):
                    outs[a][pl.ds(c * cells + source * group + w, lb, stride=3 * cells), :] = ys[
                        k
                    ][pl.ds(((a * group + w) * 3 + c) * lb, lb), :]


def call(kernel, outs, scratch, scalar, *operands):
    vmem = pl.BlockSpec(memory_space=pltpu.VMEM)
    smem = pl.BlockSpec(memory_space=pltpu.SMEM)
    return pl.pallas_call(
        kernel,
        out_shape=outs,
        in_specs=([] if scalar is None else [smem]) + [vmem] * len(operands),
        out_specs=[vmem] * len(outs),
        scratch_shapes=scratch,
        compiler_params=pltpu.CompilerParams(vmem_limit_bytes=48 * 1024 * 1024),
    )(*(() if scalar is None else (scalar,)), *operands)


def local(nb, ns, positions, momenta, molecules):
    lb, _, cells, slots = positions.shape
    mols = molecules.shape[1]
    group = cells // nb
    beads = lb * nb
    width = group + 2 * P_HALO
    b = lax.axis_index("bead").astype(jnp.int32).reshape(1)

    def shape(*dims):
        return jax.ShapeDtypeStruct(dims, F32)

    lanes = jnp.transpose(molecules, (0, 2, 1)).reshape(cells, 3 * mols)
    lanes = jnp.pad(lanes, ((0, 0), (0, slots - 3 * mols)), constant_values=slots)
    edge = shape(9 * lb + 8, slots)
    xs, ps, perm, charges, to_right, to_left = call(
        functools.partial(order_kernel, lb, cells, mols, slots),
        [shape(cells, 3 * lb, slots)] * 2
        + [jax.ShapeDtypeStruct((cells, slots, slots), BF16), shape(cells, slots), edge, edge],
        [],
        None,
        lanes,
        positions.reshape(lb * 3 * cells, slots),
        momenta.reshape(lb * 3 * cells, slots),
    )
    left = lax.ppermute(to_right, "space", [(s, (s + 1) % ns) for s in range(ns)])
    right = lax.ppermute(to_left, "space", [(s, (s - 1) % ns) for s in range(ns)])
    q_rows = -(-(cells + 2 * X_HALO) // 8) * 8
    *blocks, q_wide = call(
        functools.partial(outer_kernel, nb, group, lb, cells, mols, slots),
        [shape(2 * width * 3 * lb, slots)] * nb + [shape(q_rows, slots)],
        [pltpu.VMEM((cells + 2 * P_HALO, 3 * lb, slots), F32)]
        + pair_scratch(cells + 2 * X_HALO, lb, slots),
        b,
        xs,
        ps,
        charges,
        left,
        right,
    )
    blocks = [blocks[0]] + [
        lax.ppermute(blocks[k], "bead", [(i, (i + k) % nb) for i in range(nb)])
        for k in range(1, nb)
    ]
    step = jnp.asarray(propagator(beads, lb))
    ys = call(
        functools.partial(inner_kernel, nb, group, lb, cells, mols, slots),
        [shape(2 * group * 3 * lb, slots)] * nb,
        [pltpu.VMEM((group, 6 * beads, slots), F32)]
        + pair_scratch(width, beads, slots),
        b,
        *blocks,
        step,
        perm,
        q_wide,
    )
    ys = [ys[0]] + [
        lax.ppermute(ys[k], "bead", [(i, (i - k) % nb) for i in range(nb)]) for k in range(1, nb)
    ]
    new_x, new_p = call(
        functools.partial(unpack_kernel, nb, group, lb, cells),
        [shape(lb * 3 * cells, slots)] * 2,
        [],
        b,
        *ys,
    )
    return new_x.reshape(positions.shape), new_p.reshape(positions.shape)


def solution(mesh):
    spec = P("bead", None, "space", None)
    return jax.shard_map(
        functools.partial(local, mesh.shape["bead"], mesh.shape["space"]),
        mesh=mesh,
        in_specs=(spec, spec, P("space", None, None)),
        out_specs=(spec, spec),
        check_vma=False,
    )
```

```python
import functools

import jax
import jax.numpy as jnp
import ml_dtypes
import numpy as np
from jax import lax
from jax.experimental import pallas as pl
from jax.experimental.pallas import tpu as pltpu
from jax.sharding import PartitionSpec as P

charge_oxygen = -0.8476
charge_hydrogen = 0.4238
coulomb_scale = 24.0
coulomb_soft = 0.004
well_depth = 0.02
sigma_square = 0.0841
lennard_soft = 0.04
bond_stiffness = 20000.0
bond_square = 0.0081
angle_stiffness = 5000.0
angle_square = 0.0204
cycle_frequency = 60.0
outer_step = 0.02
inner_step = 0.01
oxygen_mass = 16.0

REACH = 1
X_HALO = 2 * REACH
P_HALO = REACH

F32 = jnp.float32
BF16 = jnp.bfloat16


def rounded(a):
    return a.astype(BF16).astype(F32)


def split3(a):
    high = rounded(a)
    rest = a - high
    mid = rounded(rest)
    return high, mid, rest - mid


def two_part(a):
    high = rounded(a)
    return high + rounded(a - high)


def dot_nn(a, b):
    return lax.dot_general(a, b, (((1,), (0,)), ((), ())), preferred_element_type=F32)


def dot_nt(a, b):
    return lax.dot_general(a, b, (((1,), (1,)), ((), ())), preferred_element_type=F32)


def propagator(beads, beads_dev):
    j = np.arange(beads)
    angles = 2.0 * np.pi * ((j[:, None] * j[None, :]) % beads) / beads
    half = beads // 2
    col = j[None, :]
    u = np.where(
        col == 0,
        np.sqrt(1.0 / beads),
        np.where(
            col < half,
            np.sqrt(2.0 / beads) * np.cos(angles),
            np.where(
                col == half,
                np.sqrt(1.0 / beads) * np.cos(angles),
                np.sqrt(2.0 / beads) * np.sin(angles),
            ),
        ),
    )
    w = 2.0 * cycle_frequency * np.sin(np.pi * j / beads)
    cosines = np.cos(w * inner_step)
    spring = w * np.sin(w * inner_step)
    drift = np.where(j == 0, inner_step, np.sin(w * inner_step) / np.where(j == 0, 1.0, w))
    def circulant(values, bead):
        first = ((u * values) @ u.T)[:, 0]
        return first[(bead[:, None] - bead[None, :]) % beads]

    out = []
    for b in range(beads // beads_dev):
        bead = ((j // beads_dev) ^ b) * beads_dev + j % beads_dev
        a = circulant(cosines, bead)
        whole = np.block([[a, circulant(drift, bead)], [-circulant(spring, bead), a]])
        high = whole.astype(ml_dtypes.bfloat16)
        rest = whole - high.astype(np.float64)
        mid = rest.astype(ml_dtypes.bfloat16)
        low = (rest - mid.astype(np.float64)).astype(ml_dtypes.bfloat16)
        out.append(np.concatenate([high, high, mid, mid, high, low], axis=1))
    return np.stack(out)


def lane_tables(lanes, mols, slots):
    lane = lax.broadcasted_iota(jnp.int32, lanes.shape, 1)
    unit = jnp.where(lane < mols, charge_oxygen / charge_hydrogen, 1.0)
    return jnp.where(lanes < slots, unit, 0.0)


def permuted(rows, perm):
    n = rows.shape[0]
    stacked = jnp.concatenate(split3(rows), axis=0).astype(BF16)
    moved = dot_nn(stacked, perm)
    return moved[:n] + moved[n : 2 * n] + moved[2 * n :]


def unpermuted(rows, perm):
    n = rows.shape[0]
    stacked = jnp.concatenate(split3(rows), axis=0).astype(BF16)
    moved = dot_nt(stacked, perm)
    return moved[:n] + moved[n : 2 * n] + moved[2 * n :]


def order_kernel(lb, cells, mols, slots, mol_hbm, x_hbm, p_hbm, *refs):
    xo, po, perm_ref, q_ref, to_right, to_left = refs[:6]
    mol_ref, x_ref, p_ref, wide, held_ref, sems = refs[6:]
    copies = [
        pltpu.make_async_copy(source, dest, sems.at[i])
        for i, (source, dest) in enumerate(
            ((mol_hbm, mol_ref), (x_hbm, x_ref), (p_hbm, p_ref))
        )
    ]
    for copy in copies:
        copy.start()
    row = lax.broadcasted_iota(jnp.int32, (slots, slots), 0)
    col = lax.broadcasted_iota(jnp.int32, (slots, slots), 1)
    upper = (row < col).astype(F32).astype(BF16)
    row = row.astype(F32)
    lane = lax.broadcasted_iota(jnp.int32, (cells, slots), 1)
    far = 4.0 * slots
    wide[...] = jnp.full(wide.shape, slots, jnp.int32)
    copies[0].wait()
    for t in range(3):
        wide[t, :, :mols] = mol_ref[t]
    lanes = jnp.where(
        lane < mols,
        wide[0],
        jnp.where(lane < 2 * mols, pltpu.roll(wide[1], mols, 1), pltpu.roll(wide[2], 2 * mols, 1)),
    )
    lanes = jnp.where(lane < 3 * mols, lanes, slots)
    charges = lane_tables(lanes, mols, slots)
    q_ref[...] = charges
    free = lanes >= slots
    key = jnp.where(
        free, far + dot_nn(free.astype(F32).astype(BF16), upper), lanes.astype(F32)
    )
    ones = jnp.ones((16, slots), BF16)
    for cell in range(cells):
        held = (row == key[cell : cell + 1]).astype(F32).astype(BF16)
        held_ref[cell : cell + 1, :] = dot_nt(ones, held)[0:1]
    used = held_ref[...]
    rank = dot_nn((1.0 - used).astype(BF16), upper)
    slot_key = jnp.where(used > 0.5, lane.astype(F32), far + rank)
    copies[1].wait()
    copies[2].wait()
    n = 3 * lb
    for cell in range(cells):
        slot_column = jnp.broadcast_to(slot_key[cell : cell + 1], (slots, slots)).T
        perm = (slot_column == key[cell : cell + 1]).astype(F32).astype(BF16)
        perm_ref[cell] = perm
        rows = [
            ref[pl.ds(comp * cells + cell, lb, stride=3 * cells), :]
            for ref in (x_ref, p_ref)
            for comp in range(3)
        ]
        moved = permuted(jnp.concatenate(rows, axis=0), perm)
        xo[cell] = moved[:n]
        po[cell] = moved[n:]
    for out, xs, ps in (
        (to_right, (cells - 2, cells - 1), cells - 1),
        (to_left, (0, 1), 0),
    ):
        out[9 * lb :, :] = jnp.zeros((8, slots), F32)
        for e, cell in enumerate(xs):
            out[pl.ds(e * n, n), :] = xo[cell]
            out[pl.ds(9 * lb + e, 1), :] = charges[cell : cell + 1]
        out[pl.ds(2 * n, n), :] = po[ps]


def put_tiles(scratch, first, count, rows):
    for index, value in rows:
        scratch[pl.ds(first * 8 + index, count, stride=8), :] = value


OFFSETS = (-1.0, 0.0, 1.0)


def build_tiles(tiles, first, count, x, y, z):
    x, y, z = two_part(x - 0.5), two_part(y - 0.5), two_part(z - 0.5)
    norm = x * x + y * y + z * z + 0.5 * coulomb_soft
    high = two_part(norm)
    low = norm - high
    put_tiles(
        tiles, first, count, ((0, x), (1, y), (2, z), (3, high), (4, low), (5, high), (6, low))
    )


def pair_scratch(count, beads, slots):
    n = count * beads
    return (
        [pltpu.VMEM((n * 8, slots), F32)] * 2
        + [pltpu.VMEM((n // 2, slots, 64), BF16)]
        + [pltpu.VMEM((n // 2, 32, slots), BF16)] * 3
        + [pltpu.VMEM((n, 32, slots), BF16)]
        + [pltpu.VMEM((slots, slots), F32)]
    )


def pair_forces(scratch, charges, count, mols, beads, slots):
    tiles, forces, lt, rr, rt, keep = *scratch[:3], scratch[3:6], *scratch[6:]
    orows = -(-mols // 8) * 8
    pair_scale = coulomb_scale * charge_hydrogen * charge_hydrogen
    k3 = sigma_square**3
    ratio = (charge_hydrogen / charge_oxygen) ** 2 / pair_scale
    lj_a = 24.0 * well_depth * 2.0 * k3 * k3 * ratio
    lj_b = 24.0 * well_depth * k3 * ratio
    row8 = lax.broadcasted_iota(jnp.int32, (8, slots), 0)
    place, norms = row8 < 3, row8 < 5
    target_rows = place | (row8 == 5) | (row8 == 6)
    ones_low = jnp.where((row8 == 3) | (row8 == 4), 1.0, 0.0)
    ones_high = jnp.where((row8 == 5) | (row8 == 6), 1.0, 0.0)
    ones_last = jnp.where(row8 == 7, 1.0, 0.0)
    lj_row = lax.broadcasted_iota(jnp.int32, (orows, slots), 0)
    lj_lane = lax.broadcasted_iota(jnp.int32, (orows, slots), 1)
    first_lanes, second_lanes = lj_lane < mols, lj_lane < 2 * mols
    corner = (lj_row < mols) & first_lanes

    i = lax.broadcasted_iota(jnp.int32, (slots, slots), 0)
    j = lax.broadcasted_iota(jnp.int32, (slots, slots), 1)
    i = jnp.where(i >= 2 * mols, i - 2 * mols, jnp.where(i >= mols, i - mols, i))
    j = jnp.where(j >= 2 * mols, j - 2 * mols, jnp.where(j >= mols, j - mols, j))
    keep[...] = (i != j).astype(F32)

    lane64 = lax.broadcasted_iota(jnp.int32, (slots, 64), 1) & 31
    odd = (lane64 >= 27) & (lane64 < 31)
    even = lane64 == 31
    signs = [
        jnp.where(odd, offset, jnp.where(even, offset * offset, 1.0)).astype(BF16)
        for offset in OFFSETS
    ]

    pairs = beads // 2
    unroll = min(pairs, 4)
    per_cell = pairs // unroll

    def tile(ref, n):
        return ref[pl.ds(pl.multiple_of(n * 8, 8), 8), :]

    def stack(values):
        return jnp.concatenate(values, axis=0).astype(BF16)

    def prepare(step, carry):
        charge = charges[lax.div(step, per_cell)]
        units = [
            jnp.where(row8 == 3, charge, jnp.where(row8 == 4, offset * charge, 0.0))
            for offset in OFFSETS
        ]
        for u in range(unroll):
            m = step * unroll + u
            left, high_rows, mid_rows = [], [], []
            for h in range(2):
                value = tile(tiles, 2 * m + h)
                high = rounded(value)
                mid = value - high
                x_high, x_mid = high[0:1], mid[0:1]
                left_high = jnp.where(place, -2.0 * high, jnp.where(norms, high, ones_high))
                left_mid = jnp.where(place, -2.0 * mid, jnp.where(norms, mid, 0.0))
                left_last = jnp.where(
                    place,
                    -2.0 * mid,
                    jnp.where(
                        row8 == 3,
                        2.0 * x_high,
                        jnp.where(row8 == 4, 2.0 * x_mid, ones_last - 2.0 * ones_high),
                    ),
                )
                left += [left_high, left_high, left_mid, left_last]
                right_high = jnp.where(target_rows, high, ones_low)
                right_mid = jnp.where(target_rows, mid, 0.0)
                right_last = jnp.where(
                    place,
                    mid,
                    jnp.where(
                        row8 == 5, x_high, jnp.where(row8 == 6, x_mid, ones_low + ones_last)
                    ),
                )
                rt[2 * m + h] = stack([right_high, right_mid, right_high, right_last])
                high_rows.append(high * charge)
                mid_rows.append(jnp.where(place, mid * charge, 0.0))
            lt[m] = stack(left).T
            for o in range(3):
                rows = []
                for h in range(2):
                    rows += [jnp.where(place, high_rows[h], units[o]), mid_rows[h]]
                rr[o][m] = stack(rows)
        return carry

    lax.fori_loop(0, count * per_cell, prepare, 0)
    zero = jnp.zeros((32, slots), BF16)

    def target(m, w):
        peers = [m - pairs, m, m + pairs]
        left = jnp.concatenate([lt[peers[o]] * signs[o] for o in range(3)], axis=0)
        right = jnp.concatenate(
            [
                jnp.concatenate([rt[2 * m], zero], axis=1),
                jnp.concatenate([zero, rt[2 * m + 1]], axis=1),
            ],
            axis=0,
        )
        squares = dot_nn(left, right)
        blocks = [[], [], []]
        for h in range(2):
            lanes = slice(h * slots, (h + 1) * slots)
            near = [squares[o * slots : o * slots + orows, lanes] for o in range(3)]
            packed = jnp.where(
                first_lanes,
                near[0],
                jnp.where(
                    second_lanes, pltpu.roll(near[1], mols, 1), pltpu.roll(near[2], 2 * mols, 1)
                ),
            )
            root = lax.rsqrt(packed + (lennard_soft - coulomb_soft))
            inverse = root * root
            cube = inverse * inverse * inverse
            lj = (cube * lj_a - lj_b) * (cube * inverse)
            for o in range(3):
                root = lax.rsqrt(squares[o * slots : (o + 1) * slots, lanes])
                strength = root * root * root
                own = pltpu.roll(lj, slots - o * mols, 1) if o else lj
                strength = jnp.concatenate(
                    [strength[:orows] + jnp.where(corner, own, 0.0), strength[orows:]], axis=0
                )
                if o == 1:
                    strength = strength * keep[...]
                high = strength.astype(BF16)
                low = (strength - high.astype(F32)).astype(BF16)
                blocks[o].append(jnp.concatenate([high, low], axis=0))
        sums = None
        for o in range(3):
            weights = rr[o][peers[o]]
            value = dot_nn(
                jnp.concatenate([weights, weights], axis=1), jnp.concatenate(blocks[o], axis=1)
            )
            sums = value if sums is None else sums + value
        scale = charges[w] * pair_scale
        for h in range(2):
            part = sums[16 * h : 16 * h + 16, h * slots : (h + 1) * slots]
            total = part[0:8] + part[8:16]
            total = total + jnp.where(row8 == 0, total[4:5], 0.0)
            n = 2 * m + h
            forces[pl.ds(pl.multiple_of(n * 8, 8), 8), :] = (
                tile(tiles, n) * total[3:4] - total
            ) * scale

    def step(index, carry):
        for u in range(unroll):
            target(index * unroll + u, lax.div(index, per_cell))
        return carry

    lax.fori_loop(per_cell, (count - 1) * per_cell, step, 0)

    def read(w, comp):
        return forces[pl.ds(w * beads * 8 + comp, beads, stride=8), :]

    return read


def outer_kernel(nb, group, lb, cells, mols, slots, b_ref, *refs):
    x_ref, p_ref, q_ref, left, right = refs[:5]
    outs, q_out = refs[5 : 5 + nb], refs[5 + nb]
    kicked, scratch = refs[6 + nb], refs[7 + nb :]
    n = 3 * lb
    count = cells + 2 * X_HALO
    b = b_ref[0]

    def cell_rows(w):
        if w < X_HALO:
            return left[pl.ds(w * n, n), :]
        if w >= cells + X_HALO:
            return right[pl.ds((w - cells - X_HALO) * n, n), :]
        return x_ref[w - X_HALO]

    charge_rows = [left[pl.ds(9 * lb + e, 1), :] for e in range(2)]
    charge_rows += [q_ref[c : c + 1, :] for c in range(cells)]
    charge_rows += [right[pl.ds(9 * lb + e, 1), :] for e in range(2)]
    q_out[...] = jnp.zeros(q_out.shape, F32)
    for w in range(count):
        q_out[w : w + 1, :] = charge_rows[w]
    for w in range(count):
        rows = cell_rows(w)
        build_tiles(scratch[0], w * lb, lb, rows[:lb], rows[lb : 2 * lb], rows[2 * lb :])

    read = pair_forces(scratch, Rows(q_out, 0), count, mols, lb, slots)
    half = 0.5 * outer_step
    for w in range(1, count - 1):
        if w < X_HALO:
            old = left[pl.ds(2 * n, n), :]
        elif w >= cells + X_HALO:
            old = right[pl.ds(2 * n, n), :]
        else:
            old = p_ref[w - X_HALO]
        force = jnp.concatenate([read(w, c) for c in range(3)], axis=0)
        kicked[w - 1] = old + half * force
    width = group + 2 * P_HALO
    for k in range(nb):
        first = jnp.bitwise_xor(b, k) * group
        for w in range(width):
            outs[k][pl.ds((width + w) * n, n), :] = kicked[first + w]
            source = first + w - P_HALO
            inside = x_ref[jnp.clip(source, 0, cells - 1)]
            if w < P_HALO:
                inside = jnp.where(source < 0, left[pl.ds(n, n), :], inside)
            elif w >= group + P_HALO:
                inside = jnp.where(source >= cells, right[pl.ds(0, n), :], inside)
            outs[k][pl.ds(w * n, n), :] = inside


class Rows:
    def __init__(self, ref, first):
        self.ref, self.first = ref, first

    def __getitem__(self, index):
        return self.ref[pl.ds(self.first + index, 1), :]


def bond_forces(x, y, z, used, mols, slots):
    def partner(a, t):
        return pltpu.roll(a, slots - t * mols, 1)

    first = [a - partner(a, 1) for a in (x, y, z)]
    second = [a - partner(a, 2) for a in (x, y, z)]
    third = [s - f for f, s in zip(first, second)]

    def pull(bond, stiffness, square):
        length = bond[0] * bond[0] + bond[1] * bond[1] + bond[2] * bond[2]
        return (stiffness * used) * (length - square)

    c1 = pull(first, bond_stiffness, bond_square)
    c2 = pull(second, bond_stiffness, bond_square)
    c3 = pull(third, angle_stiffness, angle_square)
    out = []
    for f, s, t in zip(first, second, third):
        on_first = c1 * f - c3 * t
        on_second = c2 * s + c3 * t
        on_oxygen = -(c1 * f + c2 * s)
        out.append(
            on_oxygen + pltpu.roll(on_first, mols, 1) + pltpu.roll(on_second, 2 * mols, 1)
        )
    return out


def inner_kernel(nb, group, lb, cells, mols, slots, b_ref, *refs):
    blocks = refs[:nb]
    step_ref, perm_ref, q_ref = refs[nb : nb + 3]
    ys = refs[nb + 3 : 2 * nb + 3]
    xv, scratch = refs[2 * nb + 3], refs[2 * nb + 4 :]
    beads = nb * lb
    width = group + 2 * P_HALO
    n = 3 * lb
    b = b_ref[0]
    step = step_ref[b]
    charges = Rows(q_ref, b * group + P_HALO)

    def advance(pos, vel):
        out_x, out_v = [], []
        for x, v in zip(pos, vel):
            high, mid, low = split3(jnp.concatenate([x, v], axis=0))
            stacked = jnp.concatenate([high, mid, high, mid, low, high], axis=0).astype(BF16)
            new = dot_nn(step, stacked)
            out_x.append(new[:beads])
            out_v.append(new[beads:])
        return out_x, out_v

    for w in range(width):
        def gather(a, comp):
            return jnp.concatenate(
                [block[pl.ds((a * width + w) * n + comp * lb, lb), :] for block in blocks], axis=0
            )

        q = charges[w]
        oxygen = (q < -1.5).astype(F32)
        inverse = jnp.where(q < -1.5, 1.0 / oxygen_mass, 1.0)
        pos = [gather(0, c) for c in range(3)]
        vel = [gather(1, c) * inverse for c in range(3)]
        half = (0.5 * inner_step) * inverse
        full = inner_step * inverse
        force = bond_forces(*pos, oxygen, mols, slots)
        vel = [v + half * f for v, f in zip(vel, force)]
        pos, vel = advance(pos, vel)
        force = bond_forces(*pos, oxygen, mols, slots)
        vel = [v + full * f for v, f in zip(vel, force)]
        pos, vel = advance(pos, vel)
        if 1 <= w <= width - 2:
            force = bond_forces(*pos, oxygen, mols, slots)
            vel = [v + half * f for v, f in zip(vel, force)]
            mass = jnp.where(q < -1.5, oxygen_mass, 1.0)
            for c in range(3):
                xv[w - 1, pl.ds(c * beads, beads), :] = pos[c]
                xv[w - 1, pl.ds((3 + c) * beads, beads), :] = vel[c] * mass
        build_tiles(scratch[0], w * beads, beads, *pos)

    read = pair_forces(scratch, charges, width, mols, beads, slots)
    for w in range(group):
        old = xv[w]
        m = 3 * beads
        force = jnp.concatenate([read(w + 1, c) for c in range(3)], axis=0)
        state = jnp.concatenate([old[:m], old[m:] + (0.5 * outer_step) * force], axis=0)
        state = unpermuted(state, perm_ref[b * group + w])
        for a in range(2):
            for c in range(3):
                for k in range(nb):
                    row = (a * 3 + c) * beads + k * lb
                    ys[k][pl.ds(((a * group + w) * 3 + c) * lb, lb), :] = state[row : row + lb]


def unpack_kernel(nb, group, lb, cells, b_ref, *refs):
    ys = refs[:nb]
    outs = refs[nb:]
    b = b_ref[0]
    for k in range(nb):
        source = jnp.bitwise_xor(b, k)
        for a in range(2):
            for w in range(group):
                for c in range(3):
                    outs[a][pl.ds(c * cells + source * group + w, lb, stride=3 * cells), :] = ys[
                        k
                    ][pl.ds(((a * group + w) * 3 + c) * lb, lb), :]


def call(kernel, outs, scratch, scalar, *operands, space=pltpu.VMEM):
    vmem = pl.BlockSpec(memory_space=pltpu.VMEM)
    smem = pl.BlockSpec(memory_space=pltpu.SMEM)
    return pl.pallas_call(
        kernel,
        out_shape=outs,
        in_specs=([] if scalar is None else [smem]) + [pl.BlockSpec(memory_space=space)] * len(operands),
        out_specs=[vmem] * len(outs),
        scratch_shapes=scratch,
        compiler_params=pltpu.CompilerParams(vmem_limit_bytes=48 * 1024 * 1024),
    )(*(() if scalar is None else (scalar,)), *operands)


def local(nb, ns, positions, momenta, molecules):
    lb, _, cells, slots = positions.shape
    mols = molecules.shape[1]
    group = cells // nb
    beads = lb * nb
    width = group + 2 * P_HALO
    b = lax.axis_index("bead").astype(jnp.int32).reshape(1)

    def shape(*dims):
        return jax.ShapeDtypeStruct(dims, F32)

    edge = shape(9 * lb + 8, slots)
    rows = lb * 3 * cells
    xs, ps, perm, charges, to_right, to_left = call(
        functools.partial(order_kernel, lb, cells, mols, slots),
        [shape(cells, 3 * lb, slots)] * 2
        + [jax.ShapeDtypeStruct((cells, slots, slots), BF16), shape(cells, slots), edge, edge],
        [
            pltpu.VMEM((3, cells, mols), jnp.int32),
            pltpu.VMEM((rows, slots), F32),
            pltpu.VMEM((rows, slots), F32),
            pltpu.VMEM((3, cells, slots), jnp.int32),
            pltpu.VMEM((cells, slots), F32),
            pltpu.SemaphoreType.DMA((3,)),
        ],
        None,
        jnp.transpose(molecules, (2, 0, 1)),
        positions.reshape(rows, slots),
        momenta.reshape(rows, slots),
        space=pl.ANY,
    )
    left = lax.ppermute(to_right, "space", [(s, (s + 1) % ns) for s in range(ns)])
    right = lax.ppermute(to_left, "space", [(s, (s - 1) % ns) for s in range(ns)])
    q_rows = -(-(cells + 2 * X_HALO) // 8) * 8
    *blocks, q_wide = call(
        functools.partial(outer_kernel, nb, group, lb, cells, mols, slots),
        [shape(2 * width * 3 * lb, slots)] * nb + [shape(q_rows, slots)],
        [pltpu.VMEM((cells + 2 * P_HALO, 3 * lb, slots), F32)]
        + pair_scratch(cells + 2 * X_HALO, lb, slots),
        b,
        xs,
        ps,
        charges,
        left,
        right,
    )
    blocks = [blocks[0]] + [
        lax.ppermute(blocks[k], "bead", [(i, i ^ k) for i in range(nb)])
        for k in range(1, nb)
    ]
    step = jnp.asarray(propagator(beads, lb))
    ys = call(
        functools.partial(inner_kernel, nb, group, lb, cells, mols, slots),
        [shape(2 * group * 3 * lb, slots)] * nb,
        [pltpu.VMEM((group, 6 * beads, slots), F32)]
        + pair_scratch(width, beads, slots),
        b,
        *blocks,
        step,
        perm,
        q_wide,
    )
    ys = [ys[0]] + [
        lax.ppermute(ys[k], "bead", [(i, i ^ k) for i in range(nb)]) for k in range(1, nb)
    ]
    new_x, new_p = call(
        functools.partial(unpack_kernel, nb, group, lb, cells),
        [shape(lb * 3 * cells, slots)] * 2,
        [],
        b,
        *ys,
    )
    return new_x.reshape(positions.shape), new_p.reshape(positions.shape)


def solution(mesh):
    spec = P("bead", None, "space", None)
    return jax.shard_map(
        functools.partial(local, mesh.shape["bead"], mesh.shape["space"]),
        mesh=mesh,
        in_specs=(spec, spec, P("space", None, None)),
        out_specs=(spec, spec),
        check_vma=False,
    )
```

```python
import functools

import jax
import jax.numpy as jnp
import ml_dtypes
import numpy as np
from jax import lax
from jax.experimental import pallas as pl
from jax.experimental.pallas import tpu as pltpu
from jax.sharding import PartitionSpec as P

charge_oxygen = -0.8476
charge_hydrogen = 0.4238
coulomb_scale = 24.0
coulomb_soft = 0.004
well_depth = 0.02
sigma_square = 0.0841
lennard_soft = 0.04
bond_stiffness = 20000.0
bond_square = 0.0081
angle_stiffness = 5000.0
angle_square = 0.0204
cycle_frequency = 60.0
outer_step = 0.02
inner_step = 0.01
oxygen_mass = 16.0

REACH = 1
X_HALO = 2 * REACH
P_HALO = REACH

F32 = jnp.float32
BF16 = jnp.bfloat16


def rounded(a):
    return a.astype(BF16).astype(F32)


def split3(a):
    high = rounded(a)
    rest = a - high
    mid = rounded(rest)
    return high, mid, rest - mid


def two_part(a):
    high = rounded(a)
    return high + rounded(a - high)


def dot_nn(a, b):
    return lax.dot_general(a, b, (((1,), (0,)), ((), ())), preferred_element_type=F32)


def dot_nt(a, b):
    return lax.dot_general(a, b, (((1,), (1,)), ((), ())), preferred_element_type=F32)


def propagator(beads, beads_dev):
    j = np.arange(beads)
    angles = 2.0 * np.pi * ((j[:, None] * j[None, :]) % beads) / beads
    half = beads // 2
    col = j[None, :]
    u = np.where(
        col == 0,
        np.sqrt(1.0 / beads),
        np.where(
            col < half,
            np.sqrt(2.0 / beads) * np.cos(angles),
            np.where(
                col == half,
                np.sqrt(1.0 / beads) * np.cos(angles),
                np.sqrt(2.0 / beads) * np.sin(angles),
            ),
        ),
    )
    w = 2.0 * cycle_frequency * np.sin(np.pi * j / beads)
    cosines = np.cos(w * inner_step)
    spring = w * np.sin(w * inner_step)
    drift = np.where(j == 0, inner_step, np.sin(w * inner_step) / np.where(j == 0, 1.0, w))
    def circulant(values, bead):
        first = ((u * values) @ u.T)[:, 0]
        return first[(bead[:, None] - bead[None, :]) % beads]

    out = []
    for b in range(beads // beads_dev):
        bead = ((j // beads_dev) ^ b) * beads_dev + j % beads_dev
        a = circulant(cosines, bead)
        whole = np.block([[a, circulant(drift, bead)], [-circulant(spring, bead), a]])
        high = whole.astype(ml_dtypes.bfloat16)
        rest = whole - high.astype(np.float64)
        mid = rest.astype(ml_dtypes.bfloat16)
        low = (rest - mid.astype(np.float64)).astype(ml_dtypes.bfloat16)
        out.append(np.concatenate([high, high, mid, mid, high, low], axis=1))
    return np.stack(out)


def lane_tables(lanes, mols, slots):
    lane = lax.broadcasted_iota(jnp.int32, lanes.shape, 1)
    unit = jnp.where(lane < mols, charge_oxygen / charge_hydrogen, 1.0)
    return jnp.where(lanes < slots, unit, 0.0)


def permuted(rows, perm):
    n = rows.shape[0]
    stacked = jnp.concatenate(split3(rows), axis=0).astype(BF16)
    moved = dot_nn(stacked, perm)
    return moved[:n] + moved[n : 2 * n] + moved[2 * n :]


def unpermuted(rows, perm):
    n = rows.shape[0]
    stacked = jnp.concatenate(split3(rows), axis=0).astype(BF16)
    moved = dot_nt(stacked, perm)
    return moved[:n] + moved[n : 2 * n] + moved[2 * n :]


def order_kernel(lb, cells, mols, slots, mol_hbm, x_hbm, p_hbm, *refs):
    xo, po, perm_ref, q_ref, to_right, to_left = refs[:6]
    mol_ref, x_ref, p_ref, wide, held_ref, sems = refs[6:]
    copies = [
        pltpu.make_async_copy(source, dest, sems.at[i])
        for i, (source, dest) in enumerate(
            ((mol_hbm, mol_ref), (x_hbm, x_ref), (p_hbm, p_ref))
        )
    ]
    for copy in copies:
        copy.start()
    row = lax.broadcasted_iota(jnp.int32, (slots, slots), 0)
    col = lax.broadcasted_iota(jnp.int32, (slots, slots), 1)
    upper = (row < col).astype(F32).astype(BF16)
    row = row.astype(F32)
    lane = lax.broadcasted_iota(jnp.int32, (cells, slots), 1)
    far = 4.0 * slots
    wide[...] = jnp.full(wide.shape, slots, jnp.int32)
    copies[0].wait()
    for t in range(3):
        wide[t, :, :mols] = mol_ref[t]
    lanes = jnp.where(
        lane < mols,
        wide[0],
        jnp.where(lane < 2 * mols, pltpu.roll(wide[1], mols, 1), pltpu.roll(wide[2], 2 * mols, 1)),
    )
    lanes = jnp.where(lane < 3 * mols, lanes, slots)
    charges = lane_tables(lanes, mols, slots)
    q_ref[...] = charges
    free = lanes >= slots
    key = jnp.where(
        free, far + dot_nn(free.astype(F32).astype(BF16), upper), lanes.astype(F32)
    )
    ones = jnp.ones((16, slots), BF16)
    for cell in range(cells):
        held = (row == key[cell : cell + 1]).astype(F32).astype(BF16)
        held_ref[cell : cell + 1, :] = dot_nt(ones, held)[0:1]
    used = held_ref[...]
    rank = dot_nn((1.0 - used).astype(BF16), upper)
    slot_key = jnp.where(used > 0.5, lane.astype(F32), far + rank)
    copies[1].wait()
    copies[2].wait()
    n = 3 * lb
    for cell in range(cells):
        slot_column = jnp.broadcast_to(slot_key[cell : cell + 1], (slots, slots)).T
        perm = (slot_column == key[cell : cell + 1]).astype(F32).astype(BF16)
        perm_ref[cell] = perm
        rows = [
            ref[pl.ds(comp * cells + cell, lb, stride=3 * cells), :]
            for ref in (x_ref, p_ref)
            for comp in range(3)
        ]
        moved = permuted(jnp.concatenate(rows, axis=0), perm)
        xo[cell] = moved[:n]
        po[cell] = moved[n:]
    for out, xs, ps in (
        (to_right, (cells - 2, cells - 1), cells - 1),
        (to_left, (0, 1), 0),
    ):
        out[9 * lb :, :] = jnp.zeros((8, slots), F32)
        for e, cell in enumerate(xs):
            out[pl.ds(e * n, n), :] = xo[cell]
            out[pl.ds(9 * lb + e, 1), :] = charges[cell : cell + 1]
        out[pl.ds(2 * n, n), :] = po[ps]


def put_tiles(scratch, first, count, rows):
    for index, value in rows:
        scratch[pl.ds(first * 8 + index, count, stride=8), :] = value


OFFSETS = (-1.0, 0.0, 1.0)


def build_tiles(tiles, first, count, x, y, z):
    x, y, z = two_part(x - 0.5), two_part(y - 0.5), two_part(z - 0.5)
    norm = x * x + y * y + z * z + 0.5 * coulomb_soft
    high = two_part(norm)
    low = norm - high
    put_tiles(
        tiles, first, count, ((0, x), (1, y), (2, z), (3, high), (4, low), (5, high), (6, low))
    )


def pair_scratch(count, beads, slots):
    n = count * beads
    return (
        [pltpu.VMEM((n * 8, slots), F32)] * 2
        + [pltpu.VMEM((n // 2, slots, 64), BF16)]
        + [pltpu.VMEM((n // 2, 32, slots), BF16)] * 3
        + [pltpu.VMEM((n, 32, slots), BF16)]
        + [pltpu.VMEM((slots, slots), F32)]
    )


def pair_forces(scratch, charges, count, mols, beads, slots):
    tiles, forces, lt, rr, rt, keep = *scratch[:3], scratch[3:6], *scratch[6:]
    orows = -(-mols // 8) * 8
    pair_scale = coulomb_scale * charge_hydrogen * charge_hydrogen
    k3 = sigma_square**3
    ratio = (charge_hydrogen / charge_oxygen) ** 2 / pair_scale
    lj_a = 24.0 * well_depth * 2.0 * k3 * k3 * ratio
    lj_b = 24.0 * well_depth * k3 * ratio
    row8 = lax.broadcasted_iota(jnp.int32, (8, slots), 0)
    place, norms = row8 < 3, row8 < 5
    target_rows = place | (row8 == 5) | (row8 == 6)
    ones_low = jnp.where((row8 == 3) | (row8 == 4), 1.0, 0.0)
    ones_high = jnp.where((row8 == 5) | (row8 == 6), 1.0, 0.0)
    ones_last = jnp.where(row8 == 7, 1.0, 0.0)
    lj_row = lax.broadcasted_iota(jnp.int32, (orows, slots), 0)
    lj_lane = lax.broadcasted_iota(jnp.int32, (orows, slots), 1)
    first_lanes, second_lanes = lj_lane < mols, lj_lane < 2 * mols
    corner = (lj_row < mols) & first_lanes

    i = lax.broadcasted_iota(jnp.int32, (slots, slots), 0)
    j = lax.broadcasted_iota(jnp.int32, (slots, slots), 1)
    i = jnp.where(i >= 2 * mols, i - 2 * mols, jnp.where(i >= mols, i - mols, i))
    j = jnp.where(j >= 2 * mols, j - 2 * mols, jnp.where(j >= mols, j - mols, j))
    keep[...] = (i != j).astype(F32)

    lane64 = lax.broadcasted_iota(jnp.int32, (slots, 64), 1) & 31
    odd = (lane64 >= 27) & (lane64 < 31)
    even = lane64 == 31
    signs = [
        jnp.where(odd, offset, jnp.where(even, offset * offset, 1.0)).astype(BF16)
        for offset in OFFSETS
    ]

    pairs = beads // 2
    unroll = min(pairs, 4)
    per_cell = pairs // unroll

    def tile(ref, n):
        return ref[pl.ds(pl.multiple_of(n * 8, 8), 8), :]

    def stack(values):
        return jnp.concatenate(values, axis=0).astype(BF16)

    def prepare(step, carry):
        charge = charges[lax.div(step, per_cell)]
        units = [
            jnp.where(row8 == 3, charge, jnp.where(row8 == 4, offset * charge, 0.0))
            for offset in OFFSETS
        ]
        for u in range(unroll):
            m = step * unroll + u
            left, high_rows, mid_rows = [], [], []
            for h in range(2):
                value = tile(tiles, 2 * m + h)
                high = rounded(value)
                mid = value - high
                x_high, x_mid = high[0:1], mid[0:1]
                left_high = jnp.where(place, -2.0 * high, jnp.where(norms, high, ones_high))
                left_mid = jnp.where(place, -2.0 * mid, jnp.where(norms, mid, 0.0))
                left_last = jnp.where(
                    place,
                    -2.0 * mid,
                    jnp.where(
                        row8 == 3,
                        2.0 * x_high,
                        jnp.where(row8 == 4, 2.0 * x_mid, ones_last - 2.0 * ones_high),
                    ),
                )
                left += [left_high, left_high, left_mid, left_last]
                right_high = jnp.where(target_rows, high, ones_low)
                right_mid = jnp.where(target_rows, mid, 0.0)
                right_last = jnp.where(
                    place,
                    mid,
                    jnp.where(
                        row8 == 5, x_high, jnp.where(row8 == 6, x_mid, ones_low + ones_last)
                    ),
                )
                rt[2 * m + h] = stack([right_high, right_mid, right_high, right_last])
                high_rows.append(high * charge)
                mid_rows.append(jnp.where(place, mid * charge, 0.0))
            lt[m] = stack(left).T
            for o in range(3):
                rows = []
                for h in range(2):
                    rows += [jnp.where(place, high_rows[h], units[o]), mid_rows[h]]
                rr[o][m] = stack(rows)
        return carry

    lax.fori_loop(0, count * per_cell, prepare, 0)
    zero = jnp.zeros((32, slots), BF16)

    def target(m, w):
        peers = [m - pairs, m, m + pairs]
        right = jnp.concatenate(
            [
                jnp.concatenate([rt[2 * m], zero], axis=1),
                jnp.concatenate([zero, rt[2 * m + 1]], axis=1),
            ],
            axis=0,
        )
        squares = [dot_nn(lt[peers[o]] * signs[o], right) for o in range(3)]
        blocks = [[], [], []]
        for h in range(2):
            lanes = slice(h * slots, (h + 1) * slots)
            near = [squares[o][:orows, lanes] for o in range(3)]
            packed = jnp.where(
                first_lanes,
                near[0],
                jnp.where(
                    second_lanes, pltpu.roll(near[1], mols, 1), pltpu.roll(near[2], 2 * mols, 1)
                ),
            )
            root = lax.rsqrt(packed + (lennard_soft - coulomb_soft))
            inverse = root * root
            cube = inverse * inverse * inverse
            lj = (cube * lj_a - lj_b) * (cube * inverse)
            for o in range(3):
                root = lax.rsqrt(squares[o][:, lanes])
                strength = root * root * root
                own = pltpu.roll(lj, slots - o * mols, 1) if o else lj
                strength = jnp.concatenate(
                    [strength[:orows] + jnp.where(corner, own, 0.0), strength[orows:]], axis=0
                )
                if o == 1:
                    strength = strength * keep[...]
                high = strength.astype(BF16)
                low = (strength - high.astype(F32)).astype(BF16)
                blocks[o].append(jnp.concatenate([high, low], axis=0))
        sums = None
        for o in range(3):
            weights = rr[o][peers[o]]
            value = dot_nn(
                jnp.concatenate([weights, weights], axis=1), jnp.concatenate(blocks[o], axis=1)
            )
            sums = value if sums is None else sums + value
        scale = charges[w] * pair_scale
        for h in range(2):
            part = sums[16 * h : 16 * h + 16, h * slots : (h + 1) * slots]
            total = part[0:8] + part[8:16]
            total = total + jnp.where(row8 == 0, total[4:5], 0.0)
            n = 2 * m + h
            forces[pl.ds(pl.multiple_of(n * 8, 8), 8), :] = (
                tile(tiles, n) * total[3:4] - total
            ) * scale

    def step(index, carry):
        for u in range(unroll):
            target(index * unroll + u, lax.div(index, per_cell))
        return carry

    lax.fori_loop(per_cell, (count - 1) * per_cell, step, 0)

    def read(w, comp):
        return forces[pl.ds(w * beads * 8 + comp, beads, stride=8), :]

    return read


def outer_kernel(nb, group, lb, cells, mols, slots, b_ref, *refs):
    x_ref, p_ref, q_ref, left, right = refs[:5]
    outs, q_out = refs[5 : 5 + nb], refs[5 + nb]
    kicked, scratch = refs[6 + nb], refs[7 + nb :]
    n = 3 * lb
    count = cells + 2 * X_HALO
    b = b_ref[0]

    def cell_rows(w):
        if w < X_HALO:
            return left[pl.ds(w * n, n), :]
        if w >= cells + X_HALO:
            return right[pl.ds((w - cells - X_HALO) * n, n), :]
        return x_ref[w - X_HALO]

    charge_rows = [left[pl.ds(9 * lb + e, 1), :] for e in range(2)]
    charge_rows += [q_ref[c : c + 1, :] for c in range(cells)]
    charge_rows += [right[pl.ds(9 * lb + e, 1), :] for e in range(2)]
    q_out[...] = jnp.zeros(q_out.shape, F32)
    for w in range(count):
        q_out[w : w + 1, :] = charge_rows[w]
    for w in range(count):
        rows = cell_rows(w)
        build_tiles(scratch[0], w * lb, lb, rows[:lb], rows[lb : 2 * lb], rows[2 * lb :])

    read = pair_forces(scratch, Rows(q_out, 0), count, mols, lb, slots)
    half = 0.5 * outer_step
    for w in range(1, count - 1):
        if w < X_HALO:
            old = left[pl.ds(2 * n, n), :]
        elif w >= cells + X_HALO:
            old = right[pl.ds(2 * n, n), :]
        else:
            old = p_ref[w - X_HALO]
        force = jnp.concatenate([read(w, c) for c in range(3)], axis=0)
        kicked[w - 1] = old + half * force
    width = group + 2 * P_HALO
    for k in range(nb):
        first = jnp.bitwise_xor(b, k) * group
        for w in range(width):
            outs[k][pl.ds((width + w) * n, n), :] = kicked[first + w]
            source = first + w - P_HALO
            inside = x_ref[jnp.clip(source, 0, cells - 1)]
            if w < P_HALO:
                inside = jnp.where(source < 0, left[pl.ds(n, n), :], inside)
            elif w >= group + P_HALO:
                inside = jnp.where(source >= cells, right[pl.ds(0, n), :], inside)
            outs[k][pl.ds(w * n, n), :] = inside


class Rows:
    def __init__(self, ref, first):
        self.ref, self.first = ref, first

    def __getitem__(self, index):
        return self.ref[pl.ds(self.first + index, 1), :]


def bond_forces(x, y, z, used, mols, slots):
    def partner(a, t):
        return pltpu.roll(a, slots - t * mols, 1)

    first = [a - partner(a, 1) for a in (x, y, z)]
    second = [a - partner(a, 2) for a in (x, y, z)]
    third = [s - f for f, s in zip(first, second)]

    def pull(bond, stiffness, square):
        length = bond[0] * bond[0] + bond[1] * bond[1] + bond[2] * bond[2]
        return (stiffness * used) * (length - square)

    c1 = pull(first, bond_stiffness, bond_square)
    c2 = pull(second, bond_stiffness, bond_square)
    c3 = pull(third, angle_stiffness, angle_square)
    out = []
    for f, s, t in zip(first, second, third):
        on_first = c1 * f - c3 * t
        on_second = c2 * s + c3 * t
        on_oxygen = -(c1 * f + c2 * s)
        out.append(
            on_oxygen + pltpu.roll(on_first, mols, 1) + pltpu.roll(on_second, 2 * mols, 1)
        )
    return out


def inner_kernel(nb, group, lb, cells, mols, slots, b_ref, *refs):
    blocks = refs[:nb]
    step_ref, perm_ref, q_ref = refs[nb : nb + 3]
    ys = refs[nb + 3 : 2 * nb + 3]
    xv, scratch = refs[2 * nb + 3], refs[2 * nb + 4 :]
    beads = nb * lb
    width = group + 2 * P_HALO
    n = 3 * lb
    b = b_ref[0]
    step = step_ref[b]
    charges = Rows(q_ref, b * group + P_HALO)

    def advance(pos, vel):
        out_x, out_v = [], []
        for x, v in zip(pos, vel):
            high, mid, low = split3(jnp.concatenate([x, v], axis=0))
            stacked = jnp.concatenate([high, mid, high, mid, low, high], axis=0).astype(BF16)
            new = dot_nn(step, stacked)
            out_x.append(new[:beads])
            out_v.append(new[beads:])
        return out_x, out_v

    for w in range(width):
        def gather(a, comp):
            return jnp.concatenate(
                [block[pl.ds((a * width + w) * n + comp * lb, lb), :] for block in blocks], axis=0
            )

        q = charges[w]
        oxygen = (q < -1.5).astype(F32)
        inverse = jnp.where(q < -1.5, 1.0 / oxygen_mass, 1.0)
        pos = [gather(0, c) for c in range(3)]
        vel = [gather(1, c) * inverse for c in range(3)]
        half = (0.5 * inner_step) * inverse
        full = inner_step * inverse
        force = bond_forces(*pos, oxygen, mols, slots)
        vel = [v + half * f for v, f in zip(vel, force)]
        pos, vel = advance(pos, vel)
        force = bond_forces(*pos, oxygen, mols, slots)
        vel = [v + full * f for v, f in zip(vel, force)]
        pos, vel = advance(pos, vel)
        if 1 <= w <= width - 2:
            force = bond_forces(*pos, oxygen, mols, slots)
            vel = [v + half * f for v, f in zip(vel, force)]
            mass = jnp.where(q < -1.5, oxygen_mass, 1.0)
            for c in range(3):
                xv[w - 1, pl.ds(c * beads, beads), :] = pos[c]
                xv[w - 1, pl.ds((3 + c) * beads, beads), :] = vel[c] * mass
        build_tiles(scratch[0], w * beads, beads, *pos)

    read = pair_forces(scratch, charges, width, mols, beads, slots)
    for w in range(group):
        old = xv[w]
        m = 3 * beads
        force = jnp.concatenate([read(w + 1, c) for c in range(3)], axis=0)
        state = jnp.concatenate([old[:m], old[m:] + (0.5 * outer_step) * force], axis=0)
        state = unpermuted(state, perm_ref[b * group + w])
        for a in range(2):
            for c in range(3):
                for k in range(nb):
                    row = (a * 3 + c) * beads + k * lb
                    ys[k][pl.ds(((a * group + w) * 3 + c) * lb, lb), :] = state[row : row + lb]


def unpack_kernel(nb, group, lb, cells, b_ref, *refs):
    ys = refs[:nb]
    outs = refs[nb:]
    b = b_ref[0]
    for k in range(nb):
        source = jnp.bitwise_xor(b, k)
        for a in range(2):
            for w in range(group):
                for c in range(3):
                    outs[a][pl.ds(c * cells + source * group + w, lb, stride=3 * cells), :] = ys[
                        k
                    ][pl.ds(((a * group + w) * 3 + c) * lb, lb), :]


def call(kernel, outs, scratch, scalar, *operands, space=pltpu.VMEM):
    vmem = pl.BlockSpec(memory_space=pltpu.VMEM)
    smem = pl.BlockSpec(memory_space=pltpu.SMEM)
    return pl.pallas_call(
        kernel,
        out_shape=outs,
        in_specs=([] if scalar is None else [smem]) + [pl.BlockSpec(memory_space=space)] * len(operands),
        out_specs=[vmem] * len(outs),
        scratch_shapes=scratch,
        compiler_params=pltpu.CompilerParams(vmem_limit_bytes=48 * 1024 * 1024),
    )(*(() if scalar is None else (scalar,)), *operands)


def local(nb, ns, positions, momenta, molecules):
    lb, _, cells, slots = positions.shape
    mols = molecules.shape[1]
    group = cells // nb
    beads = lb * nb
    width = group + 2 * P_HALO
    b = lax.axis_index("bead").astype(jnp.int32).reshape(1)

    def shape(*dims):
        return jax.ShapeDtypeStruct(dims, F32)

    edge = shape(9 * lb + 8, slots)
    rows = lb * 3 * cells
    xs, ps, perm, charges, to_right, to_left = call(
        functools.partial(order_kernel, lb, cells, mols, slots),
        [shape(cells, 3 * lb, slots)] * 2
        + [jax.ShapeDtypeStruct((cells, slots, slots), BF16), shape(cells, slots), edge, edge],
        [
            pltpu.VMEM((3, cells, mols), jnp.int32),
            pltpu.VMEM((rows, slots), F32),
            pltpu.VMEM((rows, slots), F32),
            pltpu.VMEM((3, cells, slots), jnp.int32),
            pltpu.VMEM((cells, slots), F32),
            pltpu.SemaphoreType.DMA((3,)),
        ],
        None,
        jnp.transpose(molecules, (2, 0, 1)),
        positions.reshape(rows, slots),
        momenta.reshape(rows, slots),
        space=pltpu.HBM,
    )
    left = lax.ppermute(to_right, "space", [(s, (s + 1) % ns) for s in range(ns)])
    right = lax.ppermute(to_left, "space", [(s, (s - 1) % ns) for s in range(ns)])
    q_rows = -(-(cells + 2 * X_HALO) // 8) * 8
    *blocks, q_wide = call(
        functools.partial(outer_kernel, nb, group, lb, cells, mols, slots),
        [shape(2 * width * 3 * lb, slots)] * nb + [shape(q_rows, slots)],
        [pltpu.VMEM((cells + 2 * P_HALO, 3 * lb, slots), F32)]
        + pair_scratch(cells + 2 * X_HALO, lb, slots),
        b,
        xs,
        ps,
        charges,
        left,
        right,
    )
    blocks = [blocks[0]] + [
        lax.ppermute(blocks[k], "bead", [(i, i ^ k) for i in range(nb)])
        for k in range(1, nb)
    ]
    step = jnp.asarray(propagator(beads, lb))
    ys = call(
        functools.partial(inner_kernel, nb, group, lb, cells, mols, slots),
        [shape(2 * group * 3 * lb, slots)] * nb,
        [pltpu.VMEM((group, 6 * beads, slots), F32)]
        + pair_scratch(width, beads, slots),
        b,
        *blocks,
        step,
        perm,
        q_wide,
    )
    ys = [ys[0]] + [
        lax.ppermute(ys[k], "bead", [(i, i ^ k) for i in range(nb)]) for k in range(1, nb)
    ]
    new_x, new_p = call(
        functools.partial(unpack_kernel, nb, group, lb, cells),
        [shape(lb * 3 * cells, slots)] * 2,
        [],
        b,
        *ys,
    )
    return new_x.reshape(positions.shape), new_p.reshape(positions.shape)


def solution(mesh):
    spec = P("bead", None, "space", None)
    return jax.shard_map(
        functools.partial(local, mesh.shape["bead"], mesh.shape["space"]),
        mesh=mesh,
        in_specs=(spec, spec, P("space", None, None)),
        out_specs=(spec, spec),
        check_vma=False,
    )
```

```python
import functools

import jax
import jax.numpy as jnp
import ml_dtypes
import numpy as np
from jax import lax
from jax.experimental import pallas as pl
from jax.experimental.pallas import tpu as pltpu
from jax.sharding import PartitionSpec as P

charge_oxygen = -0.8476
charge_hydrogen = 0.4238
coulomb_scale = 24.0
coulomb_soft = 0.004
well_depth = 0.02
sigma_square = 0.0841
lennard_soft = 0.04
bond_stiffness = 20000.0
bond_square = 0.0081
angle_stiffness = 5000.0
angle_square = 0.0204
cycle_frequency = 60.0
outer_step = 0.02
inner_step = 0.01
oxygen_mass = 16.0

REACH = 1
X_HALO = 2 * REACH
P_HALO = REACH

F32 = jnp.float32
BF16 = jnp.bfloat16


def rounded(a):
    return a.astype(BF16).astype(F32)


def split3(a):
    high = rounded(a)
    rest = a - high
    mid = rounded(rest)
    return high, mid, rest - mid


def two_part(a):
    high = rounded(a)
    return high + rounded(a - high)


def dot_nn(a, b):
    return lax.dot_general(a, b, (((1,), (0,)), ((), ())), preferred_element_type=F32)


def dot_nt(a, b):
    return lax.dot_general(a, b, (((1,), (1,)), ((), ())), preferred_element_type=F32)


def propagator(beads, beads_dev):
    j = np.arange(beads)
    angles = 2.0 * np.pi * ((j[:, None] * j[None, :]) % beads) / beads
    half = beads // 2
    col = j[None, :]
    u = np.where(
        col == 0,
        np.sqrt(1.0 / beads),
        np.where(
            col < half,
            np.sqrt(2.0 / beads) * np.cos(angles),
            np.where(
                col == half,
                np.sqrt(1.0 / beads) * np.cos(angles),
                np.sqrt(2.0 / beads) * np.sin(angles),
            ),
        ),
    )
    w = 2.0 * cycle_frequency * np.sin(np.pi * j / beads)
    cosines = np.cos(w * inner_step)
    spring = w * np.sin(w * inner_step)
    drift = np.where(j == 0, inner_step, np.sin(w * inner_step) / np.where(j == 0, 1.0, w))
    def circulant(values, bead):
        first = ((u * values) @ u.T)[:, 0]
        return first[(bead[:, None] - bead[None, :]) % beads]

    out = []
    for b in range(beads // beads_dev):
        bead = ((j // beads_dev) ^ b) * beads_dev + j % beads_dev
        a = circulant(cosines, bead)
        whole = np.block([[a, circulant(drift, bead)], [-circulant(spring, bead), a]])
        high = whole.astype(ml_dtypes.bfloat16)
        rest = whole - high.astype(np.float64)
        mid = rest.astype(ml_dtypes.bfloat16)
        low = (rest - mid.astype(np.float64)).astype(ml_dtypes.bfloat16)
        out.append(np.concatenate([high, high, mid, mid, high, low], axis=1))
    return np.stack(out)


def lane_tables(lanes, mols, slots):
    lane = lax.broadcasted_iota(jnp.int32, lanes.shape, 1)
    unit = jnp.where(lane < mols, charge_oxygen / charge_hydrogen, 1.0)
    return jnp.where(lanes < slots, unit, 0.0)


def permuted(rows, perm):
    n = rows.shape[0]
    stacked = jnp.concatenate(split3(rows), axis=0).astype(BF16)
    moved = dot_nn(stacked, perm)
    return moved[:n] + moved[n : 2 * n] + moved[2 * n :]


def unpermuted(rows, perm):
    n = rows.shape[0]
    stacked = jnp.concatenate(split3(rows), axis=0).astype(BF16)
    moved = dot_nt(stacked, perm)
    return moved[:n] + moved[n : 2 * n] + moved[2 * n :]


def order_kernel(lb, cells, mols, slots, mol_hbm, x_hbm, p_hbm, *refs):
    xo, po, perm_ref, q_ref, to_right, to_left = refs[:6]
    mol_ref, x_ref, p_ref, wide, held_ref, sems = refs[6:]
    copies = [
        pltpu.make_async_copy(source, dest, sems.at[i])
        for i, (source, dest) in enumerate(
            ((mol_hbm, mol_ref), (x_hbm, x_ref), (p_hbm, p_ref))
        )
    ]
    for copy in copies:
        copy.start()
    row = lax.broadcasted_iota(jnp.int32, (slots, slots), 0)
    col = lax.broadcasted_iota(jnp.int32, (slots, slots), 1)
    upper = (row < col).astype(F32).astype(BF16)
    row = row.astype(F32)
    lane = lax.broadcasted_iota(jnp.int32, (cells, slots), 1)
    far = 4.0 * slots
    wide[...] = jnp.full(wide.shape, slots, jnp.int32)
    copies[0].wait()
    for t in range(3):
        wide[t, :, :mols] = mol_ref[t]
    lanes = jnp.where(
        lane < mols,
        wide[0],
        jnp.where(lane < 2 * mols, pltpu.roll(wide[1], mols, 1), pltpu.roll(wide[2], 2 * mols, 1)),
    )
    lanes = jnp.where(lane < 3 * mols, lanes, slots)
    charges = lane_tables(lanes, mols, slots)
    q_ref[...] = charges
    free = lanes >= slots
    key = jnp.where(
        free, far + dot_nn(free.astype(F32).astype(BF16), upper), lanes.astype(F32)
    )
    ones = jnp.ones((16, slots), BF16)
    for cell in range(cells):
        held = (row == key[cell : cell + 1]).astype(F32).astype(BF16)
        held_ref[cell : cell + 1, :] = dot_nt(ones, held)[0:1]
    used = held_ref[...]
    rank = dot_nn((1.0 - used).astype(BF16), upper)
    slot_key = jnp.where(used > 0.5, lane.astype(F32), far + rank)
    copies[1].wait()
    copies[2].wait()
    n = 3 * lb
    for cell in range(cells):
        slot_column = jnp.broadcast_to(slot_key[cell : cell + 1], (slots, slots)).T
        perm = (slot_column == key[cell : cell + 1]).astype(F32).astype(BF16)
        perm_ref[cell] = perm
        rows = [
            ref[pl.ds(comp * cells + cell, lb, stride=3 * cells), :]
            for ref in (x_ref, p_ref)
            for comp in range(3)
        ]
        moved = permuted(jnp.concatenate(rows, axis=0), perm)
        xo[cell] = moved[:n]
        po[cell] = moved[n:]
    for out, xs, ps in (
        (to_right, (cells - 2, cells - 1), cells - 1),
        (to_left, (0, 1), 0),
    ):
        out[9 * lb :, :] = jnp.zeros((8, slots), F32)
        for e, cell in enumerate(xs):
            out[pl.ds(e * n, n), :] = xo[cell]
            out[pl.ds(9 * lb + e, 1), :] = charges[cell : cell + 1]
        out[pl.ds(2 * n, n), :] = po[ps]


def put_tiles(scratch, first, count, rows):
    for index, value in rows:
        scratch[pl.ds(first * 8 + index, count, stride=8), :] = value


OFFSETS = (-1.0, 0.0, 1.0)


def build_tiles(tiles, first, count, x, y, z):
    x, y, z = two_part(x - 0.5), two_part(y - 0.5), two_part(z - 0.5)
    norm = x * x + y * y + z * z + 0.5 * coulomb_soft
    high = two_part(norm)
    low = norm - high
    put_tiles(
        tiles, first, count, ((0, x), (1, y), (2, z), (3, high), (4, low), (5, high), (6, low))
    )


def pair_scratch(count, beads, slots):
    n = count * beads
    return (
        [pltpu.VMEM((n * 8, slots), F32)] * 2
        + [pltpu.VMEM((n // min(beads, 4), slots, 32 * min(beads, 4)), BF16)]
        + [pltpu.VMEM((n // 2, 32, slots), BF16)] * 3
        + [pltpu.VMEM((n, 32, slots), BF16)]
        + [pltpu.VMEM((slots, slots), F32)]
    )


def pair_forces(scratch, charges, count, mols, beads, slots):
    tiles, forces, lt, rr, rt, keep = *scratch[:3], scratch[3:6], *scratch[6:]
    orows = -(-mols // 8) * 8
    pair_scale = coulomb_scale * charge_hydrogen * charge_hydrogen
    k3 = sigma_square**3
    ratio = (charge_hydrogen / charge_oxygen) ** 2 / pair_scale
    lj_a = 24.0 * well_depth * 2.0 * k3 * k3 * ratio
    lj_b = 24.0 * well_depth * k3 * ratio
    row8 = lax.broadcasted_iota(jnp.int32, (8, slots), 0)
    place, norms = row8 < 3, row8 < 5
    target_rows = place | (row8 == 5) | (row8 == 6)
    ones_low = jnp.where((row8 == 3) | (row8 == 4), 1.0, 0.0)
    ones_high = jnp.where((row8 == 5) | (row8 == 6), 1.0, 0.0)
    ones_last = jnp.where(row8 == 7, 1.0, 0.0)
    lj_row = lax.broadcasted_iota(jnp.int32, (orows, slots), 0)
    lj_lane = lax.broadcasted_iota(jnp.int32, (orows, slots), 1)
    first_lanes, second_lanes = lj_lane < mols, lj_lane < 2 * mols
    corner = (lj_row < mols) & first_lanes

    i = lax.broadcasted_iota(jnp.int32, (slots, slots), 0)
    j = lax.broadcasted_iota(jnp.int32, (slots, slots), 1)
    i = jnp.where(i >= 2 * mols, i - 2 * mols, jnp.where(i >= mols, i - mols, i))
    j = jnp.where(j >= 2 * mols, j - 2 * mols, jnp.where(j >= mols, j - mols, j))
    keep[...] = (i != j).astype(F32)

    side = min(beads, 4)
    lane32 = lax.broadcasted_iota(jnp.int32, (slots, 32 * side), 1) & 31
    odd = (lane32 >= 27) & (lane32 < 31)
    even = lane32 == 31
    signs = [
        jnp.where(odd, offset, jnp.where(even, offset * offset, 1.0)).astype(BF16)
        for offset in OFFSETS
    ]

    fours = beads // side
    unroll = min(fours, 2)
    per_cell = fours // unroll
    pairs = beads // 2

    def tile(ref, n):
        return ref[pl.ds(pl.multiple_of(n * 8, 8), 8), :]

    def stack(values):
        return jnp.concatenate(values, axis=0).astype(BF16)

    def prepare(step, carry):
        charge = charges[lax.div(step, per_cell)]
        units = [
            jnp.where(row8 == 3, charge, jnp.where(row8 == 4, offset * charge, 0.0))
            for offset in OFFSETS
        ]
        for u in range(unroll):
            four = step * unroll + u
            left, high_rows, mid_rows = [], [], []
            for h in range(side):
                n = side * four + h
                value = tile(tiles, n)
                high = rounded(value)
                mid = value - high
                x_high, x_mid = high[0:1], mid[0:1]
                left_high = jnp.where(place, -2.0 * high, jnp.where(norms, high, ones_high))
                left_mid = jnp.where(place, -2.0 * mid, jnp.where(norms, mid, 0.0))
                left_last = jnp.where(
                    place,
                    -2.0 * mid,
                    jnp.where(
                        row8 == 3,
                        2.0 * x_high,
                        jnp.where(row8 == 4, 2.0 * x_mid, ones_last - 2.0 * ones_high),
                    ),
                )
                left += [left_high, left_high, left_mid, left_last]
                right_high = jnp.where(target_rows, high, ones_low)
                right_mid = jnp.where(target_rows, mid, 0.0)
                right_last = jnp.where(
                    place,
                    mid,
                    jnp.where(
                        row8 == 5, x_high, jnp.where(row8 == 6, x_mid, ones_low + ones_last)
                    ),
                )
                rt[n] = stack([right_high, right_mid, right_high, right_last])
                high_rows.append(high * charge)
                mid_rows.append(jnp.where(place, mid * charge, 0.0))
            lt[four] = stack(left).T
            for pair in range(side // 2):
                for o in range(3):
                    rows = []
                    for h in (2 * pair, 2 * pair + 1):
                        rows += [jnp.where(place, high_rows[h], units[o]), mid_rows[h]]
                    rr[o][four * (side // 2) + pair] = stack(rows)
        return carry

    lax.fori_loop(0, count * per_cell, prepare, 0)
    zero = jnp.zeros((32, slots), BF16)

    def target(four, w):
        left = jnp.concatenate(
            [lt[four + (o - 1) * fours] * signs[o] for o in range(3)], axis=0
        )
        right = jnp.concatenate(
            [
                jnp.concatenate(
                    [rt[side * four + h] if g == h else zero for g in range(side)], axis=1
                )
                for h in range(side)
            ],
            axis=0,
        )
        squares = dot_nn(left, right)
        for pair in range(side // 2):
            sums_of_pair(
                four * (side // 2) + pair,
                w,
                squares[:, 2 * pair * slots : 2 * (pair + 1) * slots],
            )

    def sums_of_pair(m, w, squares):
        blocks = [[], []]
        for h in range(2):
            lanes = slice(h * slots, (h + 1) * slots)
            near = [squares[o * slots : o * slots + orows, lanes] for o in range(3)]
            packed = jnp.where(
                first_lanes,
                near[0],
                jnp.where(
                    second_lanes, pltpu.roll(near[1], mols, 1), pltpu.roll(near[2], 2 * mols, 1)
                ),
            )
            root = lax.rsqrt(packed + (lennard_soft - coulomb_soft))
            inverse = root * root
            cube = inverse * inverse * inverse
            lj = (cube * lj_a - lj_b) * (cube * inverse)
            for o in range(3):
                root = lax.rsqrt(squares[o * slots : (o + 1) * slots, lanes])
                strength = root * root * root
                own = pltpu.roll(lj, slots - o * mols, 1) if o else lj
                strength = jnp.concatenate(
                    [strength[:orows] + jnp.where(corner, own, 0.0), strength[orows:]], axis=0
                )
                if o == 1:
                    strength = strength * keep[...]
                high = strength.astype(BF16)
                low = (strength - high.astype(F32)).astype(BF16)
                blocks[h] += [high, low]
        weights = [rr[o][m + (o - 1) * pairs] for o in (0, 0, 1, 1, 2, 2)]
        sums = dot_nn(
            jnp.concatenate(weights, axis=1),
            jnp.concatenate([jnp.concatenate(b, axis=0) for b in blocks], axis=1),
        )
        scale = charges[w] * pair_scale
        for h in range(2):
            part = sums[16 * h : 16 * h + 16, h * slots : (h + 1) * slots]
            total = part[0:8] + part[8:16]
            total = total + jnp.where(row8 == 0, total[4:5], 0.0)
            n = 2 * m + h
            forces[pl.ds(pl.multiple_of(n * 8, 8), 8), :] = (
                tile(tiles, n) * total[3:4] - total
            ) * scale

    def step(index, carry):
        for u in range(unroll):
            target(index * unroll + u, lax.div(index, per_cell))
        return carry

    lax.fori_loop(per_cell, (count - 1) * per_cell, step, 0)

    def read(w, comp):
        return forces[pl.ds(w * beads * 8 + comp, beads, stride=8), :]

    return read


def outer_kernel(nb, group, lb, cells, mols, slots, b_ref, *refs):
    x_ref, p_ref, q_ref, left, right = refs[:5]
    outs, q_out = refs[5 : 5 + nb], refs[5 + nb]
    kicked, scratch = refs[6 + nb], refs[7 + nb :]
    n = 3 * lb
    count = cells + 2 * X_HALO
    b = b_ref[0]

    def cell_rows(w):
        if w < X_HALO:
            return left[pl.ds(w * n, n), :]
        if w >= cells + X_HALO:
            return right[pl.ds((w - cells - X_HALO) * n, n), :]
        return x_ref[w - X_HALO]

    charge_rows = [left[pl.ds(9 * lb + e, 1), :] for e in range(2)]
    charge_rows += [q_ref[c : c + 1, :] for c in range(cells)]
    charge_rows += [right[pl.ds(9 * lb + e, 1), :] for e in range(2)]
    q_out[...] = jnp.zeros(q_out.shape, F32)
    for w in range(count):
        q_out[w : w + 1, :] = charge_rows[w]
    for w in range(count):
        rows = cell_rows(w)
        build_tiles(scratch[0], w * lb, lb, rows[:lb], rows[lb : 2 * lb], rows[2 * lb :])

    read = pair_forces(scratch, Rows(q_out, 0), count, mols, lb, slots)
    half = 0.5 * outer_step
    for w in range(1, count - 1):
        if w < X_HALO:
            old = left[pl.ds(2 * n, n), :]
        elif w >= cells + X_HALO:
            old = right[pl.ds(2 * n, n), :]
        else:
            old = p_ref[w - X_HALO]
        force = jnp.concatenate([read(w, c) for c in range(3)], axis=0)
        kicked[w - 1] = old + half * force
    width = group + 2 * P_HALO
    for k in range(nb):
        first = jnp.bitwise_xor(b, k) * group
        for w in range(width):
            outs[k][pl.ds((width + w) * n, n), :] = kicked[first + w]
            source = first + w - P_HALO
            inside = x_ref[jnp.clip(source, 0, cells - 1)]
            if w < P_HALO:
                inside = jnp.where(source < 0, left[pl.ds(n, n), :], inside)
            elif w >= group + P_HALO:
                inside = jnp.where(source >= cells, right[pl.ds(0, n), :], inside)
            outs[k][pl.ds(w * n, n), :] = inside


class Rows:
    def __init__(self, ref, first):
        self.ref, self.first = ref, first

    def __getitem__(self, index):
        return self.ref[pl.ds(self.first + index, 1), :]


def bond_forces(x, y, z, used, mols, slots):
    def partner(a, t):
        return pltpu.roll(a, slots - t * mols, 1)

    first = [a - partner(a, 1) for a in (x, y, z)]
    second = [a - partner(a, 2) for a in (x, y, z)]
    third = [s - f for f, s in zip(first, second)]

    def pull(bond, stiffness, square):
        length = bond[0] * bond[0] + bond[1] * bond[1] + bond[2] * bond[2]
        return (stiffness * used) * (length - square)

    c1 = pull(first, bond_stiffness, bond_square)
    c2 = pull(second, bond_stiffness, bond_square)
    c3 = pull(third, angle_stiffness, angle_square)
    out = []
    for f, s, t in zip(first, second, third):
        on_first = c1 * f - c3 * t
        on_second = c2 * s + c3 * t
        on_oxygen = -(c1 * f + c2 * s)
        out.append(
            on_oxygen + pltpu.roll(on_first, mols, 1) + pltpu.roll(on_second, 2 * mols, 1)
        )
    return out


def inner_kernel(nb, group, lb, cells, mols, slots, b_ref, *refs):
    blocks = refs[:nb]
    step_ref, perm_ref, q_ref = refs[nb : nb + 3]
    ys = refs[nb + 3 : 2 * nb + 3]
    xv, scratch = refs[2 * nb + 3], refs[2 * nb + 4 :]
    beads = nb * lb
    width = group + 2 * P_HALO
    n = 3 * lb
    b = b_ref[0]
    step = step_ref[b]
    charges = Rows(q_ref, b * group + P_HALO)

    def advance(pos, vel):
        out_x, out_v = [], []
        for x, v in zip(pos, vel):
            high, mid, low = split3(jnp.concatenate([x, v], axis=0))
            stacked = jnp.concatenate([high, mid, high, mid, low, high], axis=0).astype(BF16)
            new = dot_nn(step, stacked)
            out_x.append(new[:beads])
            out_v.append(new[beads:])
        return out_x, out_v

    for w in range(width):
        def gather(a, comp):
            return jnp.concatenate(
                [block[pl.ds((a * width + w) * n + comp * lb, lb), :] for block in blocks], axis=0
            )

        q = charges[w]
        oxygen = (q < -1.5).astype(F32)
        inverse = jnp.where(q < -1.5, 1.0 / oxygen_mass, 1.0)
        pos = [gather(0, c) for c in range(3)]
        vel = [gather(1, c) * inverse for c in range(3)]
        half = (0.5 * inner_step) * inverse
        full = inner_step * inverse
        force = bond_forces(*pos, oxygen, mols, slots)
        vel = [v + half * f for v, f in zip(vel, force)]
        pos, vel = advance(pos, vel)
        force = bond_forces(*pos, oxygen, mols, slots)
        vel = [v + full * f for v, f in zip(vel, force)]
        pos, vel = advance(pos, vel)
        if 1 <= w <= width - 2:
            force = bond_forces(*pos, oxygen, mols, slots)
            vel = [v + half * f for v, f in zip(vel, force)]
            mass = jnp.where(q < -1.5, oxygen_mass, 1.0)
            for c in range(3):
                xv[w - 1, pl.ds(c * beads, beads), :] = pos[c]
                xv[w - 1, pl.ds((3 + c) * beads, beads), :] = vel[c] * mass
        build_tiles(scratch[0], w * beads, beads, *pos)

    read = pair_forces(scratch, charges, width, mols, beads, slots)
    for w in range(group):
        old = xv[w]
        m = 3 * beads
        force = jnp.concatenate([read(w + 1, c) for c in range(3)], axis=0)
        state = jnp.concatenate([old[:m], old[m:] + (0.5 * outer_step) * force], axis=0)
        state = unpermuted(state, perm_ref[b * group + w])
        for a in range(2):
            for c in range(3):
                for k in range(nb):
                    row = (a * 3 + c) * beads + k * lb
                    ys[k][pl.ds(((a * group + w) * 3 + c) * lb, lb), :] = state[row : row + lb]


def unpack_kernel(nb, group, lb, cells, b_ref, *refs):
    ys = refs[:nb]
    outs = refs[nb:]
    b = b_ref[0]
    for k in range(nb):
        source = jnp.bitwise_xor(b, k)
        for a in range(2):
            for w in range(group):
                for c in range(3):
                    outs[a][pl.ds(c * cells + source * group + w, lb, stride=3 * cells), :] = ys[
                        k
                    ][pl.ds(((a * group + w) * 3 + c) * lb, lb), :]


def call(kernel, outs, scratch, scalar, *operands, space=pltpu.VMEM):
    vmem = pl.BlockSpec(memory_space=pltpu.VMEM)
    smem = pl.BlockSpec(memory_space=pltpu.SMEM)
    return pl.pallas_call(
        kernel,
        out_shape=outs,
        in_specs=([] if scalar is None else [smem]) + [pl.BlockSpec(memory_space=space)] * len(operands),
        out_specs=[vmem] * len(outs),
        scratch_shapes=scratch,
        compiler_params=pltpu.CompilerParams(vmem_limit_bytes=48 * 1024 * 1024),
    )(*(() if scalar is None else (scalar,)), *operands)


def local(nb, ns, positions, momenta, molecules):
    lb, _, cells, slots = positions.shape
    mols = molecules.shape[1]
    group = cells // nb
    beads = lb * nb
    width = group + 2 * P_HALO
    b = lax.axis_index("bead").astype(jnp.int32).reshape(1)

    def shape(*dims):
        return jax.ShapeDtypeStruct(dims, F32)

    edge = shape(9 * lb + 8, slots)
    rows = lb * 3 * cells
    xs, ps, perm, charges, to_right, to_left = call(
        functools.partial(order_kernel, lb, cells, mols, slots),
        [shape(cells, 3 * lb, slots)] * 2
        + [jax.ShapeDtypeStruct((cells, slots, slots), BF16), shape(cells, slots), edge, edge],
        [
            pltpu.VMEM((3, cells, mols), jnp.int32),
            pltpu.VMEM((rows, slots), F32),
            pltpu.VMEM((rows, slots), F32),
            pltpu.VMEM((3, cells, slots), jnp.int32),
            pltpu.VMEM((cells, slots), F32),
            pltpu.SemaphoreType.DMA((3,)),
        ],
        None,
        *(
            pltpu.with_memory_space_constraint(a, pltpu.HBM)
            for a in (
                jnp.transpose(molecules, (2, 0, 1)),
                positions.reshape(rows, slots),
                momenta.reshape(rows, slots),
            )
        ),
        space=pltpu.HBM,
    )
    left = lax.ppermute(to_right, "space", [(s, (s + 1) % ns) for s in range(ns)])
    right = lax.ppermute(to_left, "space", [(s, (s - 1) % ns) for s in range(ns)])
    q_rows = -(-(cells + 2 * X_HALO) // 8) * 8
    *blocks, q_wide = call(
        functools.partial(outer_kernel, nb, group, lb, cells, mols, slots),
        [shape(2 * width * 3 * lb, slots)] * nb + [shape(q_rows, slots)],
        [pltpu.VMEM((cells + 2 * P_HALO, 3 * lb, slots), F32)]
        + pair_scratch(cells + 2 * X_HALO, lb, slots),
        b,
        xs,
        ps,
        charges,
        left,
        right,
    )
    blocks = [blocks[0]] + [
        lax.ppermute(blocks[k], "bead", [(i, i ^ k) for i in range(nb)])
        for k in range(1, nb)
    ]
    step = jnp.asarray(propagator(beads, lb))
    ys = call(
        functools.partial(inner_kernel, nb, group, lb, cells, mols, slots),
        [shape(2 * group * 3 * lb, slots)] * nb,
        [pltpu.VMEM((group, 6 * beads, slots), F32)]
        + pair_scratch(width, beads, slots),
        b,
        *blocks,
        step,
        perm,
        q_wide,
    )
    ys = [ys[0]] + [
        lax.ppermute(ys[k], "bead", [(i, i ^ k) for i in range(nb)]) for k in range(1, nb)
    ]
    new_x, new_p = call(
        functools.partial(unpack_kernel, nb, group, lb, cells),
        [shape(lb * 3 * cells, slots)] * 2,
        [],
        b,
        *ys,
    )
    return new_x.reshape(positions.shape), new_p.reshape(positions.shape)


def solution(mesh):
    spec = P("bead", None, "space", None)
    return jax.shard_map(
        functools.partial(local, mesh.shape["bead"], mesh.shape["space"]),
        mesh=mesh,
        in_specs=(spec, spec, P("space", None, None)),
        out_specs=(spec, spec),
        check_vma=False,
    )
```

```python
import functools

import jax
import jax.numpy as jnp
import ml_dtypes
import numpy as np
from jax import lax
from jax.experimental import pallas as pl
from jax.experimental.pallas import tpu as pltpu
from jax.sharding import PartitionSpec as P

charge_oxygen = -0.8476
charge_hydrogen = 0.4238
coulomb_scale = 24.0
coulomb_soft = 0.004
well_depth = 0.02
sigma_square = 0.0841
lennard_soft = 0.04
bond_stiffness = 20000.0
bond_square = 0.0081
angle_stiffness = 5000.0
angle_square = 0.0204
cycle_frequency = 60.0
outer_step = 0.02
inner_step = 0.01
oxygen_mass = 16.0

REACH = 1
X_HALO = 2 * REACH
P_HALO = REACH

F32 = jnp.float32
BF16 = jnp.bfloat16


def rounded(a):
    return a.astype(BF16).astype(F32)


def split3(a):
    high = rounded(a)
    rest = a - high
    mid = rounded(rest)
    return high, mid, rest - mid


def two_part(a):
    high = rounded(a)
    return high + rounded(a - high)


def dot_nn(a, b):
    return lax.dot_general(a, b, (((1,), (0,)), ((), ())), preferred_element_type=F32)


def dot_nt(a, b):
    return lax.dot_general(a, b, (((1,), (1,)), ((), ())), preferred_element_type=F32)


def propagator(beads, beads_dev):
    j = np.arange(beads)
    angles = 2.0 * np.pi * ((j[:, None] * j[None, :]) % beads) / beads
    half = beads // 2
    col = j[None, :]
    u = np.where(
        col == 0,
        np.sqrt(1.0 / beads),
        np.where(
            col < half,
            np.sqrt(2.0 / beads) * np.cos(angles),
            np.where(
                col == half,
                np.sqrt(1.0 / beads) * np.cos(angles),
                np.sqrt(2.0 / beads) * np.sin(angles),
            ),
        ),
    )
    w = 2.0 * cycle_frequency * np.sin(np.pi * j / beads)
    cosines = np.cos(w * inner_step)
    spring = w * np.sin(w * inner_step)
    drift = np.where(j == 0, inner_step, np.sin(w * inner_step) / np.where(j == 0, 1.0, w))
    def circulant(values, bead):
        first = ((u * values) @ u.T)[:, 0]
        return first[(bead[:, None] - bead[None, :]) % beads]

    out = []
    for b in range(beads // beads_dev):
        bead = ((j // beads_dev) ^ b) * beads_dev + j % beads_dev
        a = circulant(cosines, bead)
        whole = np.block([[a, circulant(drift, bead)], [-circulant(spring, bead), a]])
        high = whole.astype(ml_dtypes.bfloat16)
        rest = whole - high.astype(np.float64)
        mid = rest.astype(ml_dtypes.bfloat16)
        low = (rest - mid.astype(np.float64)).astype(ml_dtypes.bfloat16)
        out.append(np.concatenate([high, high, mid, mid, high, low], axis=1))
    return np.stack(out)


def lane_tables(lanes, mols, slots):
    lane = lax.broadcasted_iota(jnp.int32, lanes.shape, 1)
    unit = jnp.where(lane < mols, charge_oxygen / charge_hydrogen, 1.0)
    return jnp.where(lanes < slots, unit, 0.0)


def permuted(rows, perm):
    n = rows.shape[0]
    stacked = jnp.concatenate(split3(rows), axis=0).astype(BF16)
    moved = dot_nn(stacked, perm)
    return moved[:n] + moved[n : 2 * n] + moved[2 * n :]


def unpermuted(rows, perm):
    n = rows.shape[0]
    stacked = jnp.concatenate(split3(rows), axis=0).astype(BF16)
    moved = dot_nt(stacked, perm)
    return moved[:n] + moved[n : 2 * n] + moved[2 * n :]


def order_kernel(lb, cells, mols, slots, mol_hbm, x_hbm, p_hbm, *refs):
    xo, po, perm_ref, q_ref, to_right, to_left = refs[:6]
    mol_ref, x_ref, p_ref, wide, held_ref, sems = refs[6:]
    copies = [
        pltpu.make_async_copy(source, dest, sems.at[i])
        for i, (source, dest) in enumerate(
            ((mol_hbm, mol_ref), (x_hbm, x_ref), (p_hbm, p_ref))
        )
    ]
    for copy in copies:
        copy.start()
    row = lax.broadcasted_iota(jnp.int32, (slots, slots), 0)
    col = lax.broadcasted_iota(jnp.int32, (slots, slots), 1)
    upper = (row < col).astype(F32).astype(BF16)
    row = row.astype(F32)
    lane = lax.broadcasted_iota(jnp.int32, (cells, slots), 1)
    far = 4.0 * slots
    wide[...] = jnp.full(wide.shape, slots, jnp.int32)
    copies[0].wait()
    for t in range(3):
        wide[t, :, :mols] = mol_ref[t]
    lanes = jnp.where(
        lane < mols,
        wide[0],
        jnp.where(lane < 2 * mols, pltpu.roll(wide[1], mols, 1), pltpu.roll(wide[2], 2 * mols, 1)),
    )
    lanes = jnp.where(lane < 3 * mols, lanes, slots)
    charges = lane_tables(lanes, mols, slots)
    q_ref[...] = charges
    free = lanes >= slots
    key = jnp.where(
        free, far + dot_nn(free.astype(F32).astype(BF16), upper), lanes.astype(F32)
    )
    ones = jnp.ones((16, slots), BF16)
    for cell in range(cells):
        held = (row == key[cell : cell + 1]).astype(F32).astype(BF16)
        held_ref[cell : cell + 1, :] = dot_nt(ones, held)[0:1]
    used = held_ref[...]
    rank = dot_nn((1.0 - used).astype(BF16), upper)
    slot_key = jnp.where(used > 0.5, lane.astype(F32), far + rank)
    copies[1].wait()
    copies[2].wait()
    n = 3 * lb
    for cell in range(cells):
        slot_column = jnp.broadcast_to(slot_key[cell : cell + 1], (slots, slots)).T
        perm = (slot_column == key[cell : cell + 1]).astype(F32).astype(BF16)
        perm_ref[cell] = perm
        rows = [
            ref[pl.ds(comp * cells + cell, lb, stride=3 * cells), :]
            for ref in (x_ref, p_ref)
            for comp in range(3)
        ]
        moved = permuted(jnp.concatenate(rows, axis=0), perm)
        xo[cell] = moved[:n]
        po[cell] = moved[n:]
    for out, xs, ps in (
        (to_right, (cells - 2, cells - 1), cells - 1),
        (to_left, (0, 1), 0),
    ):
        out[9 * lb :, :] = jnp.zeros((8, slots), F32)
        for e, cell in enumerate(xs):
            out[pl.ds(e * n, n), :] = xo[cell]
            out[pl.ds(9 * lb + e, 1), :] = charges[cell : cell + 1]
        out[pl.ds(2 * n, n), :] = po[ps]


def put_tiles(scratch, first, count, rows):
    for index, value in rows:
        scratch[pl.ds(first * 8 + index, count, stride=8), :] = value


OFFSETS = (-1.0, 0.0, 1.0)


def build_tiles(tiles, first, count, x, y, z):
    x, y, z = two_part(x - 0.5), two_part(y - 0.5), two_part(z - 0.5)
    norm = x * x + y * y + z * z + 0.5 * coulomb_soft
    high = two_part(norm)
    low = norm - high
    put_tiles(
        tiles, first, count, ((0, x), (1, y), (2, z), (3, high), (4, low), (5, high), (6, low))
    )


def store_shapes(count, beads, slots):
    n = count * beads
    return (
        [((n * 8, slots), F32), ((n // 2, slots, 64), BF16)]
        + [((n // 2, 32, slots), BF16)] * 3
        + [((n, 32, slots), BF16)]
    )


STORE = 6


class Store:
    def __init__(self, refs, beads):
        self.tiles, self.peers, *sums, self.targets = refs
        self.sums = sums
        self.beads = beads


def tile_of(ref, n):
    return ref[pl.ds(pl.multiple_of(n * 8, 8), 8), :]


def prepare(store, charges, count, slots):
    tiles, beads = store.tiles, store.beads
    row8 = lax.broadcasted_iota(jnp.int32, (8, slots), 0)
    place, norms = row8 < 3, row8 < 5
    target_rows = place | (row8 == 5) | (row8 == 6)
    ones_low = jnp.where((row8 == 3) | (row8 == 4), 1.0, 0.0)
    ones_high = jnp.where((row8 == 5) | (row8 == 6), 1.0, 0.0)
    ones_last = jnp.where(row8 == 7, 1.0, 0.0)
    pairs = beads // 2
    unroll = min(pairs, 4)
    per_cell = pairs // unroll

    def stack(values):
        return jnp.concatenate(values, axis=0).astype(BF16)

    def step(index, carry):
        charge = charges[lax.div(index, per_cell)]
        units = [
            jnp.where(row8 == 3, charge, jnp.where(row8 == 4, offset * charge, 0.0))
            for offset in OFFSETS
        ]
        for u in range(unroll):
            m = index * unroll + u
            left, high_rows, mid_rows = [], [], []
            for h in range(2):
                value = tile_of(tiles, 2 * m + h)
                high = rounded(value)
                mid = value - high
                x_high, x_mid = high[0:1], mid[0:1]
                left_high = jnp.where(place, -2.0 * high, jnp.where(norms, high, ones_high))
                left_mid = jnp.where(place, -2.0 * mid, jnp.where(norms, mid, 0.0))
                left_last = jnp.where(
                    place,
                    -2.0 * mid,
                    jnp.where(
                        row8 == 3,
                        2.0 * x_high,
                        jnp.where(row8 == 4, 2.0 * x_mid, ones_last - 2.0 * ones_high),
                    ),
                )
                left += [left_high, left_high, left_mid, left_last]
                right_high = jnp.where(target_rows, high, ones_low)
                right_mid = jnp.where(target_rows, mid, 0.0)
                right_last = jnp.where(
                    place,
                    mid,
                    jnp.where(
                        row8 == 5, x_high, jnp.where(row8 == 6, x_mid, ones_low + ones_last)
                    ),
                )
                store.targets[2 * m + h] = stack([right_high, right_mid, right_high, right_last])
                high_rows.append(high * charge)
                mid_rows.append(jnp.where(place, mid * charge, 0.0))
            store.peers[m] = stack(left).T
            for o in range(3):
                rows = []
                for h in range(2):
                    rows += [jnp.where(place, high_rows[h], units[o]), mid_rows[h]]
                store.sums[o][m] = stack(rows)
        return carry

    lax.fori_loop(0, count * per_cell, step, 0)


class PairLoop:
    def __init__(self, mols, slots, beads, keep):
        self.mols, self.slots, self.keep = mols, slots, keep
        self.pairs = beads // 2
        self.unroll = min(self.pairs, 4)
        self.per_cell = self.pairs // self.unroll
        orows = -(-mols // 8) * 8
        self.row8 = lax.broadcasted_iota(jnp.int32, (8, slots), 0)
        lj_row = lax.broadcasted_iota(jnp.int32, (orows, slots), 0)
        lj_lane = lax.broadcasted_iota(jnp.int32, (orows, slots), 1)
        self.first_lanes, self.second_lanes = lj_lane < mols, lj_lane < 2 * mols
        self.corner = (lj_row < mols) & self.first_lanes

        i = lax.broadcasted_iota(jnp.int32, (slots, slots), 0)
        j = lax.broadcasted_iota(jnp.int32, (slots, slots), 1)
        i = jnp.where(i >= 2 * mols, i - 2 * mols, jnp.where(i >= mols, i - mols, i))
        j = jnp.where(j >= 2 * mols, j - 2 * mols, jnp.where(j >= mols, j - mols, j))
        keep[...] = (i != j).astype(F32)

        lane64 = lax.broadcasted_iota(jnp.int32, (slots, 64), 1) & 31
        odd = (lane64 >= 27) & (lane64 < 31)
        even = lane64 == 31
        self.signs = [
            jnp.where(odd, offset, jnp.where(even, offset * offset, 1.0)).astype(BF16)
            for offset in OFFSETS
        ]
        self.zero = jnp.zeros((32, slots), BF16)

    def pair(self, peers, charge):
        mols, slots = self.mols, self.slots
        orows = self.corner.shape[0]
        pair_scale = coulomb_scale * charge_hydrogen * charge_hydrogen
        k3 = sigma_square**3
        ratio = (charge_hydrogen / charge_oxygen) ** 2 / pair_scale
        lj_a = 24.0 * well_depth * 2.0 * k3 * k3 * ratio
        lj_b = 24.0 * well_depth * k3 * ratio
        zero = self.zero
        own, m = peers[1]
        left = jnp.concatenate(
            [store.peers[index] * sign for (store, index), sign in zip(peers, self.signs)], axis=0
        )
        right = jnp.concatenate(
            [
                jnp.concatenate([own.targets[2 * m], zero], axis=1),
                jnp.concatenate([zero, own.targets[2 * m + 1]], axis=1),
            ],
            axis=0,
        )
        squares = dot_nn(left, right)
        blocks = [[], [], []]
        for h in range(2):
            lanes = slice(h * slots, (h + 1) * slots)
            near = [squares[o * slots : o * slots + orows, lanes] for o in range(3)]
            packed = jnp.where(
                self.first_lanes,
                near[0],
                jnp.where(
                    self.second_lanes,
                    pltpu.roll(near[1], mols, 1),
                    pltpu.roll(near[2], 2 * mols, 1),
                ),
            )
            root = lax.rsqrt(packed + (lennard_soft - coulomb_soft))
            inverse = root * root
            cube = inverse * inverse * inverse
            lj = (cube * lj_a - lj_b) * (cube * inverse)
            for o in range(3):
                root = lax.rsqrt(squares[o * slots : (o + 1) * slots, lanes])
                strength = root * root * root
                part = pltpu.roll(lj, slots - o * mols, 1) if o else lj
                strength = jnp.concatenate(
                    [strength[:orows] + jnp.where(self.corner, part, 0.0), strength[orows:]],
                    axis=0,
                )
                if o == 1:
                    strength = strength * self.keep[...]
                high = strength.astype(BF16)
                low = (strength - high.astype(F32)).astype(BF16)
                blocks[o].append(jnp.concatenate([high, low], axis=0))
        sums = None
        for o, (store, index) in enumerate(peers):
            weights = store.sums[o][index]
            value = dot_nn(
                jnp.concatenate([weights, weights], axis=1), jnp.concatenate(blocks[o], axis=1)
            )
            sums = value if sums is None else sums + value
        scale = charge * pair_scale
        out = []
        for h in range(2):
            part = sums[16 * h : 16 * h + 16, h * slots : (h + 1) * slots]
            total = part[0:8] + part[8:16]
            total = total + jnp.where(self.row8 == 0, total[4:5], 0.0)
            out.append((tile_of(own.tiles, 2 * m + h) * total[3:4] - total) * scale)
        return out

    def cells(self, store, charges, first, last, forces):
        def step(index, carry):
            for u in range(self.unroll):
                m = index * self.unroll + u
                peers = [(store, m - self.pairs), (store, m), (store, m + self.pairs)]
                out = self.pair(peers, charges[lax.div(index, self.per_cell)])
                for h in range(2):
                    n = 2 * (m - first * self.pairs) + h
                    forces[pl.ds(pl.multiple_of(n * 8, 8), 8), :] = out[h]
            return carry

        lax.fori_loop(first * self.per_cell, last * self.per_cell, step, 0)


def read_force(forces, w, beads, comp):
    return forces[pl.ds(w * beads * 8 + comp, beads, stride=8), :]


def own_kernel(cells, lb, slots, x_ref, q_ref, *refs):
    store = Store(refs, lb)
    for w in range(cells):
        rows = x_ref[w]
        build_tiles(store.tiles, w * lb, lb, rows[:lb], rows[lb : 2 * lb], rows[2 * lb :])
    prepare(store, Rows(q_ref, 0), cells, slots)


def interior_kernel(cells, lb, mols, slots, q_ref, *refs):
    store = Store(refs[:STORE], lb)
    forces, keep = refs[STORE:]
    PairLoop(mols, slots, lb, keep).cells(store, Rows(q_ref, 0), 1, cells - 1, forces)


def edge_kernel(nb, group, lb, cells, mols, slots, b_ref, *refs):
    x_ref, p_ref, q_ref, left, right, inner = refs[:6]
    own = Store(refs[6 : 6 + STORE], lb)
    refs = refs[6 + STORE :]
    outs, q_out = refs[:nb], refs[nb]
    kicked, halo_forces, keep = refs[nb + 1 : nb + 4]
    halo = Store(refs[nb + 4 :], lb)
    n = 3 * lb
    count = cells + 2 * X_HALO
    b = b_ref[0]

    charge_rows = [left[pl.ds(9 * lb + e, 1), :] for e in range(2)]
    charge_rows += [q_ref[c : c + 1, :] for c in range(cells)]
    charge_rows += [right[pl.ds(9 * lb + e, 1), :] for e in range(2)]
    q_out[...] = jnp.zeros(q_out.shape, F32)
    for w in range(count):
        q_out[w : w + 1, :] = charge_rows[w]
    for e in range(4):
        edge = (left, right)[e // 2]
        rows = edge[pl.ds((e % 2) * n, n), :]
        build_tiles(halo.tiles, e * lb, lb, rows[:lb], rows[lb : 2 * lb], rows[2 * lb :])

    class Edges:
        def __getitem__(self, e):
            return q_out[pl.ds(jnp.where(e < 2, e, e + cells), 1), :]

    prepare(halo, Edges(), 4, slots)
    loop = PairLoop(mols, slots, lb, keep)

    def place(w):
        if w < X_HALO:
            return halo, w
        if w >= cells + X_HALO:
            return halo, w - cells
        return own, w - X_HALO

    targets = (1, 2, cells + 1, cells + 2)

    def edge_step(step, carry):
        for e, w in enumerate(targets):
            for u in range(loop.unroll):
                index = step * loop.unroll + u
                peers = [
                    (store, cell * loop.pairs + index) for store, cell in map(place, (w - 1, w, w + 1))
                ]
                out = loop.pair(peers, charge_rows[w])
                for h in range(2):
                    at = (e * lb + 2 * index + h) * 8
                    halo_forces[pl.ds(pl.multiple_of(at, 8), 8), :] = out[h]
        return carry

    lax.fori_loop(0, loop.per_cell, edge_step, 0)
    half = 0.5 * outer_step
    for w in range(1, count - 1):
        if w < X_HALO:
            old = left[pl.ds(2 * n, n), :]
        elif w >= cells + X_HALO:
            old = right[pl.ds(2 * n, n), :]
        else:
            old = p_ref[w - X_HALO]
        source, cell = (
            (halo_forces, targets.index(w)) if w in targets else (inner, w - X_HALO - 1)
        )
        force = jnp.concatenate([read_force(source, cell, lb, c) for c in range(3)], axis=0)
        kicked[w - 1] = old + half * force
    width = group + 2 * P_HALO
    for k in range(nb):
        first = jnp.bitwise_xor(b, k) * group
        for w in range(width):
            outs[k][pl.ds((width + w) * n, n), :] = kicked[first + w]
            source = first + w - P_HALO
            inside = x_ref[jnp.clip(source, 0, cells - 1)]
            if w < P_HALO:
                inside = jnp.where(source < 0, left[pl.ds(n, n), :], inside)
            elif w >= group + P_HALO:
                inside = jnp.where(source >= cells, right[pl.ds(0, n), :], inside)
            outs[k][pl.ds(w * n, n), :] = inside


class Rows:
    def __init__(self, ref, first):
        self.ref, self.first = ref, first

    def __getitem__(self, index):
        return self.ref[pl.ds(self.first + index, 1), :]


def bond_forces(x, y, z, used, mols, slots):
    def partner(a, t):
        return pltpu.roll(a, slots - t * mols, 1)

    first = [a - partner(a, 1) for a in (x, y, z)]
    second = [a - partner(a, 2) for a in (x, y, z)]
    third = [s - f for f, s in zip(first, second)]

    def pull(bond, stiffness, square):
        length = bond[0] * bond[0] + bond[1] * bond[1] + bond[2] * bond[2]
        return (stiffness * used) * (length - square)

    c1 = pull(first, bond_stiffness, bond_square)
    c2 = pull(second, bond_stiffness, bond_square)
    c3 = pull(third, angle_stiffness, angle_square)
    out = []
    for f, s, t in zip(first, second, third):
        on_first = c1 * f - c3 * t
        on_second = c2 * s + c3 * t
        on_oxygen = -(c1 * f + c2 * s)
        out.append(
            on_oxygen + pltpu.roll(on_first, mols, 1) + pltpu.roll(on_second, 2 * mols, 1)
        )
    return out


def steps_kernel(nb, group, lb, mols, slots, b_ref, *refs):
    blocks = refs[:nb]
    step_ref, q_ref, xv = refs[nb : nb + 3]
    beads = nb * lb
    store = Store(refs[nb + 3 :], beads)
    width = group + 2 * P_HALO
    n = 3 * lb
    b = b_ref[0]
    step = step_ref[b]
    charges = Rows(q_ref, b * group + P_HALO)

    def advance(pos, vel):
        out_x, out_v = [], []
        for x, v in zip(pos, vel):
            high, mid, low = split3(jnp.concatenate([x, v], axis=0))
            stacked = jnp.concatenate([high, mid, high, mid, low, high], axis=0).astype(BF16)
            new = dot_nn(step, stacked)
            out_x.append(new[:beads])
            out_v.append(new[beads:])
        return out_x, out_v

    for w in range(width):
        def gather(a, comp):
            return jnp.concatenate(
                [block[pl.ds((a * width + w) * n + comp * lb, lb), :] for block in blocks], axis=0
            )

        q = charges[w]
        oxygen = (q < -1.5).astype(F32)
        inverse = jnp.where(q < -1.5, 1.0 / oxygen_mass, 1.0)
        pos = [gather(0, c) for c in range(3)]
        vel = [gather(1, c) * inverse for c in range(3)]
        half = (0.5 * inner_step) * inverse
        full = inner_step * inverse
        force = bond_forces(*pos, oxygen, mols, slots)
        vel = [v + half * f for v, f in zip(vel, force)]
        pos, vel = advance(pos, vel)
        force = bond_forces(*pos, oxygen, mols, slots)
        vel = [v + full * f for v, f in zip(vel, force)]
        pos, vel = advance(pos, vel)
        if 1 <= w <= width - 2:
            force = bond_forces(*pos, oxygen, mols, slots)
            vel = [v + half * f for v, f in zip(vel, force)]
            mass = jnp.where(q < -1.5, oxygen_mass, 1.0)
            for c in range(3):
                xv[w - 1, pl.ds(c * beads, beads), :] = pos[c]
                xv[w - 1, pl.ds((3 + c) * beads, beads), :] = vel[c] * mass
        build_tiles(store.tiles, w * beads, beads, *pos)

    prepare(store, charges, width, slots)


def final_kernel(nb, group, lb, mols, slots, b_ref, *refs):
    perm_ref, q_ref, xv = refs[:3]
    beads = nb * lb
    store = Store(refs[3 : 3 + STORE], beads)
    ys = refs[3 + STORE : 3 + STORE + nb]
    forces, keep = refs[3 + STORE + nb :]
    b = b_ref[0]
    charges = Rows(q_ref, b * group + P_HALO)
    PairLoop(mols, slots, beads, keep).cells(store, charges, P_HALO, P_HALO + group, forces)
    for w in range(group):
        old = xv[w]
        m = 3 * beads
        force = jnp.concatenate([read_force(forces, w, beads, c) for c in range(3)], axis=0)
        state = jnp.concatenate([old[:m], old[m:] + (0.5 * outer_step) * force], axis=0)
        state = unpermuted(state, perm_ref[b * group + w])
        for a in range(2):
            for c in range(3):
                for k in range(nb):
                    row = (a * 3 + c) * beads + k * lb
                    ys[k][pl.ds(((a * group + w) * 3 + c) * lb, lb), :] = state[row : row + lb]


def unpack_kernel(nb, group, lb, cells, b_ref, *refs):
    ys = refs[:nb]
    outs = refs[nb:]
    b = b_ref[0]
    for k in range(nb):
        source = jnp.bitwise_xor(b, k)
        for a in range(2):
            for w in range(group):
                for c in range(3):
                    outs[a][pl.ds(c * cells + source * group + w, lb, stride=3 * cells), :] = ys[
                        k
                    ][pl.ds(((a * group + w) * 3 + c) * lb, lb), :]


def call(kernel, outs, scratch, scalar, *operands, space=pltpu.VMEM):
    vmem = pl.BlockSpec(memory_space=pltpu.VMEM)
    smem = pl.BlockSpec(memory_space=pltpu.SMEM)
    return pl.pallas_call(
        kernel,
        out_shape=outs,
        in_specs=([] if scalar is None else [smem]) + [pl.BlockSpec(memory_space=space)] * len(operands),
        out_specs=[vmem] * len(outs),
        scratch_shapes=scratch,
        compiler_params=pltpu.CompilerParams(vmem_limit_bytes=24 * 1024 * 1024),
    )(*(() if scalar is None else (scalar,)), *operands)


def local(nb, ns, positions, momenta, molecules):
    lb, _, cells, slots = positions.shape
    mols = molecules.shape[1]
    group = cells // nb
    beads = lb * nb
    width = group + 2 * P_HALO
    b = lax.axis_index("bead").astype(jnp.int32).reshape(1)

    def shape(*dims):
        return jax.ShapeDtypeStruct(dims, F32)

    edge = shape(9 * lb + 8, slots)
    rows = lb * 3 * cells
    xs, ps, perm, charges, to_right, to_left = call(
        functools.partial(order_kernel, lb, cells, mols, slots),
        [shape(cells, 3 * lb, slots)] * 2
        + [jax.ShapeDtypeStruct((cells, slots, slots), BF16), shape(cells, slots), edge, edge],
        [
            pltpu.VMEM((3, cells, mols), jnp.int32),
            pltpu.VMEM((rows, slots), F32),
            pltpu.VMEM((rows, slots), F32),
            pltpu.VMEM((3, cells, slots), jnp.int32),
            pltpu.VMEM((cells, slots), F32),
            pltpu.SemaphoreType.DMA((3,)),
        ],
        None,
        *(
            pltpu.with_memory_space_constraint(a, pltpu.HBM)
            for a in (
                jnp.transpose(molecules, (2, 0, 1)),
                positions.reshape(rows, slots),
                momenta.reshape(rows, slots),
            )
        ),
        space=pltpu.HBM,
    )
    left = lax.ppermute(to_right, "space", [(s, (s + 1) % ns) for s in range(ns)])
    right = lax.ppermute(to_left, "space", [(s, (s - 1) % ns) for s in range(ns)])
    q_rows = -(-(cells + 2 * X_HALO) // 8) * 8

    def store(count, store_beads):
        return [
            jax.ShapeDtypeStruct(*entry) for entry in store_shapes(count, store_beads, slots)
        ]

    keep = pltpu.VMEM((slots, slots), F32)
    own = call(
        functools.partial(own_kernel, cells, lb, slots), store(cells, lb), [], None, xs, charges
    )
    (inner,) = call(
        functools.partial(interior_kernel, cells, lb, mols, slots),
        [shape((cells - 2) * lb * 8, slots)],
        [keep],
        None,
        charges,
        *own,
    )
    *blocks, q_wide = call(
        functools.partial(edge_kernel, nb, group, lb, cells, mols, slots),
        [shape(2 * width * 3 * lb, slots)] * nb + [shape(q_rows, slots)],
        [
            pltpu.VMEM((cells + 2 * P_HALO, 3 * lb, slots), F32),
            pltpu.VMEM((4 * lb * 8, slots), F32),
            keep,
        ]
        + [pltpu.VMEM(*entry) for entry in store_shapes(4, lb, slots)],
        b,
        xs,
        ps,
        charges,
        left,
        right,
        inner,
        *own,
    )
    blocks = [blocks[0]] + [
        lax.ppermute(blocks[k], "bead", [(i, i ^ k) for i in range(nb)]) for k in range(1, nb)
    ]
    step = jnp.asarray(propagator(beads, lb))
    xv, *stepped = call(
        functools.partial(steps_kernel, nb, group, lb, mols, slots),
        [shape(group, 6 * beads, slots)] + store(width, beads),
        [],
        b,
        *blocks,
        step,
        q_wide,
    )
    ys = call(
        functools.partial(final_kernel, nb, group, lb, mols, slots),
        [shape(2 * group * 3 * lb, slots)] * nb,
        [pltpu.VMEM((group * beads * 8, slots), F32), keep],
        b,
        perm,
        q_wide,
        xv,
        *stepped,
    )
    ys = [ys[0]] + [
        lax.ppermute(ys[k], "bead", [(i, i ^ k) for i in range(nb)]) for k in range(1, nb)
    ]
    new_x, new_p = call(
        functools.partial(unpack_kernel, nb, group, lb, cells),
        [shape(lb * 3 * cells, slots)] * 2,
        [],
        b,
        *ys,
    )
    return new_x.reshape(positions.shape), new_p.reshape(positions.shape)


def solution(mesh):
    spec = P("bead", None, "space", None)
    return jax.shard_map(
        functools.partial(local, mesh.shape["bead"], mesh.shape["space"]),
        mesh=mesh,
        in_specs=(spec, spec, P("space", None, None)),
        out_specs=(spec, spec),
        check_vma=False,
    )
```

```python
import functools

import jax
import jax.numpy as jnp
import ml_dtypes
import numpy as np
from jax import lax
from jax.experimental import pallas as pl
from jax.experimental.pallas import tpu as pltpu
from jax.sharding import PartitionSpec as P

charge_oxygen = -0.8476
charge_hydrogen = 0.4238
coulomb_scale = 24.0
coulomb_soft = 0.004
well_depth = 0.02
sigma_square = 0.0841
lennard_soft = 0.04
bond_stiffness = 20000.0
bond_square = 0.0081
angle_stiffness = 5000.0
angle_square = 0.0204
cycle_frequency = 60.0
outer_step = 0.02
inner_step = 0.01
oxygen_mass = 16.0

REACH = 1
X_HALO = 2 * REACH
P_HALO = REACH

F32 = jnp.float32
BF16 = jnp.bfloat16


def rounded(a):
    return a.astype(BF16).astype(F32)


def split3(a):
    high = rounded(a)
    rest = a - high
    mid = rounded(rest)
    return high, mid, rest - mid


def two_part(a):
    high = rounded(a)
    return high + rounded(a - high)


def dot_nn(a, b):
    return lax.dot_general(a, b, (((1,), (0,)), ((), ())), preferred_element_type=F32)


def dot_nt(a, b):
    return lax.dot_general(a, b, (((1,), (1,)), ((), ())), preferred_element_type=F32)


def propagator(beads, beads_dev):
    j = np.arange(beads)
    angles = 2.0 * np.pi * ((j[:, None] * j[None, :]) % beads) / beads
    half = beads // 2
    col = j[None, :]
    u = np.where(
        col == 0,
        np.sqrt(1.0 / beads),
        np.where(
            col < half,
            np.sqrt(2.0 / beads) * np.cos(angles),
            np.where(
                col == half,
                np.sqrt(1.0 / beads) * np.cos(angles),
                np.sqrt(2.0 / beads) * np.sin(angles),
            ),
        ),
    )
    w = 2.0 * cycle_frequency * np.sin(np.pi * j / beads)
    cosines = np.cos(w * inner_step)
    spring = w * np.sin(w * inner_step)
    drift = np.where(j == 0, inner_step, np.sin(w * inner_step) / np.where(j == 0, 1.0, w))
    def circulant(values, bead):
        first = ((u * values) @ u.T)[:, 0]
        return first[(bead[:, None] - bead[None, :]) % beads]

    out = []
    for b in range(beads // beads_dev):
        bead = ((j // beads_dev) ^ b) * beads_dev + j % beads_dev
        a = circulant(cosines, bead)
        whole = np.block([[a, circulant(drift, bead)], [-circulant(spring, bead), a]])
        high = whole.astype(ml_dtypes.bfloat16)
        rest = whole - high.astype(np.float64)
        mid = rest.astype(ml_dtypes.bfloat16)
        low = (rest - mid.astype(np.float64)).astype(ml_dtypes.bfloat16)
        out.append(np.concatenate([high, high, mid, mid, high, low], axis=1))
    return np.stack(out)


def lane_tables(lanes, mols, slots):
    lane = lax.broadcasted_iota(jnp.int32, lanes.shape, 1)
    unit = jnp.where(lane < mols, charge_oxygen / charge_hydrogen, 1.0)
    return jnp.where(lanes < slots, unit, 0.0)


def permuted(rows, perm):
    n = rows.shape[0]
    stacked = jnp.concatenate(split3(rows), axis=0).astype(BF16)
    moved = dot_nn(stacked, perm)
    return moved[:n] + moved[n : 2 * n] + moved[2 * n :]


def unpermuted(rows, perm):
    n = rows.shape[0]
    stacked = jnp.concatenate(split3(rows), axis=0).astype(BF16)
    moved = dot_nt(stacked, perm)
    return moved[:n] + moved[n : 2 * n] + moved[2 * n :]


def order_kernel(lb, cells, mols, slots, mol_hbm, x_hbm, p_hbm, *refs):
    xo, po, perm_ref, q_ref, to_right, to_left = refs[:6]
    mol_ref, x_ref, p_ref, wide, held_ref, sems = refs[6:]
    copies = [
        pltpu.make_async_copy(source, dest, sems.at[i])
        for i, (source, dest) in enumerate(
            ((mol_hbm, mol_ref), (x_hbm, x_ref), (p_hbm, p_ref))
        )
    ]
    for copy in copies:
        copy.start()
    row = lax.broadcasted_iota(jnp.int32, (slots, slots), 0)
    col = lax.broadcasted_iota(jnp.int32, (slots, slots), 1)
    upper = (row < col).astype(F32).astype(BF16)
    row = row.astype(F32)
    lane = lax.broadcasted_iota(jnp.int32, (cells, slots), 1)
    far = 4.0 * slots
    wide[...] = jnp.full(wide.shape, slots, jnp.int32)
    copies[0].wait()
    for t in range(3):
        wide[t, :, :mols] = mol_ref[t]
    lanes = jnp.where(
        lane < mols,
        wide[0],
        jnp.where(lane < 2 * mols, pltpu.roll(wide[1], mols, 1), pltpu.roll(wide[2], 2 * mols, 1)),
    )
    lanes = jnp.where(lane < 3 * mols, lanes, slots)
    charges = lane_tables(lanes, mols, slots)
    q_ref[...] = charges
    free = lanes >= slots
    key = jnp.where(
        free, far + dot_nn(free.astype(F32).astype(BF16), upper), lanes.astype(F32)
    )
    ones = jnp.ones((16, slots), BF16)
    for cell in range(cells):
        held = (row == key[cell : cell + 1]).astype(F32).astype(BF16)
        held_ref[cell : cell + 1, :] = dot_nt(ones, held)[0:1]
    used = held_ref[...]
    rank = dot_nn((1.0 - used).astype(BF16), upper)
    slot_key = jnp.where(used > 0.5, lane.astype(F32), far + rank)
    copies[1].wait()
    copies[2].wait()
    n = 3 * lb
    for cell in range(cells):
        slot_column = jnp.broadcast_to(slot_key[cell : cell + 1], (slots, slots)).T
        perm = (slot_column == key[cell : cell + 1]).astype(F32).astype(BF16)
        perm_ref[cell] = perm
        rows = [
            ref[pl.ds(comp * cells + cell, lb, stride=3 * cells), :]
            for ref in (x_ref, p_ref)
            for comp in range(3)
        ]
        moved = permuted(jnp.concatenate(rows, axis=0), perm)
        xo[cell] = moved[:n]
        po[cell] = moved[n:]
    for out, xs, ps in (
        (to_right, (cells - 2, cells - 1), cells - 1),
        (to_left, (0, 1), 0),
    ):
        out[9 * lb :, :] = jnp.zeros((8, slots), F32)
        for e, cell in enumerate(xs):
            out[pl.ds(e * n, n), :] = xo[cell]
            out[pl.ds(9 * lb + e, 1), :] = charges[cell : cell + 1]
        out[pl.ds(2 * n, n), :] = po[ps]


def put_tiles(scratch, first, count, rows):
    for index, value in rows:
        scratch[pl.ds(first * 8 + index, count, stride=8), :] = value


OFFSETS = (-1.0, 0.0, 1.0)


def build_tiles(tiles, first, count, x, y, z):
    x, y, z = two_part(x - 0.5), two_part(y - 0.5), two_part(z - 0.5)
    norm = x * x + y * y + z * z + 0.5 * coulomb_soft
    high = two_part(norm)
    low = norm - high
    put_tiles(
        tiles, first, count, ((0, x), (1, y), (2, z), (3, high), (4, low), (5, high), (6, low))
    )


def store_shapes(count, beads, slots):
    n = count * beads
    return (
        [((n * 8, slots), F32), ((n // 2, slots, 64), BF16)]
        + [((n // 2, 32, slots), BF16)] * 3
        + [((n, 32, slots), BF16)]
    )


STORE = 6


class Store:
    def __init__(self, refs, beads):
        self.tiles, self.peers, *sums, self.targets = refs
        self.sums = sums
        self.beads = beads


def tile_of(ref, n):
    return ref[pl.ds(pl.multiple_of(n * 8, 8), 8), :]


def prepare(store, charges, count, slots):
    tiles, beads = store.tiles, store.beads
    row8 = lax.broadcasted_iota(jnp.int32, (8, slots), 0)
    place, norms = row8 < 3, row8 < 5
    target_rows = place | (row8 == 5) | (row8 == 6)
    ones_low = jnp.where((row8 == 3) | (row8 == 4), 1.0, 0.0)
    ones_high = jnp.where((row8 == 5) | (row8 == 6), 1.0, 0.0)
    ones_last = jnp.where(row8 == 7, 1.0, 0.0)
    pairs = beads // 2
    unroll = min(pairs, 4)
    per_cell = pairs // unroll

    def stack(values):
        return jnp.concatenate(values, axis=0).astype(BF16)

    def step(index, carry):
        charge = charges[lax.div(index, per_cell)]
        units = [
            jnp.where(row8 == 3, charge, jnp.where(row8 == 4, offset * charge, 0.0))
            for offset in OFFSETS
        ]
        for u in range(unroll):
            m = index * unroll + u
            left, high_rows, mid_rows = [], [], []
            for h in range(2):
                value = tile_of(tiles, 2 * m + h)
                high = rounded(value)
                mid = value - high
                x_high, x_mid = high[0:1], mid[0:1]
                left_high = jnp.where(place, -2.0 * high, jnp.where(norms, high, ones_high))
                left_mid = jnp.where(place, -2.0 * mid, jnp.where(norms, mid, 0.0))
                left_last = jnp.where(
                    place,
                    -2.0 * mid,
                    jnp.where(
                        row8 == 3,
                        2.0 * x_high,
                        jnp.where(row8 == 4, 2.0 * x_mid, ones_last - 2.0 * ones_high),
                    ),
                )
                left += [left_high, left_high, left_mid, left_last]
                right_high = jnp.where(target_rows, high, ones_low)
                right_mid = jnp.where(target_rows, mid, 0.0)
                right_last = jnp.where(
                    place,
                    mid,
                    jnp.where(
                        row8 == 5, x_high, jnp.where(row8 == 6, x_mid, ones_low + ones_last)
                    ),
                )
                store.targets[2 * m + h] = stack([right_high, right_mid, right_high, right_last])
                high_rows.append(high * charge)
                mid_rows.append(jnp.where(place, mid * charge, 0.0))
            store.peers[m] = stack(left).T
            for o in range(3):
                rows = []
                for h in range(2):
                    rows += [jnp.where(place, high_rows[h], units[o]), mid_rows[h]]
                store.sums[o][m] = stack(rows)
        return carry

    lax.fori_loop(0, count * per_cell, step, 0)


class PairLoop:
    def __init__(self, mols, slots, beads, keep):
        self.mols, self.slots, self.keep = mols, slots, keep
        self.pairs = beads // 2
        self.unroll = min(self.pairs, 4)
        self.per_cell = self.pairs // self.unroll
        orows = -(-mols // 8) * 8
        self.row8 = lax.broadcasted_iota(jnp.int32, (8, slots), 0)
        lj_row = lax.broadcasted_iota(jnp.int32, (orows, slots), 0)
        lj_lane = lax.broadcasted_iota(jnp.int32, (orows, slots), 1)
        self.first_lanes, self.second_lanes = lj_lane < mols, lj_lane < 2 * mols
        self.corner = (lj_row < mols) & self.first_lanes

        i = lax.broadcasted_iota(jnp.int32, (slots, slots), 0)
        j = lax.broadcasted_iota(jnp.int32, (slots, slots), 1)
        i = jnp.where(i >= 2 * mols, i - 2 * mols, jnp.where(i >= mols, i - mols, i))
        j = jnp.where(j >= 2 * mols, j - 2 * mols, jnp.where(j >= mols, j - mols, j))
        keep[...] = (i != j).astype(F32)

        lane64 = lax.broadcasted_iota(jnp.int32, (slots, 64), 1) & 31
        odd = (lane64 >= 27) & (lane64 < 31)
        even = lane64 == 31
        self.signs = [
            jnp.where(odd, offset, jnp.where(even, offset * offset, 1.0)).astype(BF16)
            for offset in OFFSETS
        ]
        self.zero = jnp.zeros((32, slots), BF16)

    def pair(self, peers, charge):
        mols, slots = self.mols, self.slots
        orows = self.corner.shape[0]
        pair_scale = coulomb_scale * charge_hydrogen * charge_hydrogen
        k3 = sigma_square**3
        ratio = (charge_hydrogen / charge_oxygen) ** 2 / pair_scale
        lj_a = 24.0 * well_depth * 2.0 * k3 * k3 * ratio
        lj_b = 24.0 * well_depth * k3 * ratio
        zero = self.zero
        own, m = peers[1]
        left = jnp.concatenate(
            [store.peers[index] * sign for (store, index), sign in zip(peers, self.signs)], axis=0
        )
        right = jnp.concatenate(
            [
                jnp.concatenate([own.targets[2 * m], zero], axis=1),
                jnp.concatenate([zero, own.targets[2 * m + 1]], axis=1),
            ],
            axis=0,
        )
        squares = dot_nn(left, right)
        blocks = [[], [], []]
        for h in range(2):
            lanes = slice(h * slots, (h + 1) * slots)
            near = [squares[o * slots : o * slots + orows, lanes] for o in range(3)]
            packed = jnp.where(
                self.first_lanes,
                near[0],
                jnp.where(
                    self.second_lanes,
                    pltpu.roll(near[1], mols, 1),
                    pltpu.roll(near[2], 2 * mols, 1),
                ),
            )
            root = lax.rsqrt(packed + (lennard_soft - coulomb_soft))
            inverse = root * root
            cube = inverse * inverse * inverse
            lj = (cube * lj_a - lj_b) * (cube * inverse)
            for o in range(3):
                root = lax.rsqrt(squares[o * slots : (o + 1) * slots, lanes])
                strength = root * root * root
                part = pltpu.roll(lj, slots - o * mols, 1) if o else lj
                strength = jnp.concatenate(
                    [strength[:orows] + jnp.where(self.corner, part, 0.0), strength[orows:]],
                    axis=0,
                )
                if o == 1:
                    strength = strength * self.keep[...]
                high = strength.astype(BF16)
                low = (strength - high.astype(F32)).astype(BF16)
                blocks[o].append(jnp.concatenate([high, low], axis=0))
        sums = None
        for o, (store, index) in enumerate(peers):
            weights = store.sums[o][index]
            value = dot_nn(
                jnp.concatenate([weights, weights], axis=1), jnp.concatenate(blocks[o], axis=1)
            )
            sums = value if sums is None else sums + value
        scale = charge * pair_scale
        out = []
        for h in range(2):
            part = sums[16 * h : 16 * h + 16, h * slots : (h + 1) * slots]
            total = part[0:8] + part[8:16]
            total = total + jnp.where(self.row8 == 0, total[4:5], 0.0)
            out.append((tile_of(own.tiles, 2 * m + h) * total[3:4] - total) * scale)
        return out

    def cells(self, store, charges, first, last, forces):
        total = (last - first) * self.pairs
        unroll = max(n for n in range(1, 33) if total % n == 0)

        def step(index, carry):
            for u in range(unroll):
                m = index * unroll + u
                at = m + first * self.pairs
                peers = [(store, at + (o - 1) * self.pairs) for o in range(3)]
                out = self.pair(peers, charges[lax.div(at, self.pairs)])
                for h in range(2):
                    n = 2 * m + h
                    forces[pl.ds(pl.multiple_of(n * 8, 8), 8), :] = out[h]
            return carry

        lax.fori_loop(0, total // unroll, step, 0)


def read_force(forces, w, beads, comp):
    return forces[pl.ds(w * beads * 8 + comp, beads, stride=8), :]


def own_kernel(cells, lb, slots, x_ref, q_ref, *refs):
    store = Store(refs, lb)
    for w in range(cells):
        rows = x_ref[w]
        build_tiles(store.tiles, w * lb, lb, rows[:lb], rows[lb : 2 * lb], rows[2 * lb :])
    prepare(store, Rows(q_ref, 0), cells, slots)


def interior_kernel(cells, lb, mols, slots, q_ref, *refs):
    store = Store(refs[:STORE], lb)
    forces, keep = refs[STORE:]
    PairLoop(mols, slots, lb, keep).cells(store, Rows(q_ref, 0), 1, cells - 1, forces)


def edge_kernel(nb, group, lb, cells, mols, slots, b_ref, *refs):
    x_ref, p_ref, q_ref, left, right, inner = refs[:6]
    own = Store(refs[6 : 6 + STORE], lb)
    refs = refs[6 + STORE :]
    outs, q_out = refs[:nb], refs[nb]
    kicked, halo_forces, keep = refs[nb + 1 : nb + 4]
    halo = Store(refs[nb + 4 :], lb)
    n = 3 * lb
    count = cells + 2 * X_HALO
    b = b_ref[0]

    charge_rows = [left[pl.ds(9 * lb + e, 1), :] for e in range(2)]
    charge_rows += [q_ref[c : c + 1, :] for c in range(cells)]
    charge_rows += [right[pl.ds(9 * lb + e, 1), :] for e in range(2)]
    q_out[...] = jnp.zeros(q_out.shape, F32)
    for w in range(count):
        q_out[w : w + 1, :] = charge_rows[w]
    for e in range(4):
        edge = (left, right)[e // 2]
        rows = edge[pl.ds((e % 2) * n, n), :]
        build_tiles(halo.tiles, e * lb, lb, rows[:lb], rows[lb : 2 * lb], rows[2 * lb :])

    class Edges:
        def __getitem__(self, e):
            return q_out[pl.ds(jnp.where(e < 2, e, e + cells), 1), :]

    prepare(halo, Edges(), 4, slots)
    loop = PairLoop(mols, slots, lb, keep)

    def place(w):
        if w < X_HALO:
            return halo, w
        if w >= cells + X_HALO:
            return halo, w - cells
        return own, w - X_HALO

    targets = (1, 2, cells + 1, cells + 2)

    def edge_step(step, carry):
        for e, w in enumerate(targets):
            for u in range(loop.unroll):
                index = step * loop.unroll + u
                peers = [
                    (store, cell * loop.pairs + index) for store, cell in map(place, (w - 1, w, w + 1))
                ]
                out = loop.pair(peers, charge_rows[w])
                for h in range(2):
                    at = (e * lb + 2 * index + h) * 8
                    halo_forces[pl.ds(pl.multiple_of(at, 8), 8), :] = out[h]
        return carry

    lax.fori_loop(0, loop.per_cell, edge_step, 0)
    half = 0.5 * outer_step
    for w in range(1, count - 1):
        if w < X_HALO:
            old = left[pl.ds(2 * n, n), :]
        elif w >= cells + X_HALO:
            old = right[pl.ds(2 * n, n), :]
        else:
            old = p_ref[w - X_HALO]
        source, cell = (
            (halo_forces, targets.index(w)) if w in targets else (inner, w - X_HALO - 1)
        )
        force = jnp.concatenate([read_force(source, cell, lb, c) for c in range(3)], axis=0)
        kicked[w - 1] = old + half * force
    width = group + 2 * P_HALO
    for k in range(nb):
        first = jnp.bitwise_xor(b, k) * group
        for w in range(width):
            outs[k][pl.ds((width + w) * n, n), :] = kicked[first + w]
            source = first + w - P_HALO
            inside = x_ref[jnp.clip(source, 0, cells - 1)]
            if w < P_HALO:
                inside = jnp.where(source < 0, left[pl.ds(n, n), :], inside)
            elif w >= group + P_HALO:
                inside = jnp.where(source >= cells, right[pl.ds(0, n), :], inside)
            outs[k][pl.ds(w * n, n), :] = inside


class Rows:
    def __init__(self, ref, first):
        self.ref, self.first = ref, first

    def __getitem__(self, index):
        return self.ref[pl.ds(self.first + index, 1), :]


def bond_forces(x, y, z, used, mols, slots):
    def partner(a, t):
        return pltpu.roll(a, slots - t * mols, 1)

    first = [a - partner(a, 1) for a in (x, y, z)]
    second = [a - partner(a, 2) for a in (x, y, z)]
    third = [s - f for f, s in zip(first, second)]

    def pull(bond, stiffness, square):
        length = bond[0] * bond[0] + bond[1] * bond[1] + bond[2] * bond[2]
        return (stiffness * used) * (length - square)

    c1 = pull(first, bond_stiffness, bond_square)
    c2 = pull(second, bond_stiffness, bond_square)
    c3 = pull(third, angle_stiffness, angle_square)
    out = []
    for f, s, t in zip(first, second, third):
        on_first = c1 * f - c3 * t
        on_second = c2 * s + c3 * t
        on_oxygen = -(c1 * f + c2 * s)
        out.append(
            on_oxygen + pltpu.roll(on_first, mols, 1) + pltpu.roll(on_second, 2 * mols, 1)
        )
    return out


def steps_kernel(nb, group, lb, mols, slots, b_ref, *refs):
    blocks = refs[:nb]
    step_ref, q_ref, xv = refs[nb : nb + 3]
    beads = nb * lb
    store = Store(refs[nb + 3 :], beads)
    width = group + 2 * P_HALO
    n = 3 * lb
    b = b_ref[0]
    step = step_ref[b]
    charges = Rows(q_ref, b * group + P_HALO)

    def advance(pos, vel):
        out_x, out_v = [], []
        for x, v in zip(pos, vel):
            high, mid, low = split3(jnp.concatenate([x, v], axis=0))
            stacked = jnp.concatenate([high, mid, high, mid, low, high], axis=0).astype(BF16)
            new = dot_nn(step, stacked)
            out_x.append(new[:beads])
            out_v.append(new[beads:])
        return out_x, out_v

    for w in range(width):
        def gather(a, comp):
            return jnp.concatenate(
                [block[pl.ds((a * width + w) * n + comp * lb, lb), :] for block in blocks], axis=0
            )

        q = charges[w]
        oxygen = (q < -1.5).astype(F32)
        inverse = jnp.where(q < -1.5, 1.0 / oxygen_mass, 1.0)
        pos = [gather(0, c) for c in range(3)]
        vel = [gather(1, c) * inverse for c in range(3)]
        half = (0.5 * inner_step) * inverse
        full = inner_step * inverse
        force = bond_forces(*pos, oxygen, mols, slots)
        vel = [v + half * f for v, f in zip(vel, force)]
        pos, vel = advance(pos, vel)
        force = bond_forces(*pos, oxygen, mols, slots)
        vel = [v + full * f for v, f in zip(vel, force)]
        pos, vel = advance(pos, vel)
        if 1 <= w <= width - 2:
            force = bond_forces(*pos, oxygen, mols, slots)
            vel = [v + half * f for v, f in zip(vel, force)]
            mass = jnp.where(q < -1.5, oxygen_mass, 1.0)
            for c in range(3):
                xv[w - 1, pl.ds(c * beads, beads), :] = pos[c]
                xv[w - 1, pl.ds((3 + c) * beads, beads), :] = vel[c] * mass
        build_tiles(store.tiles, w * beads, beads, *pos)

    prepare(store, charges, width, slots)


def final_kernel(nb, group, lb, mols, slots, b_ref, *refs):
    perm_ref, q_ref, xv = refs[:3]
    beads = nb * lb
    store = Store(refs[3 : 3 + STORE], beads)
    ys = refs[3 + STORE : 3 + STORE + nb]
    forces, keep = refs[3 + STORE + nb :]
    b = b_ref[0]
    charges = Rows(q_ref, b * group + P_HALO)
    PairLoop(mols, slots, beads, keep).cells(store, charges, P_HALO, P_HALO + group, forces)
    for w in range(group):
        old = xv[w]
        m = 3 * beads
        force = jnp.concatenate([read_force(forces, w, beads, c) for c in range(3)], axis=0)
        state = jnp.concatenate([old[:m], old[m:] + (0.5 * outer_step) * force], axis=0)
        state = unpermuted(state, perm_ref[b * group + w])
        for a in range(2):
            for c in range(3):
                for k in range(nb):
                    row = (a * 3 + c) * beads + k * lb
                    ys[k][pl.ds(((a * group + w) * 3 + c) * lb, lb), :] = state[row : row + lb]


def unpack_kernel(nb, group, lb, cells, b_ref, *refs):
    ys = refs[:nb]
    outs = refs[nb:]
    b = b_ref[0]
    for k in range(nb):
        source = jnp.bitwise_xor(b, k)
        for a in range(2):
            for w in range(group):
                for c in range(3):
                    outs[a][pl.ds(c * cells + source * group + w, lb, stride=3 * cells), :] = ys[
                        k
                    ][pl.ds(((a * group + w) * 3 + c) * lb, lb), :]


def call(kernel, outs, scratch, scalar, *operands, space=pltpu.VMEM):
    vmem = pl.BlockSpec(memory_space=pltpu.VMEM)
    smem = pl.BlockSpec(memory_space=pltpu.SMEM)
    return pl.pallas_call(
        kernel,
        out_shape=outs,
        in_specs=([] if scalar is None else [smem]) + [pl.BlockSpec(memory_space=space)] * len(operands),
        out_specs=[vmem] * len(outs),
        scratch_shapes=scratch,
        compiler_params=pltpu.CompilerParams(vmem_limit_bytes=24 * 1024 * 1024),
    )(*(() if scalar is None else (scalar,)), *operands)


def local(nb, ns, positions, momenta, molecules):
    lb, _, cells, slots = positions.shape
    mols = molecules.shape[1]
    group = cells // nb
    beads = lb * nb
    width = group + 2 * P_HALO
    b = lax.axis_index("bead").astype(jnp.int32).reshape(1)

    def shape(*dims):
        return jax.ShapeDtypeStruct(dims, F32)

    edge = shape(9 * lb + 8, slots)
    rows = lb * 3 * cells
    xs, ps, perm, charges, to_right, to_left = call(
        functools.partial(order_kernel, lb, cells, mols, slots),
        [shape(cells, 3 * lb, slots)] * 2
        + [jax.ShapeDtypeStruct((cells, slots, slots), BF16), shape(cells, slots), edge, edge],
        [
            pltpu.VMEM((3, cells, mols), jnp.int32),
            pltpu.VMEM((rows, slots), F32),
            pltpu.VMEM((rows, slots), F32),
            pltpu.VMEM((3, cells, slots), jnp.int32),
            pltpu.VMEM((cells, slots), F32),
            pltpu.SemaphoreType.DMA((3,)),
        ],
        None,
        *(
            pltpu.with_memory_space_constraint(a, pltpu.HBM)
            for a in (
                jnp.transpose(molecules, (2, 0, 1)),
                positions.reshape(rows, slots),
                momenta.reshape(rows, slots),
            )
        ),
        space=pltpu.HBM,
    )
    left = lax.ppermute(to_right, "space", [(s, (s + 1) % ns) for s in range(ns)])
    right = lax.ppermute(to_left, "space", [(s, (s - 1) % ns) for s in range(ns)])
    q_rows = -(-(cells + 2 * X_HALO) // 8) * 8

    def store(count, store_beads):
        return [
            jax.ShapeDtypeStruct(*entry) for entry in store_shapes(count, store_beads, slots)
        ]

    keep = pltpu.VMEM((slots, slots), F32)
    own = call(
        functools.partial(own_kernel, cells, lb, slots), store(cells, lb), [], None, xs, charges
    )
    (inner,) = call(
        functools.partial(interior_kernel, cells, lb, mols, slots),
        [shape((cells - 2) * lb * 8, slots)],
        [keep],
        None,
        charges,
        *own,
    )
    *blocks, q_wide = call(
        functools.partial(edge_kernel, nb, group, lb, cells, mols, slots),
        [shape(2 * width * 3 * lb, slots)] * nb + [shape(q_rows, slots)],
        [
            pltpu.VMEM((cells + 2 * P_HALO, 3 * lb, slots), F32),
            pltpu.VMEM((4 * lb * 8, slots), F32),
            keep,
        ]
        + [pltpu.VMEM(*entry) for entry in store_shapes(4, lb, slots)],
        b,
        xs,
        ps,
        charges,
        left,
        right,
        inner,
        *own,
    )
    blocks = [blocks[0]] + [
        lax.ppermute(blocks[k], "bead", [(i, i ^ k) for i in range(nb)]) for k in range(1, nb)
    ]
    step = jnp.asarray(propagator(beads, lb))
    xv, *stepped = call(
        functools.partial(steps_kernel, nb, group, lb, mols, slots),
        [shape(group, 6 * beads, slots)] + store(width, beads),
        [],
        b,
        *blocks,
        step,
        q_wide,
    )
    ys = call(
        functools.partial(final_kernel, nb, group, lb, mols, slots),
        [shape(2 * group * 3 * lb, slots)] * nb,
        [pltpu.VMEM((group * beads * 8, slots), F32), keep],
        b,
        perm,
        q_wide,
        xv,
        *stepped,
    )
    ys = [ys[0]] + [
        lax.ppermute(ys[k], "bead", [(i, i ^ k) for i in range(nb)]) for k in range(1, nb)
    ]
    new_x, new_p = call(
        functools.partial(unpack_kernel, nb, group, lb, cells),
        [shape(lb * 3 * cells, slots)] * 2,
        [],
        b,
        *ys,
    )
    return new_x.reshape(positions.shape), new_p.reshape(positions.shape)


def solution(mesh):
    spec = P("bead", None, "space", None)
    return jax.shard_map(
        functools.partial(local, mesh.shape["bead"], mesh.shape["space"]),
        mesh=mesh,
        in_specs=(spec, spec, P("space", None, None)),
        out_specs=(spec, spec),
        check_vma=False,
    )
```

```python
import functools

import jax
import jax.numpy as jnp
import ml_dtypes
import numpy as np
from jax import lax
from jax.experimental import pallas as pl
from jax.experimental.pallas import tpu as pltpu
from jax.sharding import PartitionSpec as P

charge_oxygen = -0.8476
charge_hydrogen = 0.4238
coulomb_scale = 24.0
coulomb_soft = 0.004
well_depth = 0.02
sigma_square = 0.0841
lennard_soft = 0.04
bond_stiffness = 20000.0
bond_square = 0.0081
angle_stiffness = 5000.0
angle_square = 0.0204
cycle_frequency = 60.0
outer_step = 0.02
inner_step = 0.01
oxygen_mass = 16.0

REACH = 1
X_HALO = 2 * REACH
P_HALO = REACH

F32 = jnp.float32
BF16 = jnp.bfloat16


def rounded(a):
    return a.astype(BF16).astype(F32)


def split3(a):
    high = rounded(a)
    rest = a - high
    mid = rounded(rest)
    return high, mid, rest - mid


def two_part(a):
    high = rounded(a)
    return high + rounded(a - high)


def dot_nn(a, b):
    return lax.dot_general(a, b, (((1,), (0,)), ((), ())), preferred_element_type=F32)


def dot_nt(a, b):
    return lax.dot_general(a, b, (((1,), (1,)), ((), ())), preferred_element_type=F32)


def propagator(beads):
    j = np.arange(beads)
    angles = 2.0 * np.pi * ((j[:, None] * j[None, :]) % beads) / beads
    half = beads // 2
    col = j[None, :]
    u = np.where(
        col == 0,
        np.sqrt(1.0 / beads),
        np.where(
            col < half,
            np.sqrt(2.0 / beads) * np.cos(angles),
            np.where(
                col == half,
                np.sqrt(1.0 / beads) * np.cos(angles),
                np.sqrt(2.0 / beads) * np.sin(angles),
            ),
        ),
    )
    w = 2.0 * cycle_frequency * np.sin(np.pi * j / beads)
    cosines = np.cos(w * inner_step)
    spring = w * np.sin(w * inner_step)
    drift = np.where(j == 0, inner_step, np.sin(w * inner_step) / np.where(j == 0, 1.0, w))
    def circulant(values):
        return (u * values) @ u.T

    a = circulant(cosines)
    whole = np.block([[a, circulant(drift)], [-circulant(spring), a]])
    high = whole.astype(ml_dtypes.bfloat16)
    rest = whole - high.astype(np.float64)
    mid = rest.astype(ml_dtypes.bfloat16)
    low = (rest - mid.astype(np.float64)).astype(ml_dtypes.bfloat16)
    return np.concatenate([high, high, mid, mid, high, low], axis=1)


def lane_tables(lanes, mols, slots):
    lane = lax.broadcasted_iota(jnp.int32, lanes.shape, 1)
    unit = jnp.where(lane < mols, charge_oxygen / charge_hydrogen, 1.0)
    return jnp.where(lanes < slots, unit, 0.0)


def permuted(rows, perm):
    n = rows.shape[0]
    stacked = jnp.concatenate(split3(rows), axis=0).astype(BF16)
    moved = dot_nn(stacked, perm)
    return moved[:n] + moved[n : 2 * n] + moved[2 * n :]


def unpermuted(rows, perm):
    n = rows.shape[0]
    stacked = jnp.concatenate(split3(rows), axis=0).astype(BF16)
    moved = dot_nt(stacked, perm)
    return moved[:n] + moved[n : 2 * n] + moved[2 * n :]


def order_kernel(lb, cells, mols, slots, mol_hbm, x_hbm, p_hbm, *refs):
    xo, po, perm_ref, q_ref, to_right, to_left = refs[:6]
    mol_ref, x_ref, p_ref, wide, held_ref, sems = refs[6:]
    copies = [
        pltpu.make_async_copy(source, dest, sems.at[i])
        for i, (source, dest) in enumerate(
            ((mol_hbm, mol_ref), (x_hbm, x_ref), (p_hbm, p_ref))
        )
    ]
    for copy in copies:
        copy.start()
    row = lax.broadcasted_iota(jnp.int32, (slots, slots), 0)
    col = lax.broadcasted_iota(jnp.int32, (slots, slots), 1)
    upper = (row < col).astype(F32).astype(BF16)
    row = row.astype(F32)
    lane = lax.broadcasted_iota(jnp.int32, (cells, slots), 1)
    far = 4.0 * slots
    wide[...] = jnp.full(wide.shape, slots, jnp.int32)
    copies[0].wait()
    for t in range(3):
        wide[t, :, :mols] = mol_ref[t]
    lanes = jnp.where(
        lane < mols,
        wide[0],
        jnp.where(lane < 2 * mols, pltpu.roll(wide[1], mols, 1), pltpu.roll(wide[2], 2 * mols, 1)),
    )
    lanes = jnp.where(lane < 3 * mols, lanes, slots)
    charges = lane_tables(lanes, mols, slots)
    q_ref[...] = charges
    free = lanes >= slots
    key = jnp.where(
        free, far + dot_nn(free.astype(F32).astype(BF16), upper), lanes.astype(F32)
    )
    ones = jnp.ones((16, slots), BF16)
    for cell in range(cells):
        held = (row == key[cell : cell + 1]).astype(F32).astype(BF16)
        held_ref[cell : cell + 1, :] = dot_nt(ones, held)[0:1]
    used = held_ref[...]
    rank = dot_nn((1.0 - used).astype(BF16), upper)
    slot_key = jnp.where(used > 0.5, lane.astype(F32), far + rank)
    copies[1].wait()
    copies[2].wait()
    n = 3 * lb
    for cell in range(cells):
        slot_column = jnp.broadcast_to(slot_key[cell : cell + 1], (slots, slots)).T
        perm = (slot_column == key[cell : cell + 1]).astype(F32).astype(BF16)
        perm_ref[cell] = perm
        rows = [
            ref[pl.ds(comp * cells + cell, lb, stride=3 * cells), :]
            for ref in (x_ref, p_ref)
            for comp in range(3)
        ]
        moved = permuted(jnp.concatenate(rows, axis=0), perm)
        xo[cell] = moved[:n]
        po[cell] = moved[n:]
    for out, xs, ps in (
        (to_right, (cells - 2, cells - 1), cells - 1),
        (to_left, (0, 1), 0),
    ):
        out[9 * lb :, :] = jnp.zeros((8, slots), F32)
        for e, cell in enumerate(xs):
            out[pl.ds(e * n, n), :] = xo[cell]
            out[pl.ds(9 * lb + e, 1), :] = charges[cell : cell + 1]
        out[pl.ds(2 * n, n), :] = po[ps]


def put_tiles(scratch, first, count, rows):
    for index, value in rows:
        scratch[pl.ds(first * 8 + index, count, stride=8), :] = value


OFFSETS = (-1.0, 0.0, 1.0)


def build_tiles(tiles, first, count, x, y, z):
    x, y, z = two_part(x - 0.5), two_part(y - 0.5), two_part(z - 0.5)
    norm = x * x + y * y + z * z + 0.5 * coulomb_soft
    high = two_part(norm)
    low = norm - high
    put_tiles(
        tiles, first, count, ((0, x), (1, y), (2, z), (3, high), (4, low), (5, high), (6, low))
    )


def store_shapes(count, beads, slots):
    n = count * beads
    return (
        [((n * 8, slots), F32), ((n // 2, slots, 64), BF16)]
        + [((n // 2, 32, slots), BF16)] * 3
        + [((n, 32, slots), BF16)]
    )


STORE = 6


class Store:
    def __init__(self, refs, beads):
        self.tiles, self.peers, *sums, self.targets = refs
        self.sums = sums
        self.beads = beads


def tile_of(ref, n):
    return ref[pl.ds(pl.multiple_of(n * 8, 8), 8), :]


def prepare(store, charges, count, slots):
    tiles, beads = store.tiles, store.beads
    row8 = lax.broadcasted_iota(jnp.int32, (8, slots), 0)
    place, norms = row8 < 3, row8 < 5
    target_rows = place | (row8 == 5) | (row8 == 6)
    ones_low = jnp.where((row8 == 3) | (row8 == 4), 1.0, 0.0)
    ones_high = jnp.where((row8 == 5) | (row8 == 6), 1.0, 0.0)
    ones_last = jnp.where(row8 == 7, 1.0, 0.0)
    pairs = beads // 2
    total = count * pairs
    unroll = max(n for n in range(1, 17) if total % n == 0)

    def stack(values):
        return jnp.concatenate(values, axis=0).astype(BF16)

    def step(index, carry):
        for u in range(unroll):
            m = index * unroll + u
            charge = charges[lax.div(m, pairs)]
            units = [
                jnp.where(row8 == 3, charge, jnp.where(row8 == 4, offset * charge, 0.0))
                for offset in OFFSETS
            ]
            left, high_rows, mid_rows = [], [], []
            for h in range(2):
                value = tile_of(tiles, 2 * m + h)
                high = rounded(value)
                mid = value - high
                x_high, x_mid = high[0:1], mid[0:1]
                left_high = jnp.where(place, -2.0 * high, jnp.where(norms, high, ones_high))
                left_mid = jnp.where(place, -2.0 * mid, jnp.where(norms, mid, 0.0))
                left_last = jnp.where(
                    place,
                    -2.0 * mid,
                    jnp.where(
                        row8 == 3,
                        2.0 * x_high,
                        jnp.where(row8 == 4, 2.0 * x_mid, ones_last - 2.0 * ones_high),
                    ),
                )
                left += [left_high, left_high, left_mid, left_last]
                right_high = jnp.where(target_rows, high, ones_low)
                right_mid = jnp.where(target_rows, mid, 0.0)
                right_last = jnp.where(
                    place,
                    mid,
                    jnp.where(
                        row8 == 5, x_high, jnp.where(row8 == 6, x_mid, ones_low + ones_last)
                    ),
                )
                store.targets[2 * m + h] = stack([right_high, right_mid, right_high, right_last])
                high_rows.append(high * charge)
                mid_rows.append(jnp.where(place, mid * charge, 0.0))
            store.peers[m] = stack(left).T
            for o in range(3):
                rows = []
                for h in range(2):
                    rows += [jnp.where(place, high_rows[h], units[o]), mid_rows[h]]
                store.sums[o][m] = stack(rows)
        return carry

    lax.fori_loop(0, total // unroll, step, 0)


class PairLoop:
    def __init__(self, mols, slots, beads, keep):
        self.mols, self.slots, self.keep = mols, slots, keep
        self.pairs = beads // 2
        self.unroll = min(self.pairs, 4)
        self.per_cell = self.pairs // self.unroll
        orows = -(-mols // 8) * 8
        self.row8 = lax.broadcasted_iota(jnp.int32, (8, slots), 0)
        lj_row = lax.broadcasted_iota(jnp.int32, (orows, slots), 0)
        lj_lane = lax.broadcasted_iota(jnp.int32, (orows, slots), 1)
        self.first_lanes, self.second_lanes = lj_lane < mols, lj_lane < 2 * mols
        self.corner = (lj_row < mols) & self.first_lanes

        i = lax.broadcasted_iota(jnp.int32, (slots, slots), 0)
        j = lax.broadcasted_iota(jnp.int32, (slots, slots), 1)
        i = jnp.where(i >= 2 * mols, i - 2 * mols, jnp.where(i >= mols, i - mols, i))
        j = jnp.where(j >= 2 * mols, j - 2 * mols, jnp.where(j >= mols, j - mols, j))
        keep[...] = (i != j).astype(F32)

        lane64 = lax.broadcasted_iota(jnp.int32, (slots, 64), 1) & 31
        odd = (lane64 >= 27) & (lane64 < 31)
        even = lane64 == 31
        self.signs = [
            jnp.where(odd, offset, jnp.where(even, offset * offset, 1.0)).astype(BF16)
            for offset in OFFSETS
        ]
        self.zero = jnp.zeros((32, slots), BF16)

    def pair(self, peers, charge):
        mols, slots = self.mols, self.slots
        orows = self.corner.shape[0]
        pair_scale = coulomb_scale * charge_hydrogen * charge_hydrogen
        k3 = sigma_square**3
        ratio = (charge_hydrogen / charge_oxygen) ** 2 / pair_scale
        lj_a = 24.0 * well_depth * 2.0 * k3 * k3 * ratio
        lj_b = 24.0 * well_depth * k3 * ratio
        zero = self.zero
        own, m = peers[1]
        left = jnp.concatenate(
            [store.peers[index] * sign for (store, index), sign in zip(peers, self.signs)], axis=0
        )
        right = jnp.concatenate(
            [
                jnp.concatenate([own.targets[2 * m], zero], axis=1),
                jnp.concatenate([zero, own.targets[2 * m + 1]], axis=1),
            ],
            axis=0,
        )
        squares = dot_nn(left, right)
        blocks = [[], [], []]
        for h in range(2):
            lanes = slice(h * slots, (h + 1) * slots)
            near = [squares[o * slots : o * slots + orows, lanes] for o in range(3)]
            packed = jnp.where(
                self.first_lanes,
                near[0],
                jnp.where(
                    self.second_lanes,
                    pltpu.roll(near[1], mols, 1),
                    pltpu.roll(near[2], 2 * mols, 1),
                ),
            )
            root = lax.rsqrt(packed + (lennard_soft - coulomb_soft))
            inverse = root * root
            cube = inverse * inverse * inverse
            lj = (cube * lj_a - lj_b) * (cube * inverse)
            for o in range(3):
                root = lax.rsqrt(squares[o * slots : (o + 1) * slots, lanes])
                strength = root * root * root
                part = pltpu.roll(lj, slots - o * mols, 1) if o else lj
                strength = jnp.concatenate(
                    [strength[:orows] + jnp.where(self.corner, part, 0.0), strength[orows:]],
                    axis=0,
                )
                if o == 1:
                    strength = strength * self.keep[...]
                high = strength.astype(BF16)
                low = (strength - high.astype(F32)).astype(BF16)
                blocks[o].append(jnp.concatenate([high, low], axis=0))
        sums = None
        for o, (store, index) in enumerate(peers):
            weights = store.sums[o][index]
            value = dot_nn(
                jnp.concatenate([weights, weights], axis=1), jnp.concatenate(blocks[o], axis=1)
            )
            sums = value if sums is None else sums + value
        scale = charge * pair_scale
        out = []
        for h in range(2):
            part = sums[16 * h : 16 * h + 16, h * slots : (h + 1) * slots]
            total = part[0:8] + part[8:16]
            total = total + jnp.where(self.row8 == 0, total[4:5], 0.0)
            out.append((tile_of(own.tiles, 2 * m + h) * total[3:4] - total) * scale)
        return out

    def cells(self, store, charges, first, last, forces):
        total = (last - first) * self.pairs
        unroll = max(n for n in range(1, 65) if total % n == 0)

        def step(index, carry):
            for u in range(unroll):
                m = index * unroll + u
                at = m + first * self.pairs
                peers = [(store, at + (o - 1) * self.pairs) for o in range(3)]
                out = self.pair(peers, charges[lax.div(at, self.pairs)])
                for h in range(2):
                    n = 2 * m + h
                    forces[pl.ds(pl.multiple_of(n * 8, 8), 8), :] = out[h]
            return carry

        lax.fori_loop(0, total // unroll, step, 0)


def read_force(forces, w, beads, comp):
    return forces[pl.ds(w * beads * 8 + comp, beads, stride=8), :]


def own_kernel(cells, lb, slots, x_ref, q_ref, *refs):
    store = Store(refs, lb)
    for w in range(cells):
        rows = x_ref[w]
        build_tiles(store.tiles, w * lb, lb, rows[:lb], rows[lb : 2 * lb], rows[2 * lb :])
    prepare(store, Rows(q_ref, 0), cells, slots)


def interior_kernel(cells, lb, mols, slots, q_ref, *refs):
    store = Store(refs[:STORE], lb)
    forces, keep = refs[STORE:]
    PairLoop(mols, slots, lb, keep).cells(store, Rows(q_ref, 0), 1, cells - 1, forces)


def edge_kernel(nb, group, lb, cells, mols, slots, *refs):
    x_ref, p_ref, q_ref, left, right, inner = refs[:6]
    own = Store(refs[6 : 6 + STORE], lb)
    refs = refs[6 + STORE :]
    out, q_out, kicked, halo_forces, keep = refs[:5]
    halo = Store(refs[5:], lb)
    n = 3 * lb
    count = cells + 2 * X_HALO

    charge_rows = [left[pl.ds(9 * lb + e, 1), :] for e in range(2)]
    charge_rows += [q_ref[c : c + 1, :] for c in range(cells)]
    charge_rows += [right[pl.ds(9 * lb + e, 1), :] for e in range(2)]
    q_out[...] = jnp.zeros(q_out.shape, F32)
    for w in range(count):
        q_out[w : w + 1, :] = charge_rows[w]
    for e in range(4):
        edge = (left, right)[e // 2]
        rows = edge[pl.ds((e % 2) * n, n), :]
        build_tiles(halo.tiles, e * lb, lb, rows[:lb], rows[lb : 2 * lb], rows[2 * lb :])

    class Edges:
        def __getitem__(self, e):
            return q_out[pl.ds(jnp.where(e < 2, e, e + cells), 1), :]

    prepare(halo, Edges(), 4, slots)
    loop = PairLoop(mols, slots, lb, keep)

    def place(w):
        if w < X_HALO:
            return halo, w
        if w >= cells + X_HALO:
            return halo, w - cells
        return own, w - X_HALO

    targets = (1, 2, cells + 1, cells + 2)

    def edge_step(step, carry):
        for e, w in enumerate(targets):
            for u in range(loop.unroll):
                index = step * loop.unroll + u
                peers = [
                    (store, cell * loop.pairs + index) for store, cell in map(place, (w - 1, w, w + 1))
                ]
                out = loop.pair(peers, charge_rows[w])
                for h in range(2):
                    at = (e * lb + 2 * index + h) * 8
                    halo_forces[pl.ds(pl.multiple_of(at, 8), 8), :] = out[h]
        return carry

    lax.fori_loop(0, loop.per_cell, edge_step, 0)
    half = 0.5 * outer_step
    for w in range(1, count - 1):
        if w < X_HALO:
            old = left[pl.ds(2 * n, n), :]
        elif w >= cells + X_HALO:
            old = right[pl.ds(2 * n, n), :]
        else:
            old = p_ref[w - X_HALO]
        source, cell = (
            (halo_forces, targets.index(w)) if w in targets else (inner, w - X_HALO - 1)
        )
        force = jnp.concatenate([read_force(source, cell, lb, c) for c in range(3)], axis=0)
        kicked[w - 1] = old + half * force
    width = group + 2 * P_HALO
    for k in range(nb):
        first = k * group
        for w in range(width):
            out[k, pl.ds((width + w) * n, n), :] = kicked[first + w]
            source = first + w - P_HALO
            if source < 0:
                inside = left[pl.ds(n, n), :]
            elif source >= cells:
                inside = right[pl.ds(0, n), :]
            else:
                inside = x_ref[source]
            out[k, pl.ds(w * n, n), :] = inside


class Rows:
    def __init__(self, ref, first):
        self.ref, self.first = ref, first

    def __getitem__(self, index):
        return self.ref[pl.ds(self.first + index, 1), :]


def bond_forces(x, y, z, used, mols, slots):
    def partner(a, t):
        return pltpu.roll(a, slots - t * mols, 1)

    first = [a - partner(a, 1) for a in (x, y, z)]
    second = [a - partner(a, 2) for a in (x, y, z)]
    third = [s - f for f, s in zip(first, second)]

    def pull(bond, stiffness, square):
        length = bond[0] * bond[0] + bond[1] * bond[1] + bond[2] * bond[2]
        return (stiffness * used) * (length - square)

    c1 = pull(first, bond_stiffness, bond_square)
    c2 = pull(second, bond_stiffness, bond_square)
    c3 = pull(third, angle_stiffness, angle_square)
    out = []
    for f, s, t in zip(first, second, third):
        on_first = c1 * f - c3 * t
        on_second = c2 * s + c3 * t
        on_oxygen = -(c1 * f + c2 * s)
        out.append(
            on_oxygen + pltpu.roll(on_first, mols, 1) + pltpu.roll(on_second, 2 * mols, 1)
        )
    return out


def steps_kernel(nb, group, lb, mols, slots, b_ref, *refs):
    blocks, step_ref, q_ref, xv = refs[:4]
    beads = nb * lb
    store = Store(refs[4:], beads)
    width = group + 2 * P_HALO
    n = 3 * lb
    b = b_ref[0]
    step = step_ref[...]
    charges = Rows(q_ref, b * group + P_HALO)

    def advance(pos, vel):
        out_x, out_v = [], []
        for x, v in zip(pos, vel):
            high, mid, low = split3(jnp.concatenate([x, v], axis=0))
            stacked = jnp.concatenate([high, mid, high, mid, low, high], axis=0).astype(BF16)
            new = dot_nn(step, stacked)
            out_x.append(new[:beads])
            out_v.append(new[beads:])
        return out_x, out_v

    for w in range(width):
        def gather(a, comp):
            return jnp.concatenate(
                [blocks[k, pl.ds((a * width + w) * n + comp * lb, lb), :] for k in range(nb)],
                axis=0,
            )

        q = charges[w]
        oxygen = (q < -1.5).astype(F32)
        inverse = jnp.where(q < -1.5, 1.0 / oxygen_mass, 1.0)
        pos = [gather(0, c) for c in range(3)]
        vel = [gather(1, c) * inverse for c in range(3)]
        half = (0.5 * inner_step) * inverse
        full = inner_step * inverse
        force = bond_forces(*pos, oxygen, mols, slots)
        vel = [v + half * f for v, f in zip(vel, force)]
        pos, vel = advance(pos, vel)
        force = bond_forces(*pos, oxygen, mols, slots)
        vel = [v + full * f for v, f in zip(vel, force)]
        pos, vel = advance(pos, vel)
        if 1 <= w <= width - 2:
            force = bond_forces(*pos, oxygen, mols, slots)
            vel = [v + half * f for v, f in zip(vel, force)]
            mass = jnp.where(q < -1.5, oxygen_mass, 1.0)
            for c in range(3):
                xv[w - 1, pl.ds(c * beads, beads), :] = pos[c]
                xv[w - 1, pl.ds((3 + c) * beads, beads), :] = vel[c] * mass
        build_tiles(store.tiles, w * beads, beads, *pos)

    prepare(store, charges, width, slots)


def final_kernel(nb, group, lb, mols, slots, b_ref, *refs):
    perm_ref, q_ref, xv = refs[:3]
    beads = nb * lb
    store = Store(refs[3 : 3 + STORE], beads)
    ys, forces, keep = refs[3 + STORE :]
    b = b_ref[0]
    charges = Rows(q_ref, b * group + P_HALO)
    PairLoop(mols, slots, beads, keep).cells(store, charges, P_HALO, P_HALO + group, forces)
    for w in range(group):
        old = xv[w]
        m = 3 * beads
        force = jnp.concatenate([read_force(forces, w, beads, c) for c in range(3)], axis=0)
        state = jnp.concatenate([old[:m], old[m:] + (0.5 * outer_step) * force], axis=0)
        state = unpermuted(state, perm_ref[b * group + w])
        for a in range(2):
            for c in range(3):
                for k in range(nb):
                    row = (a * 3 + c) * beads + k * lb
                    ys[k, pl.ds(((a * group + w) * 3 + c) * lb, lb), :] = state[row : row + lb]


def unpack_kernel(nb, group, lb, cells, ys, *outs):
    for k in range(nb):
        for a in range(2):
            for w in range(group):
                for c in range(3):
                    outs[a][pl.ds(c * cells + k * group + w, lb, stride=3 * cells), :] = ys[
                        k, pl.ds(((a * group + w) * 3 + c) * lb, lb), :
                    ]


def call(kernel, outs, scratch, scalar, *operands, space=pltpu.VMEM):
    vmem = pl.BlockSpec(memory_space=pltpu.VMEM)
    smem = pl.BlockSpec(memory_space=pltpu.SMEM)
    return pl.pallas_call(
        kernel,
        out_shape=outs,
        in_specs=([] if scalar is None else [smem]) + [pl.BlockSpec(memory_space=space)] * len(operands),
        out_specs=[vmem] * len(outs),
        scratch_shapes=scratch,
        compiler_params=pltpu.CompilerParams(vmem_limit_bytes=24 * 1024 * 1024),
    )(*(() if scalar is None else (scalar,)), *operands)


def local(nb, ns, positions, momenta, molecules):
    lb, _, cells, slots = positions.shape
    mols = molecules.shape[1]
    group = cells // nb
    beads = lb * nb
    width = group + 2 * P_HALO
    b = lax.axis_index("bead").astype(jnp.int32).reshape(1)

    def shape(*dims):
        return jax.ShapeDtypeStruct(dims, F32)

    edge = shape(9 * lb + 8, slots)
    rows = lb * 3 * cells
    xs, ps, perm, charges, to_right, to_left = call(
        functools.partial(order_kernel, lb, cells, mols, slots),
        [shape(cells, 3 * lb, slots)] * 2
        + [jax.ShapeDtypeStruct((cells, slots, slots), BF16), shape(cells, slots), edge, edge],
        [
            pltpu.VMEM((3, cells, mols), jnp.int32),
            pltpu.VMEM((rows, slots), F32),
            pltpu.VMEM((rows, slots), F32),
            pltpu.VMEM((3, cells, slots), jnp.int32),
            pltpu.VMEM((cells, slots), F32),
            pltpu.SemaphoreType.DMA((3,)),
        ],
        None,
        *(
            pltpu.with_memory_space_constraint(a, pltpu.HBM)
            for a in (
                jnp.transpose(molecules, (2, 0, 1)),
                positions.reshape(rows, slots),
                momenta.reshape(rows, slots),
            )
        ),
        space=pltpu.HBM,
    )
    left = lax.ppermute(to_right, "space", [(s, (s + 1) % ns) for s in range(ns)])
    right = lax.ppermute(to_left, "space", [(s, (s - 1) % ns) for s in range(ns)])
    q_rows = -(-(cells + 2 * X_HALO) // 8) * 8

    def store(count, store_beads):
        return [
            jax.ShapeDtypeStruct(*entry) for entry in store_shapes(count, store_beads, slots)
        ]

    keep = pltpu.VMEM((slots, slots), F32)
    own = call(
        functools.partial(own_kernel, cells, lb, slots), store(cells, lb), [], None, xs, charges
    )
    (inner,) = call(
        functools.partial(interior_kernel, cells, lb, mols, slots),
        [shape((cells - 2) * lb * 8, slots)],
        [keep],
        None,
        charges,
        *own,
    )
    blocks, q_wide = call(
        functools.partial(edge_kernel, nb, group, lb, cells, mols, slots),
        [shape(nb, 2 * width * 3 * lb, slots), shape(q_rows, slots)],
        [
            pltpu.VMEM((cells + 2 * P_HALO, 3 * lb, slots), F32),
            pltpu.VMEM((4 * lb * 8, slots), F32),
            keep,
        ]
        + [pltpu.VMEM(*entry) for entry in store_shapes(4, lb, slots)],
        None,
        xs,
        ps,
        charges,
        left,
        right,
        inner,
        *own,
    )
    blocks = lax.all_to_all(blocks, "bead", split_axis=0, concat_axis=0, tiled=True)
    step = jnp.asarray(propagator(beads))
    xv, *stepped = call(
        functools.partial(steps_kernel, nb, group, lb, mols, slots),
        [shape(group, 6 * beads, slots)] + store(width, beads),
        [],
        b,
        blocks,
        step,
        q_wide,
    )
    (ys,) = call(
        functools.partial(final_kernel, nb, group, lb, mols, slots),
        [shape(nb, 2 * group * 3 * lb, slots)],
        [pltpu.VMEM((group * beads * 8, slots), F32), keep],
        b,
        perm,
        q_wide,
        xv,
        *stepped,
    )
    ys = lax.all_to_all(ys, "bead", split_axis=0, concat_axis=0, tiled=True)
    new_x, new_p = call(
        functools.partial(unpack_kernel, nb, group, lb, cells),
        [shape(lb * 3 * cells, slots)] * 2,
        [],
        None,
        ys,
    )
    return new_x.reshape(positions.shape), new_p.reshape(positions.shape)


def solution(mesh):
    spec = P("bead", None, "space", None)
    return jax.shard_map(
        functools.partial(local, mesh.shape["bead"], mesh.shape["space"]),
        mesh=mesh,
        in_specs=(spec, spec, P("space", None, None)),
        out_specs=(spec, spec),
        check_vma=False,
    )
```

```python
import functools

import jax
import jax.numpy as jnp
import ml_dtypes
import numpy as np
from jax import lax
from jax.experimental import pallas as pl
from jax.experimental.pallas import tpu as pltpu
from jax.sharding import PartitionSpec as P

charge_oxygen = -0.8476
charge_hydrogen = 0.4238
coulomb_scale = 24.0
coulomb_soft = 0.004
well_depth = 0.02
sigma_square = 0.0841
lennard_soft = 0.04
bond_stiffness = 20000.0
bond_square = 0.0081
angle_stiffness = 5000.0
angle_square = 0.0204
cycle_frequency = 60.0
outer_step = 0.02
inner_step = 0.01
oxygen_mass = 16.0

REACH = 1
X_HALO = 2 * REACH
P_HALO = REACH

F32 = jnp.float32
BF16 = jnp.bfloat16


def rounded(a):
    return a.astype(BF16).astype(F32)


def split3(a):
    high = rounded(a)
    rest = a - high
    mid = rounded(rest)
    return high, mid, rest - mid


def two_part(a):
    high = rounded(a)
    return high + rounded(a - high)


def dot_nn(a, b):
    return lax.dot_general(a, b, (((1,), (0,)), ((), ())), preferred_element_type=F32)


def dot_nt(a, b):
    return lax.dot_general(a, b, (((1,), (1,)), ((), ())), preferred_element_type=F32)


def propagator(beads, beads_dev):
    j = np.arange(beads)
    angles = 2.0 * np.pi * ((j[:, None] * j[None, :]) % beads) / beads
    half = beads // 2
    col = j[None, :]
    u = np.where(
        col == 0,
        np.sqrt(1.0 / beads),
        np.where(
            col < half,
            np.sqrt(2.0 / beads) * np.cos(angles),
            np.where(
                col == half,
                np.sqrt(1.0 / beads) * np.cos(angles),
                np.sqrt(2.0 / beads) * np.sin(angles),
            ),
        ),
    )
    w = 2.0 * cycle_frequency * np.sin(np.pi * j / beads)
    cosines = np.cos(w * inner_step)
    spring = w * np.sin(w * inner_step)
    drift = np.where(j == 0, inner_step, np.sin(w * inner_step) / np.where(j == 0, 1.0, w))
    def circulant(values, bead):
        first = ((u * values) @ u.T)[:, 0]
        return first[(bead[:, None] - bead[None, :]) % beads]

    out = []
    for b in range(beads // beads_dev):
        bead = ((j // beads_dev) ^ b) * beads_dev + j % beads_dev
        a = circulant(cosines, bead)
        whole = np.block([[a, circulant(drift, bead)], [-circulant(spring, bead), a]])
        high = whole.astype(ml_dtypes.bfloat16)
        rest = whole - high.astype(np.float64)
        mid = rest.astype(ml_dtypes.bfloat16)
        low = (rest - mid.astype(np.float64)).astype(ml_dtypes.bfloat16)
        out.append(np.concatenate([high, high, mid, mid, high, low], axis=1))
    return np.stack(out)


def lane_tables(lanes, mols, slots):
    lane = lax.broadcasted_iota(jnp.int32, lanes.shape, 1)
    unit = jnp.where(lane < mols, charge_oxygen / charge_hydrogen, 1.0)
    return jnp.where(lanes < slots, unit, 0.0)


def permuted(rows, perm):
    n = rows.shape[0]
    stacked = jnp.concatenate(split3(rows), axis=0).astype(BF16)
    moved = dot_nn(stacked, perm)
    return moved[:n] + moved[n : 2 * n] + moved[2 * n :]


def unpermuted(rows, perm):
    n = rows.shape[0]
    stacked = jnp.concatenate(split3(rows), axis=0).astype(BF16)
    moved = dot_nt(stacked, perm)
    return moved[:n] + moved[n : 2 * n] + moved[2 * n :]


def order_kernel(lb, cells, mols, slots, mol_hbm, x_hbm, p_hbm, *refs):
    xo, po, perm_ref, q_ref, to_right, to_left = refs[:6]
    mol_ref, x_ref, p_ref, wide, held_ref, sems = refs[6:]
    copies = [
        pltpu.make_async_copy(source, dest, sems.at[i])
        for i, (source, dest) in enumerate(
            ((mol_hbm, mol_ref), (x_hbm, x_ref), (p_hbm, p_ref))
        )
    ]
    for copy in copies:
        copy.start()
    row = lax.broadcasted_iota(jnp.int32, (slots, slots), 0)
    col = lax.broadcasted_iota(jnp.int32, (slots, slots), 1)
    upper = (row < col).astype(F32).astype(BF16)
    row = row.astype(F32)
    lane = lax.broadcasted_iota(jnp.int32, (cells, slots), 1)
    far = 4.0 * slots
    wide[...] = jnp.full(wide.shape, slots, jnp.int32)
    copies[0].wait()
    for t in range(3):
        wide[t, :, :mols] = mol_ref[t]
    lanes = jnp.where(
        lane < mols,
        wide[0],
        jnp.where(lane < 2 * mols, pltpu.roll(wide[1], mols, 1), pltpu.roll(wide[2], 2 * mols, 1)),
    )
    lanes = jnp.where(lane < 3 * mols, lanes, slots)
    charges = lane_tables(lanes, mols, slots)
    q_ref[...] = charges
    free = lanes >= slots
    key = jnp.where(
        free, far + dot_nn(free.astype(F32).astype(BF16), upper), lanes.astype(F32)
    )
    ones = jnp.ones((16, slots), BF16)
    for cell in range(cells):
        held = (row == key[cell : cell + 1]).astype(F32).astype(BF16)
        held_ref[cell : cell + 1, :] = dot_nt(ones, held)[0:1]
    used = held_ref[...]
    rank = dot_nn((1.0 - used).astype(BF16), upper)
    slot_key = jnp.where(used > 0.5, lane.astype(F32), far + rank)
    copies[1].wait()
    copies[2].wait()
    n = 3 * lb
    for cell in range(cells):
        slot_column = jnp.broadcast_to(slot_key[cell : cell + 1], (slots, slots)).T
        perm = (slot_column == key[cell : cell + 1]).astype(F32).astype(BF16)
        perm_ref[cell] = perm
        rows = [
            ref[pl.ds(comp * cells + cell, lb, stride=3 * cells), :]
            for ref in (x_ref, p_ref)
            for comp in range(3)
        ]
        moved = permuted(jnp.concatenate(rows, axis=0), perm)
        xo[cell] = moved[:n]
        po[cell] = moved[n:]
    for out, xs, ps in (
        (to_right, (cells - 2, cells - 1), cells - 1),
        (to_left, (0, 1), 0),
    ):
        out[9 * lb :, :] = jnp.zeros((8, slots), F32)
        for e, cell in enumerate(xs):
            out[pl.ds(e * n, n), :] = xo[cell]
            out[pl.ds(9 * lb + e, 1), :] = charges[cell : cell + 1]
        out[pl.ds(2 * n, n), :] = po[ps]


def put_tiles(scratch, first, count, rows):
    for index, value in rows:
        scratch[pl.ds(first * 8 + index, count, stride=8), :] = value


OFFSETS = (-1.0, 0.0, 1.0)


def build_tiles(tiles, first, count, x, y, z):
    x, y, z = two_part(x - 0.5), two_part(y - 0.5), two_part(z - 0.5)
    norm = x * x + y * y + z * z + 0.5 * coulomb_soft
    high = two_part(norm)
    low = norm - high
    put_tiles(
        tiles, first, count, ((0, x), (1, y), (2, z), (3, high), (4, low), (5, high), (6, low))
    )


def store_shapes(count, beads, slots):
    n = count * beads
    return (
        [((n * 8, slots), F32), ((n // 2, slots, 64), BF16)]
        + [((n // 2, 32, slots), BF16)] * 3
        + [((n, 32, slots), BF16)]
    )


STORE = 6


class Store:
    def __init__(self, refs, beads):
        self.tiles, self.peers, *sums, self.targets = refs
        self.sums = sums
        self.beads = beads


def tile_of(ref, n):
    return ref[pl.ds(pl.multiple_of(n * 8, 8), 8), :]


def prepare(store, charges, count, slots):
    tiles, beads = store.tiles, store.beads
    row8 = lax.broadcasted_iota(jnp.int32, (8, slots), 0)
    place, norms = row8 < 3, row8 < 5
    target_rows = place | (row8 == 5) | (row8 == 6)
    ones_low = jnp.where((row8 == 3) | (row8 == 4), 1.0, 0.0)
    ones_high = jnp.where((row8 == 5) | (row8 == 6), 1.0, 0.0)
    ones_last = jnp.where(row8 == 7, 1.0, 0.0)
    pairs = beads // 2
    total = count * pairs
    unroll = max(n for n in range(1, max(2, min(17, total // 4 + 1))) if total % n == 0)

    def stack(values):
        return jnp.concatenate(values, axis=0).astype(BF16)

    def step(index, carry):
        for u in range(unroll):
            m = index * unroll + u
            charge = charges[lax.div(m, pairs)]
            units = [
                jnp.where(row8 == 3, charge, jnp.where(row8 == 4, offset * charge, 0.0))
                for offset in OFFSETS
            ]
            left, high_rows, mid_rows = [], [], []
            for h in range(2):
                value = tile_of(tiles, 2 * m + h)
                high = rounded(value)
                mid = value - high
                x_high, x_mid = high[0:1], mid[0:1]
                left_high = jnp.where(place, -2.0 * high, jnp.where(norms, high, ones_high))
                left_mid = jnp.where(place, -2.0 * mid, jnp.where(norms, mid, 0.0))
                left_last = jnp.where(
                    place,
                    -2.0 * mid,
                    jnp.where(
                        row8 == 3,
                        2.0 * x_high,
                        jnp.where(row8 == 4, 2.0 * x_mid, ones_last - 2.0 * ones_high),
                    ),
                )
                left += [left_high, left_high, left_mid, left_last]
                right_high = jnp.where(target_rows, high, ones_low)
                right_mid = jnp.where(target_rows, mid, 0.0)
                right_last = jnp.where(
                    place,
                    mid,
                    jnp.where(
                        row8 == 5, x_high, jnp.where(row8 == 6, x_mid, ones_low + ones_last)
                    ),
                )
                store.targets[2 * m + h] = stack([right_high, right_mid, right_high, right_last])
                high_rows.append(high * charge)
                mid_rows.append(jnp.where(place, mid * charge, 0.0))
            store.peers[m] = stack(left).T
            for o in range(3):
                rows = []
                for h in range(2):
                    rows += [jnp.where(place, high_rows[h], units[o]), mid_rows[h]]
                store.sums[o][m] = stack(rows)
        return carry

    lax.fori_loop(0, total // unroll, step, 0)


class PairLoop:
    def __init__(self, mols, slots, beads, keep):
        self.mols, self.slots, self.keep = mols, slots, keep
        self.pairs = beads // 2
        self.unroll = min(self.pairs, 4)
        self.per_cell = self.pairs // self.unroll
        orows = -(-mols // 8) * 8
        self.row8 = lax.broadcasted_iota(jnp.int32, (8, slots), 0)
        lj_row = lax.broadcasted_iota(jnp.int32, (orows, slots), 0)
        lj_lane = lax.broadcasted_iota(jnp.int32, (orows, slots), 1)
        self.first_lanes, self.second_lanes = lj_lane < mols, lj_lane < 2 * mols
        self.corner = (lj_row < mols) & self.first_lanes

        i = lax.broadcasted_iota(jnp.int32, (slots, slots), 0)
        j = lax.broadcasted_iota(jnp.int32, (slots, slots), 1)
        i = jnp.where(i >= 2 * mols, i - 2 * mols, jnp.where(i >= mols, i - mols, i))
        j = jnp.where(j >= 2 * mols, j - 2 * mols, jnp.where(j >= mols, j - mols, j))
        keep[...] = (i != j).astype(F32)

        lane64 = lax.broadcasted_iota(jnp.int32, (slots, 64), 1) & 31
        odd = (lane64 >= 27) & (lane64 < 31)
        even = lane64 == 31
        self.signs = [
            jnp.where(odd, offset, jnp.where(even, offset * offset, 1.0)).astype(BF16)
            for offset in OFFSETS
        ]
        self.zero = jnp.zeros((32, slots), BF16)

    def pair(self, peers, charge):
        mols, slots = self.mols, self.slots
        orows = self.corner.shape[0]
        pair_scale = coulomb_scale * charge_hydrogen * charge_hydrogen
        k3 = sigma_square**3
        ratio = (charge_hydrogen / charge_oxygen) ** 2 / pair_scale
        lj_a = 24.0 * well_depth * 2.0 * k3 * k3 * ratio
        lj_b = 24.0 * well_depth * k3 * ratio
        zero = self.zero
        own, m = peers[1]
        left = jnp.concatenate(
            [store.peers[index] * sign for (store, index), sign in zip(peers, self.signs)], axis=0
        )
        right = jnp.concatenate(
            [
                jnp.concatenate([own.targets[2 * m], zero], axis=1),
                jnp.concatenate([zero, own.targets[2 * m + 1]], axis=1),
            ],
            axis=0,
        )
        squares = dot_nn(left, right)
        blocks = [[], [], []]
        for h in range(2):
            lanes = slice(h * slots, (h + 1) * slots)
            near = [squares[o * slots : o * slots + orows, lanes] for o in range(3)]
            packed = jnp.where(
                self.first_lanes,
                near[0],
                jnp.where(
                    self.second_lanes,
                    pltpu.roll(near[1], mols, 1),
                    pltpu.roll(near[2], 2 * mols, 1),
                ),
            )
            root = lax.rsqrt(packed + (lennard_soft - coulomb_soft))
            inverse = root * root
            cube = inverse * inverse * inverse
            lj = (cube * lj_a - lj_b) * (cube * inverse)
            for o in range(3):
                root = lax.rsqrt(squares[o * slots : (o + 1) * slots, lanes])
                strength = root * root * root
                part = pltpu.roll(lj, slots - o * mols, 1) if o else lj
                strength = jnp.concatenate(
                    [strength[:orows] + jnp.where(self.corner, part, 0.0), strength[orows:]],
                    axis=0,
                )
                if o == 1:
                    strength = strength * self.keep[...]
                high = strength.astype(BF16)
                low = (strength - high.astype(F32)).astype(BF16)
                blocks[o].append(jnp.concatenate([high, low], axis=0))
        sums = None
        for o, (store, index) in enumerate(peers):
            weights = store.sums[o][index]
            value = dot_nn(
                jnp.concatenate([weights, weights], axis=1), jnp.concatenate(blocks[o], axis=1)
            )
            sums = value if sums is None else sums + value
        scale = charge * pair_scale
        out = []
        for h in range(2):
            part = sums[16 * h : 16 * h + 16, h * slots : (h + 1) * slots]
            total = part[0:8] + part[8:16]
            total = total + jnp.where(self.row8 == 0, total[4:5], 0.0)
            out.append((tile_of(own.tiles, 2 * m + h) * total[3:4] - total) * scale)
        return out

    def cells(self, store, charges, first, last, forces, limit):
        total = (last - first) * self.pairs
        unroll = max(n for n in range(1, limit + 1) if total % n == 0)

        def step(index, carry):
            for u in range(unroll):
                m = index * unroll + u
                at = m + first * self.pairs
                peers = [(store, at + (o - 1) * self.pairs) for o in range(3)]
                out = self.pair(peers, charges[lax.div(at, self.pairs)])
                for h in range(2):
                    n = 2 * m + h
                    forces[pl.ds(pl.multiple_of(n * 8, 8), 8), :] = out[h]
            return carry

        lax.fori_loop(0, total // unroll, step, 0)


def read_force(forces, w, beads, comp):
    return forces[pl.ds(w * beads * 8 + comp, beads, stride=8), :]


def own_kernel(cells, lb, slots, x_ref, q_ref, *refs):
    store = Store(refs, lb)
    for w in range(cells):
        rows = x_ref[w]
        build_tiles(store.tiles, w * lb, lb, rows[:lb], rows[lb : 2 * lb], rows[2 * lb :])
    prepare(store, Rows(q_ref, 0), cells, slots)


def interior_kernel(cells, lb, mols, slots, q_ref, *refs):
    store = Store(refs[:STORE], lb)
    forces, keep = refs[STORE:]
    PairLoop(mols, slots, lb, keep).cells(store, Rows(q_ref, 0), 1, cells - 1, forces, 64)


def edge_kernel(nb, group, lb, cells, mols, slots, b_ref, *refs):
    x_ref, p_ref, q_ref, left, right, inner = refs[:6]
    own = Store(refs[6 : 6 + STORE], lb)
    refs = refs[6 + STORE :]
    outs, q_out = refs[:nb], refs[nb]
    kicked, halo_forces, keep = refs[nb + 1 : nb + 4]
    halo = Store(refs[nb + 4 :], lb)
    n = 3 * lb
    count = cells + 2 * X_HALO
    b = b_ref[0]

    charge_rows = [left[pl.ds(9 * lb + e, 1), :] for e in range(2)]
    charge_rows += [q_ref[c : c + 1, :] for c in range(cells)]
    charge_rows += [right[pl.ds(9 * lb + e, 1), :] for e in range(2)]
    q_out[...] = jnp.zeros(q_out.shape, F32)
    for w in range(count):
        q_out[w : w + 1, :] = charge_rows[w]
    for e in range(4):
        edge = (left, right)[e // 2]
        rows = edge[pl.ds((e % 2) * n, n), :]
        build_tiles(halo.tiles, e * lb, lb, rows[:lb], rows[lb : 2 * lb], rows[2 * lb :])

    class Edges:
        def __getitem__(self, e):
            return q_out[pl.ds(jnp.where(e < 2, e, e + cells), 1), :]

    prepare(halo, Edges(), 4, slots)
    loop = PairLoop(mols, slots, lb, keep)

    def place(w):
        if w < X_HALO:
            return halo, w
        if w >= cells + X_HALO:
            return halo, w - cells
        return own, w - X_HALO

    targets = (1, 2, cells + 1, cells + 2)

    def edge_step(step, carry):
        for e, w in enumerate(targets):
            for u in range(loop.unroll):
                index = step * loop.unroll + u
                peers = [
                    (store, cell * loop.pairs + index) for store, cell in map(place, (w - 1, w, w + 1))
                ]
                out = loop.pair(peers, charge_rows[w])
                for h in range(2):
                    at = (e * lb + 2 * index + h) * 8
                    halo_forces[pl.ds(pl.multiple_of(at, 8), 8), :] = out[h]
        return carry

    lax.fori_loop(0, loop.per_cell, edge_step, 0)
    half = 0.5 * outer_step
    for w in range(1, count - 1):
        if w < X_HALO:
            old = left[pl.ds(2 * n, n), :]
        elif w >= cells + X_HALO:
            old = right[pl.ds(2 * n, n), :]
        else:
            old = p_ref[w - X_HALO]
        source, cell = (
            (halo_forces, targets.index(w)) if w in targets else (inner, w - X_HALO - 1)
        )
        force = jnp.concatenate([read_force(source, cell, lb, c) for c in range(3)], axis=0)
        kicked[w - 1] = old + half * force
    width = group + 2 * P_HALO
    for k in range(nb):
        first = jnp.bitwise_xor(b, k) * group
        for w in range(width):
            outs[k][pl.ds((width + w) * n, n), :] = kicked[first + w]
            source = first + w - P_HALO
            inside = x_ref[jnp.clip(source, 0, cells - 1)]
            if w < P_HALO:
                inside = jnp.where(source < 0, left[pl.ds(n, n), :], inside)
            elif w >= group + P_HALO:
                inside = jnp.where(source >= cells, right[pl.ds(0, n), :], inside)
            outs[k][pl.ds(w * n, n), :] = inside


class Rows:
    def __init__(self, ref, first):
        self.ref, self.first = ref, first

    def __getitem__(self, index):
        return self.ref[pl.ds(self.first + index, 1), :]


def bond_forces(x, y, z, used, mols, slots):
    def partner(a, t):
        return pltpu.roll(a, slots - t * mols, 1)

    first = [a - partner(a, 1) for a in (x, y, z)]
    second = [a - partner(a, 2) for a in (x, y, z)]
    third = [s - f for f, s in zip(first, second)]

    def pull(bond, stiffness, square):
        length = bond[0] * bond[0] + bond[1] * bond[1] + bond[2] * bond[2]
        return (stiffness * used) * (length - square)

    c1 = pull(first, bond_stiffness, bond_square)
    c2 = pull(second, bond_stiffness, bond_square)
    c3 = pull(third, angle_stiffness, angle_square)
    out = []
    for f, s, t in zip(first, second, third):
        on_first = c1 * f - c3 * t
        on_second = c2 * s + c3 * t
        on_oxygen = -(c1 * f + c2 * s)
        out.append(
            on_oxygen + pltpu.roll(on_first, mols, 1) + pltpu.roll(on_second, 2 * mols, 1)
        )
    return out


def steps_kernel(nb, group, lb, mols, slots, b_ref, *refs):
    blocks = refs[:nb]
    step_ref, q_ref, xv = refs[nb : nb + 3]
    beads = nb * lb
    store = Store(refs[nb + 3 :], beads)
    width = group + 2 * P_HALO
    n = 3 * lb
    b = b_ref[0]
    step = step_ref[b]
    charges = Rows(q_ref, b * group + P_HALO)

    def advance(states):
        flat = [
            jnp.concatenate([x, v], axis=0) for pos, vel in states for x, v in zip(pos, vel)
        ]
        high, mid, low = split3(jnp.concatenate(flat, axis=1))
        stacked = jnp.concatenate([high, mid, high, mid, low, high], axis=0).astype(BF16)
        new = dot_nn(step, stacked)
        out = []
        for i in range(len(states)):
            columns = [
                new[:, (3 * i + c) * slots : (3 * i + c + 1) * slots] for c in range(3)
            ]
            out.append(([a[:beads] for a in columns], [a[beads:] for a in columns]))
        return out

    def gather(w, a, comp):
        return jnp.concatenate(
            [block[pl.ds((a * width + w) * n + comp * lb, lb), :] for block in blocks], axis=0
        )

    def kick(state, oxygen, scale):
        pos, vel = state
        force = bond_forces(*pos, oxygen, mols, slots)
        return pos, [v + scale * f for v, f in zip(vel, force)]

    for first in range(0, width, 2):
        members = range(first, min(first + 2, width))
        charge = [charges[w] for w in members]
        oxygen = [(q < -1.5).astype(F32) for q in charge]
        inverse = [jnp.where(q < -1.5, 1.0 / oxygen_mass, 1.0) for q in charge]
        states = [
            (
                [gather(w, 0, c) for c in range(3)],
                [gather(w, 1, c) * scale for c in range(3)],
            )
            for w, scale in zip(members, inverse)
        ]
        for part in (0.5, 1.0):
            states = [
                kick(state, o, (part * inner_step) * scale)
                for state, o, scale in zip(states, oxygen, inverse)
            ]
            states = advance(states)
        for w, state, q, o, scale in zip(members, states, charge, oxygen, inverse):
            if 1 <= w <= width - 2:
                pos, vel = kick(state, o, (0.5 * inner_step) * scale)
                mass = jnp.where(q < -1.5, oxygen_mass, 1.0)
                for c in range(3):
                    xv[w - 1, pl.ds(c * beads, beads), :] = pos[c]
                    xv[w - 1, pl.ds((3 + c) * beads, beads), :] = vel[c] * mass
            build_tiles(store.tiles, w * beads, beads, *state[0])
    prepare(store, charges, width, slots)


def final_kernel(nb, group, lb, mols, slots, b_ref, *refs):
    perm_ref, q_ref, xv = refs[:3]
    beads = nb * lb
    store = Store(refs[3 : 3 + STORE], beads)
    ys = refs[3 + STORE : 3 + STORE + nb]
    forces, keep = refs[3 + STORE + nb :]
    b = b_ref[0]
    charges = Rows(q_ref, b * group + P_HALO)
    loop = PairLoop(mols, slots, beads, keep)
    loop.cells(store, charges, P_HALO, P_HALO + group, forces, 32)
    for w in range(group):
        old = xv[w]
        m = 3 * beads
        force = jnp.concatenate([read_force(forces, w, beads, c) for c in range(3)], axis=0)
        state = jnp.concatenate([old[:m], old[m:] + (0.5 * outer_step) * force], axis=0)
        state = unpermuted(state, perm_ref[b * group + w])
        for a in range(2):
            for c in range(3):
                for k in range(nb):
                    row = (a * 3 + c) * beads + k * lb
                    ys[k][pl.ds(((a * group + w) * 3 + c) * lb, lb), :] = state[row : row + lb]


def unpack_kernel(nb, group, lb, cells, b_ref, *refs):
    ys = refs[:nb]
    outs = refs[nb:]
    b = b_ref[0]
    for k in range(nb):
        source = jnp.bitwise_xor(b, k)
        for a in range(2):
            for w in range(group):
                for c in range(3):
                    outs[a][pl.ds(c * cells + source * group + w, lb, stride=3 * cells), :] = ys[
                        k
                    ][pl.ds(((a * group + w) * 3 + c) * lb, lb), :]


def call(kernel, outs, scratch, scalar, *operands, space=pltpu.VMEM):
    vmem = pl.BlockSpec(memory_space=pltpu.VMEM)
    smem = pl.BlockSpec(memory_space=pltpu.SMEM)
    return pl.pallas_call(
        kernel,
        out_shape=outs,
        in_specs=([] if scalar is None else [smem]) + [pl.BlockSpec(memory_space=space)] * len(operands),
        out_specs=[vmem] * len(outs),
        scratch_shapes=scratch,
        compiler_params=pltpu.CompilerParams(vmem_limit_bytes=24 * 1024 * 1024),
    )(*(() if scalar is None else (scalar,)), *operands)


def exchange(blocks, nb):
    out = list(blocks)
    for k in reversed(range(1, nb)):
        out[k] = lax.ppermute(blocks[k], "bead", [(i, i ^ k) for i in range(nb)])
    return out


def local(nb, ns, positions, momenta, molecules):
    lb, _, cells, slots = positions.shape
    mols = molecules.shape[1]
    group = cells // nb
    beads = lb * nb
    width = group + 2 * P_HALO
    b = lax.axis_index("bead").astype(jnp.int32).reshape(1)

    def shape(*dims):
        return jax.ShapeDtypeStruct(dims, F32)

    edge = shape(9 * lb + 8, slots)
    rows = lb * 3 * cells
    xs, ps, perm, charges, to_right, to_left = call(
        functools.partial(order_kernel, lb, cells, mols, slots),
        [shape(cells, 3 * lb, slots)] * 2
        + [jax.ShapeDtypeStruct((cells, slots, slots), BF16), shape(cells, slots), edge, edge],
        [
            pltpu.VMEM((3, cells, mols), jnp.int32),
            pltpu.VMEM((rows, slots), F32),
            pltpu.VMEM((rows, slots), F32),
            pltpu.VMEM((3, cells, slots), jnp.int32),
            pltpu.VMEM((cells, slots), F32),
            pltpu.SemaphoreType.DMA((3,)),
        ],
        None,
        *(
            pltpu.with_memory_space_constraint(a, pltpu.HBM)
            for a in (
                jnp.transpose(molecules, (2, 0, 1)),
                positions.reshape(rows, slots),
                momenta.reshape(rows, slots),
            )
        ),
        space=pltpu.HBM,
    )
    left = lax.ppermute(to_right, "space", [(s, (s + 1) % ns) for s in range(ns)])
    right = lax.ppermute(to_left, "space", [(s, (s - 1) % ns) for s in range(ns)])
    q_rows = -(-(cells + 2 * X_HALO) // 8) * 8

    def store(count, store_beads):
        return [
            jax.ShapeDtypeStruct(*entry) for entry in store_shapes(count, store_beads, slots)
        ]

    keep = pltpu.VMEM((slots, slots), F32)
    own = call(
        functools.partial(own_kernel, cells, lb, slots), store(cells, lb), [], None, xs, charges
    )
    (inner,) = call(
        functools.partial(interior_kernel, cells, lb, mols, slots),
        [shape((cells - 2) * lb * 8, slots)],
        [keep],
        None,
        charges,
        *own,
    )
    *blocks, q_wide = call(
        functools.partial(edge_kernel, nb, group, lb, cells, mols, slots),
        [shape(2 * width * 3 * lb, slots)] * nb + [shape(q_rows, slots)],
        [
            pltpu.VMEM((cells + 2 * P_HALO, 3 * lb, slots), F32),
            pltpu.VMEM((4 * lb * 8, slots), F32),
            keep,
        ]
        + [pltpu.VMEM(*entry) for entry in store_shapes(4, lb, slots)],
        b,
        xs,
        ps,
        charges,
        left,
        right,
        inner,
        *own,
    )
    blocks = exchange(blocks, nb)
    step = jnp.asarray(propagator(beads, lb))
    xv, *stepped = call(
        functools.partial(steps_kernel, nb, group, lb, mols, slots),
        [shape(group, 6 * beads, slots)] + store(width, beads),
        [],
        b,
        *blocks,
        step,
        q_wide,
    )
    ys = call(
        functools.partial(final_kernel, nb, group, lb, mols, slots),
        [shape(2 * group * 3 * lb, slots)] * nb,
        [pltpu.VMEM((group * beads * 8, slots), F32), keep],
        b,
        perm,
        q_wide,
        xv,
        *stepped,
    )
    ys = exchange(ys, nb)
    new_x, new_p = call(
        functools.partial(unpack_kernel, nb, group, lb, cells),
        [shape(lb * 3 * cells, slots)] * 2,
        [],
        b,
        *ys,
    )
    return new_x.reshape(positions.shape), new_p.reshape(positions.shape)


def solution(mesh):
    spec = P("bead", None, "space", None)
    return jax.shard_map(
        functools.partial(local, mesh.shape["bead"], mesh.shape["space"]),
        mesh=mesh,
        in_specs=(spec, spec, P("space", None, None)),
        out_specs=(spec, spec),
        check_vma=False,
    )
```

```python
import functools

import jax
import jax.numpy as jnp
import ml_dtypes
import numpy as np
from jax import lax
from jax.experimental import pallas as pl
from jax.experimental.pallas import tpu as pltpu
from jax.sharding import PartitionSpec as P

charge_oxygen = -0.8476
charge_hydrogen = 0.4238
coulomb_scale = 24.0
coulomb_soft = 0.004
well_depth = 0.02
sigma_square = 0.0841
lennard_soft = 0.04
bond_stiffness = 20000.0
bond_square = 0.0081
angle_stiffness = 5000.0
angle_square = 0.0204
cycle_frequency = 60.0
outer_step = 0.02
inner_step = 0.01
oxygen_mass = 16.0

REACH = 1
X_HALO = 2 * REACH
P_HALO = REACH

F32 = jnp.float32
BF16 = jnp.bfloat16


def rounded(a):
    return a.astype(BF16).astype(F32)


def split3(a):
    high = rounded(a)
    rest = a - high
    mid = rounded(rest)
    return high, mid, rest - mid


def two_part(a):
    high = rounded(a)
    return high + rounded(a - high)


def dot_nn(a, b):
    return lax.dot_general(a, b, (((1,), (0,)), ((), ())), preferred_element_type=F32)


def dot_nt(a, b):
    return lax.dot_general(a, b, (((1,), (1,)), ((), ())), preferred_element_type=F32)


def propagator(beads, beads_dev):
    j = np.arange(beads)
    angles = 2.0 * np.pi * ((j[:, None] * j[None, :]) % beads) / beads
    half = beads // 2
    col = j[None, :]
    u = np.where(
        col == 0,
        np.sqrt(1.0 / beads),
        np.where(
            col < half,
            np.sqrt(2.0 / beads) * np.cos(angles),
            np.where(
                col == half,
                np.sqrt(1.0 / beads) * np.cos(angles),
                np.sqrt(2.0 / beads) * np.sin(angles),
            ),
        ),
    )
    w = 2.0 * cycle_frequency * np.sin(np.pi * j / beads)
    cosines = np.cos(w * inner_step)
    spring = w * np.sin(w * inner_step)
    drift = np.where(j == 0, inner_step, np.sin(w * inner_step) / np.where(j == 0, 1.0, w))
    def circulant(values, bead):
        first = ((u * values) @ u.T)[:, 0]
        return first[(bead[:, None] - bead[None, :]) % beads]

    out = []
    for b in range(beads // beads_dev):
        bead = ((j // beads_dev) ^ b) * beads_dev + j % beads_dev
        a = circulant(cosines, bead)
        whole = np.block([[a, circulant(drift, bead)], [-circulant(spring, bead), a]])
        high = whole.astype(ml_dtypes.bfloat16)
        rest = whole - high.astype(np.float64)
        mid = rest.astype(ml_dtypes.bfloat16)
        low = (rest - mid.astype(np.float64)).astype(ml_dtypes.bfloat16)
        out.append(np.concatenate([high, high, mid, mid, high, low], axis=1))
    return np.stack(out)


def lane_tables(lanes, mols, slots):
    lane = lax.broadcasted_iota(jnp.int32, lanes.shape, 1)
    unit = jnp.where(lane < mols, charge_oxygen / charge_hydrogen, 1.0)
    return jnp.where(lanes < slots, unit, 0.0)


def permuted(rows, perm):
    n = rows.shape[0]
    stacked = jnp.concatenate(split3(rows), axis=0).astype(BF16)
    moved = dot_nn(stacked, perm)
    return moved[:n] + moved[n : 2 * n] + moved[2 * n :]


def unpermuted(rows, perm):
    n = rows.shape[0]
    stacked = jnp.concatenate(split3(rows), axis=0).astype(BF16)
    moved = dot_nt(stacked, perm)
    return moved[:n] + moved[n : 2 * n] + moved[2 * n :]


def order_kernel(lb, cells, mols, slots, mol_hbm, x_hbm, p_hbm, *refs):
    xo, po, perm_ref, q_ref, to_right, to_left = refs[:6]
    mol_ref, x_ref, p_ref, wide, held_ref, sems = refs[6:]
    copies = [
        pltpu.make_async_copy(source, dest, sems.at[i])
        for i, (source, dest) in enumerate(
            ((mol_hbm, mol_ref), (x_hbm, x_ref), (p_hbm, p_ref))
        )
    ]
    for copy in copies:
        copy.start()
    row = lax.broadcasted_iota(jnp.int32, (slots, slots), 0)
    col = lax.broadcasted_iota(jnp.int32, (slots, slots), 1)
    upper = (row < col).astype(F32).astype(BF16)
    row = row.astype(F32)
    lane = lax.broadcasted_iota(jnp.int32, (cells, slots), 1)
    far = 4.0 * slots
    wide[...] = jnp.full(wide.shape, slots, jnp.int32)
    copies[0].wait()
    for t in range(3):
        wide[t, :, :mols] = mol_ref[t]
    lanes = jnp.where(
        lane < mols,
        wide[0],
        jnp.where(lane < 2 * mols, pltpu.roll(wide[1], mols, 1), pltpu.roll(wide[2], 2 * mols, 1)),
    )
    lanes = jnp.where(lane < 3 * mols, lanes, slots)
    charges = lane_tables(lanes, mols, slots)
    q_ref[...] = charges
    free = lanes >= slots
    key = jnp.where(
        free, far + dot_nn(free.astype(F32).astype(BF16), upper), lanes.astype(F32)
    )
    ones = jnp.ones((16, slots), BF16)
    for cell in range(cells):
        held = (row == key[cell : cell + 1]).astype(F32).astype(BF16)
        held_ref[cell : cell + 1, :] = dot_nt(ones, held)[0:1]
    used = held_ref[...]
    rank = dot_nn((1.0 - used).astype(BF16), upper)
    slot_key = jnp.where(used > 0.5, lane.astype(F32), far + rank)
    copies[1].wait()
    copies[2].wait()
    n = 3 * lb
    for cell in range(cells):
        slot_column = jnp.broadcast_to(slot_key[cell : cell + 1], (slots, slots)).T
        perm = (slot_column == key[cell : cell + 1]).astype(F32).astype(BF16)
        perm_ref[cell] = perm
        rows = [
            ref[pl.ds(comp * cells + cell, lb, stride=3 * cells), :]
            for ref in (x_ref, p_ref)
            for comp in range(3)
        ]
        moved = permuted(jnp.concatenate(rows, axis=0), perm)
        xo[cell] = moved[:n]
        po[cell] = moved[n:]
    for out, xs, ps in (
        (to_right, (cells - 2, cells - 1), cells - 1),
        (to_left, (0, 1), 0),
    ):
        out[9 * lb :, :] = jnp.zeros((8, slots), F32)
        for e, cell in enumerate(xs):
            out[pl.ds(e * n, n), :] = xo[cell]
            out[pl.ds(9 * lb + e, 1), :] = charges[cell : cell + 1]
        out[pl.ds(2 * n, n), :] = po[ps]


def put_tiles(scratch, first, count, rows):
    for index, value in rows:
        scratch[pl.ds(first * 8 + index, count, stride=8), :] = value


OFFSETS = (-1.0, 0.0, 1.0)


def build_tiles(tiles, first, count, x, y, z):
    x, y, z = two_part(x - 0.5), two_part(y - 0.5), two_part(z - 0.5)
    norm = x * x + y * y + z * z + 0.5 * coulomb_soft
    high = two_part(norm)
    low = norm - high
    put_tiles(
        tiles, first, count, ((0, x), (1, y), (2, z), (3, high), (4, low), (5, high), (6, low))
    )


def store_shapes(count, beads, slots):
    n = count * beads
    return (
        [((n * 8, slots), F32), ((n // 2, slots, 64), BF16)]
        + [((n // 2, 32, slots), BF16)] * 3
        + [((n, 32, slots), BF16)]
    )


STORE = 6


class Store:
    def __init__(self, refs, beads):
        self.tiles, self.peers, *sums, self.targets = refs
        self.sums = sums
        self.beads = beads


def tile_of(ref, n):
    return ref[pl.ds(pl.multiple_of(n * 8, 8), 8), :]


def prepare(store, charges, count, slots):
    tiles, beads = store.tiles, store.beads
    row8 = lax.broadcasted_iota(jnp.int32, (8, slots), 0)
    place, norms = row8 < 3, row8 < 5
    target_rows = place | (row8 == 5) | (row8 == 6)
    ones_low = jnp.where((row8 == 3) | (row8 == 4), 1.0, 0.0)
    ones_high = jnp.where((row8 == 5) | (row8 == 6), 1.0, 0.0)
    ones_last = jnp.where(row8 == 7, 1.0, 0.0)
    pairs = beads // 2
    total = count * pairs
    unroll = max(n for n in range(1, max(2, min(17, total // 4 + 1))) if total % n == 0)

    def stack(values):
        return jnp.concatenate(values, axis=0).astype(BF16)

    def step(index, carry):
        for u in range(unroll):
            m = index * unroll + u
            charge = charges[lax.div(m, pairs)]
            units = [
                jnp.where(row8 == 3, charge, jnp.where(row8 == 4, offset * charge, 0.0))
                for offset in OFFSETS
            ]
            left, high_rows, mid_rows = [], [], []
            for h in range(2):
                value = tile_of(tiles, 2 * m + h)
                high = rounded(value)
                mid = value - high
                x_high, x_mid = high[0:1], mid[0:1]
                left_high = jnp.where(place, -2.0 * high, jnp.where(norms, high, ones_high))
                left_mid = jnp.where(place, -2.0 * mid, jnp.where(norms, mid, 0.0))
                left_last = jnp.where(
                    place,
                    -2.0 * mid,
                    jnp.where(
                        row8 == 3,
                        2.0 * x_high,
                        jnp.where(row8 == 4, 2.0 * x_mid, ones_last - 2.0 * ones_high),
                    ),
                )
                left += [left_high, left_high, left_mid, left_last]
                right_high = jnp.where(target_rows, high, ones_low)
                right_mid = jnp.where(target_rows, mid, 0.0)
                right_last = jnp.where(
                    place,
                    mid,
                    jnp.where(
                        row8 == 5, x_high, jnp.where(row8 == 6, x_mid, ones_low + ones_last)
                    ),
                )
                store.targets[2 * m + h] = stack([right_high, right_mid, right_high, right_last])
                high_rows.append(high * charge)
                mid_rows.append(jnp.where(place, mid * charge, 0.0))
            store.peers[m] = stack(left).T
            for o in range(3):
                rows = []
                for h in range(2):
                    rows += [jnp.where(place, high_rows[h], units[o]), mid_rows[h]]
                store.sums[o][m] = stack(rows)
        return carry

    lax.fori_loop(0, total // unroll, step, 0)


class PairLoop:
    def __init__(self, mols, slots, beads, keep):
        self.mols, self.slots, self.keep = mols, slots, keep
        self.scale = coulomb_scale * charge_hydrogen * charge_hydrogen
        self.pairs = beads // 2
        orows = -(-mols // 8) * 8
        self.row8 = lax.broadcasted_iota(jnp.int32, (8, slots), 0)
        lj_row = lax.broadcasted_iota(jnp.int32, (orows, slots), 0)
        lj_lane = lax.broadcasted_iota(jnp.int32, (orows, slots), 1)
        self.first_lanes = lj_lane < mols
        self.corner = (lj_row < mols) & self.first_lanes

        i = lax.broadcasted_iota(jnp.int32, (slots, slots), 0)
        j = lax.broadcasted_iota(jnp.int32, (slots, slots), 1)
        i = jnp.where(i >= 2 * mols, i - 2 * mols, jnp.where(i >= mols, i - mols, i))
        j = jnp.where(j >= 2 * mols, j - 2 * mols, jnp.where(j >= mols, j - mols, j))
        keep[...] = (i != j).astype(F32)

        lane64 = lax.broadcasted_iota(jnp.int32, (slots, 64), 1) & 31
        self.own_terms = (lane64 < 27).astype(F32).astype(BF16)
        self.zero = jnp.zeros((32, slots), BF16)

    def pair(self, own, above, charge, charge_above, alone=True, onto=True, back=True):
        mols, slots = self.mols, self.slots
        orows = self.corner.shape[0]
        k3 = sigma_square**3
        ratio = (charge_hydrogen / charge_oxygen) ** 2 / self.scale
        lj_a = 24.0 * well_depth * 2.0 * k3 * k3 * ratio
        lj_b = 24.0 * well_depth * k3 * ratio
        zero = self.zero
        store, m = own
        left, kinds = [], []
        if alone:
            left.append(store.peers[m] * self.own_terms)
            kinds.append("own")
        if above is not None:
            left.append(above[0].peers[above[1]])
            kinds.append("next")
        right = jnp.concatenate(
            [
                jnp.concatenate([store.targets[2 * m], zero], axis=1),
                jnp.concatenate([zero, store.targets[2 * m + 1]], axis=1),
            ],
            axis=0,
        )
        squares = dot_nn(jnp.concatenate(left, axis=0), right)
        down, across = [], []
        for h in range(2):
            lanes = slice(h * slots, (h + 1) * slots)
            near = [squares[i * slots : i * slots + orows, lanes] for i in range(len(kinds))]
            packed = near[0]
            if len(kinds) == 2:
                packed = jnp.where(self.first_lanes, near[0], pltpu.roll(near[1], mols, 1))
            root = lax.rsqrt(packed + (lennard_soft - coulomb_soft))
            inverse = root * root
            cube = inverse * inverse * inverse
            lj = (cube * lj_a - lj_b) * (cube * inverse)
            rows = []
            for i, kind in enumerate(kinds):
                root = lax.rsqrt(squares[i * slots : (i + 1) * slots, lanes])
                strength = root * root * root
                part = pltpu.roll(lj, slots - mols, 1) if i else lj
                strength = jnp.concatenate(
                    [strength[:orows] + jnp.where(self.corner, part, 0.0), strength[orows:]],
                    axis=0,
                )
                if kind == "own":
                    strength = strength * self.keep[...]
                high = strength.astype(BF16)
                low = (strength - high.astype(F32)).astype(BF16)
                rows += [high, low]
                if kind == "next":
                    across.append(jnp.concatenate([high, low], axis=1))
            down.append(jnp.concatenate(rows, axis=0))

        def assemble(sums, tiles, index, factor):
            out = []
            for h in range(2):
                part = sums[16 * h : 16 * h + 16, h * slots : (h + 1) * slots]
                total = part[0:8] + part[8:16]
                total = total + jnp.where(self.row8 == 0, total[4:5], 0.0)
                tile = tile_of(tiles, 2 * index + h)
                out.append((tile * total[3:4] - total) * (factor * self.scale))
            return out

        on_own = on_above = None
        if onto:
            weights = []
            if alone:
                weights += [store.sums[1][m]] * 2
            if above is not None:
                weights += [above[0].sums[2][above[1]]] * 2
            sums = dot_nn(jnp.concatenate(weights, axis=1), jnp.concatenate(down, axis=1))
            on_own = assemble(sums, store.tiles, m, charge)
        if above is not None and back:
            weights = store.sums[0][m]
            sums = dot_nt(
                jnp.concatenate([weights, weights], axis=1), jnp.concatenate(across, axis=0)
            )
            on_above = assemble(sums, above[0].tiles, above[1], charge_above)
        return on_own, on_above

    def put(self, forces, n, values, more=None):
        for h in range(2):
            value = values[h] if more is None else values[h] + more[h]
            forces[pl.ds(pl.multiple_of((n + h) * 8, 8), 8), :] = value


def read_force(forces, w, beads, comp):
    return forces[pl.ds(w * beads * 8 + comp, beads, stride=8), :]


def own_kernel(cells, lb, slots, x_ref, q_ref, *refs):
    store = Store(refs, lb)
    for w in range(cells):
        rows = x_ref[w]
        build_tiles(store.tiles, w * lb, lb, rows[:lb], rows[lb : 2 * lb], rows[2 * lb :])
    prepare(store, Rows(q_ref, 0), cells, slots)


def interior_kernel(cells, lb, mols, slots, q_ref, *refs):
    store = Store(refs[:STORE], lb)
    forces, keep = refs[STORE:]
    loop = PairLoop(mols, slots, lb, keep)
    charges = Rows(q_ref, 0)
    unroll = min(loop.pairs, 4)

    def step(index, carry):
        for u in range(unroll):
            pair = index * unroll + u
            pending = None
            for w in range(cells):
                at = w * loop.pairs + pair
                above = (store, at + loop.pairs) if w + 1 < cells else None
                on_own, on_above = loop.pair(
                    (store, at), above, charges[w], charges[w + 1] if above else None
                )
                loop.put(forces, 2 * at, on_own, pending)
                pending = on_above
        return carry

    lax.fori_loop(0, loop.pairs // unroll, step, 0)


def edge_kernel(nb, group, lb, cells, mols, slots, b_ref, *refs):
    x_ref, p_ref, q_ref, left, right, inner = refs[:6]
    own = Store(refs[6 : 6 + STORE], lb)
    refs = refs[6 + STORE :]
    outs, q_out = refs[:nb], refs[nb]
    kicked, halo_forces, keep = refs[nb + 1 : nb + 4]
    halo = Store(refs[nb + 4 :], lb)
    n = 3 * lb
    count = cells + 2 * X_HALO
    b = b_ref[0]

    charge_rows = [left[pl.ds(9 * lb + e, 1), :] for e in range(2)]
    charge_rows += [q_ref[c : c + 1, :] for c in range(cells)]
    charge_rows += [right[pl.ds(9 * lb + e, 1), :] for e in range(2)]
    q_out[...] = jnp.zeros(q_out.shape, F32)
    for w in range(count):
        q_out[w : w + 1, :] = charge_rows[w]
    for e in range(4):
        edge = (left, right)[e // 2]
        rows = edge[pl.ds((e % 2) * n, n), :]
        build_tiles(halo.tiles, e * lb, lb, rows[:lb], rows[lb : 2 * lb], rows[2 * lb :])

    class Edges:
        def __getitem__(self, e):
            return q_out[pl.ds(jnp.where(e < 2, e, e + cells), 1), :]

    prepare(halo, Edges(), 4, slots)
    loop = PairLoop(mols, slots, lb, keep)

    unroll = min(loop.pairs, 4)

    def edge_step(index, carry):
        for u in range(unroll):
            pair = index * unroll + u

            def at(cell):
                return cell * loop.pairs + pair

            def partial(cell):
                return [tile_of(inner, 2 * at(cell) + h) for h in range(2)]

            rows = charge_rows
            _, below = loop.pair(
                (halo, at(0)), (halo, at(1)), rows[0], rows[1], alone=False, onto=False
            )
            on_own, on_above = loop.pair((halo, at(1)), (own, at(0)), rows[1], rows[2])
            loop.put(halo_forces, 2 * at(0), on_own, below)
            loop.put(halo_forces, 2 * at(1), on_above, partial(0))
            on_own, below = loop.pair(
                (own, at(cells - 1)), (halo, at(2)), rows[cells + 1], rows[cells + 2], alone=False
            )
            loop.put(halo_forces, 2 * at(2), on_own, partial(cells - 1))
            on_own, _ = loop.pair(
                (halo, at(2)), (halo, at(3)), rows[cells + 2], rows[cells + 3], back=False
            )
            loop.put(halo_forces, 2 * at(3), on_own, below)
        return carry

    lax.fori_loop(0, loop.pairs // unroll, edge_step, 0)
    targets = (1, 2, cells + 1, cells + 2)
    half = 0.5 * outer_step
    for w in range(1, count - 1):
        if w < X_HALO:
            old = left[pl.ds(2 * n, n), :]
        elif w >= cells + X_HALO:
            old = right[pl.ds(2 * n, n), :]
        else:
            old = p_ref[w - X_HALO]
        source, cell = (
            (halo_forces, targets.index(w)) if w in targets else (inner, w - X_HALO)
        )
        force = jnp.concatenate([read_force(source, cell, lb, c) for c in range(3)], axis=0)
        kicked[w - 1] = old + half * force
    width = group + 2 * P_HALO
    for k in range(nb):
        first = jnp.bitwise_xor(b, k) * group
        for w in range(width):
            outs[k][pl.ds((width + w) * n, n), :] = kicked[first + w]
            source = first + w - P_HALO
            inside = x_ref[jnp.clip(source, 0, cells - 1)]
            if w < P_HALO:
                inside = jnp.where(source < 0, left[pl.ds(n, n), :], inside)
            elif w >= group + P_HALO:
                inside = jnp.where(source >= cells, right[pl.ds(0, n), :], inside)
            outs[k][pl.ds(w * n, n), :] = inside


class Rows:
    def __init__(self, ref, first):
        self.ref, self.first = ref, first

    def __getitem__(self, index):
        return self.ref[pl.ds(self.first + index, 1), :]


def bond_forces(x, y, z, used, mols, slots):
    def partner(a, t):
        return pltpu.roll(a, slots - t * mols, 1)

    first = [a - partner(a, 1) for a in (x, y, z)]
    second = [a - partner(a, 2) for a in (x, y, z)]
    third = [s - f for f, s in zip(first, second)]

    def pull(bond, stiffness, square):
        length = bond[0] * bond[0] + bond[1] * bond[1] + bond[2] * bond[2]
        return (stiffness * used) * (length - square)

    c1 = pull(first, bond_stiffness, bond_square)
    c2 = pull(second, bond_stiffness, bond_square)
    c3 = pull(third, angle_stiffness, angle_square)
    out = []
    for f, s, t in zip(first, second, third):
        on_first = c1 * f - c3 * t
        on_second = c2 * s + c3 * t
        on_oxygen = -(c1 * f + c2 * s)
        out.append(
            on_oxygen + pltpu.roll(on_first, mols, 1) + pltpu.roll(on_second, 2 * mols, 1)
        )
    return out


def steps_kernel(nb, group, lb, mols, slots, b_ref, *refs):
    blocks = refs[:nb]
    step_ref, q_ref, xv = refs[nb : nb + 3]
    beads = nb * lb
    store = Store(refs[nb + 3 :], beads)
    width = group + 2 * P_HALO
    n = 3 * lb
    b = b_ref[0]
    step = step_ref[b]
    charges = Rows(q_ref, b * group + P_HALO)

    def advance(states):
        flat = [
            jnp.concatenate([x, v], axis=0) for pos, vel in states for x, v in zip(pos, vel)
        ]
        high, mid, low = split3(jnp.concatenate(flat, axis=1))
        stacked = jnp.concatenate([high, mid, high, mid, low, high], axis=0).astype(BF16)
        new = dot_nn(step, stacked)
        out = []
        for i in range(len(states)):
            columns = [
                new[:, (3 * i + c) * slots : (3 * i + c + 1) * slots] for c in range(3)
            ]
            out.append(([a[:beads] for a in columns], [a[beads:] for a in columns]))
        return out

    def gather(w, a, comp):
        return jnp.concatenate(
            [block[pl.ds((a * width + w) * n + comp * lb, lb), :] for block in blocks], axis=0
        )

    def kick(state, oxygen, scale):
        pos, vel = state
        force = bond_forces(*pos, oxygen, mols, slots)
        return pos, [v + scale * f for v, f in zip(vel, force)]

    for first in range(0, width, 2):
        members = range(first, min(first + 2, width))
        charge = [charges[w] for w in members]
        oxygen = [(q < -1.5).astype(F32) for q in charge]
        inverse = [jnp.where(q < -1.5, 1.0 / oxygen_mass, 1.0) for q in charge]
        states = [
            (
                [gather(w, 0, c) for c in range(3)],
                [gather(w, 1, c) * scale for c in range(3)],
            )
            for w, scale in zip(members, inverse)
        ]
        for part in (0.5, 1.0):
            states = [
                kick(state, o, (part * inner_step) * scale)
                for state, o, scale in zip(states, oxygen, inverse)
            ]
            states = advance(states)
        for w, state, q, o, scale in zip(members, states, charge, oxygen, inverse):
            if 1 <= w <= width - 2:
                pos, vel = kick(state, o, (0.5 * inner_step) * scale)
                mass = jnp.where(q < -1.5, oxygen_mass, 1.0)
                for c in range(3):
                    xv[w - 1, pl.ds(c * beads, beads), :] = pos[c]
                    xv[w - 1, pl.ds((3 + c) * beads, beads), :] = vel[c] * mass
            build_tiles(store.tiles, w * beads, beads, *state[0])
    prepare(store, charges, width, slots)


def final_kernel(nb, group, lb, mols, slots, b_ref, *refs):
    perm_ref, q_ref, xv = refs[:3]
    beads = nb * lb
    store = Store(refs[3 : 3 + STORE], beads)
    ys = refs[3 + STORE : 3 + STORE + nb]
    forces, keep = refs[3 + STORE + nb :]
    b = b_ref[0]
    charges = Rows(q_ref, b * group + P_HALO)
    loop = PairLoop(mols, slots, beads, keep)
    unroll = max(k for k in range(1, 9) if loop.pairs % k == 0)

    def step(index, carry):
        for u in range(unroll):
            pair = index * unroll + u
            pending = None
            for w in range(group + 1):
                at = w * loop.pairs + pair
                on_own, on_above = loop.pair(
                    (store, at),
                    (store, at + loop.pairs),
                    charges[w],
                    charges[w + 1],
                    alone=w > 0,
                    onto=w > 0,
                    back=w < group,
                )
                if w:
                    loop.put(forces, 2 * (at - loop.pairs), on_own, pending)
                pending = on_above
        return carry

    lax.fori_loop(0, loop.pairs // unroll, step, 0)
    for w in range(group):
        old = xv[w]
        m = 3 * beads
        force = jnp.concatenate([read_force(forces, w, beads, c) for c in range(3)], axis=0)
        state = jnp.concatenate([old[:m], old[m:] + (0.5 * outer_step) * force], axis=0)
        state = unpermuted(state, perm_ref[b * group + w])
        for a in range(2):
            for c in range(3):
                for k in range(nb):
                    row = (a * 3 + c) * beads + k * lb
                    ys[k][pl.ds(((a * group + w) * 3 + c) * lb, lb), :] = state[row : row + lb]


def unpack_kernel(nb, group, lb, cells, b_ref, *refs):
    ys = refs[:nb]
    outs = refs[nb:]
    b = b_ref[0]
    for k in range(nb):
        source = jnp.bitwise_xor(b, k)
        for a in range(2):
            for w in range(group):
                for c in range(3):
                    outs[a][pl.ds(c * cells + source * group + w, lb, stride=3 * cells), :] = ys[
                        k
                    ][pl.ds(((a * group + w) * 3 + c) * lb, lb), :]


def call(kernel, outs, scratch, scalar, *operands, space=pltpu.VMEM):
    vmem = pl.BlockSpec(memory_space=pltpu.VMEM)
    smem = pl.BlockSpec(memory_space=pltpu.SMEM)
    return pl.pallas_call(
        kernel,
        out_shape=outs,
        in_specs=([] if scalar is None else [smem]) + [pl.BlockSpec(memory_space=space)] * len(operands),
        out_specs=[vmem] * len(outs),
        scratch_shapes=scratch,
        compiler_params=pltpu.CompilerParams(vmem_limit_bytes=24 * 1024 * 1024),
    )(*(() if scalar is None else (scalar,)), *operands)


def exchange(blocks, nb):
    out = list(blocks)
    for k in reversed(range(1, nb)):
        out[k] = lax.ppermute(blocks[k], "bead", [(i, i ^ k) for i in range(nb)])
    return out


def local(nb, ns, positions, momenta, molecules):
    lb, _, cells, slots = positions.shape
    mols = molecules.shape[1]
    group = cells // nb
    beads = lb * nb
    width = group + 2 * P_HALO
    b = lax.axis_index("bead").astype(jnp.int32).reshape(1)

    def shape(*dims):
        return jax.ShapeDtypeStruct(dims, F32)

    edge = shape(9 * lb + 8, slots)
    rows = lb * 3 * cells
    xs, ps, perm, charges, to_right, to_left = call(
        functools.partial(order_kernel, lb, cells, mols, slots),
        [shape(cells, 3 * lb, slots)] * 2
        + [jax.ShapeDtypeStruct((cells, slots, slots), BF16), shape(cells, slots), edge, edge],
        [
            pltpu.VMEM((3, cells, mols), jnp.int32),
            pltpu.VMEM((rows, slots), F32),
            pltpu.VMEM((rows, slots), F32),
            pltpu.VMEM((3, cells, slots), jnp.int32),
            pltpu.VMEM((cells, slots), F32),
            pltpu.SemaphoreType.DMA((3,)),
        ],
        None,
        *(
            pltpu.with_memory_space_constraint(a, pltpu.HBM)
            for a in (
                jnp.transpose(molecules, (2, 0, 1)),
                positions.reshape(rows, slots),
                momenta.reshape(rows, slots),
            )
        ),
        space=pltpu.HBM,
    )
    left = lax.ppermute(to_right, "space", [(s, (s + 1) % ns) for s in range(ns)])
    right = lax.ppermute(to_left, "space", [(s, (s - 1) % ns) for s in range(ns)])
    q_rows = -(-(cells + 2 * X_HALO) // 8) * 8

    def store(count, store_beads):
        return [
            jax.ShapeDtypeStruct(*entry) for entry in store_shapes(count, store_beads, slots)
        ]

    keep = pltpu.VMEM((slots, slots), F32)
    own = call(
        functools.partial(own_kernel, cells, lb, slots), store(cells, lb), [], None, xs, charges
    )
    (inner,) = call(
        functools.partial(interior_kernel, cells, lb, mols, slots),
        [shape(cells * lb * 8, slots)],
        [keep],
        None,
        charges,
        *own,
    )
    *blocks, q_wide = call(
        functools.partial(edge_kernel, nb, group, lb, cells, mols, slots),
        [shape(2 * width * 3 * lb, slots)] * nb + [shape(q_rows, slots)],
        [
            pltpu.VMEM((cells + 2 * P_HALO, 3 * lb, slots), F32),
            pltpu.VMEM((4 * lb * 8, slots), F32),
            keep,
        ]
        + [pltpu.VMEM(*entry) for entry in store_shapes(4, lb, slots)],
        b,
        xs,
        ps,
        charges,
        left,
        right,
        inner,
        *own,
    )
    blocks = exchange(blocks, nb)
    step = jnp.asarray(propagator(beads, lb))
    xv, *stepped = call(
        functools.partial(steps_kernel, nb, group, lb, mols, slots),
        [shape(group, 6 * beads, slots)] + store(width, beads),
        [],
        b,
        *blocks,
        step,
        q_wide,
    )
    ys = call(
        functools.partial(final_kernel, nb, group, lb, mols, slots),
        [shape(2 * group * 3 * lb, slots)] * nb,
        [pltpu.VMEM((group * beads * 8, slots), F32), keep],
        b,
        perm,
        q_wide,
        xv,
        *stepped,
    )
    ys = exchange(ys, nb)
    new_x, new_p = call(
        functools.partial(unpack_kernel, nb, group, lb, cells),
        [shape(lb * 3 * cells, slots)] * 2,
        [],
        b,
        *ys,
    )
    return new_x.reshape(positions.shape), new_p.reshape(positions.shape)


def solution(mesh):
    spec = P("bead", None, "space", None)
    return jax.shard_map(
        functools.partial(local, mesh.shape["bead"], mesh.shape["space"]),
        mesh=mesh,
        in_specs=(spec, spec, P("space", None, None)),
        out_specs=(spec, spec),
        check_vma=False,
    )
```

```python
import functools

import jax
import jax.numpy as jnp
import ml_dtypes
import numpy as np
from jax import lax
from jax.experimental import pallas as pl
from jax.experimental.pallas import tpu as pltpu
from jax.sharding import PartitionSpec as P

charge_oxygen = -0.8476
charge_hydrogen = 0.4238
coulomb_scale = 24.0
coulomb_soft = 0.004
well_depth = 0.02
sigma_square = 0.0841
lennard_soft = 0.04
bond_stiffness = 20000.0
bond_square = 0.0081
angle_stiffness = 5000.0
angle_square = 0.0204
cycle_frequency = 60.0
outer_step = 0.02
inner_step = 0.01
oxygen_mass = 16.0

REACH = 1
X_HALO = 2 * REACH
P_HALO = REACH

F32 = jnp.float32
BF16 = jnp.bfloat16


def rounded(a):
    return a.astype(BF16).astype(F32)


def split3(a):
    high = rounded(a)
    rest = a - high
    mid = rounded(rest)
    return high, mid, rest - mid


def two_part(a):
    high = rounded(a)
    return high + rounded(a - high)


def dot_nn(a, b):
    return lax.dot_general(a, b, (((1,), (0,)), ((), ())), preferred_element_type=F32)


def dot_nt(a, b):
    return lax.dot_general(a, b, (((1,), (1,)), ((), ())), preferred_element_type=F32)


def block_order(nb):
    return sorted(range(nb), key=lambda k: (k > 0, -bin(k).count("1"), k))


def propagator(beads, beads_dev):
    j = np.arange(beads)
    angles = 2.0 * np.pi * ((j[:, None] * j[None, :]) % beads) / beads
    half = beads // 2
    col = j[None, :]
    u = np.where(
        col == 0,
        np.sqrt(1.0 / beads),
        np.where(
            col < half,
            np.sqrt(2.0 / beads) * np.cos(angles),
            np.where(
                col == half,
                np.sqrt(1.0 / beads) * np.cos(angles),
                np.sqrt(2.0 / beads) * np.sin(angles),
            ),
        ),
    )
    w = 2.0 * cycle_frequency * np.sin(np.pi * j / beads)
    cosines = np.cos(w * inner_step)
    spring = w * np.sin(w * inner_step)
    drift = np.where(j == 0, inner_step, np.sin(w * inner_step) / np.where(j == 0, 1.0, w))
    def circulant(values, bead):
        first = ((u * values) @ u.T)[:, 0]
        return first[(bead[:, None] - bead[None, :]) % beads]

    out = []
    for b in range(beads // beads_dev):
        block = np.array(block_order(beads // beads_dev))[j // beads_dev]
        bead = (block ^ b) * beads_dev + j % beads_dev
        a = circulant(cosines, bead)
        whole = np.block([[a, circulant(drift, bead)], [-circulant(spring, bead), a]])
        high = whole.astype(ml_dtypes.bfloat16)
        rest = whole - high.astype(np.float64)
        mid = rest.astype(ml_dtypes.bfloat16)
        low = (rest - mid.astype(np.float64)).astype(ml_dtypes.bfloat16)
        out.append(np.concatenate([high, high, mid, mid, high, low], axis=1))
    return np.stack(out)


def lane_tables(lanes, mols, slots):
    lane = lax.broadcasted_iota(jnp.int32, lanes.shape, 1)
    unit = jnp.where(lane < mols, charge_oxygen / charge_hydrogen, 1.0)
    return jnp.where(lanes < slots, unit, 0.0)


def permuted(rows, perm):
    n = rows.shape[0]
    stacked = jnp.concatenate(split3(rows), axis=0).astype(BF16)
    moved = dot_nn(stacked, perm)
    return moved[:n] + moved[n : 2 * n] + moved[2 * n :]


def unpermuted(rows, perm):
    n = rows.shape[0]
    stacked = jnp.concatenate(split3(rows), axis=0).astype(BF16)
    moved = dot_nt(stacked, perm)
    return moved[:n] + moved[n : 2 * n] + moved[2 * n :]


def order_kernel(lb, cells, mols, slots, mol_hbm, x_hbm, p_hbm, *refs):
    xo, po, perm_ref, q_ref, to_right, to_left = refs[:6]
    mol_ref, x_ref, p_ref, wide, sems = refs[6:]
    copies = [
        pltpu.make_async_copy(source, dest, sems.at[i])
        for i, (source, dest) in enumerate(
            ((mol_hbm, mol_ref), (x_hbm, x_ref), (p_hbm, p_ref))
        )
    ]
    for copy in copies:
        copy.start()
    row = lax.broadcasted_iota(jnp.int32, (slots, slots), 0)
    col = lax.broadcasted_iota(jnp.int32, (slots, slots), 1)
    upper = (row < col).astype(F32).astype(BF16)
    rows, row = row, row.astype(F32)
    lane = lax.broadcasted_iota(jnp.int32, (cells, slots), 1)
    far = 4.0 * slots
    wide[...] = jnp.full(wide.shape, slots, jnp.int32)
    copies[0].wait()
    for t in range(3):
        wide[t, :, :mols] = mol_ref[t]
    lanes = jnp.where(
        lane < mols,
        wide[0],
        jnp.where(lane < 2 * mols, pltpu.roll(wide[1], mols, 1), pltpu.roll(wide[2], 2 * mols, 1)),
    )
    lanes = jnp.where(lane < 3 * mols, lanes, slots)
    charges = lane_tables(lanes, mols, slots)
    q_ref[...] = charges
    free = lanes >= slots
    key = jnp.where(
        free, far + dot_nn(free.astype(F32).astype(BF16), upper), lanes.astype(F32)
    )
    ones = jnp.ones((slots, slots), BF16)
    used = jnp.zeros((slots, slots), F32)
    for cell in range(cells):
        held = (row == key[cell : cell + 1]).astype(F32).astype(BF16)
        used = jnp.where(col == cell, dot_nn(held, ones), used)
    rank = dot_nn((col < rows).astype(F32).astype(BF16), (1.0 - used).astype(BF16))
    slot_key = jnp.where(used > 0.5, row, far + rank)
    copies[1].wait()
    copies[2].wait()
    n = 3 * lb
    for cell in range(cells):
        slot_column = jnp.broadcast_to(slot_key[:, cell : cell + 1], (slots, slots))
        perm = (slot_column == key[cell : cell + 1]).astype(F32).astype(BF16)
        perm_ref[cell] = perm
        atoms = [
            ref[pl.ds(comp * cells + cell, lb, stride=3 * cells), :]
            for ref in (x_ref, p_ref)
            for comp in range(3)
        ]
        moved = permuted(jnp.concatenate(atoms, axis=0), perm)
        xo[cell] = moved[:n]
        po[cell] = moved[n:]
    for out, xs, ps in (
        (to_right, (cells - 2, cells - 1), cells - 1),
        (to_left, (0, 1), 0),
    ):
        out[9 * lb :, :] = jnp.zeros((8, slots), F32)
        for e, cell in enumerate(xs):
            out[pl.ds(e * n, n), :] = xo[cell]
            out[pl.ds(9 * lb + e, 1), :] = charges[cell : cell + 1]
        out[pl.ds(2 * n, n), :] = po[ps]


def put_tiles(scratch, first, count, rows):
    for index, value in rows:
        scratch[pl.ds(first * 8 + index, count, stride=8), :] = value


OFFSETS = (-1.0, 0.0, 1.0)


def build_tiles(tiles, first, count, x, y, z):
    x, y, z = two_part(x - 0.5), two_part(y - 0.5), two_part(z - 0.5)
    norm = x * x + y * y + z * z + 0.5 * coulomb_soft
    high = two_part(norm)
    low = norm - high
    put_tiles(
        tiles, first, count, ((0, x), (1, y), (2, z), (3, high), (4, low), (5, high), (6, low))
    )


def store_shapes(count, beads, slots):
    n = count * beads
    return (
        [((n * 8, slots), F32), ((n // 2, slots, 64), BF16)]
        + [((n // 2, 32, slots), BF16)] * 3
        + [((n, 32, slots), BF16)]
    )


STORE = 6


class Store:
    def __init__(self, refs, beads):
        self.tiles, self.peers, *sums, self.targets = refs
        self.sums = sums
        self.beads = beads


def tile_of(ref, n):
    return ref[pl.ds(pl.multiple_of(n * 8, 8), 8), :]


def prepare(store, charges, count, slots):
    tiles, beads = store.tiles, store.beads
    row8 = lax.broadcasted_iota(jnp.int32, (8, slots), 0)
    place, norms = row8 < 3, row8 < 5
    target_rows = place | (row8 == 5) | (row8 == 6)
    ones_low = jnp.where((row8 == 3) | (row8 == 4), 1.0, 0.0)
    ones_high = jnp.where((row8 == 5) | (row8 == 6), 1.0, 0.0)
    ones_last = jnp.where(row8 == 7, 1.0, 0.0)
    pairs = beads // 2
    total = count * pairs
    unroll = max(n for n in range(1, max(2, min(17, total // 4 + 1))) if total % n == 0)

    def stack(values):
        return jnp.concatenate(values, axis=0).astype(BF16)

    def step(index, carry):
        for u in range(unroll):
            m = index * unroll + u
            charge = charges[lax.div(m, pairs)]
            units = [
                jnp.where(row8 == 3, charge, jnp.where(row8 == 4, offset * charge, 0.0))
                for offset in OFFSETS
            ]
            left, high_rows, mid_rows = [], [], []
            for h in range(2):
                value = tile_of(tiles, 2 * m + h)
                high = rounded(value)
                mid = value - high
                x_high, x_mid = high[0:1], mid[0:1]
                left_high = jnp.where(place, -2.0 * high, jnp.where(norms, high, ones_high))
                left_mid = jnp.where(place, -2.0 * mid, jnp.where(norms, mid, 0.0))
                left_last = jnp.where(
                    place,
                    -2.0 * mid,
                    jnp.where(
                        row8 == 3,
                        2.0 * x_high,
                        jnp.where(row8 == 4, 2.0 * x_mid, ones_last - 2.0 * ones_high),
                    ),
                )
                left += [left_high, left_high, left_mid, left_last]
                right_high = jnp.where(target_rows, high, ones_low)
                right_mid = jnp.where(target_rows, mid, 0.0)
                right_last = jnp.where(
                    place,
                    mid,
                    jnp.where(
                        row8 == 5, x_high, jnp.where(row8 == 6, x_mid, ones_low + ones_last)
                    ),
                )
                store.targets[2 * m + h] = stack([right_high, right_mid, right_high, right_last])
                high_rows.append(high * charge)
                mid_rows.append(jnp.where(place, mid * charge, 0.0))
            store.peers[m] = stack(left).T
            for o in range(3):
                rows = []
                for h in range(2):
                    rows += [jnp.where(place, high_rows[h], units[o]), mid_rows[h]]
                store.sums[o][m] = stack(rows)
        return carry

    lax.fori_loop(0, total // unroll, step, 0)


class PairLoop:
    def __init__(self, mols, slots, beads, keep):
        self.mols, self.slots, self.keep = mols, slots, keep
        self.pairs = beads // 2
        self.unroll = min(self.pairs, 4)
        self.per_cell = self.pairs // self.unroll
        orows = -(-mols // 8) * 8
        self.row8 = lax.broadcasted_iota(jnp.int32, (8, slots), 0)
        lj_row = lax.broadcasted_iota(jnp.int32, (orows, slots), 0)
        lj_lane = lax.broadcasted_iota(jnp.int32, (orows, slots), 1)
        self.first_lanes, self.second_lanes = lj_lane < mols, lj_lane < 2 * mols
        self.corner = (lj_row < mols) & self.first_lanes

        i = lax.broadcasted_iota(jnp.int32, (slots, slots), 0)
        j = lax.broadcasted_iota(jnp.int32, (slots, slots), 1)
        i = jnp.where(i >= 2 * mols, i - 2 * mols, jnp.where(i >= mols, i - mols, i))
        j = jnp.where(j >= 2 * mols, j - 2 * mols, jnp.where(j >= mols, j - mols, j))
        keep[...] = (i != j).astype(F32)

        lane64 = lax.broadcasted_iota(jnp.int32, (slots, 64), 1) & 31
        odd = (lane64 >= 27) & (lane64 < 31)
        even = lane64 == 31
        self.signs = [
            jnp.where(odd, -1.0, 1.0).astype(BF16),
            jnp.where(odd | even, 0.0, 1.0).astype(BF16),
            None,
        ]
        self.zero = jnp.zeros((32, slots), BF16)

    def pair(self, peers, charge):
        mols, slots = self.mols, self.slots
        orows = self.corner.shape[0]
        pair_scale = coulomb_scale * charge_hydrogen * charge_hydrogen
        k3 = sigma_square**3
        ratio = (charge_hydrogen / charge_oxygen) ** 2 / pair_scale
        lj_a = 24.0 * well_depth * 2.0 * k3 * k3 * ratio
        lj_b = 24.0 * well_depth * k3 * ratio
        zero = self.zero
        own, m = peers[1]
        left = jnp.concatenate(
            [
                store.peers[index] if sign is None else store.peers[index] * sign
                for (store, index), sign in zip(peers, self.signs)
            ],
            axis=0,
        )
        right = jnp.concatenate(
            [
                jnp.concatenate([own.targets[2 * m], zero], axis=1),
                jnp.concatenate([zero, own.targets[2 * m + 1]], axis=1),
            ],
            axis=0,
        )
        squares = dot_nn(left, right)
        blocks = [[], [], []]
        for h in range(2):
            lanes = slice(h * slots, (h + 1) * slots)
            near = [squares[o * slots : o * slots + orows, lanes] for o in range(3)]
            packed = jnp.where(
                self.first_lanes,
                near[0],
                jnp.where(
                    self.second_lanes,
                    pltpu.roll(near[1], mols, 1),
                    pltpu.roll(near[2], 2 * mols, 1),
                ),
            )
            root = lax.rsqrt(packed + (lennard_soft - coulomb_soft))
            inverse = root * root
            cube = inverse * inverse * inverse
            lj = (cube * lj_a - lj_b) * (cube * inverse)
            for o in range(3):
                root = lax.rsqrt(squares[o * slots : (o + 1) * slots, lanes])
                strength = root * root * root
                part = pltpu.roll(lj, slots - o * mols, 1) if o else lj
                strength = jnp.concatenate(
                    [strength[:orows] + jnp.where(self.corner, part, 0.0), strength[orows:]],
                    axis=0,
                )
                if o == 1:
                    strength = strength * self.keep[...]
                high = strength.astype(BF16)
                low = (strength - high.astype(F32)).astype(BF16)
                blocks[o].append(jnp.concatenate([high, low], axis=0))
        sums = None
        for o, (store, index) in enumerate(peers):
            weights = store.sums[o][index]
            value = dot_nn(
                jnp.concatenate([weights, weights], axis=1), jnp.concatenate(blocks[o], axis=1)
            )
            sums = value if sums is None else sums + value
        scale = charge * pair_scale
        out = []
        for h in range(2):
            part = sums[16 * h : 16 * h + 16, h * slots : (h + 1) * slots]
            total = part[0:8] + part[8:16]
            total = total + jnp.where(self.row8 == 0, total[4:5], 0.0)
            out.append((tile_of(own.tiles, 2 * m + h) * total[3:4] - total) * scale)
        return out

    def cells(self, store, charges, first, last, forces, limit):
        total = (last - first) * self.pairs
        unroll = max(n for n in range(1, limit + 1) if total % n == 0)

        def step(index, carry):
            for u in range(unroll):
                m = index * unroll + u
                at = m + first * self.pairs
                peers = [(store, at + (o - 1) * self.pairs) for o in range(3)]
                out = self.pair(peers, charges[lax.div(at, self.pairs)])
                for h in range(2):
                    n = 2 * m + h
                    forces[pl.ds(pl.multiple_of(n * 8, 8), 8), :] = out[h]
            return carry

        lax.fori_loop(0, total // unroll, step, 0)


def read_force(forces, w, beads, comp):
    return forces[pl.ds(w * beads * 8 + comp, beads, stride=8), :]


def own_kernel(cells, lb, slots, x_ref, q_ref, *refs):
    store = Store(refs, lb)
    for w in range(cells):
        rows = x_ref[w]
        build_tiles(store.tiles, w * lb, lb, rows[:lb], rows[lb : 2 * lb], rows[2 * lb :])
    prepare(store, Rows(q_ref, 0), cells, slots)


def interior_kernel(cells, lb, mols, slots, q_ref, *refs):
    store = Store(refs[:STORE], lb)
    forces, keep = refs[STORE:]
    PairLoop(mols, slots, lb, keep).cells(store, Rows(q_ref, 0), 1, cells - 1, forces, 64)


def edge_kernel(nb, group, lb, cells, mols, slots, b_ref, *refs):
    x_ref, p_ref, q_ref, left, right, inner = refs[:6]
    own = Store(refs[6 : 6 + STORE], lb)
    refs = refs[6 + STORE :]
    outs, q_out = refs[:nb], refs[nb]
    kicked, halo_forces, keep = refs[nb + 1 : nb + 4]
    halo = Store(refs[nb + 4 :], lb)
    n = 3 * lb
    count = cells + 2 * X_HALO
    b = b_ref[0]

    charge_rows = [left[pl.ds(9 * lb + e, 1), :] for e in range(2)]
    charge_rows += [q_ref[c : c + 1, :] for c in range(cells)]
    charge_rows += [right[pl.ds(9 * lb + e, 1), :] for e in range(2)]
    q_out[...] = jnp.zeros(q_out.shape, F32)
    for w in range(count):
        q_out[w : w + 1, :] = charge_rows[w]
    for e in range(4):
        edge = (left, right)[e // 2]
        rows = edge[pl.ds((e % 2) * n, n), :]
        build_tiles(halo.tiles, e * lb, lb, rows[:lb], rows[lb : 2 * lb], rows[2 * lb :])

    class Edges:
        def __getitem__(self, e):
            return q_out[pl.ds(jnp.where(e < 2, e, e + cells), 1), :]

    prepare(halo, Edges(), 4, slots)
    loop = PairLoop(mols, slots, lb, keep)

    def place(w):
        if w < X_HALO:
            return halo, w
        if w >= cells + X_HALO:
            return halo, w - cells
        return own, w - X_HALO

    targets = (1, 2, cells + 1, cells + 2)

    def edge_step(step, carry):
        for e, w in enumerate(targets):
            for u in range(loop.unroll):
                index = step * loop.unroll + u
                peers = [
                    (store, cell * loop.pairs + index) for store, cell in map(place, (w - 1, w, w + 1))
                ]
                out = loop.pair(peers, charge_rows[w])
                for h in range(2):
                    at = (e * lb + 2 * index + h) * 8
                    halo_forces[pl.ds(pl.multiple_of(at, 8), 8), :] = out[h]
        return carry

    lax.fori_loop(0, loop.per_cell, edge_step, 0)
    half = 0.5 * outer_step
    for w in range(1, count - 1):
        if w < X_HALO:
            old = left[pl.ds(2 * n, n), :]
        elif w >= cells + X_HALO:
            old = right[pl.ds(2 * n, n), :]
        else:
            old = p_ref[w - X_HALO]
        source, cell = (
            (halo_forces, targets.index(w)) if w in targets else (inner, w - X_HALO - 1)
        )
        force = jnp.concatenate([read_force(source, cell, lb, c) for c in range(3)], axis=0)
        kicked[w - 1] = old + half * force
    width = group + 2 * P_HALO
    for i, k in enumerate(block_order(nb)):
        first = jnp.bitwise_xor(b, k) * group
        for w in range(width):
            outs[i][pl.ds((width + w) * n, n), :] = kicked[first + w]
            source = first + w - P_HALO
            inside = x_ref[jnp.clip(source, 0, cells - 1)]
            if w < P_HALO:
                inside = jnp.where(source < 0, left[pl.ds(n, n), :], inside)
            elif w >= group + P_HALO:
                inside = jnp.where(source >= cells, right[pl.ds(0, n), :], inside)
            outs[i][pl.ds(w * n, n), :] = inside


class Rows:
    def __init__(self, ref, first):
        self.ref, self.first = ref, first

    def __getitem__(self, index):
        return self.ref[pl.ds(self.first + index, 1), :]


def bond_forces(x, y, z, used, mols, slots):
    def partner(a, t):
        return pltpu.roll(a, slots - t * mols, 1)

    first = [a - partner(a, 1) for a in (x, y, z)]
    second = [a - partner(a, 2) for a in (x, y, z)]
    third = [s - f for f, s in zip(first, second)]

    def pull(bond, stiffness, square):
        length = bond[0] * bond[0] + bond[1] * bond[1] + bond[2] * bond[2]
        return (stiffness * used) * (length - square)

    c1 = pull(first, bond_stiffness, bond_square)
    c2 = pull(second, bond_stiffness, bond_square)
    c3 = pull(third, angle_stiffness, angle_square)
    out = []
    for f, s, t in zip(first, second, third):
        on_first = c1 * f - c3 * t
        on_second = c2 * s + c3 * t
        on_oxygen = -(c1 * f + c2 * s)
        out.append(
            on_oxygen + pltpu.roll(on_first, mols, 1) + pltpu.roll(on_second, 2 * mols, 1)
        )
    return out


def steps_kernel(nb, group, lb, mols, slots, b_ref, *refs):
    blocks = refs[:nb]
    step_ref, q_ref, xv = refs[nb : nb + 3]
    beads = nb * lb
    store = Store(refs[nb + 3 :], beads)
    width = group + 2 * P_HALO
    n = 3 * lb
    b = b_ref[0]
    step = step_ref[b]
    charges = Rows(q_ref, b * group + P_HALO)

    def advance(states):
        flat = [
            jnp.concatenate([x, v], axis=0) for pos, vel in states for x, v in zip(pos, vel)
        ]
        high, mid, low = split3(jnp.concatenate(flat, axis=1))
        stacked = jnp.concatenate([high, mid, high, mid, low, high], axis=0).astype(BF16)
        new = dot_nn(step, stacked)
        out = []
        for i in range(len(states)):
            columns = [
                new[:, (3 * i + c) * slots : (3 * i + c + 1) * slots] for c in range(3)
            ]
            out.append(([a[:beads] for a in columns], [a[beads:] for a in columns]))
        return out

    def gather(w, a, comp):
        return jnp.concatenate(
            [block[pl.ds((a * width + w) * n + comp * lb, lb), :] for block in blocks], axis=0
        )

    def kick(state, oxygen, scale):
        pos, vel = state
        force = bond_forces(*pos, oxygen, mols, slots)
        return pos, [v + scale * f for v, f in zip(vel, force)]

    for first in range(0, width, 2):
        members = range(first, min(first + 2, width))
        charge = [charges[w] for w in members]
        oxygen = [(q < -1.5).astype(F32) for q in charge]
        inverse = [jnp.where(q < -1.5, 1.0 / oxygen_mass, 1.0) for q in charge]
        states = [
            (
                [gather(w, 0, c) for c in range(3)],
                [gather(w, 1, c) * scale for c in range(3)],
            )
            for w, scale in zip(members, inverse)
        ]
        for part in (0.5, 1.0):
            states = [
                kick(state, o, (part * inner_step) * scale)
                for state, o, scale in zip(states, oxygen, inverse)
            ]
            states = advance(states)
        for w, state, q, o, scale in zip(members, states, charge, oxygen, inverse):
            if 1 <= w <= width - 2:
                pos, vel = kick(state, o, (0.5 * inner_step) * scale)
                mass = jnp.where(q < -1.5, oxygen_mass, 1.0)
                for c in range(3):
                    xv[w - 1, pl.ds(c * beads, beads), :] = pos[c]
                    xv[w - 1, pl.ds((3 + c) * beads, beads), :] = vel[c] * mass
            build_tiles(store.tiles, w * beads, beads, *state[0])
    prepare(store, charges, width, slots)


def final_kernel(nb, group, lb, mols, slots, b_ref, *refs):
    perm_ref, q_ref, xv = refs[:3]
    beads = nb * lb
    store = Store(refs[3 : 3 + STORE], beads)
    ys = refs[3 + STORE : 3 + STORE + nb]
    forces, keep = refs[3 + STORE + nb :]
    b = b_ref[0]
    charges = Rows(q_ref, b * group + P_HALO)
    loop = PairLoop(mols, slots, beads, keep)
    loop.cells(store, charges, P_HALO, P_HALO + group, forces, 32)
    for w in range(group):
        old = xv[w]
        m = 3 * beads
        force = jnp.concatenate([read_force(forces, w, beads, c) for c in range(3)], axis=0)
        state = jnp.concatenate([old[:m], old[m:] + (0.5 * outer_step) * force], axis=0)
        state = unpermuted(state, perm_ref[b * group + w])
        for a in range(2):
            for c in range(3):
                for k in range(nb):
                    row = (a * 3 + c) * beads + k * lb
                    ys[k][pl.ds(((a * group + w) * 3 + c) * lb, lb), :] = state[row : row + lb]


def unpack_kernel(nb, group, lb, cells, b_ref, *refs):
    ys = refs[:nb]
    outs = refs[nb:]
    b = b_ref[0]
    for i, k in enumerate(block_order(nb)):
        source = jnp.bitwise_xor(b, k)
        for a in range(2):
            for w in range(group):
                for c in range(3):
                    outs[a][pl.ds(c * cells + source * group + w, lb, stride=3 * cells), :] = ys[
                        i
                    ][pl.ds(((a * group + w) * 3 + c) * lb, lb), :]


def call(kernel, outs, scratch, scalar, *operands, space=pltpu.VMEM):
    vmem = pl.BlockSpec(memory_space=pltpu.VMEM)
    smem = pl.BlockSpec(memory_space=pltpu.SMEM)
    return pl.pallas_call(
        kernel,
        out_shape=outs,
        in_specs=([] if scalar is None else [smem]) + [pl.BlockSpec(memory_space=space)] * len(operands),
        out_specs=[vmem] * len(outs),
        scratch_shapes=scratch,
        compiler_params=pltpu.CompilerParams(vmem_limit_bytes=24 * 1024 * 1024),
    )(*(() if scalar is None else (scalar,)), *operands)


def exchange(blocks, nb):
    return [
        lax.ppermute(block, "bead", [(i, i ^ k) for i in range(nb)]) if k else block
        for block, k in zip(blocks, block_order(nb))
    ]


def local(nb, ns, positions, momenta, molecules):
    lb, _, cells, slots = positions.shape
    mols = molecules.shape[1]
    group = cells // nb
    beads = lb * nb
    width = group + 2 * P_HALO
    b = lax.axis_index("bead").astype(jnp.int32).reshape(1)

    def shape(*dims):
        return jax.ShapeDtypeStruct(dims, F32)

    edge = shape(9 * lb + 8, slots)
    rows = lb * 3 * cells
    xs, ps, perm, charges, to_right, to_left = call(
        functools.partial(order_kernel, lb, cells, mols, slots),
        [shape(cells, 3 * lb, slots)] * 2
        + [jax.ShapeDtypeStruct((cells, slots, slots), BF16), shape(cells, slots), edge, edge],
        [
            pltpu.VMEM((3, cells, mols), jnp.int32),
            pltpu.VMEM((rows, slots), F32),
            pltpu.VMEM((rows, slots), F32),
            pltpu.VMEM((3, cells, slots), jnp.int32),
            pltpu.SemaphoreType.DMA((3,)),
        ],
        None,
        *(
            pltpu.with_memory_space_constraint(a, pltpu.HBM)
            for a in (
                jnp.transpose(molecules, (2, 0, 1)),
                positions.reshape(rows, slots),
                momenta.reshape(rows, slots),
            )
        ),
        space=pltpu.HBM,
    )
    left = lax.ppermute(to_right, "space", [(s, (s + 1) % ns) for s in range(ns)])
    right = lax.ppermute(to_left, "space", [(s, (s - 1) % ns) for s in range(ns)])
    q_rows = -(-(cells + 2 * X_HALO) // 8) * 8

    def store(count, store_beads):
        return [
            jax.ShapeDtypeStruct(*entry) for entry in store_shapes(count, store_beads, slots)
        ]

    keep = pltpu.VMEM((slots, slots), F32)
    own = call(
        functools.partial(own_kernel, cells, lb, slots), store(cells, lb), [], None, xs, charges
    )
    (inner,) = call(
        functools.partial(interior_kernel, cells, lb, mols, slots),
        [shape((cells - 2) * lb * 8, slots)],
        [keep],
        None,
        charges,
        *own,
    )
    *blocks, q_wide = call(
        functools.partial(edge_kernel, nb, group, lb, cells, mols, slots),
        [shape(2 * width * 3 * lb, slots)] * nb + [shape(q_rows, slots)],
        [
            pltpu.VMEM((cells + 2 * P_HALO, 3 * lb, slots), F32),
            pltpu.VMEM((4 * lb * 8, slots), F32),
            keep,
        ]
        + [pltpu.VMEM(*entry) for entry in store_shapes(4, lb, slots)],
        b,
        xs,
        ps,
        charges,
        left,
        right,
        inner,
        *own,
    )
    blocks = exchange(blocks, nb)
    step = jnp.asarray(propagator(beads, lb))
    xv, *stepped = call(
        functools.partial(steps_kernel, nb, group, lb, mols, slots),
        [shape(group, 6 * beads, slots)] + store(width, beads),
        [],
        b,
        *blocks,
        step,
        q_wide,
    )
    ys = call(
        functools.partial(final_kernel, nb, group, lb, mols, slots),
        [shape(2 * group * 3 * lb, slots)] * nb,
        [pltpu.VMEM((group * beads * 8, slots), F32), keep],
        b,
        perm,
        q_wide,
        xv,
        *stepped,
    )
    ys = exchange(ys, nb)
    new_x, new_p = call(
        functools.partial(unpack_kernel, nb, group, lb, cells),
        [shape(lb * 3 * cells, slots)] * 2,
        [],
        b,
        *ys,
    )
    return new_x.reshape(positions.shape), new_p.reshape(positions.shape)


def solution(mesh):
    spec = P("bead", None, "space", None)
    return jax.shard_map(
        functools.partial(local, mesh.shape["bead"], mesh.shape["space"]),
        mesh=mesh,
        in_specs=(spec, spec, P("space", None, None)),
        out_specs=(spec, spec),
        check_vma=False,
    )
```

```python
import functools

import jax
import jax.numpy as jnp
import ml_dtypes
import numpy as np
from jax import lax
from jax.experimental import pallas as pl
from jax.experimental.pallas import tpu as pltpu
from jax.sharding import PartitionSpec as P

charge_oxygen = -0.8476
charge_hydrogen = 0.4238
coulomb_scale = 24.0
coulomb_soft = 0.004
well_depth = 0.02
sigma_square = 0.0841
lennard_soft = 0.04
bond_stiffness = 20000.0
bond_square = 0.0081
angle_stiffness = 5000.0
angle_square = 0.0204
cycle_frequency = 60.0
outer_step = 0.02
inner_step = 0.01
oxygen_mass = 16.0

REACH = 1
X_HALO = 2 * REACH
P_HALO = REACH

F32 = jnp.float32
BF16 = jnp.bfloat16


def rounded(a):
    return a.astype(BF16).astype(F32)


def split3(a):
    high = rounded(a)
    rest = a - high
    mid = rounded(rest)
    return high, mid, rest - mid


def two_part(a):
    high = rounded(a)
    return high + rounded(a - high)


def dot_nn(a, b):
    return lax.dot_general(a, b, (((1,), (0,)), ((), ())), preferred_element_type=F32)


def dot_nt(a, b):
    return lax.dot_general(a, b, (((1,), (1,)), ((), ())), preferred_element_type=F32)


def block_order(nb):
    return sorted(range(nb), key=lambda k: (k > 0, -bin(k).count("1"), k))


def propagator(beads, beads_dev):
    j = np.arange(beads)
    angles = 2.0 * np.pi * ((j[:, None] * j[None, :]) % beads) / beads
    half = beads // 2
    col = j[None, :]
    u = np.where(
        col == 0,
        np.sqrt(1.0 / beads),
        np.where(
            col < half,
            np.sqrt(2.0 / beads) * np.cos(angles),
            np.where(
                col == half,
                np.sqrt(1.0 / beads) * np.cos(angles),
                np.sqrt(2.0 / beads) * np.sin(angles),
            ),
        ),
    )
    w = 2.0 * cycle_frequency * np.sin(np.pi * j / beads)
    cosines = np.cos(w * inner_step)
    spring = w * np.sin(w * inner_step)
    drift = np.where(j == 0, inner_step, np.sin(w * inner_step) / np.where(j == 0, 1.0, w))
    def circulant(values, bead):
        first = ((u * values) @ u.T)[:, 0]
        return first[(bead[:, None] - bead[None, :]) % beads]

    out = []
    for b in range(beads // beads_dev):
        block = np.array(block_order(beads // beads_dev))[j // beads_dev]
        bead = (block ^ b) * beads_dev + j % beads_dev
        a = circulant(cosines, bead)
        whole = np.block([[a, circulant(drift, bead)], [-circulant(spring, bead), a]])
        high = whole.astype(ml_dtypes.bfloat16)
        rest = whole - high.astype(np.float64)
        mid = rest.astype(ml_dtypes.bfloat16)
        low = (rest - mid.astype(np.float64)).astype(ml_dtypes.bfloat16)
        out.append(np.concatenate([high, high, mid, mid, high, low], axis=1))
    return np.stack(out)


def lane_tables(lanes, mols, slots):
    lane = lax.broadcasted_iota(jnp.int32, lanes.shape, 1)
    unit = jnp.where(lane < mols, charge_oxygen / charge_hydrogen, 1.0)
    return jnp.where(lanes < slots, unit, 0.0)


def permuted(rows, perm):
    n = rows.shape[0]
    stacked = jnp.concatenate(split3(rows), axis=0).astype(BF16)
    moved = dot_nn(stacked, perm)
    return moved[:n] + moved[n : 2 * n] + moved[2 * n :]


def unpermuted(rows, perm):
    n = rows.shape[0]
    stacked = jnp.concatenate(split3(rows), axis=0).astype(BF16)
    moved = dot_nt(stacked, perm)
    return moved[:n] + moved[n : 2 * n] + moved[2 * n :]


def order_kernel(lb, cells, mols, slots, odd_ref, mol_hbm, x_hbm, p_hbm, *refs):
    xo, po, perm_ref, q_ref, first_out, second_out = refs[:6]
    mol_ref, x_ref, p_ref, wide, sems = refs[6:]
    copies = [
        pltpu.make_async_copy(source, dest, sems.at[i])
        for i, (source, dest) in enumerate(
            ((mol_hbm, mol_ref), (x_hbm, x_ref), (p_hbm, p_ref))
        )
    ]
    for copy in copies:
        copy.start()
    row = lax.broadcasted_iota(jnp.int32, (slots, slots), 0)
    col = lax.broadcasted_iota(jnp.int32, (slots, slots), 1)
    upper = (row < col).astype(F32).astype(BF16)
    rows, row = row, row.astype(F32)
    lane = lax.broadcasted_iota(jnp.int32, (cells, slots), 1)
    far = 4.0 * slots
    wide[...] = jnp.full(wide.shape, slots, jnp.int32)
    copies[0].wait()
    for t in range(3):
        wide[t, :, :mols] = mol_ref[t]
    lanes = jnp.where(
        lane < mols,
        wide[0],
        jnp.where(lane < 2 * mols, pltpu.roll(wide[1], mols, 1), pltpu.roll(wide[2], 2 * mols, 1)),
    )
    lanes = jnp.where(lane < 3 * mols, lanes, slots)
    charges = lane_tables(lanes, mols, slots)
    q_ref[...] = charges
    free = lanes >= slots
    key = jnp.where(
        free, far + dot_nn(free.astype(F32).astype(BF16), upper), lanes.astype(F32)
    )
    ones = jnp.ones((slots, slots), BF16)
    used = jnp.zeros((slots, slots), F32)
    for cell in range(cells):
        held = (row == key[cell : cell + 1]).astype(F32).astype(BF16)
        used = jnp.where(col == cell, dot_nn(held, ones), used)
    rank = dot_nn((col < rows).astype(F32).astype(BF16), (1.0 - used).astype(BF16))
    slot_key = jnp.where(used > 0.5, row, far + rank)
    copies[1].wait()
    copies[2].wait()
    n = 3 * lb
    for cell in range(cells):
        slot_column = jnp.broadcast_to(slot_key[:, cell : cell + 1], (slots, slots))
        perm = (slot_column == key[cell : cell + 1]).astype(F32).astype(BF16)
        perm_ref[cell] = perm
        atoms = [
            ref[pl.ds(comp * cells + cell, lb, stride=3 * cells), :]
            for ref in (x_ref, p_ref)
            for comp in range(3)
        ]
        moved = permuted(jnp.concatenate(atoms, axis=0), perm)
        xo[cell] = moved[:n]
        po[cell] = moved[n:]
    odd = odd_ref[0]
    for out, low in ((first_out, odd), (second_out, 1 - odd)):
        out[9 * lb :, :] = jnp.zeros((8, slots), F32)
        for e in range(2):
            cell = jnp.where(low == 1, e, cells - 2 + e)
            out[pl.ds(e * n, n), :] = xo[cell]
            out[pl.ds(9 * lb + e, 1), :] = q_ref[pl.ds(cell, 1), :]
        out[pl.ds(2 * n, n), :] = po[jnp.where(low == 1, 0, cells - 1)]


def put_tiles(scratch, first, count, rows):
    for index, value in rows:
        scratch[pl.ds(first * 8 + index, count, stride=8), :] = value


OFFSETS = (-1.0, 0.0, 1.0)


def build_tiles(tiles, first, count, x, y, z):
    x, y, z = two_part(x - 0.5), two_part(y - 0.5), two_part(z - 0.5)
    norm = x * x + y * y + z * z + 0.5 * coulomb_soft
    high = two_part(norm)
    low = norm - high
    put_tiles(
        tiles, first, count, ((0, x), (1, y), (2, z), (3, high), (4, low), (5, high), (6, low))
    )


def store_shapes(count, beads, slots):
    n = count * beads
    return (
        [((n * 8, slots), F32), ((n // 2, slots, 64), BF16)]
        + [((n // 2, 32, slots), BF16)] * 3
        + [((n, 32, slots), BF16)]
    )


STORE = 6


class Store:
    def __init__(self, refs, beads):
        self.tiles, self.peers, *sums, self.targets = refs
        self.sums = sums
        self.beads = beads


def tile_of(ref, n):
    return ref[pl.ds(pl.multiple_of(n * 8, 8), 8), :]


def prepare(store, charges, count, slots):
    tiles, beads = store.tiles, store.beads
    row8 = lax.broadcasted_iota(jnp.int32, (8, slots), 0)
    place, norms = row8 < 3, row8 < 5
    target_rows = place | (row8 == 5) | (row8 == 6)
    ones_low = jnp.where((row8 == 3) | (row8 == 4), 1.0, 0.0)
    ones_high = jnp.where((row8 == 5) | (row8 == 6), 1.0, 0.0)
    ones_last = jnp.where(row8 == 7, 1.0, 0.0)
    pairs = beads // 2
    total = count * pairs
    unroll = max(n for n in range(1, max(2, min(17, total // 4 + 1))) if total % n == 0)

    def stack(values):
        return jnp.concatenate(values, axis=0).astype(BF16)

    def step(index, carry):
        for u in range(unroll):
            m = index * unroll + u
            charge = charges[lax.div(m, pairs)]
            units = [
                jnp.where(row8 == 3, charge, jnp.where(row8 == 4, offset * charge, 0.0))
                for offset in OFFSETS
            ]
            left, high_rows, mid_rows = [], [], []
            for h in range(2):
                value = tile_of(tiles, 2 * m + h)
                high = rounded(value)
                mid = value - high
                x_high, x_mid = high[0:1], mid[0:1]
                left_high = jnp.where(place, -2.0 * high, jnp.where(norms, high, ones_high))
                left_mid = jnp.where(place, -2.0 * mid, jnp.where(norms, mid, 0.0))
                left_last = jnp.where(
                    place,
                    -2.0 * mid,
                    jnp.where(
                        row8 == 3,
                        2.0 * x_high,
                        jnp.where(row8 == 4, 2.0 * x_mid, ones_last - 2.0 * ones_high),
                    ),
                )
                left += [left_high, left_high, left_mid, left_last]
                right_high = jnp.where(target_rows, high, ones_low)
                right_mid = jnp.where(target_rows, mid, 0.0)
                right_last = jnp.where(
                    place,
                    mid,
                    jnp.where(
                        row8 == 5, x_high, jnp.where(row8 == 6, x_mid, ones_low + ones_last)
                    ),
                )
                store.targets[2 * m + h] = stack([right_high, right_mid, right_high, right_last])
                high_rows.append(high * charge)
                mid_rows.append(jnp.where(place, mid * charge, 0.0))
            store.peers[m] = stack(left).T
            for o in range(3):
                rows = []
                for h in range(2):
                    rows += [jnp.where(place, high_rows[h], units[o]), mid_rows[h]]
                store.sums[o][m] = stack(rows)
        return carry

    lax.fori_loop(0, total // unroll, step, 0)


class PairLoop:
    def __init__(self, mols, slots, beads, keep):
        self.mols, self.slots, self.keep = mols, slots, keep
        self.pairs = beads // 2
        self.unroll = min(self.pairs, 4)
        self.per_cell = self.pairs // self.unroll
        orows = -(-mols // 8) * 8
        self.row8 = lax.broadcasted_iota(jnp.int32, (8, slots), 0)
        lj_row = lax.broadcasted_iota(jnp.int32, (orows, slots), 0)
        lj_lane = lax.broadcasted_iota(jnp.int32, (orows, slots), 1)
        self.first_lanes, self.second_lanes = lj_lane < mols, lj_lane < 2 * mols
        self.corner = (lj_row < mols) & self.first_lanes

        i = lax.broadcasted_iota(jnp.int32, (slots, slots), 0)
        j = lax.broadcasted_iota(jnp.int32, (slots, slots), 1)
        i = jnp.where(i >= 2 * mols, i - 2 * mols, jnp.where(i >= mols, i - mols, i))
        j = jnp.where(j >= 2 * mols, j - 2 * mols, jnp.where(j >= mols, j - mols, j))
        keep[...] = (i != j).astype(F32)

        lane64 = lax.broadcasted_iota(jnp.int32, (slots, 64), 1) & 31
        odd = (lane64 >= 27) & (lane64 < 31)
        even = lane64 == 31
        self.signs = [
            jnp.where(odd, -1.0, 1.0).astype(BF16),
            jnp.where(odd | even, 0.0, 1.0).astype(BF16),
            None,
        ]
        self.zero = jnp.zeros((32, slots), BF16)

    def pair(self, peers, charge):
        mols, slots = self.mols, self.slots
        orows = self.corner.shape[0]
        pair_scale = coulomb_scale * charge_hydrogen * charge_hydrogen
        k3 = sigma_square**3
        ratio = (charge_hydrogen / charge_oxygen) ** 2 / pair_scale
        lj_a = 24.0 * well_depth * 2.0 * k3 * k3 * ratio
        lj_b = 24.0 * well_depth * k3 * ratio
        zero = self.zero
        own, m = peers[1]
        left = jnp.concatenate(
            [
                store.peers[index] if sign is None else store.peers[index] * sign
                for (store, index), sign in zip(peers, self.signs)
            ],
            axis=0,
        )
        right = jnp.concatenate(
            [
                jnp.concatenate([own.targets[2 * m], zero], axis=1),
                jnp.concatenate([zero, own.targets[2 * m + 1]], axis=1),
            ],
            axis=0,
        )
        squares = dot_nn(left, right)
        blocks = [[], [], []]
        for h in range(2):
            lanes = slice(h * slots, (h + 1) * slots)
            near = [squares[o * slots : o * slots + orows, lanes] for o in range(3)]
            packed = jnp.where(
                self.first_lanes,
                near[0],
                jnp.where(
                    self.second_lanes,
                    pltpu.roll(near[1], mols, 1),
                    pltpu.roll(near[2], 2 * mols, 1),
                ),
            )
            root = lax.rsqrt(packed + (lennard_soft - coulomb_soft))
            inverse = root * root
            cube = inverse * inverse * inverse
            lj = (cube * lj_a - lj_b) * (cube * inverse)
            for o in range(3):
                root = lax.rsqrt(squares[o * slots : (o + 1) * slots, lanes])
                strength = root * root * root
                part = pltpu.roll(lj, slots - o * mols, 1) if o else lj
                strength = jnp.concatenate(
                    [strength[:orows] + jnp.where(self.corner, part, 0.0), strength[orows:]],
                    axis=0,
                )
                if o == 1:
                    strength = strength * self.keep[...]
                high = strength.astype(BF16)
                low = (strength - high.astype(F32)).astype(BF16)
                blocks[o].append(jnp.concatenate([high, low], axis=0))
        sums = None
        for o, (store, index) in enumerate(peers):
            weights = store.sums[o][index]
            value = dot_nn(
                jnp.concatenate([weights, weights], axis=1), jnp.concatenate(blocks[o], axis=1)
            )
            sums = value if sums is None else sums + value
        scale = charge * pair_scale
        out = []
        for h in range(2):
            part = sums[16 * h : 16 * h + 16, h * slots : (h + 1) * slots]
            total = part[0:8] + part[8:16]
            total = total + jnp.where(self.row8 == 0, total[4:5], 0.0)
            out.append((tile_of(own.tiles, 2 * m + h) * total[3:4] - total) * scale)
        return out

    def cells(self, store, charges, first, last, forces, limit):
        total = (last - first) * self.pairs
        unroll = max(n for n in range(1, limit + 1) if total % n == 0)

        def step(index, carry):
            for u in range(unroll):
                m = index * unroll + u
                at = m + first * self.pairs
                peers = [(store, at + (o - 1) * self.pairs) for o in range(3)]
                out = self.pair(peers, charges[lax.div(at, self.pairs)])
                for h in range(2):
                    n = 2 * m + h
                    forces[pl.ds(pl.multiple_of(n * 8, 8), 8), :] = out[h]
            return carry

        lax.fori_loop(0, total // unroll, step, 0)


def read_force(forces, w, beads, comp):
    return forces[pl.ds(w * beads * 8 + comp, beads, stride=8), :]


def own_kernel(cells, lb, slots, x_ref, q_ref, *refs):
    store = Store(refs, lb)
    for w in range(cells):
        rows = x_ref[w]
        build_tiles(store.tiles, w * lb, lb, rows[:lb], rows[lb : 2 * lb], rows[2 * lb :])
    prepare(store, Rows(q_ref, 0), cells, slots)


def interior_kernel(cells, lb, mols, slots, q_ref, *refs):
    store = Store(refs[:STORE], lb)
    forces, keep = refs[STORE:]
    PairLoop(mols, slots, lb, keep).cells(store, Rows(q_ref, 0), 1, cells - 1, forces, 64)


def edge_kernel(nb, group, lb, cells, mols, slots, b_ref, *refs):
    x_ref, p_ref, q_ref, first, second, inner = refs[:6]
    own = Store(refs[6 : 6 + STORE], lb)
    refs = refs[6 + STORE :]
    outs, q_out = refs[:nb], refs[nb]
    kicked, halo_forces, keep, left, right = refs[nb + 1 : nb + 6]
    halo = Store(refs[nb + 6 :], lb)
    odd = b_ref[1] == 1
    left[...] = jnp.where(odd, first[...], second[...])
    right[...] = jnp.where(odd, second[...], first[...])
    n = 3 * lb
    count = cells + 2 * X_HALO
    b = b_ref[0]

    charge_rows = [left[pl.ds(9 * lb + e, 1), :] for e in range(2)]
    charge_rows += [q_ref[c : c + 1, :] for c in range(cells)]
    charge_rows += [right[pl.ds(9 * lb + e, 1), :] for e in range(2)]
    q_out[...] = jnp.zeros(q_out.shape, F32)
    for w in range(count):
        q_out[w : w + 1, :] = charge_rows[w]
    for e in range(4):
        edge = (left, right)[e // 2]
        rows = edge[pl.ds((e % 2) * n, n), :]
        build_tiles(halo.tiles, e * lb, lb, rows[:lb], rows[lb : 2 * lb], rows[2 * lb :])

    class Edges:
        def __getitem__(self, e):
            return q_out[pl.ds(jnp.where(e < 2, e, e + cells), 1), :]

    prepare(halo, Edges(), 4, slots)
    loop = PairLoop(mols, slots, lb, keep)

    def place(w):
        if w < X_HALO:
            return halo, w
        if w >= cells + X_HALO:
            return halo, w - cells
        return own, w - X_HALO

    targets = (1, 2, cells + 1, cells + 2)

    def edge_step(step, carry):
        for e, w in enumerate(targets):
            for u in range(loop.unroll):
                index = step * loop.unroll + u
                peers = [
                    (store, cell * loop.pairs + index) for store, cell in map(place, (w - 1, w, w + 1))
                ]
                out = loop.pair(peers, charge_rows[w])
                for h in range(2):
                    at = (e * lb + 2 * index + h) * 8
                    halo_forces[pl.ds(pl.multiple_of(at, 8), 8), :] = out[h]
        return carry

    lax.fori_loop(0, loop.per_cell, edge_step, 0)
    half = 0.5 * outer_step
    for w in range(1, count - 1):
        if w < X_HALO:
            old = left[pl.ds(2 * n, n), :]
        elif w >= cells + X_HALO:
            old = right[pl.ds(2 * n, n), :]
        else:
            old = p_ref[w - X_HALO]
        source, cell = (
            (halo_forces, targets.index(w)) if w in targets else (inner, w - X_HALO - 1)
        )
        force = jnp.concatenate([read_force(source, cell, lb, c) for c in range(3)], axis=0)
        kicked[w - 1] = old + half * force
    width = group + 2 * P_HALO
    for i, k in enumerate(block_order(nb)):
        first = jnp.bitwise_xor(b, k) * group
        for w in range(width):
            outs[i][pl.ds((width + w) * n, n), :] = kicked[first + w]
            source = first + w - P_HALO
            inside = x_ref[jnp.clip(source, 0, cells - 1)]
            if w < P_HALO:
                inside = jnp.where(source < 0, left[pl.ds(n, n), :], inside)
            elif w >= group + P_HALO:
                inside = jnp.where(source >= cells, right[pl.ds(0, n), :], inside)
            outs[i][pl.ds(w * n, n), :] = inside


class Rows:
    def __init__(self, ref, first):
        self.ref, self.first = ref, first

    def __getitem__(self, index):
        return self.ref[pl.ds(self.first + index, 1), :]


def bond_forces(x, y, z, used, mols, slots):
    def partner(a, t):
        return pltpu.roll(a, slots - t * mols, 1)

    first = [a - partner(a, 1) for a in (x, y, z)]
    second = [a - partner(a, 2) for a in (x, y, z)]
    third = [s - f for f, s in zip(first, second)]

    def pull(bond, stiffness, square):
        length = bond[0] * bond[0] + bond[1] * bond[1] + bond[2] * bond[2]
        return (stiffness * used) * (length - square)

    c1 = pull(first, bond_stiffness, bond_square)
    c2 = pull(second, bond_stiffness, bond_square)
    c3 = pull(third, angle_stiffness, angle_square)
    out = []
    for f, s, t in zip(first, second, third):
        on_first = c1 * f - c3 * t
        on_second = c2 * s + c3 * t
        on_oxygen = -(c1 * f + c2 * s)
        out.append(
            on_oxygen + pltpu.roll(on_first, mols, 1) + pltpu.roll(on_second, 2 * mols, 1)
        )
    return out


def steps_kernel(nb, group, lb, mols, slots, b_ref, *refs):
    blocks = refs[:nb]
    step_ref, q_ref, xv = refs[nb : nb + 3]
    beads = nb * lb
    store = Store(refs[nb + 3 :], beads)
    width = group + 2 * P_HALO
    n = 3 * lb
    b = b_ref[0]
    step = step_ref[b]
    charges = Rows(q_ref, b * group + P_HALO)

    def advance(states):
        flat = [
            jnp.concatenate([x, v], axis=0) for pos, vel in states for x, v in zip(pos, vel)
        ]
        high, mid, low = split3(jnp.concatenate(flat, axis=1))
        stacked = jnp.concatenate([high, mid, high, mid, low, high], axis=0).astype(BF16)
        new = dot_nn(step, stacked)
        out = []
        for i in range(len(states)):
            columns = [
                new[:, (3 * i + c) * slots : (3 * i + c + 1) * slots] for c in range(3)
            ]
            out.append(([a[:beads] for a in columns], [a[beads:] for a in columns]))
        return out

    def gather(w, a, comp):
        return jnp.concatenate(
            [block[pl.ds((a * width + w) * n + comp * lb, lb), :] for block in blocks], axis=0
        )

    def kick(state, oxygen, scale):
        pos, vel = state
        force = bond_forces(*pos, oxygen, mols, slots)
        return pos, [v + scale * f for v, f in zip(vel, force)]

    for first in range(0, width, 2):
        members = range(first, min(first + 2, width))
        charge = [charges[w] for w in members]
        oxygen = [(q < -1.5).astype(F32) for q in charge]
        inverse = [jnp.where(q < -1.5, 1.0 / oxygen_mass, 1.0) for q in charge]
        states = [
            (
                [gather(w, 0, c) for c in range(3)],
                [gather(w, 1, c) * scale for c in range(3)],
            )
            for w, scale in zip(members, inverse)
        ]
        for part in (0.5, 1.0):
            states = [
                kick(state, o, (part * inner_step) * scale)
                for state, o, scale in zip(states, oxygen, inverse)
            ]
            states = advance(states)
        for w, state, q, o, scale in zip(members, states, charge, oxygen, inverse):
            if 1 <= w <= width - 2:
                pos, vel = kick(state, o, (0.5 * inner_step) * scale)
                mass = jnp.where(q < -1.5, oxygen_mass, 1.0)
                for c in range(3):
                    xv[w - 1, pl.ds(c * beads, beads), :] = pos[c]
                    xv[w - 1, pl.ds((3 + c) * beads, beads), :] = vel[c] * mass
            build_tiles(store.tiles, w * beads, beads, *state[0])
    prepare(store, charges, width, slots)


def final_kernel(nb, group, lb, mols, slots, b_ref, *refs):
    perm_ref, q_ref, xv = refs[:3]
    beads = nb * lb
    store = Store(refs[3 : 3 + STORE], beads)
    ys = refs[3 + STORE : 3 + STORE + nb]
    forces, keep = refs[3 + STORE + nb :]
    b = b_ref[0]
    charges = Rows(q_ref, b * group + P_HALO)
    loop = PairLoop(mols, slots, beads, keep)
    loop.cells(store, charges, P_HALO, P_HALO + group, forces, 32)
    for w in range(group):
        old = xv[w]
        m = 3 * beads
        force = jnp.concatenate([read_force(forces, w, beads, c) for c in range(3)], axis=0)
        state = jnp.concatenate([old[:m], old[m:] + (0.5 * outer_step) * force], axis=0)
        state = unpermuted(state, perm_ref[b * group + w])
        for a in range(2):
            for c in range(3):
                for i, k in enumerate(block_order(nb)):
                    row = (a * 3 + c) * beads + i * lb
                    ys[k][pl.ds(((a * group + w) * 3 + c) * lb, lb), :] = state[row : row + lb]


def unpack_kernel(nb, group, lb, cells, b_ref, *refs):
    ys = refs[:nb]
    outs = refs[nb:]
    b = b_ref[0]
    for k in range(nb):
        source = jnp.bitwise_xor(b, k)
        for a in range(2):
            for w in range(group):
                for c in range(3):
                    outs[a][pl.ds(c * cells + source * group + w, lb, stride=3 * cells), :] = ys[
                        k
                    ][pl.ds(((a * group + w) * 3 + c) * lb, lb), :]


def call(kernel, outs, scratch, scalar, *operands, space=pltpu.VMEM):
    vmem = pl.BlockSpec(memory_space=pltpu.VMEM)
    smem = pl.BlockSpec(memory_space=pltpu.SMEM)
    return pl.pallas_call(
        kernel,
        out_shape=outs,
        in_specs=([] if scalar is None else [smem]) + [pl.BlockSpec(memory_space=space)] * len(operands),
        out_specs=[vmem] * len(outs),
        scratch_shapes=scratch,
        compiler_params=pltpu.CompilerParams(vmem_limit_bytes=24 * 1024 * 1024),
    )(*(() if scalar is None else (scalar,)), *operands)


def exchange(blocks, order):
    return [
        lax.ppermute(block, "bead", [(i, i ^ k) for i in range(len(order))]) if k else block
        for block, k in zip(blocks, order)
    ]


def local(nb, ns, positions, momenta, molecules):
    lb, _, cells, slots = positions.shape
    mols = molecules.shape[1]
    group = cells // nb
    beads = lb * nb
    width = group + 2 * P_HALO
    b = lax.axis_index("bead").astype(jnp.int32).reshape(1)
    odd = (lax.axis_index("space").astype(jnp.int32) & 1).reshape(1)

    def shape(*dims):
        return jax.ShapeDtypeStruct(dims, F32)

    edge = shape(9 * lb + 8, slots)
    rows = lb * 3 * cells
    xs, ps, perm, charges, first, second = call(
        functools.partial(order_kernel, lb, cells, mols, slots),
        [shape(cells, 3 * lb, slots)] * 2
        + [jax.ShapeDtypeStruct((cells, slots, slots), BF16), shape(cells, slots), edge, edge],
        [
            pltpu.VMEM((3, cells, mols), jnp.int32),
            pltpu.VMEM((rows, slots), F32),
            pltpu.VMEM((rows, slots), F32),
            pltpu.VMEM((3, cells, slots), jnp.int32),
            pltpu.SemaphoreType.DMA((3,)),
        ],
        odd,
        *(
            pltpu.with_memory_space_constraint(a, pltpu.HBM)
            for a in (
                jnp.transpose(molecules, (2, 0, 1)),
                positions.reshape(rows, slots),
                momenta.reshape(rows, slots),
            )
        ),
        space=pltpu.HBM,
    )
    first = lax.ppermute(first, "space", [(s, s ^ 1) for s in range(ns)])
    second = lax.ppermute(
        second, "space", [(s, (s + 1 if s % 2 else s - 1) % ns) for s in range(ns)]
    )
    q_rows = -(-(cells + 2 * X_HALO) // 8) * 8

    def store(count, store_beads):
        return [
            jax.ShapeDtypeStruct(*entry) for entry in store_shapes(count, store_beads, slots)
        ]

    keep = pltpu.VMEM((slots, slots), F32)
    own = call(
        functools.partial(own_kernel, cells, lb, slots), store(cells, lb), [], None, xs, charges
    )
    (inner,) = call(
        functools.partial(interior_kernel, cells, lb, mols, slots),
        [shape((cells - 2) * lb * 8, slots)],
        [keep],
        None,
        charges,
        *own,
    )
    *blocks, q_wide = call(
        functools.partial(edge_kernel, nb, group, lb, cells, mols, slots),
        [shape(2 * width * 3 * lb, slots)] * nb + [shape(q_rows, slots)],
        [
            pltpu.VMEM((cells + 2 * P_HALO, 3 * lb, slots), F32),
            pltpu.VMEM((4 * lb * 8, slots), F32),
            keep,
            pltpu.VMEM(edge.shape, F32),
            pltpu.VMEM(edge.shape, F32),
        ]
        + [pltpu.VMEM(*entry) for entry in store_shapes(4, lb, slots)],
        jnp.concatenate([b, odd]),
        xs,
        ps,
        charges,
        first,
        second,
        inner,
        *own,
    )
    blocks = exchange(blocks, block_order(nb))
    step = jnp.asarray(propagator(beads, lb))
    xv, *stepped = call(
        functools.partial(steps_kernel, nb, group, lb, mols, slots),
        [shape(group, 6 * beads, slots)] + store(width, beads),
        [],
        b,
        *blocks,
        step,
        q_wide,
    )
    ys = call(
        functools.partial(final_kernel, nb, group, lb, mols, slots),
        [shape(2 * group * 3 * lb, slots)] * nb,
        [pltpu.VMEM((group * beads * 8, slots), F32), keep],
        b,
        perm,
        q_wide,
        xv,
        *stepped,
    )
    ys = exchange(ys, range(nb))
    new_x, new_p = call(
        functools.partial(unpack_kernel, nb, group, lb, cells),
        [shape(lb * 3 * cells, slots)] * 2,
        [],
        b,
        *ys,
    )
    return new_x.reshape(positions.shape), new_p.reshape(positions.shape)


def solution(mesh):
    spec = P("bead", None, "space", None)
    return jax.shard_map(
        functools.partial(local, mesh.shape["bead"], mesh.shape["space"]),
        mesh=mesh,
        in_specs=(spec, spec, P("space", None, None)),
        out_specs=(spec, spec),
        check_vma=False,
    )
```

```python
import functools

import jax
import jax.numpy as jnp
import ml_dtypes
import numpy as np
from jax import lax
from jax.experimental import pallas as pl
from jax.experimental.pallas import tpu as pltpu
from jax.sharding import PartitionSpec as P

charge_oxygen = -0.8476
charge_hydrogen = 0.4238
coulomb_scale = 24.0
coulomb_soft = 0.004
well_depth = 0.02
sigma_square = 0.0841
lennard_soft = 0.04
bond_stiffness = 20000.0
bond_square = 0.0081
angle_stiffness = 5000.0
angle_square = 0.0204
cycle_frequency = 60.0
outer_step = 0.02
inner_step = 0.01
oxygen_mass = 16.0

REACH = 1
X_HALO = 2 * REACH
P_HALO = REACH

F32 = jnp.float32
BF16 = jnp.bfloat16


def rounded(a):
    return a.astype(BF16).astype(F32)


def split3(a):
    high = rounded(a)
    rest = a - high
    mid = rounded(rest)
    return high, mid, rest - mid


def two_part(a):
    high = rounded(a)
    return high + rounded(a - high)


def dot_nn(a, b):
    return lax.dot_general(a, b, (((1,), (0,)), ((), ())), preferred_element_type=F32)


def dot_nt(a, b):
    return lax.dot_general(a, b, (((1,), (1,)), ((), ())), preferred_element_type=F32)


def block_order(nb):
    return sorted(range(nb), key=lambda k: (k > 0, -bin(k).count("1"), k))


def propagator(beads, beads_dev):
    j = np.arange(beads)
    angles = 2.0 * np.pi * ((j[:, None] * j[None, :]) % beads) / beads
    half = beads // 2
    col = j[None, :]
    u = np.where(
        col == 0,
        np.sqrt(1.0 / beads),
        np.where(
            col < half,
            np.sqrt(2.0 / beads) * np.cos(angles),
            np.where(
                col == half,
                np.sqrt(1.0 / beads) * np.cos(angles),
                np.sqrt(2.0 / beads) * np.sin(angles),
            ),
        ),
    )
    w = 2.0 * cycle_frequency * np.sin(np.pi * j / beads)
    cosines = np.cos(w * inner_step)
    spring = w * np.sin(w * inner_step)
    drift = np.where(j == 0, inner_step, np.sin(w * inner_step) / np.where(j == 0, 1.0, w))
    def circulant(values, bead):
        first = ((u * values) @ u.T)[:, 0]
        return first[(bead[:, None] - bead[None, :]) % beads]

    out = []
    for b in range(beads // beads_dev):
        block = np.array(block_order(beads // beads_dev))[j // beads_dev]
        bead = (block ^ b) * beads_dev + j % beads_dev
        a = circulant(cosines, bead)
        whole = np.block([[a, circulant(drift, bead)], [-circulant(spring, bead), a]])
        high = whole.astype(ml_dtypes.bfloat16)
        rest = whole - high.astype(np.float64)
        mid = rest.astype(ml_dtypes.bfloat16)
        low = (rest - mid.astype(np.float64)).astype(ml_dtypes.bfloat16)
        out.append(np.concatenate([high, high, mid, mid, high, low], axis=1))
    return np.stack(out)


def lane_tables(lanes, mols, slots):
    lane = lax.broadcasted_iota(jnp.int32, lanes.shape, 1)
    unit = jnp.where(lane < mols, charge_oxygen / charge_hydrogen, 1.0)
    return jnp.where(lanes < slots, unit, 0.0)


def permuted(rows, perm):
    n = rows.shape[0]
    stacked = jnp.concatenate(split3(rows), axis=0).astype(BF16)
    moved = dot_nn(stacked, perm)
    return moved[:n] + moved[n : 2 * n] + moved[2 * n :]


def unpermuted(rows, perm):
    n = rows.shape[0]
    stacked = jnp.concatenate(split3(rows), axis=0).astype(BF16)
    moved = dot_nt(stacked, perm)
    return moved[:n] + moved[n : 2 * n] + moved[2 * n :]


def order_kernel(lb, cells, mols, slots, mol_hbm, x_hbm, p_hbm, *refs):
    xo, po, perm_ref, q_ref, ends = refs[:5]
    mol_ref, x_ref, p_ref, wide, sems = refs[5:]
    copies = [
        pltpu.make_async_copy(source, dest, sems.at[i])
        for i, (source, dest) in enumerate(
            ((mol_hbm, mol_ref), (x_hbm, x_ref), (p_hbm, p_ref))
        )
    ]
    for copy in copies:
        copy.start()
    row = lax.broadcasted_iota(jnp.int32, (slots, slots), 0)
    col = lax.broadcasted_iota(jnp.int32, (slots, slots), 1)
    upper = (row < col).astype(F32).astype(BF16)
    rows, row = row, row.astype(F32)
    lane = lax.broadcasted_iota(jnp.int32, (cells, slots), 1)
    far = 4.0 * slots
    wide[...] = jnp.full(wide.shape, slots, jnp.int32)
    copies[0].wait()
    for t in range(3):
        wide[t, :, :mols] = mol_ref[t]
    lanes = jnp.where(
        lane < mols,
        wide[0],
        jnp.where(lane < 2 * mols, pltpu.roll(wide[1], mols, 1), pltpu.roll(wide[2], 2 * mols, 1)),
    )
    lanes = jnp.where(lane < 3 * mols, lanes, slots)
    charges = lane_tables(lanes, mols, slots)
    q_ref[...] = charges
    free = lanes >= slots
    key = jnp.where(
        free, far + dot_nn(free.astype(F32).astype(BF16), upper), lanes.astype(F32)
    )
    ones = jnp.ones((slots, slots), BF16)
    used = jnp.zeros((slots, slots), F32)
    for cell in range(cells):
        held = (row == key[cell : cell + 1]).astype(F32).astype(BF16)
        used = jnp.where(col == cell, dot_nn(held, ones), used)
    rank = dot_nn((col < rows).astype(F32).astype(BF16), (1.0 - used).astype(BF16))
    slot_key = jnp.where(used > 0.5, row, far + rank)
    copies[1].wait()
    copies[2].wait()
    n = 3 * lb
    for cell in range(cells):
        slot_column = jnp.broadcast_to(slot_key[:, cell : cell + 1], (slots, slots))
        perm = (slot_column == key[cell : cell + 1]).astype(F32).astype(BF16)
        perm_ref[cell] = perm
        atoms = [
            ref[pl.ds(comp * cells + cell, lb, stride=3 * cells), :]
            for ref in (x_ref, p_ref)
            for comp in range(3)
        ]
        moved = permuted(jnp.concatenate(atoms, axis=0), perm)
        xo[cell] = moved[:n]
        po[cell] = moved[n:]
    for out, xs, ps in (
        (ends.at[0], (cells - 2, cells - 1), cells - 1),
        (ends.at[1], (0, 1), 0),
    ):
        out[9 * lb :, :] = jnp.zeros((8, slots), F32)
        for e, cell in enumerate(xs):
            out[pl.ds(e * n, n), :] = xo[cell]
            out[pl.ds(9 * lb + e, 1), :] = charges[cell : cell + 1]
        out[pl.ds(2 * n, n), :] = po[ps]


def put_tiles(scratch, first, count, rows):
    for index, value in rows:
        scratch[pl.ds(first * 8 + index, count, stride=8), :] = value


OFFSETS = (-1.0, 0.0, 1.0)


def build_tiles(tiles, first, count, x, y, z):
    x, y, z = two_part(x - 0.5), two_part(y - 0.5), two_part(z - 0.5)
    norm = x * x + y * y + z * z + 0.5 * coulomb_soft
    high = two_part(norm)
    low = norm - high
    put_tiles(
        tiles, first, count, ((0, x), (1, y), (2, z), (3, high), (4, low), (5, high), (6, low))
    )


def store_shapes(count, beads, slots):
    n = count * beads
    return (
        [((n * 8, slots), F32), ((n // 2, slots, 64), BF16)]
        + [((n // 2, 32, slots), BF16)] * 3
        + [((n, 32, slots), BF16)]
    )


STORE = 6


class Store:
    def __init__(self, refs, beads):
        self.tiles, self.peers, *sums, self.targets = refs
        self.sums = sums
        self.beads = beads


def tile_of(ref, n):
    return ref[pl.ds(pl.multiple_of(n * 8, 8), 8), :]


def prepare(store, charges, count, slots):
    tiles, beads = store.tiles, store.beads
    row8 = lax.broadcasted_iota(jnp.int32, (8, slots), 0)
    place, norms = row8 < 3, row8 < 5
    target_rows = place | (row8 == 5) | (row8 == 6)
    ones_low = jnp.where((row8 == 3) | (row8 == 4), 1.0, 0.0)
    ones_high = jnp.where((row8 == 5) | (row8 == 6), 1.0, 0.0)
    ones_last = jnp.where(row8 == 7, 1.0, 0.0)
    pairs = beads // 2
    total = count * pairs
    unroll = max(n for n in range(1, max(2, min(17, total // 4 + 1))) if total % n == 0)

    def stack(values):
        return jnp.concatenate(values, axis=0).astype(BF16)

    def step(index, carry):
        for u in range(unroll):
            m = index * unroll + u
            charge = charges[lax.div(m, pairs)]
            units = [
                jnp.where(row8 == 3, charge, jnp.where(row8 == 4, offset * charge, 0.0))
                for offset in OFFSETS
            ]
            left, high_rows, mid_rows = [], [], []
            for h in range(2):
                value = tile_of(tiles, 2 * m + h)
                high = rounded(value)
                mid = value - high
                x_high, x_mid = high[0:1], mid[0:1]
                left_high = jnp.where(place, -2.0 * high, jnp.where(norms, high, ones_high))
                left_mid = jnp.where(place, -2.0 * mid, jnp.where(norms, mid, 0.0))
                left_last = jnp.where(
                    place,
                    -2.0 * mid,
                    jnp.where(
                        row8 == 3,
                        2.0 * x_high,
                        jnp.where(row8 == 4, 2.0 * x_mid, ones_last - 2.0 * ones_high),
                    ),
                )
                left += [left_high, left_high, left_mid, left_last]
                right_high = jnp.where(target_rows, high, ones_low)
                right_mid = jnp.where(target_rows, mid, 0.0)
                right_last = jnp.where(
                    place,
                    mid,
                    jnp.where(
                        row8 == 5, x_high, jnp.where(row8 == 6, x_mid, ones_low + ones_last)
                    ),
                )
                store.targets[2 * m + h] = stack([right_high, right_mid, right_high, right_last])
                high_rows.append(high * charge)
                mid_rows.append(jnp.where(place, mid * charge, 0.0))
            store.peers[m] = stack(left).T
            for o in range(3):
                rows = []
                for h in range(2):
                    rows += [jnp.where(place, high_rows[h], units[o]), mid_rows[h]]
                store.sums[o][m] = stack(rows)
        return carry

    lax.fori_loop(0, total // unroll, step, 0)


class PairLoop:
    def __init__(self, mols, slots, beads, keep):
        self.mols, self.slots, self.keep = mols, slots, keep
        self.pairs = beads // 2
        self.unroll = min(self.pairs, 4)
        self.per_cell = self.pairs // self.unroll
        orows = -(-mols // 8) * 8
        self.row8 = lax.broadcasted_iota(jnp.int32, (8, slots), 0)
        lj_row = lax.broadcasted_iota(jnp.int32, (orows, slots), 0)
        lj_lane = lax.broadcasted_iota(jnp.int32, (orows, slots), 1)
        self.first_lanes, self.second_lanes = lj_lane < mols, lj_lane < 2 * mols
        self.corner = (lj_row < mols) & self.first_lanes

        i = lax.broadcasted_iota(jnp.int32, (slots, slots), 0)
        j = lax.broadcasted_iota(jnp.int32, (slots, slots), 1)
        i = jnp.where(i >= 2 * mols, i - 2 * mols, jnp.where(i >= mols, i - mols, i))
        j = jnp.where(j >= 2 * mols, j - 2 * mols, jnp.where(j >= mols, j - mols, j))
        keep[...] = (i != j).astype(F32)

        lane64 = lax.broadcasted_iota(jnp.int32, (slots, 64), 1) & 31
        odd = (lane64 >= 27) & (lane64 < 31)
        even = lane64 == 31
        self.signs = [
            jnp.where(odd, -1.0, 1.0).astype(BF16),
            jnp.where(odd | even, 0.0, 1.0).astype(BF16),
            None,
        ]
        self.zero = jnp.zeros((32, slots), BF16)

    def pair(self, peers, charge):
        mols, slots = self.mols, self.slots
        orows = self.corner.shape[0]
        pair_scale = coulomb_scale * charge_hydrogen * charge_hydrogen
        k3 = sigma_square**3
        ratio = (charge_hydrogen / charge_oxygen) ** 2 / pair_scale
        lj_a = 24.0 * well_depth * 2.0 * k3 * k3 * ratio
        lj_b = 24.0 * well_depth * k3 * ratio
        zero = self.zero
        own, m = peers[1]
        left = jnp.concatenate(
            [
                store.peers[index] if sign is None else store.peers[index] * sign
                for (store, index), sign in zip(peers, self.signs)
            ],
            axis=0,
        )
        right = jnp.concatenate(
            [
                jnp.concatenate([own.targets[2 * m], zero], axis=1),
                jnp.concatenate([zero, own.targets[2 * m + 1]], axis=1),
            ],
            axis=0,
        )
        squares = dot_nn(left, right)
        blocks = [[], [], []]
        for h in range(2):
            lanes = slice(h * slots, (h + 1) * slots)
            near = [squares[o * slots : o * slots + orows, lanes] for o in range(3)]
            packed = jnp.where(
                self.first_lanes,
                near[0],
                jnp.where(
                    self.second_lanes,
                    pltpu.roll(near[1], mols, 1),
                    pltpu.roll(near[2], 2 * mols, 1),
                ),
            )
            root = lax.rsqrt(packed + (lennard_soft - coulomb_soft))
            inverse = root * root
            cube = inverse * inverse * inverse
            lj = (cube * lj_a - lj_b) * (cube * inverse)
            for o in range(3):
                root = lax.rsqrt(squares[o * slots : (o + 1) * slots, lanes])
                strength = root * root * root
                part = pltpu.roll(lj, slots - o * mols, 1) if o else lj
                strength = jnp.concatenate(
                    [strength[:orows] + jnp.where(self.corner, part, 0.0), strength[orows:]],
                    axis=0,
                )
                if o == 1:
                    strength = strength * self.keep[...]
                high = strength.astype(BF16)
                low = (strength - high.astype(F32)).astype(BF16)
                blocks[o].append(jnp.concatenate([high, low], axis=0))
        sums = None
        for o, (store, index) in enumerate(peers):
            weights = store.sums[o][index]
            value = dot_nn(
                jnp.concatenate([weights, weights], axis=1), jnp.concatenate(blocks[o], axis=1)
            )
            sums = value if sums is None else sums + value
        scale = charge * pair_scale
        out = []
        for h in range(2):
            part = sums[16 * h : 16 * h + 16, h * slots : (h + 1) * slots]
            total = part[0:8] + part[8:16]
            total = total + jnp.where(self.row8 == 0, total[4:5], 0.0)
            out.append((tile_of(own.tiles, 2 * m + h) * total[3:4] - total) * scale)
        return out

    def cells(self, store, charges, first, last, forces, limit):
        total = (last - first) * self.pairs
        unroll = max(n for n in range(1, limit + 1) if total % n == 0)

        def step(index, carry):
            for u in range(unroll):
                m = index * unroll + u
                at = m + first * self.pairs
                peers = [(store, at + (o - 1) * self.pairs) for o in range(3)]
                out = self.pair(peers, charges[lax.div(at, self.pairs)])
                for h in range(2):
                    n = 2 * m + h
                    forces[pl.ds(pl.multiple_of(n * 8, 8), 8), :] = out[h]
            return carry

        lax.fori_loop(0, total // unroll, step, 0)


def read_force(forces, w, beads, comp):
    return forces[pl.ds(w * beads * 8 + comp, beads, stride=8), :]


def own_kernel(cells, lb, slots, x_ref, q_ref, *refs):
    store = Store(refs, lb)
    for w in range(cells):
        rows = x_ref[w]
        build_tiles(store.tiles, w * lb, lb, rows[:lb], rows[lb : 2 * lb], rows[2 * lb :])
    prepare(store, Rows(q_ref, 0), cells, slots)


def interior_kernel(cells, lb, mols, slots, q_ref, *refs):
    store = Store(refs[:STORE], lb)
    forces, keep = refs[STORE:]
    PairLoop(mols, slots, lb, keep).cells(store, Rows(q_ref, 0), 1, cells - 1, forces, 64)


def edge_kernel(nb, group, lb, cells, mols, slots, b_ref, *refs):
    x_ref, p_ref, q_ref, ends, inner = refs[:5]
    own = Store(refs[5 : 5 + STORE], lb)
    refs = refs[5 + STORE :]
    ns = ends.shape[0]
    left = ends.at[lax.rem(b_ref[1] + ns - 1, ns), 0]
    right = ends.at[lax.rem(b_ref[1] + 1, ns), 1]
    outs, q_out = refs[:nb], refs[nb]
    kicked, halo_forces, keep = refs[nb + 1 : nb + 4]
    halo = Store(refs[nb + 4 :], lb)
    n = 3 * lb
    count = cells + 2 * X_HALO
    b = b_ref[0]

    charge_rows = [left[pl.ds(9 * lb + e, 1), :] for e in range(2)]
    charge_rows += [q_ref[c : c + 1, :] for c in range(cells)]
    charge_rows += [right[pl.ds(9 * lb + e, 1), :] for e in range(2)]
    q_out[...] = jnp.zeros(q_out.shape, F32)
    for w in range(count):
        q_out[w : w + 1, :] = charge_rows[w]
    for e in range(4):
        edge = (left, right)[e // 2]
        rows = edge[pl.ds((e % 2) * n, n), :]
        build_tiles(halo.tiles, e * lb, lb, rows[:lb], rows[lb : 2 * lb], rows[2 * lb :])

    class Edges:
        def __getitem__(self, e):
            return q_out[pl.ds(jnp.where(e < 2, e, e + cells), 1), :]

    prepare(halo, Edges(), 4, slots)
    loop = PairLoop(mols, slots, lb, keep)

    def place(w):
        if w < X_HALO:
            return halo, w
        if w >= cells + X_HALO:
            return halo, w - cells
        return own, w - X_HALO

    targets = (1, 2, cells + 1, cells + 2)

    def edge_step(step, carry):
        for e, w in enumerate(targets):
            for u in range(loop.unroll):
                index = step * loop.unroll + u
                peers = [
                    (store, cell * loop.pairs + index) for store, cell in map(place, (w - 1, w, w + 1))
                ]
                out = loop.pair(peers, charge_rows[w])
                for h in range(2):
                    at = (e * lb + 2 * index + h) * 8
                    halo_forces[pl.ds(pl.multiple_of(at, 8), 8), :] = out[h]
        return carry

    lax.fori_loop(0, loop.per_cell, edge_step, 0)
    half = 0.5 * outer_step
    for w in range(1, count - 1):
        if w < X_HALO:
            old = left[pl.ds(2 * n, n), :]
        elif w >= cells + X_HALO:
            old = right[pl.ds(2 * n, n), :]
        else:
            old = p_ref[w - X_HALO]
        source, cell = (
            (halo_forces, targets.index(w)) if w in targets else (inner, w - X_HALO - 1)
        )
        force = jnp.concatenate([read_force(source, cell, lb, c) for c in range(3)], axis=0)
        kicked[w - 1] = old + half * force
    width = group + 2 * P_HALO
    for i, k in enumerate(block_order(nb)):
        first = jnp.bitwise_xor(b, k) * group
        for w in range(width):
            outs[i][pl.ds((width + w) * n, n), :] = kicked[first + w]
            source = first + w - P_HALO
            inside = x_ref[jnp.clip(source, 0, cells - 1)]
            if w < P_HALO:
                inside = jnp.where(source < 0, left[pl.ds(n, n), :], inside)
            elif w >= group + P_HALO:
                inside = jnp.where(source >= cells, right[pl.ds(0, n), :], inside)
            outs[i][pl.ds(w * n, n), :] = inside


class Rows:
    def __init__(self, ref, first):
        self.ref, self.first = ref, first

    def __getitem__(self, index):
        return self.ref[pl.ds(self.first + index, 1), :]


def bond_forces(x, y, z, used, mols, slots):
    def partner(a, t):
        return pltpu.roll(a, slots - t * mols, 1)

    first = [a - partner(a, 1) for a in (x, y, z)]
    second = [a - partner(a, 2) for a in (x, y, z)]
    third = [s - f for f, s in zip(first, second)]

    def pull(bond, stiffness, square):
        length = bond[0] * bond[0] + bond[1] * bond[1] + bond[2] * bond[2]
        return (stiffness * used) * (length - square)

    c1 = pull(first, bond_stiffness, bond_square)
    c2 = pull(second, bond_stiffness, bond_square)
    c3 = pull(third, angle_stiffness, angle_square)
    out = []
    for f, s, t in zip(first, second, third):
        on_first = c1 * f - c3 * t
        on_second = c2 * s + c3 * t
        on_oxygen = -(c1 * f + c2 * s)
        out.append(
            on_oxygen + pltpu.roll(on_first, mols, 1) + pltpu.roll(on_second, 2 * mols, 1)
        )
    return out


def steps_kernel(nb, group, lb, mols, slots, b_ref, *refs):
    blocks = refs[:nb]
    step_ref, q_ref, xv = refs[nb : nb + 3]
    beads = nb * lb
    store = Store(refs[nb + 3 :], beads)
    width = group + 2 * P_HALO
    n = 3 * lb
    b = b_ref[0]
    step = step_ref[b]
    charges = Rows(q_ref, b * group + P_HALO)

    def advance(states):
        flat = [
            jnp.concatenate([x, v], axis=0) for pos, vel in states for x, v in zip(pos, vel)
        ]
        high, mid, low = split3(jnp.concatenate(flat, axis=1))
        stacked = jnp.concatenate([high, mid, high, mid, low, high], axis=0).astype(BF16)
        new = dot_nn(step, stacked)
        out = []
        for i in range(len(states)):
            columns = [
                new[:, (3 * i + c) * slots : (3 * i + c + 1) * slots] for c in range(3)
            ]
            out.append(([a[:beads] for a in columns], [a[beads:] for a in columns]))
        return out

    def gather(w, a, comp):
        return jnp.concatenate(
            [block[pl.ds((a * width + w) * n + comp * lb, lb), :] for block in blocks], axis=0
        )

    def kick(state, oxygen, scale):
        pos, vel = state
        force = bond_forces(*pos, oxygen, mols, slots)
        return pos, [v + scale * f for v, f in zip(vel, force)]

    for first in range(0, width, 2):
        members = range(first, min(first + 2, width))
        charge = [charges[w] for w in members]
        oxygen = [(q < -1.5).astype(F32) for q in charge]
        inverse = [jnp.where(q < -1.5, 1.0 / oxygen_mass, 1.0) for q in charge]
        states = [
            (
                [gather(w, 0, c) for c in range(3)],
                [gather(w, 1, c) * scale for c in range(3)],
            )
            for w, scale in zip(members, inverse)
        ]
        for part in (0.5, 1.0):
            states = [
                kick(state, o, (part * inner_step) * scale)
                for state, o, scale in zip(states, oxygen, inverse)
            ]
            states = advance(states)
        for w, state, q, o, scale in zip(members, states, charge, oxygen, inverse):
            if 1 <= w <= width - 2:
                pos, vel = kick(state, o, (0.5 * inner_step) * scale)
                mass = jnp.where(q < -1.5, oxygen_mass, 1.0)
                for c in range(3):
                    xv[w - 1, pl.ds(c * beads, beads), :] = pos[c]
                    xv[w - 1, pl.ds((3 + c) * beads, beads), :] = vel[c] * mass
            build_tiles(store.tiles, w * beads, beads, *state[0])
    prepare(store, charges, width, slots)


def final_kernel(nb, group, lb, mols, slots, b_ref, *refs):
    perm_ref, q_ref, xv = refs[:3]
    beads = nb * lb
    store = Store(refs[3 : 3 + STORE], beads)
    ys = refs[3 + STORE : 3 + STORE + nb]
    forces, keep = refs[3 + STORE + nb :]
    b = b_ref[0]
    charges = Rows(q_ref, b * group + P_HALO)
    loop = PairLoop(mols, slots, beads, keep)
    loop.cells(store, charges, P_HALO, P_HALO + group, forces, 32)
    for w in range(group):
        old = xv[w]
        m = 3 * beads
        force = jnp.concatenate([read_force(forces, w, beads, c) for c in range(3)], axis=0)
        state = jnp.concatenate([old[:m], old[m:] + (0.5 * outer_step) * force], axis=0)
        state = unpermuted(state, perm_ref[b * group + w])
        for a in range(2):
            for c in range(3):
                for k in range(nb):
                    row = (a * 3 + c) * beads + k * lb
                    ys[k][pl.ds(((a * group + w) * 3 + c) * lb, lb), :] = state[row : row + lb]


def unpack_kernel(nb, group, lb, cells, b_ref, *refs):
    ys = refs[:nb]
    outs = refs[nb:]
    b = b_ref[0]
    for i, k in enumerate(block_order(nb)):
        source = jnp.bitwise_xor(b, k)
        for a in range(2):
            for w in range(group):
                for c in range(3):
                    outs[a][pl.ds(c * cells + source * group + w, lb, stride=3 * cells), :] = ys[
                        i
                    ][pl.ds(((a * group + w) * 3 + c) * lb, lb), :]


def call(kernel, outs, scratch, scalar, *operands, space=pltpu.VMEM):
    vmem = pl.BlockSpec(memory_space=pltpu.VMEM)
    smem = pl.BlockSpec(memory_space=pltpu.SMEM)
    return pl.pallas_call(
        kernel,
        out_shape=outs,
        in_specs=([] if scalar is None else [smem]) + [pl.BlockSpec(memory_space=space)] * len(operands),
        out_specs=[vmem] * len(outs),
        scratch_shapes=scratch,
        compiler_params=pltpu.CompilerParams(vmem_limit_bytes=24 * 1024 * 1024),
    )(*(() if scalar is None else (scalar,)), *operands)


def exchange(blocks, nb):
    return [
        lax.ppermute(block, "bead", [(i, i ^ k) for i in range(nb)]) if k else block
        for block, k in zip(blocks, block_order(nb))
    ]


def local(nb, ns, positions, momenta, molecules):
    lb, _, cells, slots = positions.shape
    mols = molecules.shape[1]
    group = cells // nb
    beads = lb * nb
    width = group + 2 * P_HALO
    b = lax.axis_index("bead").astype(jnp.int32).reshape(1)

    def shape(*dims):
        return jax.ShapeDtypeStruct(dims, F32)

    rows = lb * 3 * cells
    xs, ps, perm, charges, ends = call(
        functools.partial(order_kernel, lb, cells, mols, slots),
        [shape(cells, 3 * lb, slots)] * 2
        + [jax.ShapeDtypeStruct((cells, slots, slots), BF16), shape(cells, slots)]
        + [shape(2, 9 * lb + 8, slots)],
        [
            pltpu.VMEM((3, cells, mols), jnp.int32),
            pltpu.VMEM((rows, slots), F32),
            pltpu.VMEM((rows, slots), F32),
            pltpu.VMEM((3, cells, slots), jnp.int32),
            pltpu.SemaphoreType.DMA((3,)),
        ],
        None,
        *(
            pltpu.with_memory_space_constraint(a, pltpu.HBM)
            for a in (
                jnp.transpose(molecules, (2, 0, 1)),
                positions.reshape(rows, slots),
                momenta.reshape(rows, slots),
            )
        ),
        space=pltpu.HBM,
    )
    ends = lax.all_gather(ends, "space")
    q_rows = -(-(cells + 2 * X_HALO) // 8) * 8

    def store(count, store_beads):
        return [
            jax.ShapeDtypeStruct(*entry) for entry in store_shapes(count, store_beads, slots)
        ]

    keep = pltpu.VMEM((slots, slots), F32)
    own = call(
        functools.partial(own_kernel, cells, lb, slots), store(cells, lb), [], None, xs, charges
    )
    (inner,) = call(
        functools.partial(interior_kernel, cells, lb, mols, slots),
        [shape((cells - 2) * lb * 8, slots)],
        [keep],
        None,
        charges,
        *own,
    )
    *blocks, q_wide = call(
        functools.partial(edge_kernel, nb, group, lb, cells, mols, slots),
        [shape(2 * width * 3 * lb, slots)] * nb + [shape(q_rows, slots)],
        [
            pltpu.VMEM((cells + 2 * P_HALO, 3 * lb, slots), F32),
            pltpu.VMEM((4 * lb * 8, slots), F32),
            keep,
        ]
        + [pltpu.VMEM(*entry) for entry in store_shapes(4, lb, slots)],
        jnp.stack([lax.axis_index(a).astype(jnp.int32) for a in ("bead", "space")]),
        xs,
        ps,
        charges,
        ends,
        inner,
        *own,
    )
    blocks = exchange(blocks, nb)
    step = jnp.asarray(propagator(beads, lb))
    xv, *stepped = call(
        functools.partial(steps_kernel, nb, group, lb, mols, slots),
        [shape(group, 6 * beads, slots)] + store(width, beads),
        [],
        b,
        *blocks,
        step,
        q_wide,
    )
    ys = call(
        functools.partial(final_kernel, nb, group, lb, mols, slots),
        [shape(2 * group * 3 * lb, slots)] * nb,
        [pltpu.VMEM((group * beads * 8, slots), F32), keep],
        b,
        perm,
        q_wide,
        xv,
        *stepped,
    )
    ys = exchange(ys, nb)
    new_x, new_p = call(
        functools.partial(unpack_kernel, nb, group, lb, cells),
        [shape(lb * 3 * cells, slots)] * 2,
        [],
        b,
        *ys,
    )
    return new_x.reshape(positions.shape), new_p.reshape(positions.shape)


def solution(mesh):
    spec = P("bead", None, "space", None)
    return jax.shard_map(
        functools.partial(local, mesh.shape["bead"], mesh.shape["space"]),
        mesh=mesh,
        in_specs=(spec, spec, P("space", None, None)),
        out_specs=(spec, spec),
        check_vma=False,
    )
```

```python
import functools

import jax
import jax.numpy as jnp
import ml_dtypes
import numpy as np
from jax import lax
from jax.experimental import pallas as pl
from jax.experimental.pallas import tpu as pltpu
from jax.sharding import PartitionSpec as P

charge_oxygen = -0.8476
charge_hydrogen = 0.4238
coulomb_scale = 24.0
coulomb_soft = 0.004
well_depth = 0.02
sigma_square = 0.0841
lennard_soft = 0.04
bond_stiffness = 20000.0
bond_square = 0.0081
angle_stiffness = 5000.0
angle_square = 0.0204
cycle_frequency = 60.0
outer_step = 0.02
inner_step = 0.01
oxygen_mass = 16.0

REACH = 1
X_HALO = 2 * REACH
P_HALO = REACH

F32 = jnp.float32
BF16 = jnp.bfloat16


def rounded(a):
    return a.astype(BF16).astype(F32)


def split3(a):
    high = rounded(a)
    rest = a - high
    mid = rounded(rest)
    return high, mid, rest - mid


def two_part(a):
    high = rounded(a)
    return high + rounded(a - high)


def dot_nn(a, b):
    return lax.dot_general(a, b, (((1,), (0,)), ((), ())), preferred_element_type=F32)


def dot_nt(a, b):
    return lax.dot_general(a, b, (((1,), (1,)), ((), ())), preferred_element_type=F32)


def block_order(nb):
    return sorted(range(nb), key=lambda k: (k > 0, -bin(k).count("1"), k))


def propagator(beads, beads_dev):
    j = np.arange(beads)
    angles = 2.0 * np.pi * ((j[:, None] * j[None, :]) % beads) / beads
    half = beads // 2
    col = j[None, :]
    u = np.where(
        col == 0,
        np.sqrt(1.0 / beads),
        np.where(
            col < half,
            np.sqrt(2.0 / beads) * np.cos(angles),
            np.where(
                col == half,
                np.sqrt(1.0 / beads) * np.cos(angles),
                np.sqrt(2.0 / beads) * np.sin(angles),
            ),
        ),
    )
    w = 2.0 * cycle_frequency * np.sin(np.pi * j / beads)
    cosines = np.cos(w * inner_step)
    spring = w * np.sin(w * inner_step)
    drift = np.where(j == 0, inner_step, np.sin(w * inner_step) / np.where(j == 0, 1.0, w))
    def circulant(values, bead):
        first = ((u * values) @ u.T)[:, 0]
        return first[(bead[:, None] - bead[None, :]) % beads]

    out = []
    for b in range(beads // beads_dev):
        block = np.array(block_order(beads // beads_dev))[j // beads_dev]
        bead = (block ^ b) * beads_dev + j % beads_dev
        a = circulant(cosines, bead)
        whole = np.block([[a, circulant(drift, bead)], [-circulant(spring, bead), a]])
        high = whole.astype(ml_dtypes.bfloat16)
        rest = whole - high.astype(np.float64)
        mid = rest.astype(ml_dtypes.bfloat16)
        low = (rest - mid.astype(np.float64)).astype(ml_dtypes.bfloat16)
        out.append(np.concatenate([high, high, mid, mid, high, low], axis=1))
    return np.stack(out)


def lane_tables(lanes, mols, slots):
    lane = lax.broadcasted_iota(jnp.int32, lanes.shape, 1)
    unit = jnp.where(lane < mols, charge_oxygen / charge_hydrogen, 1.0)
    return jnp.where(lanes < slots, unit, 0.0)


def permuted(rows, perm):
    n = rows.shape[0]
    stacked = jnp.concatenate(split3(rows), axis=0).astype(BF16)
    moved = dot_nn(stacked, perm)
    return moved[:n] + moved[n : 2 * n] + moved[2 * n :]


def unpermuted(rows, perm):
    n = rows.shape[0]
    stacked = jnp.concatenate(split3(rows), axis=0).astype(BF16)
    moved = dot_nt(stacked, perm)
    return moved[:n] + moved[n : 2 * n] + moved[2 * n :]


def order_kernel(lb, cells, mols, slots, mol_hbm, x_hbm, p_hbm, *refs):
    xo, po, perm_ref, q_ref, to_right, to_left = refs[:6]
    mol_ref, x_ref, p_ref, wide, sems = refs[6:]
    copies = [
        pltpu.make_async_copy(source, dest, sems.at[i])
        for i, (source, dest) in enumerate(
            ((mol_hbm, mol_ref), (x_hbm, x_ref), (p_hbm, p_ref))
        )
    ]
    for copy in copies:
        copy.start()
    row = lax.broadcasted_iota(jnp.int32, (slots, slots), 0)
    col = lax.broadcasted_iota(jnp.int32, (slots, slots), 1)
    upper = (row < col).astype(F32).astype(BF16)
    rows, row = row, row.astype(F32)
    lane = lax.broadcasted_iota(jnp.int32, (cells, slots), 1)
    far = 4.0 * slots
    wide[...] = jnp.full(wide.shape, slots, jnp.int32)
    copies[0].wait()
    for t in range(3):
        wide[t, :, :mols] = mol_ref[t]
    lanes = jnp.where(
        lane < mols,
        wide[0],
        jnp.where(lane < 2 * mols, pltpu.roll(wide[1], mols, 1), pltpu.roll(wide[2], 2 * mols, 1)),
    )
    lanes = jnp.where(lane < 3 * mols, lanes, slots)
    charges = lane_tables(lanes, mols, slots)
    q_ref[...] = charges
    free = lanes >= slots
    key = jnp.where(
        free, far + dot_nn(free.astype(F32).astype(BF16), upper), lanes.astype(F32)
    )
    ones = jnp.ones((slots, slots), BF16)
    used = jnp.zeros((slots, slots), F32)
    for cell in range(cells):
        held = (row == key[cell : cell + 1]).astype(F32).astype(BF16)
        used = jnp.where(col == cell, dot_nn(held, ones), used)
    rank = dot_nn((col < rows).astype(F32).astype(BF16), (1.0 - used).astype(BF16))
    slot_key = jnp.where(used > 0.5, row, far + rank)
    copies[1].wait()
    copies[2].wait()
    n = 3 * lb
    for cell in range(cells):
        slot_column = jnp.broadcast_to(slot_key[:, cell : cell + 1], (slots, slots))
        perm = (slot_column == key[cell : cell + 1]).astype(F32).astype(BF16)
        perm_ref[cell] = perm
        atoms = [
            ref[pl.ds(comp * cells + cell, lb, stride=3 * cells), :]
            for ref in (x_ref, p_ref)
            for comp in range(3)
        ]
        moved = permuted(jnp.concatenate(atoms, axis=0), perm)
        xo[cell] = moved[:n]
        po[cell] = moved[n:]
    for out, xs, ps in (
        (to_right, (cells - 2, cells - 1), cells - 1),
        (to_left, (0, 1), 0),
    ):
        out[9 * lb :, :] = jnp.zeros((8, slots), F32)
        for e, cell in enumerate(xs):
            out[pl.ds(e * n, n), :] = xo[cell]
            out[pl.ds(9 * lb + e, 1), :] = charges[cell : cell + 1]
        out[pl.ds(2 * n, n), :] = po[ps]


def put_tiles(scratch, first, count, rows):
    for index, value in rows:
        scratch[pl.ds(first * 8 + index, count, stride=8), :] = value


OFFSETS = (-1.0, 0.0, 1.0)


def build_tiles(tiles, first, count, x, y, z):
    x, y, z = two_part(x - 0.5), two_part(y - 0.5), two_part(z - 0.5)
    norm = x * x + y * y + z * z + 0.5 * coulomb_soft
    high = two_part(norm)
    low = norm - high
    put_tiles(
        tiles, first, count, ((0, x), (1, y), (2, z), (3, high), (4, low), (5, high), (6, low))
    )


def store_shapes(count, beads, slots):
    n = count * beads
    return (
        [((n * 8, slots), F32), ((n // 2, slots, 64), BF16)]
        + [((n // 2, 32, slots), BF16)] * 3
        + [((n, 32, slots), BF16)]
    )


STORE = 6


class Store:
    def __init__(self, refs, beads):
        self.tiles, self.peers, *sums, self.targets = refs
        self.sums = sums
        self.beads = beads


def tile_of(ref, n):
    return ref[pl.ds(pl.multiple_of(n * 8, 8), 8), :]


def prepare(store, charges, count, slots):
    tiles, beads = store.tiles, store.beads
    row8 = lax.broadcasted_iota(jnp.int32, (8, slots), 0)
    place, norms = row8 < 3, row8 < 5
    target_rows = place | (row8 == 5) | (row8 == 6)
    ones_low = jnp.where((row8 == 3) | (row8 == 4), 1.0, 0.0)
    ones_high = jnp.where((row8 == 5) | (row8 == 6), 1.0, 0.0)
    ones_last = jnp.where(row8 == 7, 1.0, 0.0)
    pairs = beads // 2
    total = count * pairs
    unroll = max(n for n in range(1, max(2, min(17, total // 4 + 1))) if total % n == 0)

    def stack(values):
        return jnp.concatenate(values, axis=0).astype(BF16)

    def step(index, carry):
        for u in range(unroll):
            m = index * unroll + u
            charge = charges[lax.div(m, pairs)]
            units = [
                jnp.where(row8 == 3, charge, jnp.where(row8 == 4, offset * charge, 0.0))
                for offset in OFFSETS
            ]
            left, high_rows, mid_rows = [], [], []
            for h in range(2):
                value = tile_of(tiles, 2 * m + h)
                high = rounded(value)
                mid = value - high
                x_high, x_mid = high[0:1], mid[0:1]
                left_high = jnp.where(place, -2.0 * high, jnp.where(norms, high, ones_high))
                left_mid = jnp.where(place, -2.0 * mid, jnp.where(norms, mid, 0.0))
                left_last = jnp.where(
                    place,
                    -2.0 * mid,
                    jnp.where(
                        row8 == 3,
                        2.0 * x_high,
                        jnp.where(row8 == 4, 2.0 * x_mid, ones_last - 2.0 * ones_high),
                    ),
                )
                left += [left_high, left_high, left_mid, left_last]
                right_high = jnp.where(target_rows, high, ones_low)
                right_mid = jnp.where(target_rows, mid, 0.0)
                right_last = jnp.where(
                    place,
                    mid,
                    jnp.where(
                        row8 == 5, x_high, jnp.where(row8 == 6, x_mid, ones_low + ones_last)
                    ),
                )
                store.targets[2 * m + h] = stack([right_high, right_mid, right_high, right_last])
                high_rows.append(high * charge)
                mid_rows.append(jnp.where(place, mid * charge, 0.0))
            store.peers[m] = stack(left).T
            for o in range(3):
                rows = []
                for h in range(2):
                    rows += [jnp.where(place, high_rows[h], units[o]), mid_rows[h]]
                store.sums[o][m] = stack(rows)
        return carry

    lax.fori_loop(0, total // unroll, step, 0)


class PairLoop:
    def __init__(self, mols, slots, beads, keep):
        self.mols, self.slots, self.keep = mols, slots, keep
        self.pairs = beads // 2
        self.unroll = min(self.pairs, 4)
        self.per_cell = self.pairs // self.unroll
        orows = -(-mols // 8) * 8
        self.row8 = lax.broadcasted_iota(jnp.int32, (8, slots), 0)
        lj_row = lax.broadcasted_iota(jnp.int32, (orows, slots), 0)
        lj_lane = lax.broadcasted_iota(jnp.int32, (orows, slots), 1)
        self.first_lanes, self.second_lanes = lj_lane < mols, lj_lane < 2 * mols
        self.corner = (lj_row < mols) & self.first_lanes

        i = lax.broadcasted_iota(jnp.int32, (slots, slots), 0)
        j = lax.broadcasted_iota(jnp.int32, (slots, slots), 1)
        i = jnp.where(i >= 2 * mols, i - 2 * mols, jnp.where(i >= mols, i - mols, i))
        j = jnp.where(j >= 2 * mols, j - 2 * mols, jnp.where(j >= mols, j - mols, j))
        keep[...] = (i != j).astype(F32)

        lane64 = lax.broadcasted_iota(jnp.int32, (slots, 64), 1) & 31
        odd = (lane64 >= 27) & (lane64 < 31)
        even = lane64 == 31
        self.signs = [
            jnp.where(odd, -1.0, 1.0).astype(BF16),
            jnp.where(odd | even, 0.0, 1.0).astype(BF16),
            None,
        ]
        self.zero = jnp.zeros((32, slots), BF16)

    def pair(self, peers, charge):
        mols, slots = self.mols, self.slots
        orows = self.corner.shape[0]
        pair_scale = coulomb_scale * charge_hydrogen * charge_hydrogen
        k3 = sigma_square**3
        ratio = (charge_hydrogen / charge_oxygen) ** 2 / pair_scale
        lj_a = 24.0 * well_depth * 2.0 * k3 * k3 * ratio
        lj_b = 24.0 * well_depth * k3 * ratio
        zero = self.zero
        own, m = peers[1]
        left = jnp.concatenate(
            [
                store.peers[index] if sign is None else store.peers[index] * sign
                for (store, index), sign in zip(peers, self.signs)
            ],
            axis=0,
        )
        right = jnp.concatenate(
            [
                jnp.concatenate([own.targets[2 * m], zero], axis=1),
                jnp.concatenate([zero, own.targets[2 * m + 1]], axis=1),
            ],
            axis=0,
        )
        squares = dot_nn(left, right)
        blocks = [[], [], []]
        for h in range(2):
            lanes = slice(h * slots, (h + 1) * slots)
            near = [squares[o * slots : o * slots + orows, lanes] for o in range(3)]
            packed = jnp.where(
                self.first_lanes,
                near[0],
                jnp.where(
                    self.second_lanes,
                    pltpu.roll(near[1], mols, 1),
                    pltpu.roll(near[2], 2 * mols, 1),
                ),
            )
            root = lax.rsqrt(packed + (lennard_soft - coulomb_soft))
            inverse = root * root
            cube = inverse * inverse * inverse
            lj = (cube * lj_a - lj_b) * (cube * inverse)
            for o in range(3):
                root = lax.rsqrt(squares[o * slots : (o + 1) * slots, lanes])
                strength = root * root * root
                part = pltpu.roll(lj, slots - o * mols, 1) if o else lj
                strength = jnp.concatenate(
                    [strength[:orows] + jnp.where(self.corner, part, 0.0), strength[orows:]],
                    axis=0,
                )
                if o == 1:
                    strength = strength * self.keep[...]
                high = strength.astype(BF16)
                low = (strength - high.astype(F32)).astype(BF16)
                blocks[o].append(jnp.concatenate([high, low], axis=0))
        sums = None
        for o, (store, index) in enumerate(peers):
            weights = store.sums[o][index]
            value = dot_nn(
                jnp.concatenate([weights, weights], axis=1), jnp.concatenate(blocks[o], axis=1)
            )
            sums = value if sums is None else sums + value
        scale = charge * pair_scale
        out = []
        for h in range(2):
            part = sums[16 * h : 16 * h + 16, h * slots : (h + 1) * slots]
            total = part[0:8] + part[8:16]
            total = total + jnp.where(self.row8 == 0, total[4:5], 0.0)
            out.append((tile_of(own.tiles, 2 * m + h) * total[3:4] - total) * scale)
        return out

    def cells(self, store, charges, first, last, forces, limit):
        total = (last - first) * self.pairs
        unroll = max(n for n in range(1, limit + 1) if total % n == 0)

        def step(index, carry):
            for u in range(unroll):
                m = index * unroll + u
                at = m + first * self.pairs
                peers = [(store, at + (o - 1) * self.pairs) for o in range(3)]
                out = self.pair(peers, charges[lax.div(at, self.pairs)])
                for h in range(2):
                    n = 2 * m + h
                    forces[pl.ds(pl.multiple_of(n * 8, 8), 8), :] = out[h]
            return carry

        lax.fori_loop(0, total // unroll, step, 0)

    def some(self, store, charges, first, last, pairs, forces):
        index = 0
        for w in range(first, last):
            for pair in pairs:
                at = w * self.pairs + pair
                peers = [(store, at + (o - 1) * self.pairs) for o in range(3)]
                for value in self.pair(peers, charges[w]):
                    forces[pl.ds(8 * index, 8), :] = value
                    index += 1


def read_force(forces, w, beads, comp):
    return forces[pl.ds(w * beads * 8 + comp, beads, stride=8), :]


def own_kernel(cells, lb, slots, x_ref, q_ref, *refs):
    store = Store(refs, lb)
    for w in range(cells):
        rows = x_ref[w]
        build_tiles(store.tiles, w * lb, lb, rows[:lb], rows[lb : 2 * lb], rows[2 * lb :])
    prepare(store, Rows(q_ref, 0), cells, slots)


def interior_kernel(cells, lb, mols, slots, q_ref, *refs):
    store = Store(refs[:STORE], lb)
    forces, keep = refs[STORE:]
    PairLoop(mols, slots, lb, keep).cells(store, Rows(q_ref, 0), 1, cells - 1, forces, 64)


def edge_kernel(nb, group, lb, cells, mols, slots, b_ref, *refs):
    x_ref, p_ref, q_ref, left, right, inner = refs[:6]
    own = Store(refs[6 : 6 + STORE], lb)
    refs = refs[6 + STORE :]
    outs, q_out = refs[:nb], refs[nb]
    kicked, halo_forces, keep = refs[nb + 1 : nb + 4]
    halo = Store(refs[nb + 4 :], lb)
    n = 3 * lb
    count = cells + 2 * X_HALO
    b = b_ref[0]

    charge_rows = [left[pl.ds(9 * lb + e, 1), :] for e in range(2)]
    charge_rows += [q_ref[c : c + 1, :] for c in range(cells)]
    charge_rows += [right[pl.ds(9 * lb + e, 1), :] for e in range(2)]
    q_out[...] = jnp.zeros(q_out.shape, F32)
    for w in range(count):
        q_out[w : w + 1, :] = charge_rows[w]
    for e in range(4):
        edge = (left, right)[e // 2]
        rows = edge[pl.ds((e % 2) * n, n), :]
        build_tiles(halo.tiles, e * lb, lb, rows[:lb], rows[lb : 2 * lb], rows[2 * lb :])

    class Edges:
        def __getitem__(self, e):
            return q_out[pl.ds(jnp.where(e < 2, e, e + cells), 1), :]

    prepare(halo, Edges(), 4, slots)
    loop = PairLoop(mols, slots, lb, keep)

    def place(w):
        if w < X_HALO:
            return halo, w
        if w >= cells + X_HALO:
            return halo, w - cells
        return own, w - X_HALO

    targets = (1, 2, cells + 1, cells + 2)

    def edge_step(step, carry):
        for e, w in enumerate(targets):
            for u in range(loop.unroll):
                index = step * loop.unroll + u
                peers = [
                    (store, cell * loop.pairs + index) for store, cell in map(place, (w - 1, w, w + 1))
                ]
                out = loop.pair(peers, charge_rows[w])
                for h in range(2):
                    at = (e * lb + 2 * index + h) * 8
                    halo_forces[pl.ds(pl.multiple_of(at, 8), 8), :] = out[h]
        return carry

    lax.fori_loop(0, loop.per_cell, edge_step, 0)
    half = 0.5 * outer_step
    for w in range(1, count - 1):
        if w < X_HALO:
            old = left[pl.ds(2 * n, n), :]
        elif w >= cells + X_HALO:
            old = right[pl.ds(2 * n, n), :]
        else:
            old = p_ref[w - X_HALO]
        source, cell = (
            (halo_forces, targets.index(w)) if w in targets else (inner, w - X_HALO - 1)
        )
        force = jnp.concatenate([read_force(source, cell, lb, c) for c in range(3)], axis=0)
        kicked[w - 1] = old + half * force
    width = group + 2 * P_HALO
    for i, k in enumerate(block_order(nb)):
        first = jnp.bitwise_xor(b, k) * group
        for w in range(width):
            outs[i][pl.ds((width + w) * n, n), :] = kicked[first + w]
            source = first + w - P_HALO
            inside = x_ref[jnp.clip(source, 0, cells - 1)]
            if w < P_HALO:
                inside = jnp.where(source < 0, left[pl.ds(n, n), :], inside)
            elif w >= group + P_HALO:
                inside = jnp.where(source >= cells, right[pl.ds(0, n), :], inside)
            outs[i][pl.ds(w * n, n), :] = inside


class Rows:
    def __init__(self, ref, first):
        self.ref, self.first = ref, first

    def __getitem__(self, index):
        return self.ref[pl.ds(self.first + index, 1), :]


def bond_forces(x, y, z, used, mols, slots):
    def partner(a, t):
        return pltpu.roll(a, slots - t * mols, 1)

    first = [a - partner(a, 1) for a in (x, y, z)]
    second = [a - partner(a, 2) for a in (x, y, z)]
    third = [s - f for f, s in zip(first, second)]

    def pull(bond, stiffness, square):
        length = bond[0] * bond[0] + bond[1] * bond[1] + bond[2] * bond[2]
        return (stiffness * used) * (length - square)

    c1 = pull(first, bond_stiffness, bond_square)
    c2 = pull(second, bond_stiffness, bond_square)
    c3 = pull(third, angle_stiffness, angle_square)
    out = []
    for f, s, t in zip(first, second, third):
        on_first = c1 * f - c3 * t
        on_second = c2 * s + c3 * t
        on_oxygen = -(c1 * f + c2 * s)
        out.append(
            on_oxygen + pltpu.roll(on_first, mols, 1) + pltpu.roll(on_second, 2 * mols, 1)
        )
    return out


def steps_kernel(nb, group, lb, mols, slots, b_ref, *refs):
    blocks = refs[:nb]
    step_ref, q_ref, xv = refs[nb : nb + 3]
    beads = nb * lb
    store = Store(refs[nb + 3 :], beads)
    width = group + 2 * P_HALO
    n = 3 * lb
    b = b_ref[0]
    step = step_ref[b]
    charges = Rows(q_ref, b * group + P_HALO)

    def advance(states):
        flat = [
            jnp.concatenate([x, v], axis=0) for pos, vel in states for x, v in zip(pos, vel)
        ]
        high, mid, low = split3(jnp.concatenate(flat, axis=1))
        stacked = jnp.concatenate([high, mid, high, mid, low, high], axis=0).astype(BF16)
        new = dot_nn(step, stacked)
        out = []
        for i in range(len(states)):
            columns = [
                new[:, (3 * i + c) * slots : (3 * i + c + 1) * slots] for c in range(3)
            ]
            out.append(([a[:beads] for a in columns], [a[beads:] for a in columns]))
        return out

    def gather(w, a, comp):
        return jnp.concatenate(
            [block[pl.ds((a * width + w) * n + comp * lb, lb), :] for block in blocks], axis=0
        )

    def kick(state, oxygen, scale):
        pos, vel = state
        force = bond_forces(*pos, oxygen, mols, slots)
        return pos, [v + scale * f for v, f in zip(vel, force)]

    for first in range(0, width, 2):
        members = range(first, min(first + 2, width))
        charge = [charges[w] for w in members]
        oxygen = [(q < -1.5).astype(F32) for q in charge]
        inverse = [jnp.where(q < -1.5, 1.0 / oxygen_mass, 1.0) for q in charge]
        states = [
            (
                [gather(w, 0, c) for c in range(3)],
                [gather(w, 1, c) * scale for c in range(3)],
            )
            for w, scale in zip(members, inverse)
        ]
        for part in (0.5, 1.0):
            states = [
                kick(state, o, (part * inner_step) * scale)
                for state, o, scale in zip(states, oxygen, inverse)
            ]
            states = advance(states)
        for w, state, q, o, scale in zip(members, states, charge, oxygen, inverse):
            if 1 <= w <= width - 2:
                pos, vel = kick(state, o, (0.5 * inner_step) * scale)
                mass = jnp.where(q < -1.5, oxygen_mass, 1.0)
                for c in range(3):
                    xv[w - 1, pl.ds(c * beads, beads), :] = pos[c]
                    xv[w - 1, pl.ds((3 + c) * beads, beads), :] = vel[c] * mass
            build_tiles(store.tiles, w * beads, beads, *state[0])
    prepare(store, charges, width, slots)


def final_kernel(nb, group, lb, mols, slots, which, b_ref, *refs):
    perm_ref, q_ref, xv = refs[:3]
    beads = nb * lb
    store = Store(refs[3 : 3 + STORE], beads)
    ys = refs[3 + STORE : 3 + STORE + len(which)]
    forces, keep = refs[3 + STORE + len(which) :]
    b = b_ref[0]
    charges = Rows(q_ref, b * group + P_HALO)
    loop = PairLoop(mols, slots, beads, keep)
    pairs = [i * (lb // 2) + u for i in which for u in range(lb // 2)]
    loop.some(store, charges, P_HALO, P_HALO + group, pairs, forces)
    some = len(which) * lb
    for w in range(group):
        rows = []
        for a in range(2):
            for c in range(3):
                old = [xv[w, pl.ds((a * 3 + c) * beads + i * lb, lb), :] for i in which]
                old = jnp.concatenate(old, axis=0)
                if a:
                    old = old + (0.5 * outer_step) * read_force(forces, w, some, c)
                rows.append(old)
        state = unpermuted(jnp.concatenate(rows, axis=0), perm_ref[b * group + w])
        for a in range(2):
            for c in range(3):
                for i in range(len(which)):
                    row = (a * 3 + c) * some + i * lb
                    ys[i][pl.ds(((a * group + w) * 3 + c) * lb, lb), :] = state[row : row + lb]


def unpack_kernel(nb, group, lb, cells, b_ref, *refs):
    ys = refs[:nb]
    outs = refs[nb:]
    b = b_ref[0]
    for i, k in enumerate(block_order(nb)):
        source = jnp.bitwise_xor(b, k)
        for a in range(2):
            for w in range(group):
                for c in range(3):
                    outs[a][pl.ds(c * cells + source * group + w, lb, stride=3 * cells), :] = ys[
                        i
                    ][pl.ds(((a * group + w) * 3 + c) * lb, lb), :]


def call(kernel, outs, scratch, scalar, *operands, space=pltpu.VMEM, flops=0):
    vmem = pl.BlockSpec(memory_space=pltpu.VMEM)
    smem = pl.BlockSpec(memory_space=pltpu.SMEM)
    return pl.pallas_call(
        kernel,
        out_shape=outs,
        in_specs=([] if scalar is None else [smem]) + [pl.BlockSpec(memory_space=space)] * len(operands),
        out_specs=[vmem] * len(outs),
        scratch_shapes=scratch,
        cost_estimate=(
            pl.CostEstimate(flops=flops, bytes_accessed=0, transcendentals=0) if flops else None
        ),
        compiler_params=pltpu.CompilerParams(vmem_limit_bytes=24 * 1024 * 1024),
    )(*(() if scalar is None else (scalar,)), *operands)


def exchange(blocks, nb, order):
    return [
        lax.ppermute(block, "bead", [(i, i ^ k) for i in range(nb)]) if k else block
        for block, k in zip(blocks, order)
    ]


def local(nb, ns, positions, momenta, molecules):
    lb, _, cells, slots = positions.shape
    mols = molecules.shape[1]
    group = cells // nb
    beads = lb * nb
    width = group + 2 * P_HALO
    b = lax.axis_index("bead").astype(jnp.int32).reshape(1)

    def shape(*dims):
        return jax.ShapeDtypeStruct(dims, F32)

    edge = shape(9 * lb + 8, slots)
    rows = lb * 3 * cells
    xs, ps, perm, charges, to_right, to_left = call(
        functools.partial(order_kernel, lb, cells, mols, slots),
        [shape(cells, 3 * lb, slots)] * 2
        + [jax.ShapeDtypeStruct((cells, slots, slots), BF16), shape(cells, slots), edge, edge],
        [
            pltpu.VMEM((3, cells, mols), jnp.int32),
            pltpu.VMEM((rows, slots), F32),
            pltpu.VMEM((rows, slots), F32),
            pltpu.VMEM((3, cells, slots), jnp.int32),
            pltpu.SemaphoreType.DMA((3,)),
        ],
        None,
        *(
            pltpu.with_memory_space_constraint(a, pltpu.HBM)
            for a in (
                jnp.transpose(molecules, (2, 0, 1)),
                positions.reshape(rows, slots),
                momenta.reshape(rows, slots),
            )
        ),
        space=pltpu.HBM,
    )
    left = lax.ppermute(to_right, "space", [(s, (s + 1) % ns) for s in range(ns)])
    right = lax.ppermute(to_left, "space", [(s, (s - 1) % ns) for s in range(ns)])
    q_rows = -(-(cells + 2 * X_HALO) // 8) * 8

    def store(count, store_beads):
        return [
            jax.ShapeDtypeStruct(*entry) for entry in store_shapes(count, store_beads, slots)
        ]

    keep = pltpu.VMEM((slots, slots), F32)
    own = call(
        functools.partial(own_kernel, cells, lb, slots), store(cells, lb), [], None, xs, charges
    )
    (inner,) = call(
        functools.partial(interior_kernel, cells, lb, mols, slots),
        [shape((cells - 2) * lb * 8, slots)],
        [keep],
        None,
        charges,
        *own,
    )
    *blocks, q_wide = call(
        functools.partial(edge_kernel, nb, group, lb, cells, mols, slots),
        [shape(2 * width * 3 * lb, slots)] * nb + [shape(q_rows, slots)],
        [
            pltpu.VMEM((cells + 2 * P_HALO, 3 * lb, slots), F32),
            pltpu.VMEM((4 * lb * 8, slots), F32),
            keep,
        ]
        + [pltpu.VMEM(*entry) for entry in store_shapes(4, lb, slots)],
        b,
        xs,
        ps,
        charges,
        left,
        right,
        inner,
        *own,
    )
    blocks = exchange(blocks, nb, block_order(nb))
    step = jnp.asarray(propagator(beads, lb))
    xv, *stepped = call(
        functools.partial(steps_kernel, nb, group, lb, mols, slots),
        [shape(group, 6 * beads, slots)] + store(width, beads),
        [],
        b,
        *blocks,
        step,
        q_wide,
    )
    order = block_order(nb)
    early = list(range(1, nb // 2 + 1))
    late = [0] + list(range(nb // 2 + 1, nb))
    ys = [None] * nb
    for which in (early, late):
        out = call(
            functools.partial(final_kernel, nb, group, lb, mols, slots, which),
            [shape(2 * group * 3 * lb, slots)] * len(which),
            [pltpu.VMEM((group * len(which) * lb * 8, slots), F32), keep],
            b,
            perm,
            q_wide,
            xv,
            *stepped,
            flops=group * len(which) * lb * 3 * slots * slots * 1024,
        )
        arrived = [block for block in ys if block is not None]
        out, xv, arrived = lax.optimization_barrier((out, xv, arrived))
        for i, block in zip([i for i in range(nb) if ys[i] is not None], arrived):
            ys[i] = block
        for i, block in zip(which, exchange(out, nb, [order[i] for i in which])):
            ys[i] = block
    new_x, new_p = call(
        functools.partial(unpack_kernel, nb, group, lb, cells),
        [shape(lb * 3 * cells, slots)] * 2,
        [],
        b,
        *ys,
    )
    return new_x.reshape(positions.shape), new_p.reshape(positions.shape)


def solution(mesh):
    spec = P("bead", None, "space", None)
    return jax.shard_map(
        functools.partial(local, mesh.shape["bead"], mesh.shape["space"]),
        mesh=mesh,
        in_specs=(spec, spec, P("space", None, None)),
        out_specs=(spec, spec),
        check_vma=False,
    )
```

```python
import functools

import jax
import jax.numpy as jnp
import ml_dtypes
import numpy as np
from jax import lax
from jax.experimental import pallas as pl
from jax.experimental.pallas import tpu as pltpu
from jax.sharding import PartitionSpec as P

charge_oxygen = -0.8476
charge_hydrogen = 0.4238
coulomb_scale = 24.0
coulomb_soft = 0.004
well_depth = 0.02
sigma_square = 0.0841
lennard_soft = 0.04
bond_stiffness = 20000.0
bond_square = 0.0081
angle_stiffness = 5000.0
angle_square = 0.0204
cycle_frequency = 60.0
outer_step = 0.02
inner_step = 0.01
oxygen_mass = 16.0

F32 = jnp.float32
BF16 = jnp.bfloat16


def rounded(a):
    return a.astype(BF16).astype(F32)


def split3(a):
    high = rounded(a)
    rest = a - high
    mid = rounded(rest)
    return high, mid, rest - mid


def two_part(a):
    high = rounded(a)
    return high + rounded(a - high)


def dot_nn(a, b):
    return lax.dot_general(a, b, (((1,), (0,)), ((), ())), preferred_element_type=F32)


def dot_nt(a, b):
    return lax.dot_general(a, b, (((1,), (1,)), ((), ())), preferred_element_type=F32)


def block_order(nb):
    return sorted(range(nb), key=lambda k: (k > 0, -bin(k).count("1"), k))


def propagator(beads, beads_dev):
    j = np.arange(beads)
    angles = 2.0 * np.pi * ((j[:, None] * j[None, :]) % beads) / beads
    half = beads // 2
    col = j[None, :]
    u = np.where(
        col == 0,
        np.sqrt(1.0 / beads),
        np.where(
            col < half,
            np.sqrt(2.0 / beads) * np.cos(angles),
            np.where(
                col == half,
                np.sqrt(1.0 / beads) * np.cos(angles),
                np.sqrt(2.0 / beads) * np.sin(angles),
            ),
        ),
    )
    w = 2.0 * cycle_frequency * np.sin(np.pi * j / beads)
    cosines = np.cos(w * inner_step)
    spring = w * np.sin(w * inner_step)
    drift = np.where(j == 0, inner_step, np.sin(w * inner_step) / np.where(j == 0, 1.0, w))
    def circulant(values, bead):
        first = ((u * values) @ u.T)[:, 0]
        return first[(bead[:, None] - bead[None, :]) % beads]

    out = []
    for b in range(beads // beads_dev):
        block = np.array(block_order(beads // beads_dev))[j // beads_dev]
        bead = (block ^ b) * beads_dev + j % beads_dev
        a = circulant(cosines, bead)
        whole = np.block([[a, circulant(drift, bead)], [-circulant(spring, bead), a]])
        high = whole.astype(ml_dtypes.bfloat16)
        rest = whole - high.astype(np.float64)
        mid = rest.astype(ml_dtypes.bfloat16)
        low = (rest - mid.astype(np.float64)).astype(ml_dtypes.bfloat16)
        out.append(np.concatenate([high, high, mid, mid, high, low], axis=1))
    return np.stack(out)


def lane_tables(lanes, mols, slots):
    lane = lax.broadcasted_iota(jnp.int32, lanes.shape, 1)
    unit = jnp.where(lane < mols, charge_oxygen / charge_hydrogen, 1.0)
    return jnp.where(lanes < slots, unit, 0.0)


def permuted(rows, perm):
    n = rows.shape[0]
    stacked = jnp.concatenate(split3(rows), axis=0).astype(BF16)
    moved = dot_nn(stacked, perm)
    return moved[:n] + moved[n : 2 * n] + moved[2 * n :]


def unpermuted(rows, perm):
    n = rows.shape[0]
    stacked = jnp.concatenate(split3(rows), axis=0).astype(BF16)
    moved = dot_nt(stacked, perm)
    return moved[:n] + moved[n : 2 * n] + moved[2 * n :]


def order_kernel(lb, cells, mols, slots, mol_hbm, x_hbm, p_hbm, *refs):
    xo, po, perm_ref, q_ref, to_right, to_left = refs[:6]
    mol_ref, x_ref, p_ref, wide, sems = refs[6:]
    copies = [
        pltpu.make_async_copy(source, dest, sems.at[i])
        for i, (source, dest) in enumerate(
            ((mol_hbm, mol_ref), (x_hbm, x_ref), (p_hbm, p_ref))
        )
    ]
    for copy in copies:
        copy.start()
    row = lax.broadcasted_iota(jnp.int32, (slots, slots), 0)
    col = lax.broadcasted_iota(jnp.int32, (slots, slots), 1)
    upper = (row < col).astype(F32).astype(BF16)
    rows, row = row, row.astype(F32)
    lane = lax.broadcasted_iota(jnp.int32, (cells, slots), 1)
    far = 4.0 * slots
    wide[...] = jnp.full(wide.shape, slots, jnp.int32)
    copies[0].wait()
    for t in range(3):
        wide[t, :, :mols] = mol_ref[t]
    lanes = jnp.where(
        lane < mols,
        wide[0],
        jnp.where(lane < 2 * mols, pltpu.roll(wide[1], mols, 1), pltpu.roll(wide[2], 2 * mols, 1)),
    )
    lanes = jnp.where(lane < 3 * mols, lanes, slots)
    charges = lane_tables(lanes, mols, slots)
    q_ref[...] = charges
    free = lanes >= slots
    key = jnp.where(
        free, far + dot_nn(free.astype(F32).astype(BF16), upper), lanes.astype(F32)
    )
    ones = jnp.ones((slots, slots), BF16)
    used = jnp.zeros((slots, slots), F32)
    for cell in range(cells):
        held = (row == key[cell : cell + 1]).astype(F32).astype(BF16)
        used = jnp.where(col == cell, dot_nn(held, ones), used)
    rank = dot_nn((col < rows).astype(F32).astype(BF16), (1.0 - used).astype(BF16))
    slot_key = jnp.where(used > 0.5, row, far + rank)
    copies[1].wait()
    copies[2].wait()
    n = 3 * lb
    for cell in range(cells):
        slot_column = jnp.broadcast_to(slot_key[:, cell : cell + 1], (slots, slots))
        perm = (slot_column == key[cell : cell + 1]).astype(F32).astype(BF16)
        perm_ref[cell] = perm
        atoms = [
            ref[pl.ds(comp * cells + cell, lb, stride=3 * cells), :]
            for ref in (x_ref, p_ref)
            for comp in range(3)
        ]
        moved = permuted(jnp.concatenate(atoms, axis=0), perm)
        xo[cell] = moved[:n]
        po[cell] = moved[n:]
    write_ends(to_right, to_left, xo, charges, lb, cells, slots)


def write_ends(to_right, to_left, xs, charges, lb, cells, slots):
    for out, cell in ((to_right, cells - 1), (to_left, 0)):
        out[3 * lb :, :] = jnp.zeros((8, slots), F32)
        out[pl.ds(0, 3 * lb), :] = xs[cell]
        out[pl.ds(3 * lb, 1), :] = charges[cell : cell + 1, :]


def put_tiles(scratch, first, count, rows):
    for index, value in rows:
        scratch[pl.ds(first * 8 + index, count, stride=8), :] = value


OFFSETS = (-1.0, 0.0, 1.0)


def build_tiles(tiles, first, count, x, y, z):
    x, y, z = two_part(x - 0.5), two_part(y - 0.5), two_part(z - 0.5)
    norm = x * x + y * y + z * z + 0.5 * coulomb_soft
    high = two_part(norm)
    low = norm - high
    put_tiles(
        tiles, first, count, ((0, x), (1, y), (2, z), (3, high), (4, low), (5, high), (6, low))
    )


def store_shapes(count, beads, slots):
    n = count * beads
    return (
        [((n * 8, slots), F32), ((n // 2, slots, 64), BF16)]
        + [((n // 2, 32, slots), BF16)] * 3
        + [((n, 32, slots), BF16)]
    )


STORE = 6


class Store:
    def __init__(self, refs, beads):
        self.tiles, self.peers, *sums, self.targets = refs
        self.sums = sums
        self.beads = beads


def tile_of(ref, n):
    return ref[pl.ds(pl.multiple_of(n * 8, 8), 8), :]


def prepare(store, charges, count, slots):
    tiles, beads = store.tiles, store.beads
    row8 = lax.broadcasted_iota(jnp.int32, (8, slots), 0)
    place, norms = row8 < 3, row8 < 5
    target_rows = place | (row8 == 5) | (row8 == 6)
    ones_low = jnp.where((row8 == 3) | (row8 == 4), 1.0, 0.0)
    ones_high = jnp.where((row8 == 5) | (row8 == 6), 1.0, 0.0)
    ones_last = jnp.where(row8 == 7, 1.0, 0.0)
    pairs = beads // 2
    total = count * pairs
    unroll = max(n for n in range(1, max(2, min(17, total // 4 + 1))) if total % n == 0)

    def stack(values):
        return jnp.concatenate(values, axis=0).astype(BF16)

    def step(index, carry):
        for u in range(unroll):
            m = index * unroll + u
            charge = charges[lax.div(m, pairs)]
            units = [
                jnp.where(row8 == 3, charge, jnp.where(row8 == 4, offset * charge, 0.0))
                for offset in OFFSETS
            ]
            left, high_rows, mid_rows = [], [], []
            for h in range(2):
                value = tile_of(tiles, 2 * m + h)
                high = rounded(value)
                mid = value - high
                x_high, x_mid = high[0:1], mid[0:1]
                left_high = jnp.where(place, -2.0 * high, jnp.where(norms, high, ones_high))
                left_mid = jnp.where(place, -2.0 * mid, jnp.where(norms, mid, 0.0))
                left_last = jnp.where(
                    place,
                    -2.0 * mid,
                    jnp.where(
                        row8 == 3,
                        2.0 * x_high,
                        jnp.where(row8 == 4, 2.0 * x_mid, ones_last - 2.0 * ones_high),
                    ),
                )
                left += [left_high, left_high, left_mid, left_last]
                right_high = jnp.where(target_rows, high, ones_low)
                right_mid = jnp.where(target_rows, mid, 0.0)
                right_last = jnp.where(
                    place,
                    mid,
                    jnp.where(
                        row8 == 5, x_high, jnp.where(row8 == 6, x_mid, ones_low + ones_last)
                    ),
                )
                store.targets[2 * m + h] = stack([right_high, right_mid, right_high, right_last])
                high_rows.append(high * charge)
                mid_rows.append(jnp.where(place, mid * charge, 0.0))
            store.peers[m] = stack(left).T
            for o in range(3):
                rows = []
                for h in range(2):
                    rows += [jnp.where(place, high_rows[h], units[o]), mid_rows[h]]
                store.sums[o][m] = stack(rows)
        return carry

    lax.fori_loop(0, total // unroll, step, 0)


class PairLoop:
    def __init__(self, mols, slots, beads, keep):
        self.mols, self.slots, self.keep = mols, slots, keep
        self.pairs = beads // 2
        self.unroll = min(self.pairs, 4)
        self.per_cell = self.pairs // self.unroll
        orows = -(-mols // 8) * 8
        self.row8 = lax.broadcasted_iota(jnp.int32, (8, slots), 0)
        lj_row = lax.broadcasted_iota(jnp.int32, (orows, slots), 0)
        lj_lane = lax.broadcasted_iota(jnp.int32, (orows, slots), 1)
        self.first_lanes, self.second_lanes = lj_lane < mols, lj_lane < 2 * mols
        self.corner = (lj_row < mols) & self.first_lanes

        i = lax.broadcasted_iota(jnp.int32, (slots, slots), 0)
        j = lax.broadcasted_iota(jnp.int32, (slots, slots), 1)
        i = jnp.where(i >= 2 * mols, i - 2 * mols, jnp.where(i >= mols, i - mols, i))
        j = jnp.where(j >= 2 * mols, j - 2 * mols, jnp.where(j >= mols, j - mols, j))
        keep[...] = (i != j).astype(F32)

        lane64 = lax.broadcasted_iota(jnp.int32, (slots, 64), 1) & 31
        odd = (lane64 >= 27) & (lane64 < 31)
        even = lane64 == 31
        self.signs = [
            jnp.where(odd, -1.0, 1.0).astype(BF16),
            jnp.where(odd | even, 0.0, 1.0).astype(BF16),
            None,
        ]
        self.zero = jnp.zeros((32, slots), BF16)

    def pair(self, peers, charge):
        mols, slots = self.mols, self.slots
        orows = self.corner.shape[0]
        pair_scale = coulomb_scale * charge_hydrogen * charge_hydrogen
        k3 = sigma_square**3
        ratio = (charge_hydrogen / charge_oxygen) ** 2 / pair_scale
        lj_a = 24.0 * well_depth * 2.0 * k3 * k3 * ratio
        lj_b = 24.0 * well_depth * k3 * ratio
        zero = self.zero
        own, m = peers[1]
        left = jnp.concatenate(
            [
                store.peers[index] if sign is None else store.peers[index] * sign
                for (store, index), sign in zip(peers, self.signs)
            ],
            axis=0,
        )
        right = jnp.concatenate(
            [
                jnp.concatenate([own.targets[2 * m], zero], axis=1),
                jnp.concatenate([zero, own.targets[2 * m + 1]], axis=1),
            ],
            axis=0,
        )
        squares = dot_nn(left, right)
        blocks = [[], [], []]
        for h in range(2):
            lanes = slice(h * slots, (h + 1) * slots)
            near = [squares[o * slots : o * slots + orows, lanes] for o in range(3)]
            packed = jnp.where(
                self.first_lanes,
                near[0],
                jnp.where(
                    self.second_lanes,
                    pltpu.roll(near[1], mols, 1),
                    pltpu.roll(near[2], 2 * mols, 1),
                ),
            )
            root = lax.rsqrt(packed + (lennard_soft - coulomb_soft))
            inverse = root * root
            cube = inverse * inverse * inverse
            lj = (cube * lj_a - lj_b) * (cube * inverse)
            for o in range(3):
                root = lax.rsqrt(squares[o * slots : (o + 1) * slots, lanes])
                strength = root * root * root
                part = pltpu.roll(lj, slots - o * mols, 1) if o else lj
                strength = jnp.concatenate(
                    [strength[:orows] + jnp.where(self.corner, part, 0.0), strength[orows:]],
                    axis=0,
                )
                if o == 1:
                    strength = strength * self.keep[...]
                high = strength.astype(BF16)
                low = (strength - high.astype(F32)).astype(BF16)
                blocks[o].append(jnp.concatenate([high, low], axis=0))
        sums = None
        for o, (store, index) in enumerate(peers):
            weights = store.sums[o][index]
            value = dot_nn(
                jnp.concatenate([weights, weights], axis=1), jnp.concatenate(blocks[o], axis=1)
            )
            sums = value if sums is None else sums + value
        scale = charge * pair_scale
        out = []
        for h in range(2):
            part = sums[16 * h : 16 * h + 16, h * slots : (h + 1) * slots]
            total = part[0:8] + part[8:16]
            total = total + jnp.where(self.row8 == 0, total[4:5], 0.0)
            out.append((tile_of(own.tiles, 2 * m + h) * total[3:4] - total) * scale)
        return out

    def cells(self, store, charges, first, last, forces, limit):
        total = (last - first) * self.pairs
        unroll = max(n for n in range(1, limit + 1) if total % n == 0)

        def step(index, carry):
            for u in range(unroll):
                m = index * unroll + u
                at = m + first * self.pairs
                peers = [(store, at + (o - 1) * self.pairs) for o in range(3)]
                out = self.pair(peers, charges[lax.div(at, self.pairs)])
                for h in range(2):
                    n = 2 * m + h
                    forces[pl.ds(pl.multiple_of(n * 8, 8), 8), :] = out[h]
            return carry

        lax.fori_loop(0, total // unroll, step, 0)


def read_force(forces, w, beads, comp):
    return forces[pl.ds(w * beads * 8 + comp, beads, stride=8), :]


def own_kernel(cells, lb, slots, x_ref, q_ref, *refs):
    store = Store(refs, lb)
    for w in range(cells):
        rows = x_ref[w]
        build_tiles(store.tiles, w * lb, lb, rows[:lb], rows[lb : 2 * lb], rows[2 * lb :])
    prepare(store, Rows(q_ref, 0), cells, slots)


def interior_kernel(cells, lb, mols, slots, q_ref, *refs):
    store = Store(refs[:STORE], lb)
    forces, keep = refs[STORE:]
    PairLoop(mols, slots, lb, keep).cells(store, Rows(q_ref, 0), 1, cells - 1, forces, 64)


def edge_forces(cells, lb, mols, slots, x_ref, q_ref, left, right, inner, own, scratch):
    forces, keep = scratch[:2]
    halo = Store(scratch[2:], lb)
    n = 3 * lb
    charge = [left[pl.ds(n, 1), :], right[pl.ds(n, 1), :]]
    for e, edge in enumerate((left, right)):
        rows = edge[pl.ds(0, n), :]
        build_tiles(halo.tiles, e * lb, lb, rows[:lb], rows[lb : 2 * lb], rows[2 * lb :])

    class Edges:
        def __getitem__(self, e):
            return jnp.where(e == 0, charge[0], charge[1])

    prepare(halo, Edges(), 2, slots)
    loop = PairLoop(mols, slots, lb, keep)
    last = cells - 1
    near = (
        (0, ((halo, 0), (own, 0), (own, 1))),
        (last, ((own, last - 1), (own, last), (halo, 1))),
    )
    for e, (cell, stores) in enumerate(near):
        for pair in range(loop.pairs):
            peers = [(store, at * loop.pairs + pair) for store, at in stores]
            out = loop.pair(peers, q_ref[cell : cell + 1, :])
            for h in range(2):
                forces[pl.ds((e * lb + 2 * pair + h) * 8, 8), :] = out[h]

    def read(w):
        source, at = (inner, w - 1) if 0 < w < last else (forces, 0 if w == 0 else 1)
        return jnp.concatenate([read_force(source, at, lb, c) for c in range(3)], axis=0)

    return read


def kick_kernel(nb, group, lb, cells, mols, slots, b_ref, *refs):
    x_ref, p_ref, q_ref, left, right, inner = refs[:6]
    own = Store(refs[6 : 6 + STORE], lb)
    outs = refs[6 + STORE : 6 + STORE + nb]
    kicked, *scratch = refs[6 + STORE + nb :]
    read = edge_forces(cells, lb, mols, slots, x_ref, q_ref, left, right, inner, own, scratch)
    n = 3 * lb
    for w in range(cells):
        kicked[w] = p_ref[w] + (0.5 * outer_step) * read(w)
    for i, k in enumerate(block_order(nb)):
        first = jnp.bitwise_xor(b_ref[0], k) * group
        for w in range(group):
            outs[i][pl.ds(w * n, n), :] = x_ref[first + w]
            outs[i][pl.ds((group + w) * n, n), :] = kicked[first + w]


def gather_kernel(nb, group, lb, cells, slots, b_ref, *refs):
    blocks, q_ref = refs[:nb], refs[nb]
    xs, ps, to_right, to_left = refs[nb + 1 :]
    n = 3 * lb
    for i, k in enumerate(block_order(nb)):
        first = jnp.bitwise_xor(b_ref[0], k) * group
        for w in range(group):
            xs[first + w] = blocks[i][pl.ds(w * n, n), :]
            ps[first + w] = blocks[i][pl.ds((group + w) * n, n), :]
    write_ends(to_right, to_left, xs, q_ref, lb, cells, slots)


def final_kernel(cells, lb, mols, slots, *refs):
    x_ref, p_ref, q_ref, left, right, inner, perm_ref = refs[:7]
    own = Store(refs[7 : 7 + STORE], lb)
    outs, scratch = refs[7 + STORE : 9 + STORE], refs[9 + STORE :]
    read = edge_forces(cells, lb, mols, slots, x_ref, q_ref, left, right, inner, own, scratch)
    for w in range(cells):
        state = jnp.concatenate([x_ref[w], p_ref[w] + (0.5 * outer_step) * read(w)], axis=0)
        state = unpermuted(state, perm_ref[w])
        for a in range(2):
            for c in range(3):
                row = (a * 3 + c) * lb
                outs[a][pl.ds(c * cells + w, lb, stride=3 * cells), :] = state[row : row + lb]


class Rows:
    def __init__(self, ref, first):
        self.ref, self.first = ref, first

    def __getitem__(self, index):
        return self.ref[pl.ds(self.first + index, 1), :]


def bond_forces(x, y, z, used, mols, slots):
    def partner(a, t):
        return pltpu.roll(a, slots - t * mols, 1)

    first = [a - partner(a, 1) for a in (x, y, z)]
    second = [a - partner(a, 2) for a in (x, y, z)]
    third = [s - f for f, s in zip(first, second)]

    def pull(bond, stiffness, square):
        length = bond[0] * bond[0] + bond[1] * bond[1] + bond[2] * bond[2]
        return (stiffness * used) * (length - square)

    c1 = pull(first, bond_stiffness, bond_square)
    c2 = pull(second, bond_stiffness, bond_square)
    c3 = pull(third, angle_stiffness, angle_square)
    out = []
    for f, s, t in zip(first, second, third):
        on_first = c1 * f - c3 * t
        on_second = c2 * s + c3 * t
        on_oxygen = -(c1 * f + c2 * s)
        out.append(
            on_oxygen + pltpu.roll(on_first, mols, 1) + pltpu.roll(on_second, 2 * mols, 1)
        )
    return out


def steps_kernel(nb, group, lb, mols, slots, b_ref, *refs):
    blocks = refs[:nb]
    step_ref, q_ref = refs[nb : nb + 2]
    outs = refs[nb + 2 :]
    beads = nb * lb
    n = 3 * lb
    b = b_ref[0]
    step = step_ref[b]
    charges = Rows(q_ref, b * group)

    def advance(states):
        flat = [
            jnp.concatenate([x, v], axis=0) for pos, vel in states for x, v in zip(pos, vel)
        ]
        high, mid, low = split3(jnp.concatenate(flat, axis=1))
        stacked = jnp.concatenate([high, mid, high, mid, low, high], axis=0).astype(BF16)
        new = dot_nn(step, stacked)
        out = []
        for i in range(len(states)):
            columns = [
                new[:, (3 * i + c) * slots : (3 * i + c + 1) * slots] for c in range(3)
            ]
            out.append(([a[:beads] for a in columns], [a[beads:] for a in columns]))
        return out

    def gather(w, a, comp):
        return jnp.concatenate(
            [block[pl.ds((a * group + w) * n + comp * lb, lb), :] for block in blocks], axis=0
        )

    def kick(state, oxygen, scale):
        pos, vel = state
        force = bond_forces(*pos, oxygen, mols, slots)
        return pos, [v + scale * f for v, f in zip(vel, force)]

    for first in range(0, group, 2):
        members = range(first, min(first + 2, group))
        charge = [charges[w] for w in members]
        oxygen = [(q < -1.5).astype(F32) for q in charge]
        inverse = [jnp.where(q < -1.5, 1.0 / oxygen_mass, 1.0) for q in charge]
        states = [
            (
                [gather(w, 0, c) for c in range(3)],
                [gather(w, 1, c) * scale for c in range(3)],
            )
            for w, scale in zip(members, inverse)
        ]
        for part in (0.5, 1.0):
            states = [
                kick(state, o, (part * inner_step) * scale)
                for state, o, scale in zip(states, oxygen, inverse)
            ]
            states = advance(states)
        for w, state, q, o, scale in zip(members, states, charge, oxygen, inverse):
            pos, vel = kick(state, o, (0.5 * inner_step) * scale)
            mass = jnp.where(q < -1.5, oxygen_mass, 1.0)
            for a, values in enumerate((pos, [v * mass for v in vel])):
                for c in range(3):
                    for i in range(nb):
                        rows = values[c][i * lb : (i + 1) * lb]
                        outs[i][pl.ds((a * group + w) * n + c * lb, lb), :] = rows


def call(kernel, outs, scratch, scalar, *operands, space=pltpu.VMEM):
    vmem = pl.BlockSpec(memory_space=pltpu.VMEM)
    smem = pl.BlockSpec(memory_space=pltpu.SMEM)
    return pl.pallas_call(
        kernel,
        out_shape=outs,
        in_specs=([] if scalar is None else [smem]) + [pl.BlockSpec(memory_space=space)] * len(operands),
        out_specs=[vmem] * len(outs),
        scratch_shapes=scratch,
        compiler_params=pltpu.CompilerParams(vmem_limit_bytes=24 * 1024 * 1024),
    )(*(() if scalar is None else (scalar,)), *operands)


def exchange(blocks, nb):
    return [
        lax.ppermute(block, "bead", [(i, i ^ k) for i in range(nb)]) if k else block
        for block, k in zip(blocks, block_order(nb))
    ]


def local(nb, ns, positions, momenta, molecules):
    lb, _, cells, slots = positions.shape
    mols = molecules.shape[1]
    group = cells // nb
    beads = lb * nb
    b = lax.axis_index("bead").astype(jnp.int32).reshape(1)

    def shape(*dims):
        return jax.ShapeDtypeStruct(dims, F32)

    rows = lb * 3 * cells
    state = [shape(cells, 3 * lb, slots)] * 2
    ends = [shape(3 * lb + 8, slots)] * 2
    blocks = [shape(2 * group * 3 * lb, slots)] * nb
    store = [jax.ShapeDtypeStruct(*entry) for entry in store_shapes(cells, lb, slots)]
    keep = pltpu.VMEM((slots, slots), F32)
    edge_scratch = [pltpu.VMEM((2 * lb * 8, slots), F32), keep] + [
        pltpu.VMEM(*entry) for entry in store_shapes(2, lb, slots)
    ]

    def halos(to_right, to_left):
        left = lax.ppermute(to_right, "space", [(s, (s + 1) % ns) for s in range(ns)])
        right = lax.ppermute(to_left, "space", [(s, (s - 1) % ns) for s in range(ns)])
        return left, right

    def inside(xs, charges):
        own = call(
            functools.partial(own_kernel, cells, lb, slots), store, [], None, xs, charges
        )
        (inner,) = call(
            functools.partial(interior_kernel, cells, lb, mols, slots),
            [shape((cells - 2) * lb * 8, slots)],
            [keep],
            None,
            charges,
            *own,
        )
        return own, inner

    xs, ps, perm, charges, to_right, to_left = call(
        functools.partial(order_kernel, lb, cells, mols, slots),
        state
        + [jax.ShapeDtypeStruct((cells, slots, slots), BF16), shape(cells, slots)]
        + ends,
        [
            pltpu.VMEM((3, cells, mols), jnp.int32),
            pltpu.VMEM((rows, slots), F32),
            pltpu.VMEM((rows, slots), F32),
            pltpu.VMEM((3, cells, slots), jnp.int32),
            pltpu.SemaphoreType.DMA((3,)),
        ],
        None,
        *(
            pltpu.with_memory_space_constraint(a, pltpu.HBM)
            for a in (
                jnp.transpose(molecules, (2, 0, 1)),
                positions.reshape(rows, slots),
                momenta.reshape(rows, slots),
            )
        ),
        space=pltpu.HBM,
    )
    left, right = halos(to_right, to_left)
    own, inner = inside(xs, charges)
    sent = call(
        functools.partial(kick_kernel, nb, group, lb, cells, mols, slots),
        blocks,
        [pltpu.VMEM((cells, 3 * lb, slots), F32)] + edge_scratch,
        b,
        xs,
        ps,
        charges,
        left,
        right,
        inner,
        *own,
    )
    stepped = call(
        functools.partial(steps_kernel, nb, group, lb, mols, slots),
        blocks,
        [],
        b,
        *exchange(sent, nb),
        jnp.asarray(propagator(beads, lb)),
        charges,
    )
    xs, ps, to_right, to_left = call(
        functools.partial(gather_kernel, nb, group, lb, cells, slots),
        state + ends,
        [],
        b,
        *exchange(stepped, nb),
        charges,
    )
    left, right = halos(to_right, to_left)
    own, inner = inside(xs, charges)
    new_x, new_p = call(
        functools.partial(final_kernel, cells, lb, mols, slots),
        [shape(rows, slots)] * 2,
        edge_scratch,
        None,
        xs,
        ps,
        charges,
        left,
        right,
        inner,
        perm,
        *own,
    )
    return new_x.reshape(positions.shape), new_p.reshape(positions.shape)


def solution(mesh):
    spec = P("bead", None, "space", None)
    return jax.shard_map(
        functools.partial(local, mesh.shape["bead"], mesh.shape["space"]),
        mesh=mesh,
        in_specs=(spec, spec, P("space", None, None)),
        out_specs=(spec, spec),
        check_vma=False,
    )
```

```python
import functools

import jax
import jax.numpy as jnp
import ml_dtypes
import numpy as np
from jax import lax
from jax.experimental import pallas as pl
from jax.experimental.pallas import tpu as pltpu
from jax.sharding import PartitionSpec as P

charge_oxygen = -0.8476
charge_hydrogen = 0.4238
coulomb_scale = 24.0
coulomb_soft = 0.004
well_depth = 0.02
sigma_square = 0.0841
lennard_soft = 0.04
bond_stiffness = 20000.0
bond_square = 0.0081
angle_stiffness = 5000.0
angle_square = 0.0204
cycle_frequency = 60.0
outer_step = 0.02
inner_step = 0.01
oxygen_mass = 16.0

F32 = jnp.float32
BF16 = jnp.bfloat16


def rounded(a):
    return a.astype(BF16).astype(F32)


def split3(a):
    high = rounded(a)
    rest = a - high
    mid = rounded(rest)
    return high, mid, rest - mid


def two_part(a):
    high = rounded(a)
    return high + rounded(a - high)


def dot_nn(a, b):
    return lax.dot_general(a, b, (((1,), (0,)), ((), ())), preferred_element_type=F32)


def dot_nt(a, b):
    return lax.dot_general(a, b, (((1,), (1,)), ((), ())), preferred_element_type=F32)


def block_order(nb):
    return list(range(nb))


def propagator(beads, beads_dev):
    j = np.arange(beads)
    angles = 2.0 * np.pi * ((j[:, None] * j[None, :]) % beads) / beads
    half = beads // 2
    col = j[None, :]
    u = np.where(
        col == 0,
        np.sqrt(1.0 / beads),
        np.where(
            col < half,
            np.sqrt(2.0 / beads) * np.cos(angles),
            np.where(
                col == half,
                np.sqrt(1.0 / beads) * np.cos(angles),
                np.sqrt(2.0 / beads) * np.sin(angles),
            ),
        ),
    )
    w = 2.0 * cycle_frequency * np.sin(np.pi * j / beads)
    cosines = np.cos(w * inner_step)
    spring = w * np.sin(w * inner_step)
    drift = np.where(j == 0, inner_step, np.sin(w * inner_step) / np.where(j == 0, 1.0, w))
    def circulant(values, bead):
        first = ((u * values) @ u.T)[:, 0]
        return first[(bead[:, None] - bead[None, :]) % beads]

    out = []
    for b in range(beads // beads_dev):
        block = np.array(block_order(beads // beads_dev))[j // beads_dev]
        bead = (block ^ b) * beads_dev + j % beads_dev
        a = circulant(cosines, bead)
        whole = np.block([[a, circulant(drift, bead)], [-circulant(spring, bead), a]])
        high = whole.astype(ml_dtypes.bfloat16)
        rest = whole - high.astype(np.float64)
        mid = rest.astype(ml_dtypes.bfloat16)
        low = (rest - mid.astype(np.float64)).astype(ml_dtypes.bfloat16)
        out.append(np.concatenate([high, high, mid, mid, high, low], axis=1))
    return np.stack(out)


def lane_tables(lanes, mols, slots):
    lane = lax.broadcasted_iota(jnp.int32, lanes.shape, 1)
    unit = jnp.where(lane < mols, charge_oxygen / charge_hydrogen, 1.0)
    return jnp.where(lanes < slots, unit, 0.0)


def permuted(rows, perm):
    n = rows.shape[0]
    stacked = jnp.concatenate(split3(rows), axis=0).astype(BF16)
    moved = dot_nn(stacked, perm)
    return moved[:n] + moved[n : 2 * n] + moved[2 * n :]


def unpermuted(rows, perm):
    n = rows.shape[0]
    stacked = jnp.concatenate(split3(rows), axis=0).astype(BF16)
    moved = dot_nt(stacked, perm)
    return moved[:n] + moved[n : 2 * n] + moved[2 * n :]


def order_kernel(lb, cells, mols, slots, mol_hbm, x_hbm, p_hbm, *refs):
    xo, po, perm_ref, q_ref, to_right, to_left = refs[:6]
    mol_ref, x_ref, p_ref, wide, sems = refs[6:]
    copies = [
        pltpu.make_async_copy(source, dest, sems.at[i])
        for i, (source, dest) in enumerate(
            ((mol_hbm, mol_ref), (x_hbm, x_ref), (p_hbm, p_ref))
        )
    ]
    for copy in copies:
        copy.start()
    row = lax.broadcasted_iota(jnp.int32, (slots, slots), 0)
    col = lax.broadcasted_iota(jnp.int32, (slots, slots), 1)
    upper = (row < col).astype(F32).astype(BF16)
    rows, row = row, row.astype(F32)
    lane = lax.broadcasted_iota(jnp.int32, (cells, slots), 1)
    far = 4.0 * slots
    wide[...] = jnp.full(wide.shape, slots, jnp.int32)
    copies[0].wait()
    for t in range(3):
        wide[t, :, :mols] = mol_ref[t]
    lanes = jnp.where(
        lane < mols,
        wide[0],
        jnp.where(lane < 2 * mols, pltpu.roll(wide[1], mols, 1), pltpu.roll(wide[2], 2 * mols, 1)),
    )
    lanes = jnp.where(lane < 3 * mols, lanes, slots)
    charges = lane_tables(lanes, mols, slots)
    q_ref[...] = charges
    free = lanes >= slots
    key = jnp.where(
        free, far + dot_nn(free.astype(F32).astype(BF16), upper), lanes.astype(F32)
    )
    ones = jnp.ones((slots, slots), BF16)
    used = jnp.zeros((slots, slots), F32)
    for cell in range(cells):
        held = (row == key[cell : cell + 1]).astype(F32).astype(BF16)
        used = jnp.where(col == cell, dot_nn(held, ones), used)
    rank = dot_nn((col < rows).astype(F32).astype(BF16), (1.0 - used).astype(BF16))
    slot_key = jnp.where(used > 0.5, row, far + rank)
    copies[1].wait()
    copies[2].wait()
    n = 3 * lb
    for cell in range(cells):
        slot_column = jnp.broadcast_to(slot_key[:, cell : cell + 1], (slots, slots))
        perm = (slot_column == key[cell : cell + 1]).astype(F32).astype(BF16)
        perm_ref[cell] = perm
        atoms = [
            ref[pl.ds(comp * cells + cell, lb, stride=3 * cells), :]
            for ref in (x_ref, p_ref)
            for comp in range(3)
        ]
        moved = permuted(jnp.concatenate(atoms, axis=0), perm)
        xo[cell] = moved[:n]
        po[cell] = moved[n:]
    write_ends(to_right, to_left, xo, charges, lb, cells, slots)


def write_ends(to_right, to_left, xs, charges, lb, cells, slots):
    for out, cell in ((to_right, cells - 1), (to_left, 0)):
        out[3 * lb :, :] = jnp.zeros((8, slots), F32)
        out[pl.ds(0, 3 * lb), :] = xs[cell]
        out[pl.ds(3 * lb, 1), :] = charges[cell : cell + 1, :]


def put_tiles(scratch, first, count, rows):
    for index, value in rows:
        scratch[pl.ds(first * 8 + index, count, stride=8), :] = value


OFFSETS = (-1.0, 0.0, 1.0)


def build_tiles(tiles, first, count, x, y, z):
    x, y, z = two_part(x - 0.5), two_part(y - 0.5), two_part(z - 0.5)
    norm = x * x + y * y + z * z + 0.5 * coulomb_soft
    high = two_part(norm)
    low = norm - high
    put_tiles(
        tiles, first, count, ((0, x), (1, y), (2, z), (3, high), (4, low), (5, high), (6, low))
    )


def store_shapes(count, beads, slots):
    n = count * beads
    return (
        [((n * 8, slots), F32), ((n // 2, slots, 64), BF16)]
        + [((n // 2, 32, slots), BF16)] * 3
        + [((n, 32, slots), BF16)]
    )


STORE = 6


class Store:
    def __init__(self, refs, beads):
        self.tiles, self.peers, *sums, self.targets = refs
        self.sums = sums
        self.beads = beads


def tile_of(ref, n):
    return ref[pl.ds(pl.multiple_of(n * 8, 8), 8), :]


def prepare(store, charges, count, slots):
    tiles, beads = store.tiles, store.beads
    row8 = lax.broadcasted_iota(jnp.int32, (8, slots), 0)
    place, norms = row8 < 3, row8 < 5
    target_rows = place | (row8 == 5) | (row8 == 6)
    ones_low = jnp.where((row8 == 3) | (row8 == 4), 1.0, 0.0)
    ones_high = jnp.where((row8 == 5) | (row8 == 6), 1.0, 0.0)
    ones_last = jnp.where(row8 == 7, 1.0, 0.0)
    pairs = beads // 2
    total = count * pairs
    unroll = max(n for n in range(1, min(16, max(total // 4, 4)) + 1) if total % n == 0)

    def stack(values):
        return jnp.concatenate(values, axis=0).astype(BF16)

    def step(index, carry):
        for u in range(unroll):
            m = index * unroll + u
            charge = charges[lax.div(m, pairs)]
            units = [
                jnp.where(row8 == 3, charge, jnp.where(row8 == 4, offset * charge, 0.0))
                for offset in OFFSETS
            ]
            left, high_rows, mid_rows = [], [], []
            for h in range(2):
                value = tile_of(tiles, 2 * m + h)
                high = rounded(value)
                mid = value - high
                x_high, x_mid = high[0:1], mid[0:1]
                left_high = jnp.where(place, -2.0 * high, jnp.where(norms, high, ones_high))
                left_mid = jnp.where(place, -2.0 * mid, jnp.where(norms, mid, 0.0))
                left_last = jnp.where(
                    place,
                    -2.0 * mid,
                    jnp.where(
                        row8 == 3,
                        2.0 * x_high,
                        jnp.where(row8 == 4, 2.0 * x_mid, ones_last - 2.0 * ones_high),
                    ),
                )
                left += [left_high, left_high, left_mid, left_last]
                right_high = jnp.where(target_rows, high, ones_low)
                right_mid = jnp.where(target_rows, mid, 0.0)
                right_last = jnp.where(
                    place,
                    mid,
                    jnp.where(
                        row8 == 5, x_high, jnp.where(row8 == 6, x_mid, ones_low + ones_last)
                    ),
                )
                store.targets[2 * m + h] = stack([right_high, right_mid, right_high, right_last])
                high_rows.append(high * charge)
                mid_rows.append(jnp.where(place, mid * charge, 0.0))
            store.peers[m] = stack(left).T
            for o in range(3):
                rows = []
                for h in range(2):
                    rows += [jnp.where(place, high_rows[h], units[o]), mid_rows[h]]
                store.sums[o][m] = stack(rows)
        return carry

    lax.fori_loop(0, total // unroll, step, 0)


class PairLoop:
    def __init__(self, mols, slots, beads, keep):
        self.mols, self.slots, self.keep = mols, slots, keep
        self.pairs = beads // 2
        self.unroll = min(self.pairs, 4)
        self.per_cell = self.pairs // self.unroll
        orows = -(-mols // 8) * 8
        self.row8 = lax.broadcasted_iota(jnp.int32, (8, slots), 0)
        lj_row = lax.broadcasted_iota(jnp.int32, (orows, slots), 0)
        lj_lane = lax.broadcasted_iota(jnp.int32, (orows, slots), 1)
        self.first_lanes, self.second_lanes = lj_lane < mols, lj_lane < 2 * mols
        self.corner = (lj_row < mols) & self.first_lanes

        i = lax.broadcasted_iota(jnp.int32, (slots, slots), 0)
        j = lax.broadcasted_iota(jnp.int32, (slots, slots), 1)
        i = jnp.where(i >= 2 * mols, i - 2 * mols, jnp.where(i >= mols, i - mols, i))
        j = jnp.where(j >= 2 * mols, j - 2 * mols, jnp.where(j >= mols, j - mols, j))
        keep[...] = (i != j).astype(F32)

        lane64 = lax.broadcasted_iota(jnp.int32, (slots, 64), 1) & 31
        odd = (lane64 >= 27) & (lane64 < 31)
        even = lane64 == 31
        self.signs = [
            jnp.where(odd, -1.0, 1.0).astype(BF16),
            jnp.where(odd | even, 0.0, 1.0).astype(BF16),
            None,
        ]
        self.zero = jnp.zeros((32, slots), BF16)

    def pair(self, peers, charge):
        mols, slots = self.mols, self.slots
        orows = self.corner.shape[0]
        pair_scale = coulomb_scale * charge_hydrogen * charge_hydrogen
        k3 = sigma_square**3
        ratio = (charge_hydrogen / charge_oxygen) ** 2 / pair_scale
        lj_a = 24.0 * well_depth * 2.0 * k3 * k3 * ratio
        lj_b = 24.0 * well_depth * k3 * ratio
        zero = self.zero
        own, m = peers[1]
        left = jnp.concatenate(
            [
                store.peers[index] if sign is None else store.peers[index] * sign
                for (store, index), sign in zip(peers, self.signs)
            ],
            axis=0,
        )
        right = jnp.concatenate(
            [
                jnp.concatenate([own.targets[2 * m], zero], axis=1),
                jnp.concatenate([zero, own.targets[2 * m + 1]], axis=1),
            ],
            axis=0,
        )
        squares = dot_nn(left, right)
        blocks = [[], [], []]
        for h in range(2):
            lanes = slice(h * slots, (h + 1) * slots)
            near = [squares[o * slots : o * slots + orows, lanes] for o in range(3)]
            packed = jnp.where(
                self.first_lanes,
                near[0],
                jnp.where(
                    self.second_lanes,
                    pltpu.roll(near[1], mols, 1),
                    pltpu.roll(near[2], 2 * mols, 1),
                ),
            )
            root = lax.rsqrt(packed + (lennard_soft - coulomb_soft))
            inverse = root * root
            cube = inverse * inverse * inverse
            lj = (cube * lj_a - lj_b) * (cube * inverse)
            for o in range(3):
                root = lax.rsqrt(squares[o * slots : (o + 1) * slots, lanes])
                strength = root * root * root
                part = pltpu.roll(lj, slots - o * mols, 1) if o else lj
                strength = jnp.concatenate(
                    [strength[:orows] + jnp.where(self.corner, part, 0.0), strength[orows:]],
                    axis=0,
                )
                if o == 1:
                    strength = strength * self.keep[...]
                high = strength.astype(BF16)
                low = (strength - high.astype(F32)).astype(BF16)
                blocks[o].append(jnp.concatenate([high, low], axis=0))
        sums = None
        for o, (store, index) in enumerate(peers):
            weights = store.sums[o][index]
            value = dot_nn(
                jnp.concatenate([weights, weights], axis=1), jnp.concatenate(blocks[o], axis=1)
            )
            sums = value if sums is None else sums + value
        scale = charge * pair_scale
        out = []
        for h in range(2):
            part = sums[16 * h : 16 * h + 16, h * slots : (h + 1) * slots]
            total = part[0:8] + part[8:16]
            total = total + jnp.where(self.row8 == 0, total[4:5], 0.0)
            out.append((tile_of(own.tiles, 2 * m + h) * total[3:4] - total) * scale)
        return out

    def cells(self, store, charges, first, last, forces, limit):
        total = (last - first) * self.pairs
        unroll = max(n for n in range(1, limit + 1) if total % n == 0)

        def step(index, carry):
            for u in range(unroll):
                m = index * unroll + u
                at = m + first * self.pairs
                peers = [(store, at + (o - 1) * self.pairs) for o in range(3)]
                out = self.pair(peers, charges[lax.div(at, self.pairs)])
                for h in range(2):
                    n = 2 * m + h
                    forces[pl.ds(pl.multiple_of(n * 8, 8), 8), :] = out[h]
            return carry

        lax.fori_loop(0, total // unroll, step, 0)


def read_force(forces, w, beads, comp):
    return forces[pl.ds(w * beads * 8 + comp, beads, stride=8), :]


def own_kernel(cells, lb, slots, x_ref, q_ref, *refs):
    store = Store(refs, lb)
    for w in range(cells):
        rows = x_ref[w]
        build_tiles(store.tiles, w * lb, lb, rows[:lb], rows[lb : 2 * lb], rows[2 * lb :])
    prepare(store, Rows(q_ref, 0), cells, slots)


def interior_kernel(cells, lb, mols, slots, q_ref, *refs):
    store = Store(refs[:STORE], lb)
    forces, keep = refs[STORE:]
    PairLoop(mols, slots, lb, keep).cells(store, Rows(q_ref, 0), 1, cells - 1, forces, 64)


def edge_forces(cells, lb, mols, slots, x_ref, q_ref, left, right, inner, own, scratch):
    forces, keep = scratch[:2]
    halo = Store(scratch[2:], lb)
    n = 3 * lb
    charge = [left[pl.ds(n, 1), :], right[pl.ds(n, 1), :]]
    for e, edge in enumerate((left, right)):
        rows = edge[pl.ds(0, n), :]
        build_tiles(halo.tiles, e * lb, lb, rows[:lb], rows[lb : 2 * lb], rows[2 * lb :])

    class Edges:
        def __getitem__(self, e):
            return jnp.where(e == 0, charge[0], charge[1])

    prepare(halo, Edges(), 2, slots)
    loop = PairLoop(mols, slots, lb, keep)
    last = cells - 1
    near = (
        (0, ((halo, 0), (own, 0), (own, 1))),
        (last, ((own, last - 1), (own, last), (halo, 1))),
    )
    for e, (cell, stores) in enumerate(near):
        for pair in range(loop.pairs):
            peers = [(store, at * loop.pairs + pair) for store, at in stores]
            out = loop.pair(peers, q_ref[cell : cell + 1, :])
            for h in range(2):
                forces[pl.ds((e * lb + 2 * pair + h) * 8, 8), :] = out[h]

    def read(w):
        source, at = (inner, w - 1) if 0 < w < last else (forces, 0 if w == 0 else 1)
        return jnp.concatenate([read_force(source, at, lb, c) for c in range(3)], axis=0)

    return read


def kick_kernel(nb, group, lb, cells, mols, slots, b_ref, *refs):
    x_ref, p_ref, q_ref, left, right, inner = refs[:6]
    own = Store(refs[6 : 6 + STORE], lb)
    outs = refs[6 + STORE : 6 + STORE + nb]
    kicked, *scratch = refs[6 + STORE + nb :]
    read = edge_forces(cells, lb, mols, slots, x_ref, q_ref, left, right, inner, own, scratch)
    n = 3 * lb
    for w in range(cells):
        kicked[w] = p_ref[w] + (0.5 * outer_step) * read(w)
    for i, k in enumerate(block_order(nb)):
        first = jnp.bitwise_xor(b_ref[0], k) * group
        for w in range(group):
            outs[i][pl.ds(w * n, n), :] = x_ref[first + w]
            outs[i][pl.ds((group + w) * n, n), :] = kicked[first + w]


def gather_kernel(nb, group, lb, cells, slots, b_ref, *refs):
    blocks, q_ref = refs[:nb], refs[nb]
    xs, ps, to_right, to_left = refs[nb + 1 :]
    n = 3 * lb
    for i, k in enumerate(block_order(nb)):
        first = jnp.bitwise_xor(b_ref[0], k) * group
        for w in range(group):
            xs[first + w] = blocks[i][pl.ds(w * n, n), :]
            ps[first + w] = blocks[i][pl.ds((group + w) * n, n), :]
    write_ends(to_right, to_left, xs, q_ref, lb, cells, slots)


def final_kernel(cells, lb, mols, slots, *refs):
    x_ref, p_ref, q_ref, left, right, inner, perm_ref = refs[:7]
    own = Store(refs[7 : 7 + STORE], lb)
    outs, scratch = refs[7 + STORE : 9 + STORE], refs[9 + STORE :]
    read = edge_forces(cells, lb, mols, slots, x_ref, q_ref, left, right, inner, own, scratch)
    for w in range(cells):
        state = jnp.concatenate([x_ref[w], p_ref[w] + (0.5 * outer_step) * read(w)], axis=0)
        state = unpermuted(state, perm_ref[w])
        for a in range(2):
            for c in range(3):
                row = (a * 3 + c) * lb
                outs[a][pl.ds(c * cells + w, lb, stride=3 * cells), :] = state[row : row + lb]


class Rows:
    def __init__(self, ref, first):
        self.ref, self.first = ref, first

    def __getitem__(self, index):
        return self.ref[pl.ds(self.first + index, 1), :]


def bond_forces(x, y, z, used, mols, slots):
    def partner(a, t):
        return pltpu.roll(a, slots - t * mols, 1)

    first = [a - partner(a, 1) for a in (x, y, z)]
    second = [a - partner(a, 2) for a in (x, y, z)]
    third = [s - f for f, s in zip(first, second)]

    def pull(bond, stiffness, square):
        length = bond[0] * bond[0] + bond[1] * bond[1] + bond[2] * bond[2]
        return (stiffness * used) * (length - square)

    c1 = pull(first, bond_stiffness, bond_square)
    c2 = pull(second, bond_stiffness, bond_square)
    c3 = pull(third, angle_stiffness, angle_square)
    out = []
    for f, s, t in zip(first, second, third):
        on_first = c1 * f - c3 * t
        on_second = c2 * s + c3 * t
        on_oxygen = -(c1 * f + c2 * s)
        out.append(
            on_oxygen + pltpu.roll(on_first, mols, 1) + pltpu.roll(on_second, 2 * mols, 1)
        )
    return out


def steps_kernel(nb, group, lb, mols, slots, b_ref, *refs):
    blocks = refs[:nb]
    step_ref, q_ref = refs[nb : nb + 2]
    outs = refs[nb + 2 :]
    beads = nb * lb
    n = 3 * lb
    b = b_ref[0]
    step = step_ref[b]
    charges = Rows(q_ref, b * group)

    def advance(states):
        flat = [
            jnp.concatenate([x, v], axis=0) for pos, vel in states for x, v in zip(pos, vel)
        ]
        high, mid, low = split3(jnp.concatenate(flat, axis=1))
        stacked = jnp.concatenate([high, mid, high, mid, low, high], axis=0).astype(BF16)
        new = dot_nn(step, stacked)
        out = []
        for i in range(len(states)):
            columns = [
                new[:, (3 * i + c) * slots : (3 * i + c + 1) * slots] for c in range(3)
            ]
            out.append(([a[:beads] for a in columns], [a[beads:] for a in columns]))
        return out

    def gather(w, a, comp):
        return jnp.concatenate(
            [block[pl.ds((a * group + w) * n + comp * lb, lb), :] for block in blocks], axis=0
        )

    def kick(state, oxygen, scale):
        pos, vel = state
        force = bond_forces(*pos, oxygen, mols, slots)
        return pos, [v + scale * f for v, f in zip(vel, force)]

    for first in range(0, group, 2):
        members = range(first, min(first + 2, group))
        charge = [charges[w] for w in members]
        oxygen = [(q < -1.5).astype(F32) for q in charge]
        inverse = [jnp.where(q < -1.5, 1.0 / oxygen_mass, 1.0) for q in charge]
        states = [
            (
                [gather(w, 0, c) for c in range(3)],
                [gather(w, 1, c) * scale for c in range(3)],
            )
            for w, scale in zip(members, inverse)
        ]
        for part in (0.5, 1.0):
            states = [
                kick(state, o, (part * inner_step) * scale)
                for state, o, scale in zip(states, oxygen, inverse)
            ]
            states = advance(states)
        for w, state, q, o, scale in zip(members, states, charge, oxygen, inverse):
            pos, vel = kick(state, o, (0.5 * inner_step) * scale)
            mass = jnp.where(q < -1.5, oxygen_mass, 1.0)
            for a, values in enumerate((pos, [v * mass for v in vel])):
                for c in range(3):
                    for i in range(nb):
                        rows = values[c][i * lb : (i + 1) * lb]
                        outs[i][pl.ds((a * group + w) * n + c * lb, lb), :] = rows


def call(kernel, outs, scratch, scalar, *operands, space=pltpu.VMEM):
    vmem = pl.BlockSpec(memory_space=pltpu.VMEM)
    smem = pl.BlockSpec(memory_space=pltpu.SMEM)
    return pl.pallas_call(
        kernel,
        out_shape=outs,
        in_specs=([] if scalar is None else [smem]) + [pl.BlockSpec(memory_space=space)] * len(operands),
        out_specs=[vmem] * len(outs),
        scratch_shapes=scratch,
        compiler_params=pltpu.CompilerParams(vmem_limit_bytes=24 * 1024 * 1024),
    )(*(() if scalar is None else (scalar,)), *operands)


def exchange(blocks, nb):
    return [
        lax.ppermute(block, "bead", [(i, i ^ k) for i in range(nb)]) if k else block
        for block, k in zip(blocks, block_order(nb))
    ]


def local(nb, ns, positions, momenta, molecules):
    lb, _, cells, slots = positions.shape
    mols = molecules.shape[1]
    group = cells // nb
    beads = lb * nb
    b = lax.axis_index("bead").astype(jnp.int32).reshape(1)

    def shape(*dims):
        return jax.ShapeDtypeStruct(dims, F32)

    rows = lb * 3 * cells
    state = [shape(cells, 3 * lb, slots)] * 2
    ends = [shape(3 * lb + 8, slots)] * 2
    blocks = [shape(2 * group * 3 * lb, slots)] * nb
    store = [jax.ShapeDtypeStruct(*entry) for entry in store_shapes(cells, lb, slots)]
    keep = pltpu.VMEM((slots, slots), F32)
    edge_scratch = [pltpu.VMEM((2 * lb * 8, slots), F32), keep] + [
        pltpu.VMEM(*entry) for entry in store_shapes(2, lb, slots)
    ]

    def halos(to_right, to_left):
        left = lax.ppermute(to_right, "space", [(s, (s + 1) % ns) for s in range(ns)])
        right = lax.ppermute(to_left, "space", [(s, (s - 1) % ns) for s in range(ns)])
        return left, right

    def inside(xs, charges):
        own = call(
            functools.partial(own_kernel, cells, lb, slots), store, [], None, xs, charges
        )
        (inner,) = call(
            functools.partial(interior_kernel, cells, lb, mols, slots),
            [shape((cells - 2) * lb * 8, slots)],
            [keep],
            None,
            charges,
            *own,
        )
        return own, inner

    xs, ps, perm, charges, to_right, to_left = call(
        functools.partial(order_kernel, lb, cells, mols, slots),
        state
        + [jax.ShapeDtypeStruct((cells, slots, slots), BF16), shape(cells, slots)]
        + ends,
        [
            pltpu.VMEM((3, cells, mols), jnp.int32),
            pltpu.VMEM((rows, slots), F32),
            pltpu.VMEM((rows, slots), F32),
            pltpu.VMEM((3, cells, slots), jnp.int32),
            pltpu.SemaphoreType.DMA((3,)),
        ],
        None,
        *(
            pltpu.with_memory_space_constraint(a, pltpu.HBM)
            for a in (
                jnp.transpose(molecules, (2, 0, 1)),
                positions.reshape(rows, slots),
                momenta.reshape(rows, slots),
            )
        ),
        space=pltpu.HBM,
    )
    left, right = halos(to_right, to_left)
    own, inner = inside(xs, charges)
    sent = call(
        functools.partial(kick_kernel, nb, group, lb, cells, mols, slots),
        blocks,
        [pltpu.VMEM((cells, 3 * lb, slots), F32)] + edge_scratch,
        b,
        xs,
        ps,
        charges,
        left,
        right,
        inner,
        *own,
    )
    stepped = call(
        functools.partial(steps_kernel, nb, group, lb, mols, slots),
        blocks,
        [],
        b,
        *exchange(sent, nb),
        jnp.asarray(propagator(beads, lb)),
        charges,
    )
    xs, ps, to_right, to_left = call(
        functools.partial(gather_kernel, nb, group, lb, cells, slots),
        state + ends,
        [],
        b,
        *exchange(stepped, nb),
        charges,
    )
    left, right = halos(to_right, to_left)
    own, inner = inside(xs, charges)
    new_x, new_p = call(
        functools.partial(final_kernel, cells, lb, mols, slots),
        [shape(rows, slots)] * 2,
        edge_scratch,
        None,
        xs,
        ps,
        charges,
        left,
        right,
        inner,
        perm,
        *own,
    )
    return new_x.reshape(positions.shape), new_p.reshape(positions.shape)


def solution(mesh):
    spec = P("bead", None, "space", None)
    return jax.shard_map(
        functools.partial(local, mesh.shape["bead"], mesh.shape["space"]),
        mesh=mesh,
        in_specs=(spec, spec, P("space", None, None)),
        out_specs=(spec, spec),
        check_vma=False,
    )
```

```python
import functools

import jax
import jax.numpy as jnp
import ml_dtypes
import numpy as np
from jax import lax
from jax.experimental import pallas as pl
from jax.experimental.pallas import tpu as pltpu
from jax.sharding import PartitionSpec as P

charge_oxygen = -0.8476
charge_hydrogen = 0.4238
coulomb_scale = 24.0
coulomb_soft = 0.004
well_depth = 0.02
sigma_square = 0.0841
lennard_soft = 0.04
bond_stiffness = 20000.0
bond_square = 0.0081
angle_stiffness = 5000.0
angle_square = 0.0204
cycle_frequency = 60.0
outer_step = 0.02
inner_step = 0.01
oxygen_mass = 16.0

REACH = 1
X_HALO = 2 * REACH
P_HALO = REACH

F32 = jnp.float32
BF16 = jnp.bfloat16


def rounded(a):
    return a.astype(BF16).astype(F32)


def split3(a):
    high = rounded(a)
    rest = a - high
    mid = rounded(rest)
    return high, mid, rest - mid


def two_part(a):
    high = rounded(a)
    return high + rounded(a - high)


def dot_nn(a, b):
    return lax.dot_general(a, b, (((1,), (0,)), ((), ())), preferred_element_type=F32)


def dot_nt(a, b):
    return lax.dot_general(a, b, (((1,), (1,)), ((), ())), preferred_element_type=F32)


def block_order(nb):
    return sorted(range(nb), key=lambda k: (k > 0, -bin(k).count("1"), k))


def propagator(beads, beads_dev):
    j = np.arange(beads)
    angles = 2.0 * np.pi * ((j[:, None] * j[None, :]) % beads) / beads
    half = beads // 2
    col = j[None, :]
    u = np.where(
        col == 0,
        np.sqrt(1.0 / beads),
        np.where(
            col < half,
            np.sqrt(2.0 / beads) * np.cos(angles),
            np.where(
                col == half,
                np.sqrt(1.0 / beads) * np.cos(angles),
                np.sqrt(2.0 / beads) * np.sin(angles),
            ),
        ),
    )
    w = 2.0 * cycle_frequency * np.sin(np.pi * j / beads)
    cosines = np.cos(w * inner_step)
    spring = w * np.sin(w * inner_step)
    drift = np.where(j == 0, inner_step, np.sin(w * inner_step) / np.where(j == 0, 1.0, w))
    def circulant(values, bead):
        first = ((u * values) @ u.T)[:, 0]
        return first[(bead[:, None] - bead[None, :]) % beads]

    out = []
    for b in range(beads // beads_dev):
        block = np.array(block_order(beads // beads_dev))[j // beads_dev]
        bead = (block ^ b) * beads_dev + j % beads_dev
        a = circulant(cosines, bead)
        whole = np.block([[a, circulant(drift, bead)], [-circulant(spring, bead), a]])
        high = whole.astype(ml_dtypes.bfloat16)
        rest = whole - high.astype(np.float64)
        mid = rest.astype(ml_dtypes.bfloat16)
        low = (rest - mid.astype(np.float64)).astype(ml_dtypes.bfloat16)
        out.append(np.concatenate([high, high, mid, mid, high, low], axis=1))
    return np.stack(out)


def lane_tables(lanes, mols, slots):
    lane = lax.broadcasted_iota(jnp.int32, lanes.shape, 1)
    unit = jnp.where(lane < mols, charge_oxygen / charge_hydrogen, 1.0)
    return jnp.where(lanes < slots, unit, 0.0)


def permuted(rows, perm):
    n = rows.shape[0]
    stacked = jnp.concatenate(split3(rows), axis=0).astype(BF16)
    moved = dot_nn(stacked, perm)
    return moved[:n] + moved[n : 2 * n] + moved[2 * n :]


def unpermuted(rows, perm):
    n = rows.shape[0]
    stacked = jnp.concatenate(split3(rows), axis=0).astype(BF16)
    moved = dot_nt(stacked, perm)
    return moved[:n] + moved[n : 2 * n] + moved[2 * n :]


def order_kernel(lb, cells, mols, slots, mol_hbm, x_hbm, p_hbm, *refs):
    xo, po, perm_ref, q_ref, to_right, to_left = refs[:6]
    mol_ref, x_ref, p_ref, wide, sems = refs[6:]
    copies = [
        pltpu.make_async_copy(source, dest, sems.at[i])
        for i, (source, dest) in enumerate(
            ((mol_hbm, mol_ref), (x_hbm, x_ref), (p_hbm, p_ref))
        )
    ]
    for copy in copies:
        copy.start()
    row = lax.broadcasted_iota(jnp.int32, (slots, slots), 0)
    col = lax.broadcasted_iota(jnp.int32, (slots, slots), 1)
    upper = (row < col).astype(F32).astype(BF16)
    rows, row = row, row.astype(F32)
    lane = lax.broadcasted_iota(jnp.int32, (cells, slots), 1)
    far = 4.0 * slots
    wide[...] = jnp.full(wide.shape, slots, jnp.int32)
    copies[0].wait()
    for t in range(3):
        wide[t, :, :mols] = mol_ref[t]
    lanes = jnp.where(
        lane < mols,
        wide[0],
        jnp.where(lane < 2 * mols, pltpu.roll(wide[1], mols, 1), pltpu.roll(wide[2], 2 * mols, 1)),
    )
    lanes = jnp.where(lane < 3 * mols, lanes, slots)
    charges = lane_tables(lanes, mols, slots)
    q_ref[...] = charges
    free = lanes >= slots
    key = jnp.where(
        free, far + dot_nn(free.astype(F32).astype(BF16), upper), lanes.astype(F32)
    )
    ones = jnp.ones((slots, slots), BF16)
    used = jnp.zeros((slots, slots), F32)
    for cell in range(cells):
        held = (row == key[cell : cell + 1]).astype(F32).astype(BF16)
        used = jnp.where(col == cell, dot_nn(held, ones), used)
    rank = dot_nn((col < rows).astype(F32).astype(BF16), (1.0 - used).astype(BF16))
    slot_key = jnp.where(used > 0.5, row, far + rank)
    copies[1].wait()
    copies[2].wait()
    n = 3 * lb
    for cell in range(cells):
        slot_column = jnp.broadcast_to(slot_key[:, cell : cell + 1], (slots, slots))
        perm = (slot_column == key[cell : cell + 1]).astype(F32).astype(BF16)
        perm_ref[cell] = perm
        atoms = [
            ref[pl.ds(comp * cells + cell, lb, stride=3 * cells), :]
            for ref in (x_ref, p_ref)
            for comp in range(3)
        ]
        moved = permuted(jnp.concatenate(atoms, axis=0), perm)
        xo[cell] = moved[:n]
        po[cell] = moved[n:]
    for out, xs, ps in (
        (to_right, (cells - 2, cells - 1), cells - 1),
        (to_left, (0, 1), 0),
    ):
        out[9 * lb :, :] = jnp.zeros((8, slots), F32)
        for e, cell in enumerate(xs):
            out[pl.ds(e * n, n), :] = xo[cell]
            out[pl.ds(9 * lb + e, 1), :] = charges[cell : cell + 1]
        out[pl.ds(2 * n, n), :] = po[ps]


def put_tiles(scratch, first, count, rows):
    for index, value in rows:
        scratch[pl.ds(first * 8 + index, count, stride=8), :] = value


OFFSETS = (-1.0, 0.0, 1.0)


def build_tiles(tiles, first, count, x, y, z):
    x, y, z = two_part(x - 0.5), two_part(y - 0.5), two_part(z - 0.5)
    norm = x * x + y * y + z * z + 0.5 * coulomb_soft
    high = two_part(norm)
    low = norm - high
    put_tiles(
        tiles, first, count, ((0, x), (1, y), (2, z), (3, high), (4, low), (5, high), (6, low))
    )


def store_shapes(count, beads, slots):
    n = count * beads
    return (
        [((n * 8, slots), F32), ((n // 2, slots, 64), BF16)]
        + [((n // 2, 32, slots), BF16)] * 3
        + [((n, 32, slots), BF16)]
    )


STORE = 6


class Store:
    def __init__(self, refs, beads):
        self.tiles, self.peers, *sums, self.targets = refs
        self.sums = sums
        self.beads = beads


def tile_of(ref, n):
    return ref[pl.ds(pl.multiple_of(n * 8, 8), 8), :]


def prepare(store, charges, count, slots):
    tiles, beads = store.tiles, store.beads
    row8 = lax.broadcasted_iota(jnp.int32, (8, slots), 0)
    place, norms = row8 < 3, row8 < 5
    target_rows = place | (row8 == 5) | (row8 == 6)
    ones_low = jnp.where((row8 == 3) | (row8 == 4), 1.0, 0.0)
    ones_high = jnp.where((row8 == 5) | (row8 == 6), 1.0, 0.0)
    ones_last = jnp.where(row8 == 7, 1.0, 0.0)
    pairs = beads // 2
    total = count * pairs
    unroll = max(n for n in range(1, max(2, min(17, total // 4 + 1))) if total % n == 0)

    def stack(values):
        return jnp.concatenate(values, axis=0).astype(BF16)

    def step(index, carry):
        for u in range(unroll):
            m = index * unroll + u
            charge = charges[lax.div(m, pairs)]
            units = [
                jnp.where(row8 == 3, charge, jnp.where(row8 == 4, offset * charge, 0.0))
                for offset in OFFSETS
            ]
            left, high_rows, mid_rows = [], [], []
            for h in range(2):
                value = tile_of(tiles, 2 * m + h)
                high = rounded(value)
                mid = value - high
                x_high, x_mid = high[0:1], mid[0:1]
                left_high = jnp.where(place, -2.0 * high, jnp.where(norms, high, ones_high))
                left_mid = jnp.where(place, -2.0 * mid, jnp.where(norms, mid, 0.0))
                left_last = jnp.where(
                    place,
                    -2.0 * mid,
                    jnp.where(
                        row8 == 3,
                        2.0 * x_high,
                        jnp.where(row8 == 4, 2.0 * x_mid, ones_last - 2.0 * ones_high),
                    ),
                )
                left += [left_high, left_high, left_mid, left_last]
                right_high = jnp.where(target_rows, high, ones_low)
                right_mid = jnp.where(target_rows, mid, 0.0)
                right_last = jnp.where(
                    place,
                    mid,
                    jnp.where(
                        row8 == 5, x_high, jnp.where(row8 == 6, x_mid, ones_low + ones_last)
                    ),
                )
                store.targets[2 * m + h] = stack([right_high, right_mid, right_high, right_last])
                high_rows.append(high * charge)
                mid_rows.append(jnp.where(place, mid * charge, 0.0))
            store.peers[m] = stack(left).T
            for o in range(3):
                rows = []
                for h in range(2):
                    rows += [jnp.where(place, high_rows[h], units[o]), mid_rows[h]]
                store.sums[o][m] = stack(rows)
        return carry

    lax.fori_loop(0, total // unroll, step, 0)


class PairLoop:
    def __init__(self, mols, slots, beads, keep):
        self.mols, self.slots, self.keep = mols, slots, keep
        self.pairs = beads // 2
        self.unroll = min(self.pairs, 4)
        self.per_cell = self.pairs // self.unroll
        orows = -(-mols // 8) * 8
        self.row8 = lax.broadcasted_iota(jnp.int32, (8, slots), 0)
        lj_row = lax.broadcasted_iota(jnp.int32, (orows, slots), 0)
        lj_lane = lax.broadcasted_iota(jnp.int32, (orows, slots), 1)
        self.first_lanes, self.second_lanes = lj_lane < mols, lj_lane < 2 * mols
        self.corner = (lj_row < mols) & self.first_lanes

        i = lax.broadcasted_iota(jnp.int32, (slots, slots), 0)
        j = lax.broadcasted_iota(jnp.int32, (slots, slots), 1)
        i = jnp.where(i >= 2 * mols, i - 2 * mols, jnp.where(i >= mols, i - mols, i))
        j = jnp.where(j >= 2 * mols, j - 2 * mols, jnp.where(j >= mols, j - mols, j))
        keep[...] = (i != j).astype(F32)

        lane64 = lax.broadcasted_iota(jnp.int32, (slots, 64), 1) & 31
        odd = (lane64 >= 27) & (lane64 < 31)
        even = lane64 == 31
        self.signs = [
            jnp.where(odd, -1.0, 1.0).astype(BF16),
            jnp.where(odd | even, 0.0, 1.0).astype(BF16),
            None,
        ]
        self.zero = jnp.zeros((32, slots), BF16)

    def pair(self, peers, charge):
        mols, slots = self.mols, self.slots
        orows = self.corner.shape[0]
        pair_scale = coulomb_scale * charge_hydrogen * charge_hydrogen
        k3 = sigma_square**3
        ratio = (charge_hydrogen / charge_oxygen) ** 2 / pair_scale
        lj_a = 24.0 * well_depth * 2.0 * k3 * k3 * ratio
        lj_b = 24.0 * well_depth * k3 * ratio
        zero = self.zero
        own, m = peers[1]
        left = jnp.concatenate(
            [
                store.peers[index] if sign is None else store.peers[index] * sign
                for (store, index), sign in zip(peers, self.signs)
            ],
            axis=0,
        )
        right = jnp.concatenate(
            [
                jnp.concatenate([own.targets[2 * m], zero], axis=1),
                jnp.concatenate([zero, own.targets[2 * m + 1]], axis=1),
            ],
            axis=0,
        )
        squares = dot_nn(left, right)
        blocks = [[], [], []]
        for h in range(2):
            lanes = slice(h * slots, (h + 1) * slots)
            near = [squares[o * slots : o * slots + orows, lanes] for o in range(3)]
            packed = jnp.where(
                self.first_lanes,
                near[0],
                jnp.where(
                    self.second_lanes,
                    pltpu.roll(near[1], mols, 1),
                    pltpu.roll(near[2], 2 * mols, 1),
                ),
            )
            root = lax.rsqrt(packed + (lennard_soft - coulomb_soft))
            inverse = root * root
            cube = inverse * inverse * inverse
            lj = (cube * lj_a - lj_b) * (cube * inverse)
            for o in range(3):
                root = lax.rsqrt(squares[o * slots : (o + 1) * slots, lanes])
                strength = root * root * root
                part = pltpu.roll(lj, slots - o * mols, 1) if o else lj
                strength = jnp.concatenate(
                    [strength[:orows] + jnp.where(self.corner, part, 0.0), strength[orows:]],
                    axis=0,
                )
                if o == 1:
                    strength = strength * self.keep[...]
                high = strength.astype(BF16)
                low = (strength - high.astype(F32)).astype(BF16)
                blocks[o].append(jnp.concatenate([high, low], axis=0))
        sums = None
        for o, (store, index) in enumerate(peers):
            weights = store.sums[o][index]
            value = dot_nn(
                jnp.concatenate([weights, weights], axis=1), jnp.concatenate(blocks[o], axis=1)
            )
            sums = value if sums is None else sums + value
        scale = charge * pair_scale
        out = []
        for h in range(2):
            part = sums[16 * h : 16 * h + 16, h * slots : (h + 1) * slots]
            total = part[0:8] + part[8:16]
            total = total + jnp.where(self.row8 == 0, total[4:5], 0.0)
            out.append((tile_of(own.tiles, 2 * m + h) * total[3:4] - total) * scale)
        return out

    def cells(self, store, charges, first, last, forces, limit):
        total = (last - first) * self.pairs
        unroll = max(n for n in range(1, limit + 1) if total % n == 0)

        def step(index, carry):
            for u in range(unroll):
                m = index * unroll + u
                at = m + first * self.pairs
                peers = [(store, at + (o - 1) * self.pairs) for o in range(3)]
                out = self.pair(peers, charges[lax.div(at, self.pairs)])
                for h in range(2):
                    n = 2 * m + h
                    forces[pl.ds(pl.multiple_of(n * 8, 8), 8), :] = out[h]
            return carry

        lax.fori_loop(0, total // unroll, step, 0)


def read_force(forces, w, beads, comp):
    return forces[pl.ds(w * beads * 8 + comp, beads, stride=8), :]


def own_kernel(cells, lb, slots, x_ref, q_ref, *refs):
    store = Store(refs, lb)
    for w in range(cells):
        rows = x_ref[w]
        build_tiles(store.tiles, w * lb, lb, rows[:lb], rows[lb : 2 * lb], rows[2 * lb :])
    prepare(store, Rows(q_ref, 0), cells, slots)


def interior_kernel(cells, lb, mols, slots, q_ref, *refs):
    store = Store(refs[:STORE], lb)
    forces, keep = refs[STORE:]
    PairLoop(mols, slots, lb, keep).cells(store, Rows(q_ref, 0), 1, cells - 1, forces, 64)


def edge_kernel(nb, group, lb, cells, mols, slots, b_ref, *refs):
    x_ref, p_ref, q_ref, left, right, inner = refs[:6]
    own = Store(refs[6 : 6 + STORE], lb)
    refs = refs[6 + STORE :]
    outs, q_out = refs[:nb], refs[nb]
    kicked, halo_forces, keep = refs[nb + 1 : nb + 4]
    halo = Store(refs[nb + 4 :], lb)
    n = 3 * lb
    count = cells + 2 * X_HALO
    b = b_ref[0]

    charge_rows = [left[pl.ds(9 * lb + e, 1), :] for e in range(2)]
    charge_rows += [q_ref[c : c + 1, :] for c in range(cells)]
    charge_rows += [right[pl.ds(9 * lb + e, 1), :] for e in range(2)]
    q_out[...] = jnp.zeros(q_out.shape, F32)
    for w in range(count):
        q_out[w : w + 1, :] = charge_rows[w]
    for e in range(4):
        edge = (left, right)[e // 2]
        rows = edge[pl.ds((e % 2) * n, n), :]
        build_tiles(halo.tiles, e * lb, lb, rows[:lb], rows[lb : 2 * lb], rows[2 * lb :])

    class Edges:
        def __getitem__(self, e):
            return q_out[pl.ds(jnp.where(e < 2, e, e + cells), 1), :]

    prepare(halo, Edges(), 4, slots)
    loop = PairLoop(mols, slots, lb, keep)

    def place(w):
        if w < X_HALO:
            return halo, w
        if w >= cells + X_HALO:
            return halo, w - cells
        return own, w - X_HALO

    targets = (1, 2, cells + 1, cells + 2)

    def edge_step(step, carry):
        for e, w in enumerate(targets):
            for u in range(loop.unroll):
                index = step * loop.unroll + u
                peers = [
                    (store, cell * loop.pairs + index) for store, cell in map(place, (w - 1, w, w + 1))
                ]
                out = loop.pair(peers, charge_rows[w])
                for h in range(2):
                    at = (e * lb + 2 * index + h) * 8
                    halo_forces[pl.ds(pl.multiple_of(at, 8), 8), :] = out[h]
        return carry

    lax.fori_loop(0, loop.per_cell, edge_step, 0)
    half = 0.5 * outer_step
    for w in range(1, count - 1):
        if w < X_HALO:
            old = left[pl.ds(2 * n, n), :]
        elif w >= cells + X_HALO:
            old = right[pl.ds(2 * n, n), :]
        else:
            old = p_ref[w - X_HALO]
        source, cell = (
            (halo_forces, targets.index(w)) if w in targets else (inner, w - X_HALO - 1)
        )
        force = jnp.concatenate([read_force(source, cell, lb, c) for c in range(3)], axis=0)
        kicked[w - 1] = old + half * force
    width = group + 2 * P_HALO
    for i, k in enumerate(block_order(nb)):
        first = jnp.bitwise_xor(b, k) * group
        for w in range(width):
            outs[i][pl.ds((width + w) * n, n), :] = kicked[first + w]
            source = first + w - P_HALO
            inside = x_ref[jnp.clip(source, 0, cells - 1)]
            if w < P_HALO:
                inside = jnp.where(source < 0, left[pl.ds(n, n), :], inside)
            elif w >= group + P_HALO:
                inside = jnp.where(source >= cells, right[pl.ds(0, n), :], inside)
            outs[i][pl.ds(w * n, n), :] = inside


class Rows:
    def __init__(self, ref, first):
        self.ref, self.first = ref, first

    def __getitem__(self, index):
        return self.ref[pl.ds(self.first + index, 1), :]


def bond_forces(x, y, z, used, mols, slots):
    def partner(a, t):
        return pltpu.roll(a, slots - t * mols, 1)

    first = [a - partner(a, 1) for a in (x, y, z)]
    second = [a - partner(a, 2) for a in (x, y, z)]
    third = [s - f for f, s in zip(first, second)]

    def pull(bond, stiffness, square):
        length = bond[0] * bond[0] + bond[1] * bond[1] + bond[2] * bond[2]
        return (stiffness * used) * (length - square)

    c1 = pull(first, bond_stiffness, bond_square)
    c2 = pull(second, bond_stiffness, bond_square)
    c3 = pull(third, angle_stiffness, angle_square)
    out = []
    for f, s, t in zip(first, second, third):
        on_first = c1 * f - c3 * t
        on_second = c2 * s + c3 * t
        on_oxygen = -(c1 * f + c2 * s)
        out.append(
            on_oxygen + pltpu.roll(on_first, mols, 1) + pltpu.roll(on_second, 2 * mols, 1)
        )
    return out


def steps_kernel(nb, group, lb, mols, slots, b_ref, *refs):
    blocks = refs[:nb]
    step_ref, q_ref, xv = refs[nb : nb + 3]
    beads = nb * lb
    store = Store(refs[nb + 3 :], beads)
    width = group + 2 * P_HALO
    n = 3 * lb
    b = b_ref[0]
    step = step_ref[b]
    charges = Rows(q_ref, b * group + P_HALO)

    def advance(states):
        flat = [
            jnp.concatenate([x, v], axis=0) for pos, vel in states for x, v in zip(pos, vel)
        ]
        high, mid, low = split3(jnp.concatenate(flat, axis=1))
        stacked = jnp.concatenate([high, mid, high, mid, low, high], axis=0).astype(BF16)
        new = dot_nn(step, stacked)
        out = []
        for i in range(len(states)):
            columns = [
                new[:, (3 * i + c) * slots : (3 * i + c + 1) * slots] for c in range(3)
            ]
            out.append(([a[:beads] for a in columns], [a[beads:] for a in columns]))
        return out

    def gather(w, a, comp):
        return jnp.concatenate(
            [block[pl.ds((a * width + w) * n + comp * lb, lb), :] for block in blocks], axis=0
        )

    def kick(state, oxygen, scale):
        pos, vel = state
        force = bond_forces(*pos, oxygen, mols, slots)
        return pos, [v + scale * f for v, f in zip(vel, force)]

    for first in range(0, width, 2):
        members = range(first, min(first + 2, width))
        charge = [charges[w] for w in members]
        oxygen = [(q < -1.5).astype(F32) for q in charge]
        inverse = [jnp.where(q < -1.5, 1.0 / oxygen_mass, 1.0) for q in charge]
        states = [
            (
                [gather(w, 0, c) for c in range(3)],
                [gather(w, 1, c) * scale for c in range(3)],
            )
            for w, scale in zip(members, inverse)
        ]
        for part in (0.5, 1.0):
            states = [
                kick(state, o, (part * inner_step) * scale)
                for state, o, scale in zip(states, oxygen, inverse)
            ]
            states = advance(states)
        for w, state, q, o, scale in zip(members, states, charge, oxygen, inverse):
            if 1 <= w <= width - 2:
                pos, vel = kick(state, o, (0.5 * inner_step) * scale)
                mass = jnp.where(q < -1.5, oxygen_mass, 1.0)
                for c in range(3):
                    xv[w - 1, pl.ds(c * beads, beads), :] = pos[c]
                    xv[w - 1, pl.ds((3 + c) * beads, beads), :] = vel[c] * mass
            build_tiles(store.tiles, w * beads, beads, *state[0])
    prepare(store, charges, width, slots)


def final_kernel(nb, group, lb, mols, slots, b_ref, *refs):
    perm_ref, q_ref, xv = refs[:3]
    beads = nb * lb
    store = Store(refs[3 : 3 + STORE], beads)
    ys = refs[3 + STORE : 3 + STORE + nb]
    forces, keep = refs[3 + STORE + nb :]
    b = b_ref[0]
    charges = Rows(q_ref, b * group + P_HALO)
    loop = PairLoop(mols, slots, beads, keep)
    loop.cells(store, charges, P_HALO, P_HALO + group, forces, 32)
    for w in range(group):
        old = xv[w]
        m = 3 * beads
        force = jnp.concatenate([read_force(forces, w, beads, c) for c in range(3)], axis=0)
        state = jnp.concatenate([old[:m], old[m:] + (0.5 * outer_step) * force], axis=0)
        state = unpermuted(state, perm_ref[b * group + w])
        for a in range(2):
            for c in range(3):
                for i, k in enumerate(block_order(nb)):
                    row = (a * 3 + c) * beads + i * lb
                    ys[k][pl.ds(((a * group + w) * 3 + c) * lb, lb), :] = state[row : row + lb]


def unpack_kernel(nb, group, lb, cells, b_ref, *refs):
    ys = refs[:nb]
    outs = refs[nb:]
    b = b_ref[0]
    for k in range(nb):
        source = jnp.bitwise_xor(b, k)
        for a in range(2):
            for w in range(group):
                for c in range(3):
                    outs[a][pl.ds(c * cells + source * group + w, lb, stride=3 * cells), :] = ys[
                        k
                    ][pl.ds(((a * group + w) * 3 + c) * lb, lb), :]


def call(kernel, outs, scratch, scalar, *operands, space=pltpu.VMEM):
    vmem = pl.BlockSpec(memory_space=pltpu.VMEM)
    smem = pl.BlockSpec(memory_space=pltpu.SMEM)
    return pl.pallas_call(
        kernel,
        out_shape=outs,
        in_specs=([] if scalar is None else [smem]) + [pl.BlockSpec(memory_space=space)] * len(operands),
        out_specs=[vmem] * len(outs),
        scratch_shapes=scratch,
        compiler_params=pltpu.CompilerParams(vmem_limit_bytes=24 * 1024 * 1024),
    )(*(() if scalar is None else (scalar,)), *operands)


def exchange(blocks, order):
    return [
        lax.ppermute(block, "bead", [(i, i ^ k) for i in range(len(order))]) if k else block
        for block, k in zip(blocks, order)
    ]


def local(nb, ns, positions, momenta, molecules):
    lb, _, cells, slots = positions.shape
    mols = molecules.shape[1]
    group = cells // nb
    beads = lb * nb
    width = group + 2 * P_HALO
    b = lax.axis_index("bead").astype(jnp.int32).reshape(1)

    def shape(*dims):
        return jax.ShapeDtypeStruct(dims, F32)

    edge = shape(9 * lb + 8, slots)
    rows = lb * 3 * cells
    xs, ps, perm, charges, to_right, to_left = call(
        functools.partial(order_kernel, lb, cells, mols, slots),
        [shape(cells, 3 * lb, slots)] * 2
        + [jax.ShapeDtypeStruct((cells, slots, slots), BF16), shape(cells, slots), edge, edge],
        [
            pltpu.VMEM((3, cells, mols), jnp.int32),
            pltpu.VMEM((rows, slots), F32),
            pltpu.VMEM((rows, slots), F32),
            pltpu.VMEM((3, cells, slots), jnp.int32),
            pltpu.SemaphoreType.DMA((3,)),
        ],
        None,
        *(
            pltpu.with_memory_space_constraint(a, pltpu.HBM)
            for a in (
                jnp.transpose(molecules, (2, 0, 1)),
                positions.reshape(rows, slots),
                momenta.reshape(rows, slots),
            )
        ),
        space=pltpu.HBM,
    )
    left = lax.ppermute(to_right, "space", [(s, (s + 1) % ns) for s in range(ns)])
    right = lax.ppermute(to_left, "space", [(s, (s - 1) % ns) for s in range(ns)])
    q_rows = -(-(cells + 2 * X_HALO) // 8) * 8

    def store(count, store_beads):
        return [
            jax.ShapeDtypeStruct(*entry) for entry in store_shapes(count, store_beads, slots)
        ]

    keep = pltpu.VMEM((slots, slots), F32)
    own = call(
        functools.partial(own_kernel, cells, lb, slots), store(cells, lb), [], None, xs, charges
    )
    (inner,) = call(
        functools.partial(interior_kernel, cells, lb, mols, slots),
        [shape((cells - 2) * lb * 8, slots)],
        [keep],
        None,
        charges,
        *own,
    )
    *blocks, q_wide = call(
        functools.partial(edge_kernel, nb, group, lb, cells, mols, slots),
        [shape(2 * width * 3 * lb, slots)] * nb + [shape(q_rows, slots)],
        [
            pltpu.VMEM((cells + 2 * P_HALO, 3 * lb, slots), F32),
            pltpu.VMEM((4 * lb * 8, slots), F32),
            keep,
        ]
        + [pltpu.VMEM(*entry) for entry in store_shapes(4, lb, slots)],
        b,
        xs,
        ps,
        charges,
        left,
        right,
        inner,
        *own,
    )
    blocks = exchange(blocks, block_order(nb))
    step = jnp.asarray(propagator(beads, lb))
    xv, *stepped = call(
        functools.partial(steps_kernel, nb, group, lb, mols, slots),
        [shape(group, 6 * beads, slots)] + store(width, beads),
        [],
        b,
        *blocks,
        step,
        q_wide,
    )
    ys = call(
        functools.partial(final_kernel, nb, group, lb, mols, slots),
        [shape(2 * group * 3 * lb, slots)] * nb,
        [pltpu.VMEM((group * beads * 8, slots), F32), keep],
        b,
        perm,
        q_wide,
        xv,
        *stepped,
    )
    ys = exchange(ys, range(nb))
    new_x, new_p = call(
        functools.partial(unpack_kernel, nb, group, lb, cells),
        [shape(lb * 3 * cells, slots)] * 2,
        [],
        b,
        *ys,
    )
    return new_x.reshape(positions.shape), new_p.reshape(positions.shape)


def solution(mesh):
    spec = P("bead", None, "space", None)
    return jax.shard_map(
        functools.partial(local, mesh.shape["bead"], mesh.shape["space"]),
        mesh=mesh,
        in_specs=(spec, spec, P("space", None, None)),
        out_specs=(spec, spec),
        check_vma=False,
    )
```

```python
import functools

import jax
import jax.numpy as jnp
import ml_dtypes
import numpy as np
from jax import lax
from jax.experimental import pallas as pl
from jax.experimental.pallas import tpu as pltpu
from jax.sharding import PartitionSpec as P

charge_oxygen = -0.8476
charge_hydrogen = 0.4238
coulomb_scale = 24.0
coulomb_soft = 0.004
well_depth = 0.02
sigma_square = 0.0841
lennard_soft = 0.04
bond_stiffness = 20000.0
bond_square = 0.0081
angle_stiffness = 5000.0
angle_square = 0.0204
cycle_frequency = 60.0
outer_step = 0.02
inner_step = 0.01
oxygen_mass = 16.0

REACH = 1
X_HALO = 2 * REACH
P_HALO = REACH

F32 = jnp.float32
BF16 = jnp.bfloat16


def rounded(a):
    return a.astype(BF16).astype(F32)


def split3(a):
    high = rounded(a)
    rest = a - high
    mid = rounded(rest)
    return high, mid, rest - mid


def two_part(a):
    high = rounded(a)
    return high + rounded(a - high)


def dot_nn(a, b):
    return lax.dot_general(a, b, (((1,), (0,)), ((), ())), preferred_element_type=F32)


def dot_nt(a, b):
    return lax.dot_general(a, b, (((1,), (1,)), ((), ())), preferred_element_type=F32)


def block_order(nb):
    return sorted(range(nb), key=lambda k: (k > 0, -bin(k).count("1"), k))


def propagator(beads, beads_dev):
    j = np.arange(beads)
    angles = 2.0 * np.pi * ((j[:, None] * j[None, :]) % beads) / beads
    half = beads // 2
    col = j[None, :]
    u = np.where(
        col == 0,
        np.sqrt(1.0 / beads),
        np.where(
            col < half,
            np.sqrt(2.0 / beads) * np.cos(angles),
            np.where(
                col == half,
                np.sqrt(1.0 / beads) * np.cos(angles),
                np.sqrt(2.0 / beads) * np.sin(angles),
            ),
        ),
    )
    w = 2.0 * cycle_frequency * np.sin(np.pi * j / beads)
    cosines = np.cos(w * inner_step)
    spring = w * np.sin(w * inner_step)
    drift = np.where(j == 0, inner_step, np.sin(w * inner_step) / np.where(j == 0, 1.0, w))
    def circulant(values, bead):
        first = ((u * values) @ u.T)[:, 0]
        return first[(bead[:, None] - bead[None, :]) % beads]

    out = []
    for b in range(beads // beads_dev):
        block = np.array(block_order(beads // beads_dev))[j // beads_dev]
        bead = (block ^ b) * beads_dev + j % beads_dev
        a = circulant(cosines, bead)
        whole = np.block([[a, circulant(drift, bead)], [-circulant(spring, bead), a]])
        high = whole.astype(ml_dtypes.bfloat16)
        rest = whole - high.astype(np.float64)
        mid = rest.astype(ml_dtypes.bfloat16)
        low = (rest - mid.astype(np.float64)).astype(ml_dtypes.bfloat16)
        out.append(np.concatenate([high, high, mid, mid, high, low], axis=1))
    return np.stack(out)


def lane_tables(lanes, mols, slots):
    lane = lax.broadcasted_iota(jnp.int32, lanes.shape, 1)
    unit = jnp.where(lane < mols, charge_oxygen / charge_hydrogen, 1.0)
    return jnp.where(lanes < slots, unit, 0.0)


def permuted(rows, perm):
    n = rows.shape[0]
    stacked = jnp.concatenate(split3(rows), axis=0).astype(BF16)
    moved = dot_nn(stacked, perm)
    return moved[:n] + moved[n : 2 * n] + moved[2 * n :]


def unpermuted(rows, perm):
    n = rows.shape[0]
    stacked = jnp.concatenate(split3(rows), axis=0).astype(BF16)
    moved = dot_nt(stacked, perm)
    return moved[:n] + moved[n : 2 * n] + moved[2 * n :]


def order_kernel(lb, cells, mols, slots, mol_hbm, x_hbm, p_hbm, *refs):
    xo, po, perm_ref, q_ref, to_right, to_left = refs[:6]
    mol_ref, x_ref, p_ref, wide, sems = refs[6:]
    copies = [
        pltpu.make_async_copy(source, dest, sems.at[i])
        for i, (source, dest) in enumerate(
            ((mol_hbm, mol_ref), (x_hbm, x_ref), (p_hbm, p_ref))
        )
    ]
    for copy in copies:
        copy.start()
    row = lax.broadcasted_iota(jnp.int32, (slots, slots), 0)
    col = lax.broadcasted_iota(jnp.int32, (slots, slots), 1)
    upper = (row < col).astype(F32).astype(BF16)
    rows, row = row, row.astype(F32)
    lane = lax.broadcasted_iota(jnp.int32, (cells, slots), 1)
    far = 4.0 * slots
    wide[...] = jnp.full(wide.shape, slots, jnp.int32)
    copies[0].wait()
    for t in range(3):
        wide[t, :, :mols] = mol_ref[t]
    lanes = jnp.where(
        lane < mols,
        wide[0],
        jnp.where(lane < 2 * mols, pltpu.roll(wide[1], mols, 1), pltpu.roll(wide[2], 2 * mols, 1)),
    )
    lanes = jnp.where(lane < 3 * mols, lanes, slots)
    charges = lane_tables(lanes, mols, slots)
    q_ref[...] = charges
    free = lanes >= slots
    key = jnp.where(
        free, far + dot_nn(free.astype(F32).astype(BF16), upper), lanes.astype(F32)
    )
    ones = jnp.ones((slots, slots), BF16)
    used = jnp.zeros((slots, slots), F32)
    for cell in range(cells):
        held = (row == key[cell : cell + 1]).astype(F32).astype(BF16)
        used = jnp.where(col == cell, dot_nn(held, ones), used)
    rank = dot_nn((col < rows).astype(F32).astype(BF16), (1.0 - used).astype(BF16))
    slot_key = jnp.where(used > 0.5, row, far + rank)
    copies[1].wait()
    copies[2].wait()
    n = 3 * lb
    for cell in range(cells):
        slot_column = jnp.broadcast_to(slot_key[:, cell : cell + 1], (slots, slots))
        perm = (slot_column == key[cell : cell + 1]).astype(F32).astype(BF16)
        perm_ref[cell] = perm
        atoms = [
            ref[pl.ds(comp * cells + cell, lb, stride=3 * cells), :]
            for ref in (x_ref, p_ref)
            for comp in range(3)
        ]
        moved = permuted(jnp.concatenate(atoms, axis=0), perm)
        xo[cell] = moved[:n]
        po[cell] = moved[n:]
    for out, xs, ps in (
        (to_right, (cells - 2, cells - 1), cells - 1),
        (to_left, (0, 1), 0),
    ):
        out[9 * lb :, :] = jnp.zeros((8, slots), F32)
        for e, cell in enumerate(xs):
            out[pl.ds(e * n, n), :] = xo[cell]
            out[pl.ds(9 * lb + e, 1), :] = charges[cell : cell + 1]
        out[pl.ds(2 * n, n), :] = po[ps]


def put_tiles(scratch, first, count, rows):
    for index, value in rows:
        scratch[pl.ds(first * 8 + index, count, stride=8), :] = value


OFFSETS = (-1.0, 0.0, 1.0)


def build_tiles(tiles, first, count, x, y, z):
    x, y, z = two_part(x - 0.5), two_part(y - 0.5), two_part(z - 0.5)
    norm = x * x + y * y + z * z + 0.5 * coulomb_soft
    high = two_part(norm)
    low = norm - high
    put_tiles(
        tiles, first, count, ((0, x), (1, y), (2, z), (3, high), (4, low), (5, high), (6, low))
    )


def store_shapes(count, beads, slots):
    n = count * beads
    return (
        [((n * 8, slots), F32), ((n // 2, slots, 64), BF16)]
        + [((n // 2, 32, slots), BF16)] * 3
        + [((n, 32, slots), BF16)]
    )


STORE = 6


class Store:
    def __init__(self, refs, beads):
        self.tiles, self.peers, *sums, self.targets = refs
        self.sums = sums
        self.beads = beads


def tile_of(ref, n):
    return ref[pl.ds(pl.multiple_of(n * 8, 8), 8), :]


def prepare(store, charges, count, slots):
    tiles, beads = store.tiles, store.beads
    row8 = lax.broadcasted_iota(jnp.int32, (8, slots), 0)
    place, norms = row8 < 3, row8 < 5
    target_rows = place | (row8 == 5) | (row8 == 6)
    ones_low = jnp.where((row8 == 3) | (row8 == 4), 1.0, 0.0)
    ones_high = jnp.where((row8 == 5) | (row8 == 6), 1.0, 0.0)
    ones_last = jnp.where(row8 == 7, 1.0, 0.0)
    pairs = beads // 2
    total = count * pairs
    unroll = max(n for n in range(1, max(2, min(17, total // 4 + 1))) if total % n == 0)

    def stack(values):
        return jnp.concatenate(values, axis=0).astype(BF16)

    def step(index, carry):
        for u in range(unroll):
            m = index * unroll + u
            charge = charges[lax.div(m, pairs)]
            units = [
                jnp.where(row8 == 3, charge, jnp.where(row8 == 4, offset * charge, 0.0))
                for offset in OFFSETS
            ]
            left, high_rows, mid_rows = [], [], []
            for h in range(2):
                value = tile_of(tiles, 2 * m + h)
                high = rounded(value)
                mid = value - high
                x_high, x_mid = high[0:1], mid[0:1]
                left_high = jnp.where(place, -2.0 * high, jnp.where(norms, high, ones_high))
                left_mid = jnp.where(place, -2.0 * mid, jnp.where(norms, mid, 0.0))
                left_last = jnp.where(
                    place,
                    -2.0 * mid,
                    jnp.where(
                        row8 == 3,
                        2.0 * x_high,
                        jnp.where(row8 == 4, 2.0 * x_mid, ones_last - 2.0 * ones_high),
                    ),
                )
                left += [left_high, left_high, left_mid, left_last]
                right_high = jnp.where(target_rows, high, ones_low)
                right_mid = jnp.where(target_rows, mid, 0.0)
                right_last = jnp.where(
                    place,
                    mid,
                    jnp.where(
                        row8 == 5, x_high, jnp.where(row8 == 6, x_mid, ones_low + ones_last)
                    ),
                )
                store.targets[2 * m + h] = stack([right_high, right_mid, right_high, right_last])
                high_rows.append(high * charge)
                mid_rows.append(jnp.where(place, mid * charge, 0.0))
            store.peers[m] = stack(left).T
            for o in range(3):
                rows = []
                for h in range(2):
                    rows += [jnp.where(place, high_rows[h], units[o]), mid_rows[h]]
                store.sums[o][m] = stack(rows)
        return carry

    lax.fori_loop(0, total // unroll, step, 0)


class PairLoop:
    def __init__(self, mols, slots, beads, keep):
        self.mols, self.slots, self.keep = mols, slots, keep
        self.pairs = beads // 2
        self.unroll = min(self.pairs, 4)
        self.per_cell = self.pairs // self.unroll
        orows = -(-mols // 8) * 8
        self.row8 = lax.broadcasted_iota(jnp.int32, (8, slots), 0)
        lj_row = lax.broadcasted_iota(jnp.int32, (orows, slots), 0)
        lj_lane = lax.broadcasted_iota(jnp.int32, (orows, slots), 1)
        self.corner = (lj_row < mols) & (lj_lane < mols)

        i = lax.broadcasted_iota(jnp.int32, (slots, slots), 0)
        j = lax.broadcasted_iota(jnp.int32, (slots, slots), 1)
        i = jnp.where(i >= 2 * mols, i - 2 * mols, jnp.where(i >= mols, i - mols, i))
        j = jnp.where(j >= 2 * mols, j - 2 * mols, jnp.where(j >= mols, j - mols, j))
        keep[...] = (i != j).astype(F32)

        lane64 = lax.broadcasted_iota(jnp.int32, (slots, 64), 1) & 31
        odd = (lane64 >= 27) & (lane64 < 31)
        even = lane64 == 31
        self.signs = [
            jnp.where(odd, -1.0, 1.0).astype(BF16),
            jnp.where(odd | even, 0.0, 1.0).astype(BF16),
            None,
        ]
        self.zero = jnp.zeros((32, slots), BF16)

    def pair(self, peers, charge):
        mols, slots = self.mols, self.slots
        orows = self.corner.shape[0]
        pair_scale = coulomb_scale * charge_hydrogen * charge_hydrogen
        k3 = sigma_square**3
        ratio = (charge_hydrogen / charge_oxygen) ** 2 / pair_scale
        lj_a = 24.0 * well_depth * 2.0 * k3 * k3 * ratio
        lj_b = 24.0 * well_depth * k3 * ratio
        zero = self.zero
        own, m = peers[1]
        left = jnp.concatenate(
            [
                store.peers[index] if sign is None else store.peers[index] * sign
                for (store, index), sign in zip(peers, self.signs)
            ],
            axis=0,
        )
        right = jnp.concatenate(
            [
                jnp.concatenate([own.targets[2 * m], zero], axis=1),
                jnp.concatenate([zero, own.targets[2 * m + 1]], axis=1),
            ],
            axis=0,
        )
        squares = dot_nn(left, right)
        blocks = [[], [], []]
        for h in range(2):
            lanes = slice(h * slots, (h + 1) * slots)
            for o in range(3):
                root = lax.rsqrt(squares[o * slots : (o + 1) * slots, lanes])
                strength = root * root * root
                near = squares[o * slots : o * slots + orows, lanes]
                inverse = lax.rsqrt(near + (lennard_soft - coulomb_soft))
                inverse = inverse * inverse
                cube = inverse * inverse * inverse
                lj = (cube * lj_a - lj_b) * (cube * inverse)
                strength = jnp.concatenate(
                    [strength[:orows] + jnp.where(self.corner, lj, 0.0), strength[orows:]],
                    axis=0,
                )
                if o == 1:
                    strength = strength * self.keep[...]
                high = strength.astype(BF16)
                low = (strength - high.astype(F32)).astype(BF16)
                blocks[o].append(jnp.concatenate([high, low], axis=0))
        sums = None
        for o, (store, index) in enumerate(peers):
            weights = store.sums[o][index]
            value = dot_nn(
                jnp.concatenate([weights, weights], axis=1), jnp.concatenate(blocks[o], axis=1)
            )
            sums = value if sums is None else sums + value
        scale = charge * pair_scale
        out = []
        for h in range(2):
            part = sums[16 * h : 16 * h + 16, h * slots : (h + 1) * slots]
            total = part[0:8] + part[8:16]
            total = total + jnp.where(self.row8 == 0, total[4:5], 0.0)
            out.append((tile_of(own.tiles, 2 * m + h) * total[3:4] - total) * scale)
        return out

    def cells(self, store, charges, first, last, forces, limit):
        total = (last - first) * self.pairs
        unroll = max(n for n in range(1, limit + 1) if total % n == 0)

        def step(index, carry):
            for u in range(unroll):
                m = index * unroll + u
                at = m + first * self.pairs
                peers = [(store, at + (o - 1) * self.pairs) for o in range(3)]
                out = self.pair(peers, charges[lax.div(at, self.pairs)])
                for h in range(2):
                    n = 2 * m + h
                    forces[pl.ds(pl.multiple_of(n * 8, 8), 8), :] = out[h]
            return carry

        lax.fori_loop(0, total // unroll, step, 0)


def read_force(forces, w, beads, comp):
    return forces[pl.ds(w * beads * 8 + comp, beads, stride=8), :]


def own_kernel(cells, lb, slots, x_ref, q_ref, *refs):
    store = Store(refs, lb)
    for w in range(cells):
        rows = x_ref[w]
        build_tiles(store.tiles, w * lb, lb, rows[:lb], rows[lb : 2 * lb], rows[2 * lb :])
    prepare(store, Rows(q_ref, 0), cells, slots)


def interior_kernel(cells, lb, mols, slots, q_ref, *refs):
    store = Store(refs[:STORE], lb)
    forces, keep = refs[STORE:]
    PairLoop(mols, slots, lb, keep).cells(store, Rows(q_ref, 0), 1, cells - 1, forces, 64)


def edge_kernel(nb, group, lb, cells, mols, slots, b_ref, *refs):
    x_ref, p_ref, q_ref, left, right, inner = refs[:6]
    own = Store(refs[6 : 6 + STORE], lb)
    refs = refs[6 + STORE :]
    outs, q_out = refs[:nb], refs[nb]
    kicked, halo_forces, keep = refs[nb + 1 : nb + 4]
    halo = Store(refs[nb + 4 :], lb)
    n = 3 * lb
    count = cells + 2 * X_HALO
    b = b_ref[0]

    charge_rows = [left[pl.ds(9 * lb + e, 1), :] for e in range(2)]
    charge_rows += [q_ref[c : c + 1, :] for c in range(cells)]
    charge_rows += [right[pl.ds(9 * lb + e, 1), :] for e in range(2)]
    q_out[...] = jnp.zeros(q_out.shape, F32)
    for w in range(count):
        q_out[w : w + 1, :] = charge_rows[w]
    for e in range(4):
        edge = (left, right)[e // 2]
        rows = edge[pl.ds((e % 2) * n, n), :]
        build_tiles(halo.tiles, e * lb, lb, rows[:lb], rows[lb : 2 * lb], rows[2 * lb :])

    class Edges:
        def __getitem__(self, e):
            return q_out[pl.ds(jnp.where(e < 2, e, e + cells), 1), :]

    prepare(halo, Edges(), 4, slots)
    loop = PairLoop(mols, slots, lb, keep)

    def place(w):
        if w < X_HALO:
            return halo, w
        if w >= cells + X_HALO:
            return halo, w - cells
        return own, w - X_HALO

    targets = (1, 2, cells + 1, cells + 2)

    def edge_step(step, carry):
        for e, w in enumerate(targets):
            for u in range(loop.unroll):
                index = step * loop.unroll + u
                peers = [
                    (store, cell * loop.pairs + index) for store, cell in map(place, (w - 1, w, w + 1))
                ]
                out = loop.pair(peers, charge_rows[w])
                for h in range(2):
                    at = (e * lb + 2 * index + h) * 8
                    halo_forces[pl.ds(pl.multiple_of(at, 8), 8), :] = out[h]
        return carry

    lax.fori_loop(0, loop.per_cell, edge_step, 0)
    half = 0.5 * outer_step
    for w in range(1, count - 1):
        if w < X_HALO:
            old = left[pl.ds(2 * n, n), :]
        elif w >= cells + X_HALO:
            old = right[pl.ds(2 * n, n), :]
        else:
            old = p_ref[w - X_HALO]
        source, cell = (
            (halo_forces, targets.index(w)) if w in targets else (inner, w - X_HALO - 1)
        )
        force = jnp.concatenate([read_force(source, cell, lb, c) for c in range(3)], axis=0)
        kicked[w - 1] = old + half * force
    width = group + 2 * P_HALO
    for i, k in enumerate(block_order(nb)):
        first = jnp.bitwise_xor(b, k) * group
        for w in range(width):
            outs[i][pl.ds((width + w) * n, n), :] = kicked[first + w]
            source = first + w - P_HALO
            inside = x_ref[jnp.clip(source, 0, cells - 1)]
            if w < P_HALO:
                inside = jnp.where(source < 0, left[pl.ds(n, n), :], inside)
            elif w >= group + P_HALO:
                inside = jnp.where(source >= cells, right[pl.ds(0, n), :], inside)
            outs[i][pl.ds(w * n, n), :] = inside


class Rows:
    def __init__(self, ref, first):
        self.ref, self.first = ref, first

    def __getitem__(self, index):
        return self.ref[pl.ds(self.first + index, 1), :]


def bond_forces(x, y, z, used, mols, slots):
    def partner(a, t):
        return pltpu.roll(a, slots - t * mols, 1)

    first = [a - partner(a, 1) for a in (x, y, z)]
    second = [a - partner(a, 2) for a in (x, y, z)]
    third = [s - f for f, s in zip(first, second)]

    def pull(bond, stiffness, square):
        length = bond[0] * bond[0] + bond[1] * bond[1] + bond[2] * bond[2]
        return (stiffness * used) * (length - square)

    c1 = pull(first, bond_stiffness, bond_square)
    c2 = pull(second, bond_stiffness, bond_square)
    c3 = pull(third, angle_stiffness, angle_square)
    out = []
    for f, s, t in zip(first, second, third):
        on_first = c1 * f - c3 * t
        on_second = c2 * s + c3 * t
        on_oxygen = -(c1 * f + c2 * s)
        out.append(
            on_oxygen + pltpu.roll(on_first, mols, 1) + pltpu.roll(on_second, 2 * mols, 1)
        )
    return out


def steps_kernel(nb, group, lb, mols, slots, b_ref, *refs):
    blocks = refs[:nb]
    step_ref, q_ref, xv = refs[nb : nb + 3]
    beads = nb * lb
    store = Store(refs[nb + 3 :], beads)
    width = group + 2 * P_HALO
    n = 3 * lb
    b = b_ref[0]
    step = step_ref[b]
    charges = Rows(q_ref, b * group + P_HALO)

    def advance(states):
        flat = [
            jnp.concatenate([x, v], axis=0) for pos, vel in states for x, v in zip(pos, vel)
        ]
        high, mid, low = split3(jnp.concatenate(flat, axis=1))
        stacked = jnp.concatenate([high, mid, high, mid, low, high], axis=0).astype(BF16)
        new = dot_nn(step, stacked)
        out = []
        for i in range(len(states)):
            columns = [
                new[:, (3 * i + c) * slots : (3 * i + c + 1) * slots] for c in range(3)
            ]
            out.append(([a[:beads] for a in columns], [a[beads:] for a in columns]))
        return out

    def gather(w, a, comp):
        return jnp.concatenate(
            [block[pl.ds((a * width + w) * n + comp * lb, lb), :] for block in blocks], axis=0
        )

    def kick(state, oxygen, scale):
        pos, vel = state
        force = bond_forces(*pos, oxygen, mols, slots)
        return pos, [v + scale * f for v, f in zip(vel, force)]

    for first in range(0, width, 2):
        members = range(first, min(first + 2, width))
        charge = [charges[w] for w in members]
        oxygen = [(q < -1.5).astype(F32) for q in charge]
        inverse = [jnp.where(q < -1.5, 1.0 / oxygen_mass, 1.0) for q in charge]
        states = [
            (
                [gather(w, 0, c) for c in range(3)],
                [gather(w, 1, c) * scale for c in range(3)],
            )
            for w, scale in zip(members, inverse)
        ]
        for part in (0.5, 1.0):
            states = [
                kick(state, o, (part * inner_step) * scale)
                for state, o, scale in zip(states, oxygen, inverse)
            ]
            states = advance(states)
        for w, state, q, o, scale in zip(members, states, charge, oxygen, inverse):
            if 1 <= w <= width - 2:
                pos, vel = kick(state, o, (0.5 * inner_step) * scale)
                mass = jnp.where(q < -1.5, oxygen_mass, 1.0)
                for c in range(3):
                    xv[w - 1, pl.ds(c * beads, beads), :] = pos[c]
                    xv[w - 1, pl.ds((3 + c) * beads, beads), :] = vel[c] * mass
            build_tiles(store.tiles, w * beads, beads, *state[0])
    prepare(store, charges, width, slots)


def final_kernel(nb, group, lb, mols, slots, b_ref, *refs):
    perm_ref, q_ref, xv = refs[:3]
    beads = nb * lb
    store = Store(refs[3 : 3 + STORE], beads)
    ys = refs[3 + STORE : 3 + STORE + nb]
    forces, keep = refs[3 + STORE + nb :]
    b = b_ref[0]
    charges = Rows(q_ref, b * group + P_HALO)
    loop = PairLoop(mols, slots, beads, keep)
    loop.cells(store, charges, P_HALO, P_HALO + group, forces, 32)
    for w in range(group):
        old = xv[w]
        m = 3 * beads
        force = jnp.concatenate([read_force(forces, w, beads, c) for c in range(3)], axis=0)
        state = jnp.concatenate([old[:m], old[m:] + (0.5 * outer_step) * force], axis=0)
        state = unpermuted(state, perm_ref[b * group + w])
        for a in range(2):
            for c in range(3):
                for k in range(nb):
                    row = (a * 3 + c) * beads + k * lb
                    ys[k][pl.ds(((a * group + w) * 3 + c) * lb, lb), :] = state[row : row + lb]


def unpack_kernel(nb, group, lb, cells, b_ref, *refs):
    ys = refs[:nb]
    outs = refs[nb:]
    b = b_ref[0]
    for i, k in enumerate(block_order(nb)):
        source = jnp.bitwise_xor(b, k)
        for a in range(2):
            for w in range(group):
                for c in range(3):
                    outs[a][pl.ds(c * cells + source * group + w, lb, stride=3 * cells), :] = ys[
                        i
                    ][pl.ds(((a * group + w) * 3 + c) * lb, lb), :]


def call(kernel, outs, scratch, scalar, *operands, space=pltpu.VMEM):
    vmem = pl.BlockSpec(memory_space=pltpu.VMEM)
    smem = pl.BlockSpec(memory_space=pltpu.SMEM)
    return pl.pallas_call(
        kernel,
        out_shape=outs,
        in_specs=([] if scalar is None else [smem]) + [pl.BlockSpec(memory_space=space)] * len(operands),
        out_specs=[vmem] * len(outs),
        scratch_shapes=scratch,
        compiler_params=pltpu.CompilerParams(vmem_limit_bytes=24 * 1024 * 1024),
    )(*(() if scalar is None else (scalar,)), *operands)


def exchange(blocks, nb):
    return [
        lax.ppermute(block, "bead", [(i, i ^ k) for i in range(nb)]) if k else block
        for block, k in zip(blocks, block_order(nb))
    ]


def local(nb, ns, positions, momenta, molecules):
    lb, _, cells, slots = positions.shape
    mols = molecules.shape[1]
    group = cells // nb
    beads = lb * nb
    width = group + 2 * P_HALO
    b = lax.axis_index("bead").astype(jnp.int32).reshape(1)

    def shape(*dims):
        return jax.ShapeDtypeStruct(dims, F32)

    edge = shape(9 * lb + 8, slots)
    rows = lb * 3 * cells
    xs, ps, perm, charges, to_right, to_left = call(
        functools.partial(order_kernel, lb, cells, mols, slots),
        [shape(cells, 3 * lb, slots)] * 2
        + [jax.ShapeDtypeStruct((cells, slots, slots), BF16), shape(cells, slots), edge, edge],
        [
            pltpu.VMEM((3, cells, mols), jnp.int32),
            pltpu.VMEM((rows, slots), F32),
            pltpu.VMEM((rows, slots), F32),
            pltpu.VMEM((3, cells, slots), jnp.int32),
            pltpu.SemaphoreType.DMA((3,)),
        ],
        None,
        *(
            pltpu.with_memory_space_constraint(a, pltpu.HBM)
            for a in (
                jnp.transpose(molecules, (2, 0, 1)),
                positions.reshape(rows, slots),
                momenta.reshape(rows, slots),
            )
        ),
        space=pltpu.HBM,
    )
    left = lax.ppermute(to_right, "space", [(s, (s + 1) % ns) for s in range(ns)])
    right = lax.ppermute(to_left, "space", [(s, (s - 1) % ns) for s in range(ns)])
    q_rows = -(-(cells + 2 * X_HALO) // 8) * 8

    def store(count, store_beads):
        return [
            jax.ShapeDtypeStruct(*entry) for entry in store_shapes(count, store_beads, slots)
        ]

    keep = pltpu.VMEM((slots, slots), F32)
    own = call(
        functools.partial(own_kernel, cells, lb, slots), store(cells, lb), [], None, xs, charges
    )
    (inner,) = call(
        functools.partial(interior_kernel, cells, lb, mols, slots),
        [shape((cells - 2) * lb * 8, slots)],
        [keep],
        None,
        charges,
        *own,
    )
    *blocks, q_wide = call(
        functools.partial(edge_kernel, nb, group, lb, cells, mols, slots),
        [shape(2 * width * 3 * lb, slots)] * nb + [shape(q_rows, slots)],
        [
            pltpu.VMEM((cells + 2 * P_HALO, 3 * lb, slots), F32),
            pltpu.VMEM((4 * lb * 8, slots), F32),
            keep,
        ]
        + [pltpu.VMEM(*entry) for entry in store_shapes(4, lb, slots)],
        b,
        xs,
        ps,
        charges,
        left,
        right,
        inner,
        *own,
    )
    blocks = exchange(blocks, nb)
    step = jnp.asarray(propagator(beads, lb))
    xv, *stepped = call(
        functools.partial(steps_kernel, nb, group, lb, mols, slots),
        [shape(group, 6 * beads, slots)] + store(width, beads),
        [],
        b,
        *blocks,
        step,
        q_wide,
    )
    ys = call(
        functools.partial(final_kernel, nb, group, lb, mols, slots),
        [shape(2 * group * 3 * lb, slots)] * nb,
        [pltpu.VMEM((group * beads * 8, slots), F32), keep],
        b,
        perm,
        q_wide,
        xv,
        *stepped,
    )
    ys = exchange(ys, nb)
    new_x, new_p = call(
        functools.partial(unpack_kernel, nb, group, lb, cells),
        [shape(lb * 3 * cells, slots)] * 2,
        [],
        b,
        *ys,
    )
    return new_x.reshape(positions.shape), new_p.reshape(positions.shape)


def solution(mesh):
    spec = P("bead", None, "space", None)
    return jax.shard_map(
        functools.partial(local, mesh.shape["bead"], mesh.shape["space"]),
        mesh=mesh,
        in_specs=(spec, spec, P("space", None, None)),
        out_specs=(spec, spec),
        check_vma=False,
    )
```

```python
import functools

import jax
import jax.numpy as jnp
import ml_dtypes
import numpy as np
from jax import lax
from jax.experimental import pallas as pl
from jax.experimental.pallas import tpu as pltpu
from jax.sharding import PartitionSpec as P

charge_oxygen = -0.8476
charge_hydrogen = 0.4238
coulomb_scale = 24.0
coulomb_soft = 0.004
well_depth = 0.02
sigma_square = 0.0841
lennard_soft = 0.04
bond_stiffness = 20000.0
bond_square = 0.0081
angle_stiffness = 5000.0
angle_square = 0.0204
cycle_frequency = 60.0
outer_step = 0.02
inner_step = 0.01
oxygen_mass = 16.0

F32 = jnp.float32
BF16 = jnp.bfloat16


def rounded(a):
    return a.astype(BF16).astype(F32)


def split3(a):
    high = rounded(a)
    rest = a - high
    mid = rounded(rest)
    return high, mid, rest - mid


def two_part(a):
    high = rounded(a)
    return high + rounded(a - high)


def dot_nn(a, b):
    return lax.dot_general(a, b, (((1,), (0,)), ((), ())), preferred_element_type=F32)


def dot_nt(a, b):
    return lax.dot_general(a, b, (((1,), (1,)), ((), ())), preferred_element_type=F32)


def block_order(nb):
    return sorted(range(nb), key=lambda k: (k > 0, -bin(k).count("1"), k))


def propagator(beads, beads_dev):
    j = np.arange(beads)
    angles = 2.0 * np.pi * ((j[:, None] * j[None, :]) % beads) / beads
    half = beads // 2
    col = j[None, :]
    u = np.where(
        col == 0,
        np.sqrt(1.0 / beads),
        np.where(
            col < half,
            np.sqrt(2.0 / beads) * np.cos(angles),
            np.where(
                col == half,
                np.sqrt(1.0 / beads) * np.cos(angles),
                np.sqrt(2.0 / beads) * np.sin(angles),
            ),
        ),
    )
    w = 2.0 * cycle_frequency * np.sin(np.pi * j / beads)
    cosines = np.cos(w * inner_step)
    spring = w * np.sin(w * inner_step)
    drift = np.where(j == 0, inner_step, np.sin(w * inner_step) / np.where(j == 0, 1.0, w))
    def circulant(values, bead):
        first = ((u * values) @ u.T)[:, 0]
        return first[(bead[:, None] - bead[None, :]) % beads]

    out = []
    for b in range(beads // beads_dev):
        block = np.array(block_order(beads // beads_dev))[j // beads_dev]
        bead = (block ^ b) * beads_dev + j % beads_dev
        a = circulant(cosines, bead)
        whole = np.block([[a, circulant(drift, bead)], [-circulant(spring, bead), a]])
        high = whole.astype(ml_dtypes.bfloat16)
        rest = whole - high.astype(np.float64)
        mid = rest.astype(ml_dtypes.bfloat16)
        low = (rest - mid.astype(np.float64)).astype(ml_dtypes.bfloat16)
        out.append(np.concatenate([high, high, mid, mid, high, low], axis=1))
    return np.stack(out)


def lane_tables(lanes, mols, slots):
    lane = lax.broadcasted_iota(jnp.int32, lanes.shape, 1)
    unit = jnp.where(lane < mols, charge_oxygen / charge_hydrogen, 1.0)
    return jnp.where(lanes < slots, unit, 0.0)


def permuted(rows, perm):
    n = rows.shape[0]
    stacked = jnp.concatenate(split3(rows), axis=0).astype(BF16)
    moved = dot_nn(stacked, perm)
    return moved[:n] + moved[n : 2 * n] + moved[2 * n :]


def unpermuted(rows, perm):
    n = rows.shape[0]
    stacked = jnp.concatenate(split3(rows), axis=0).astype(BF16)
    moved = dot_nt(stacked, perm)
    return moved[:n] + moved[n : 2 * n] + moved[2 * n :]


def order_kernel(lb, cells, mols, slots, mol_hbm, x_hbm, p_hbm, *refs):
    xo, po, perm_ref, q_ref, to_right, to_left = refs[:6]
    mol_ref, x_ref, p_ref, wide, sems = refs[6:]
    copies = [
        pltpu.make_async_copy(source, dest, sems.at[i])
        for i, (source, dest) in enumerate(
            ((mol_hbm, mol_ref), (x_hbm, x_ref), (p_hbm, p_ref))
        )
    ]
    for copy in copies:
        copy.start()
    row = lax.broadcasted_iota(jnp.int32, (slots, slots), 0)
    col = lax.broadcasted_iota(jnp.int32, (slots, slots), 1)
    upper = (row < col).astype(F32).astype(BF16)
    rows, row = row, row.astype(F32)
    lane = lax.broadcasted_iota(jnp.int32, (cells, slots), 1)
    far = 4.0 * slots
    wide[...] = jnp.full(wide.shape, slots, jnp.int32)
    copies[0].wait()
    for t in range(3):
        wide[t, :, :mols] = mol_ref[t]
    lanes = jnp.where(
        lane < mols,
        wide[0],
        jnp.where(lane < 2 * mols, pltpu.roll(wide[1], mols, 1), pltpu.roll(wide[2], 2 * mols, 1)),
    )
    lanes = jnp.where(lane < 3 * mols, lanes, slots)
    charges = lane_tables(lanes, mols, slots)
    q_ref[...] = charges
    free = lanes >= slots
    key = jnp.where(
        free, far + dot_nn(free.astype(F32).astype(BF16), upper), lanes.astype(F32)
    )
    ones = jnp.ones((slots, slots), BF16)
    used = jnp.zeros((slots, slots), F32)
    for cell in range(cells):
        held = (row == key[cell : cell + 1]).astype(F32).astype(BF16)
        used = jnp.where(col == cell, dot_nn(held, ones), used)
    rank = dot_nn((col < rows).astype(F32).astype(BF16), (1.0 - used).astype(BF16))
    slot_key = jnp.where(used > 0.5, row, far + rank)
    copies[1].wait()
    copies[2].wait()
    n = 3 * lb
    for cell in range(cells):
        slot_column = jnp.broadcast_to(slot_key[:, cell : cell + 1], (slots, slots))
        perm = (slot_column == key[cell : cell + 1]).astype(F32).astype(BF16)
        perm_ref[cell] = perm
        atoms = [
            ref[pl.ds(comp * cells + cell, lb, stride=3 * cells), :]
            for ref in (x_ref, p_ref)
            for comp in range(3)
        ]
        moved = permuted(jnp.concatenate(atoms, axis=0), perm)
        xo[cell] = moved[:n]
        po[cell] = moved[n:]
    write_ends(to_right, to_left, xo, charges, lb, cells, slots)


def write_ends(to_right, to_left, xs, charges, lb, cells, slots):
    for out, cell in ((to_right, cells - 1), (to_left, 0)):
        out[3 * lb :, :] = jnp.zeros((8, slots), F32)
        out[pl.ds(0, 3 * lb), :] = xs[cell]
        out[pl.ds(3 * lb, 1), :] = charges[cell : cell + 1, :]


def put_tiles(scratch, first, count, rows):
    for index, value in rows:
        scratch[pl.ds(first * 8 + index, count, stride=8), :] = value


OFFSETS = (-1.0, 0.0, 1.0)


def build_tiles(tiles, first, count, x, y, z):
    x, y, z = two_part(x - 0.5), two_part(y - 0.5), two_part(z - 0.5)
    norm = x * x + y * y + z * z + 0.5 * coulomb_soft
    high = two_part(norm)
    low = norm - high
    put_tiles(
        tiles, first, count, ((0, x), (1, y), (2, z), (3, high), (4, low), (5, high), (6, low))
    )


def store_shapes(count, beads, slots):
    n = count * beads
    return (
        [((n * 8, slots), F32), ((n // 2, slots, 64), BF16)]
        + [((n // 2, 32, slots), BF16)] * 3
        + [((n, 32, slots), BF16)]
    )


STORE = 6


class Store:
    def __init__(self, refs, beads):
        self.tiles, self.peers, *sums, self.targets = refs
        self.sums = sums
        self.beads = beads


def tile_of(ref, n):
    return ref[pl.ds(pl.multiple_of(n * 8, 8), 8), :]


def prepare(store, charges, count, slots):
    tiles, beads = store.tiles, store.beads
    row8 = lax.broadcasted_iota(jnp.int32, (8, slots), 0)
    place, norms = row8 < 3, row8 < 5
    target_rows = place | (row8 == 5) | (row8 == 6)
    ones_low = jnp.where((row8 == 3) | (row8 == 4), 1.0, 0.0)
    ones_high = jnp.where((row8 == 5) | (row8 == 6), 1.0, 0.0)
    ones_last = jnp.where(row8 == 7, 1.0, 0.0)
    pairs = beads // 2
    total = count * pairs
    unroll = max(n for n in range(1, min(16, max(total // 4, 4)) + 1) if total % n == 0)

    def stack(values):
        return jnp.concatenate(values, axis=0).astype(BF16)

    def step(index, carry):
        for u in range(unroll):
            m = index * unroll + u
            charge = charges[lax.div(m, pairs)]
            units = [
                jnp.where(row8 == 3, charge, jnp.where(row8 == 4, offset * charge, 0.0))
                for offset in OFFSETS
            ]
            left, high_rows, mid_rows = [], [], []
            for h in range(2):
                value = tile_of(tiles, 2 * m + h)
                high = rounded(value)
                mid = value - high
                x_high, x_mid = high[0:1], mid[0:1]
                left_high = jnp.where(place, -2.0 * high, jnp.where(norms, high, ones_high))
                left_mid = jnp.where(place, -2.0 * mid, jnp.where(norms, mid, 0.0))
                left_last = jnp.where(
                    place,
                    -2.0 * mid,
                    jnp.where(
                        row8 == 3,
                        2.0 * x_high,
                        jnp.where(row8 == 4, 2.0 * x_mid, ones_last - 2.0 * ones_high),
                    ),
                )
                left += [left_high, left_high, left_mid, left_last]
                right_high = jnp.where(target_rows, high, ones_low)
                right_mid = jnp.where(target_rows, mid, 0.0)
                right_last = jnp.where(
                    place,
                    mid,
                    jnp.where(
                        row8 == 5, x_high, jnp.where(row8 == 6, x_mid, ones_low + ones_last)
                    ),
                )
                store.targets[2 * m + h] = stack([right_high, right_mid, right_high, right_last])
                high_rows.append(high * charge)
                mid_rows.append(jnp.where(place, mid * charge, 0.0))
            store.peers[m] = stack(left).T
            for o in range(3):
                rows = []
                for h in range(2):
                    rows += [jnp.where(place, high_rows[h], units[o]), mid_rows[h]]
                store.sums[o][m] = stack(rows)
        return carry

    lax.fori_loop(0, total // unroll, step, 0)


class PairLoop:
    def __init__(self, mols, slots, beads, keep):
        self.mols, self.slots, self.keep = mols, slots, keep
        self.pairs = beads // 2
        self.unroll = min(self.pairs, 4)
        self.per_cell = self.pairs // self.unroll
        orows = -(-mols // 8) * 8
        self.row8 = lax.broadcasted_iota(jnp.int32, (8, slots), 0)
        lj_row = lax.broadcasted_iota(jnp.int32, (orows, slots), 0)
        lj_lane = lax.broadcasted_iota(jnp.int32, (orows, slots), 1)
        self.first_lanes, self.second_lanes = lj_lane < mols, lj_lane < 2 * mols
        self.corner = (lj_row < mols) & self.first_lanes

        i = lax.broadcasted_iota(jnp.int32, (slots, slots), 0)
        j = lax.broadcasted_iota(jnp.int32, (slots, slots), 1)
        i = jnp.where(i >= 2 * mols, i - 2 * mols, jnp.where(i >= mols, i - mols, i))
        j = jnp.where(j >= 2 * mols, j - 2 * mols, jnp.where(j >= mols, j - mols, j))
        keep[...] = (i != j).astype(F32)

        lane64 = lax.broadcasted_iota(jnp.int32, (slots, 64), 1) & 31
        odd = (lane64 >= 27) & (lane64 < 31)
        even = lane64 == 31
        self.signs = [
            jnp.where(odd, -1.0, 1.0).astype(BF16),
            jnp.where(odd | even, 0.0, 1.0).astype(BF16),
            None,
        ]
        self.zero = jnp.zeros((32, slots), BF16)

    def pair(self, peers, charge):
        mols, slots = self.mols, self.slots
        orows = self.corner.shape[0]
        pair_scale = coulomb_scale * charge_hydrogen * charge_hydrogen
        k3 = sigma_square**3
        ratio = (charge_hydrogen / charge_oxygen) ** 2 / pair_scale
        lj_a = 24.0 * well_depth * 2.0 * k3 * k3 * ratio
        lj_b = 24.0 * well_depth * k3 * ratio
        zero = self.zero
        own, m = peers[1]
        left = jnp.concatenate(
            [
                store.peers[index] if sign is None else store.peers[index] * sign
                for (store, index), sign in zip(peers, self.signs)
            ],
            axis=0,
        )
        right = jnp.concatenate(
            [
                jnp.concatenate([own.targets[2 * m], zero], axis=1),
                jnp.concatenate([zero, own.targets[2 * m + 1]], axis=1),
            ],
            axis=0,
        )
        squares = dot_nn(left, right)
        blocks = [[], [], []]
        for h in range(2):
            lanes = slice(h * slots, (h + 1) * slots)
            near = [squares[o * slots : o * slots + orows, lanes] for o in range(3)]
            packed = jnp.where(
                self.first_lanes,
                near[0],
                jnp.where(
                    self.second_lanes,
                    pltpu.roll(near[1], mols, 1),
                    pltpu.roll(near[2], 2 * mols, 1),
                ),
            )
            root = lax.rsqrt(packed + (lennard_soft - coulomb_soft))
            inverse = root * root
            cube = inverse * inverse * inverse
            lj = (cube * lj_a - lj_b) * (cube * inverse)
            for o in range(3):
                root = lax.rsqrt(squares[o * slots : (o + 1) * slots, lanes])
                strength = root * root * root
                part = pltpu.roll(lj, slots - o * mols, 1) if o else lj
                strength = jnp.concatenate(
                    [strength[:orows] + jnp.where(self.corner, part, 0.0), strength[orows:]],
                    axis=0,
                )
                if o == 1:
                    strength = strength * self.keep[...]
                high = strength.astype(BF16)
                low = (strength - high.astype(F32)).astype(BF16)
                blocks[o].append(jnp.concatenate([high, low], axis=0))
        sums = None
        for o, (store, index) in enumerate(peers):
            weights = store.sums[o][index]
            value = dot_nn(
                jnp.concatenate([weights, weights], axis=1), jnp.concatenate(blocks[o], axis=1)
            )
            sums = value if sums is None else sums + value
        scale = charge * pair_scale
        out = []
        for h in range(2):
            part = sums[16 * h : 16 * h + 16, h * slots : (h + 1) * slots]
            total = part[0:8] + part[8:16]
            total = total + jnp.where(self.row8 == 0, total[4:5], 0.0)
            out.append((tile_of(own.tiles, 2 * m + h) * total[3:4] - total) * scale)
        return out

    def cells(self, store, charges, first, last, forces, limit):
        total = (last - first) * self.pairs
        unroll = max(n for n in range(1, limit + 1) if total % n == 0)

        def step(index, carry):
            for u in range(unroll):
                m = index * unroll + u
                at = m + first * self.pairs
                peers = [(store, at + (o - 1) * self.pairs) for o in range(3)]
                out = self.pair(peers, charges[lax.div(at, self.pairs)])
                for h in range(2):
                    n = 2 * m + h
                    forces[pl.ds(pl.multiple_of(n * 8, 8), 8), :] = out[h]
            return carry

        lax.fori_loop(0, total // unroll, step, 0)


def read_force(forces, w, beads, comp):
    return forces[pl.ds(w * beads * 8 + comp, beads, stride=8), :]


def own_kernel(cells, lb, slots, x_ref, q_ref, *refs):
    store = Store(refs, lb)
    for w in range(cells):
        rows = x_ref[w]
        build_tiles(store.tiles, w * lb, lb, rows[:lb], rows[lb : 2 * lb], rows[2 * lb :])
    prepare(store, Rows(q_ref, 0), cells, slots)


def interior_kernel(cells, lb, mols, slots, q_ref, *refs):
    store = Store(refs[:STORE], lb)
    forces, keep = refs[STORE:]
    PairLoop(mols, slots, lb, keep).cells(store, Rows(q_ref, 0), 1, cells - 1, forces, 64)


def edge_forces(cells, lb, mols, slots, x_ref, q_ref, left, right, inner, own, scratch):
    forces, keep = scratch[:2]
    halo = Store(scratch[2:], lb)
    n = 3 * lb
    charge = [left[pl.ds(n, 1), :], right[pl.ds(n, 1), :]]
    for e, edge in enumerate((left, right)):
        rows = edge[pl.ds(0, n), :]
        build_tiles(halo.tiles, e * lb, lb, rows[:lb], rows[lb : 2 * lb], rows[2 * lb :])

    class Edges:
        def __getitem__(self, e):
            return jnp.where(e == 0, charge[0], charge[1])

    prepare(halo, Edges(), 2, slots)
    loop = PairLoop(mols, slots, lb, keep)
    last = cells - 1
    near = (
        (0, ((halo, 0), (own, 0), (own, 1))),
        (last, ((own, last - 1), (own, last), (halo, 1))),
    )
    for e, (cell, stores) in enumerate(near):
        for pair in range(loop.pairs):
            peers = [(store, at * loop.pairs + pair) for store, at in stores]
            out = loop.pair(peers, q_ref[cell : cell + 1, :])
            for h in range(2):
                forces[pl.ds((e * lb + 2 * pair + h) * 8, 8), :] = out[h]

    def read(w):
        source, at = (inner, w - 1) if 0 < w < last else (forces, 0 if w == 0 else 1)
        return jnp.concatenate([read_force(source, at, lb, c) for c in range(3)], axis=0)

    return read


def kick_kernel(nb, group, lb, cells, mols, slots, b_ref, *refs):
    x_ref, p_ref, q_ref, left, right, inner = refs[:6]
    own = Store(refs[6 : 6 + STORE], lb)
    outs = refs[6 + STORE : 6 + STORE + nb]
    kicked, *scratch = refs[6 + STORE + nb :]
    read = edge_forces(cells, lb, mols, slots, x_ref, q_ref, left, right, inner, own, scratch)
    n = 3 * lb
    for w in range(cells):
        kicked[w] = p_ref[w] + (0.5 * outer_step) * read(w)
    for i, k in enumerate(block_order(nb)):
        first = jnp.bitwise_xor(b_ref[0], k) * group
        for w in range(group):
            outs[i][pl.ds(w * n, n), :] = x_ref[first + w]
            outs[i][pl.ds((group + w) * n, n), :] = kicked[first + w]


def gather_kernel(nb, group, lb, cells, slots, b_ref, *refs):
    blocks, q_ref = refs[:nb], refs[nb]
    xs, ps, to_right, to_left = refs[nb + 1 :]
    n = 3 * lb
    for k in range(nb):
        first = jnp.bitwise_xor(b_ref[0], k) * group
        for w in range(group):
            xs[first + w] = blocks[k][pl.ds(w * n, n), :]
            ps[first + w] = blocks[k][pl.ds((group + w) * n, n), :]
    write_ends(to_right, to_left, xs, q_ref, lb, cells, slots)


def final_kernel(cells, lb, mols, slots, *refs):
    x_ref, p_ref, q_ref, left, right, inner, perm_ref = refs[:7]
    own = Store(refs[7 : 7 + STORE], lb)
    outs, scratch = refs[7 + STORE : 9 + STORE], refs[9 + STORE :]
    read = edge_forces(cells, lb, mols, slots, x_ref, q_ref, left, right, inner, own, scratch)
    for w in range(cells):
        state = jnp.concatenate([x_ref[w], p_ref[w] + (0.5 * outer_step) * read(w)], axis=0)
        state = unpermuted(state, perm_ref[w])
        for a in range(2):
            for c in range(3):
                row = (a * 3 + c) * lb
                outs[a][pl.ds(c * cells + w, lb, stride=3 * cells), :] = state[row : row + lb]


class Rows:
    def __init__(self, ref, first):
        self.ref, self.first = ref, first

    def __getitem__(self, index):
        return self.ref[pl.ds(self.first + index, 1), :]


def bond_forces(x, y, z, used, mols, slots):
    def partner(a, t):
        return pltpu.roll(a, slots - t * mols, 1)

    first = [a - partner(a, 1) for a in (x, y, z)]
    second = [a - partner(a, 2) for a in (x, y, z)]
    third = [s - f for f, s in zip(first, second)]

    def pull(bond, stiffness, square):
        length = bond[0] * bond[0] + bond[1] * bond[1] + bond[2] * bond[2]
        return (stiffness * used) * (length - square)

    c1 = pull(first, bond_stiffness, bond_square)
    c2 = pull(second, bond_stiffness, bond_square)
    c3 = pull(third, angle_stiffness, angle_square)
    out = []
    for f, s, t in zip(first, second, third):
        on_first = c1 * f - c3 * t
        on_second = c2 * s + c3 * t
        on_oxygen = -(c1 * f + c2 * s)
        out.append(
            on_oxygen + pltpu.roll(on_first, mols, 1) + pltpu.roll(on_second, 2 * mols, 1)
        )
    return out


def steps_kernel(nb, group, lb, mols, slots, b_ref, *refs):
    blocks = refs[:nb]
    step_ref, q_ref = refs[nb : nb + 2]
    outs = refs[nb + 2 :]
    beads = nb * lb
    n = 3 * lb
    b = b_ref[0]
    step = step_ref[b]
    charges = Rows(q_ref, b * group)

    def advance(states):
        flat = [
            jnp.concatenate([x, v], axis=0) for pos, vel in states for x, v in zip(pos, vel)
        ]
        high, mid, low = split3(jnp.concatenate(flat, axis=1))
        stacked = jnp.concatenate([high, mid, high, mid, low, high], axis=0).astype(BF16)
        new = dot_nn(step, stacked)
        out = []
        for i in range(len(states)):
            columns = [
                new[:, (3 * i + c) * slots : (3 * i + c + 1) * slots] for c in range(3)
            ]
            out.append(([a[:beads] for a in columns], [a[beads:] for a in columns]))
        return out

    def gather(w, a, comp):
        return jnp.concatenate(
            [block[pl.ds((a * group + w) * n + comp * lb, lb), :] for block in blocks], axis=0
        )

    def kick(state, oxygen, scale):
        pos, vel = state
        force = bond_forces(*pos, oxygen, mols, slots)
        return pos, [v + scale * f for v, f in zip(vel, force)]

    for first in range(0, group, 2):
        members = range(first, min(first + 2, group))
        charge = [charges[w] for w in members]
        oxygen = [(q < -1.5).astype(F32) for q in charge]
        inverse = [jnp.where(q < -1.5, 1.0 / oxygen_mass, 1.0) for q in charge]
        states = [
            (
                [gather(w, 0, c) for c in range(3)],
                [gather(w, 1, c) * scale for c in range(3)],
            )
            for w, scale in zip(members, inverse)
        ]
        for part in (0.5, 1.0):
            states = [
                kick(state, o, (part * inner_step) * scale)
                for state, o, scale in zip(states, oxygen, inverse)
            ]
            states = advance(states)
        for w, state, q, o, scale in zip(members, states, charge, oxygen, inverse):
            pos, vel = kick(state, o, (0.5 * inner_step) * scale)
            mass = jnp.where(q < -1.5, oxygen_mass, 1.0)
            for a, values in enumerate((pos, [v * mass for v in vel])):
                for c in range(3):
                    for i, k in enumerate(block_order(nb)):
                        rows = values[c][i * lb : (i + 1) * lb]
                        outs[k][pl.ds((a * group + w) * n + c * lb, lb), :] = rows


def call(kernel, outs, scratch, scalar, *operands, space=pltpu.VMEM):
    vmem = pl.BlockSpec(memory_space=pltpu.VMEM)
    smem = pl.BlockSpec(memory_space=pltpu.SMEM)
    return pl.pallas_call(
        kernel,
        out_shape=outs,
        in_specs=([] if scalar is None else [smem]) + [pl.BlockSpec(memory_space=space)] * len(operands),
        out_specs=[vmem] * len(outs),
        scratch_shapes=scratch,
        compiler_params=pltpu.CompilerParams(vmem_limit_bytes=24 * 1024 * 1024),
    )(*(() if scalar is None else (scalar,)), *operands)


def exchange(blocks, order):
    return [
        lax.ppermute(block, "bead", [(i, i ^ k) for i in range(len(order))]) if k else block
        for block, k in zip(blocks, order)
    ]


def local(nb, ns, positions, momenta, molecules):
    lb, _, cells, slots = positions.shape
    mols = molecules.shape[1]
    group = cells // nb
    beads = lb * nb
    b = lax.axis_index("bead").astype(jnp.int32).reshape(1)

    def shape(*dims):
        return jax.ShapeDtypeStruct(dims, F32)

    rows = lb * 3 * cells
    state = [shape(cells, 3 * lb, slots)] * 2
    ends = [shape(3 * lb + 8, slots)] * 2
    blocks = [shape(2 * group * 3 * lb, slots)] * nb
    store = [jax.ShapeDtypeStruct(*entry) for entry in store_shapes(cells, lb, slots)]
    keep = pltpu.VMEM((slots, slots), F32)
    edge_scratch = [pltpu.VMEM((2 * lb * 8, slots), F32), keep] + [
        pltpu.VMEM(*entry) for entry in store_shapes(2, lb, slots)
    ]

    def halos(to_right, to_left):
        left = lax.ppermute(to_right, "space", [(s, (s + 1) % ns) for s in range(ns)])
        right = lax.ppermute(to_left, "space", [(s, (s - 1) % ns) for s in range(ns)])
        return left, right

    def inside(xs, charges):
        own = call(
            functools.partial(own_kernel, cells, lb, slots), store, [], None, xs, charges
        )
        (inner,) = call(
            functools.partial(interior_kernel, cells, lb, mols, slots),
            [shape((cells - 2) * lb * 8, slots)],
            [keep],
            None,
            charges,
            *own,
        )
        return own, inner

    xs, ps, perm, charges, to_right, to_left = call(
        functools.partial(order_kernel, lb, cells, mols, slots),
        state
        + [jax.ShapeDtypeStruct((cells, slots, slots), BF16), shape(cells, slots)]
        + ends,
        [
            pltpu.VMEM((3, cells, mols), jnp.int32),
            pltpu.VMEM((rows, slots), F32),
            pltpu.VMEM((rows, slots), F32),
            pltpu.VMEM((3, cells, slots), jnp.int32),
            pltpu.SemaphoreType.DMA((3,)),
        ],
        None,
        *(
            pltpu.with_memory_space_constraint(a, pltpu.HBM)
            for a in (
                jnp.transpose(molecules, (2, 0, 1)),
                positions.reshape(rows, slots),
                momenta.reshape(rows, slots),
            )
        ),
        space=pltpu.HBM,
    )
    left, right = halos(to_right, to_left)
    own, inner = inside(xs, charges)
    sent = call(
        functools.partial(kick_kernel, nb, group, lb, cells, mols, slots),
        blocks,
        [pltpu.VMEM((cells, 3 * lb, slots), F32)] + edge_scratch,
        b,
        xs,
        ps,
        charges,
        left,
        right,
        inner,
        *own,
    )
    stepped = call(
        functools.partial(steps_kernel, nb, group, lb, mols, slots),
        blocks,
        [],
        b,
        *exchange(sent, block_order(nb)),
        jnp.asarray(propagator(beads, lb)),
        charges,
    )
    xs, ps, to_right, to_left = call(
        functools.partial(gather_kernel, nb, group, lb, cells, slots),
        state + ends,
        [],
        b,
        *exchange(stepped, range(nb)),
        charges,
    )
    left, right = halos(to_right, to_left)
    own, inner = inside(xs, charges)
    new_x, new_p = call(
        functools.partial(final_kernel, cells, lb, mols, slots),
        [shape(rows, slots)] * 2,
        edge_scratch,
        None,
        xs,
        ps,
        charges,
        left,
        right,
        inner,
        perm,
        *own,
    )
    return new_x.reshape(positions.shape), new_p.reshape(positions.shape)


def solution(mesh):
    spec = P("bead", None, "space", None)
    return jax.shard_map(
        functools.partial(local, mesh.shape["bead"], mesh.shape["space"]),
        mesh=mesh,
        in_specs=(spec, spec, P("space", None, None)),
        out_specs=(spec, spec),
        check_vma=False,
    )
```
